32 devices in a mesh: rec: 8 (over z, x), feat: 4 (over y, core).
Axes of the slice: x: 2, y: 2, z: 4, core: 2. Of those that a mesh axis runs over, the one named last changes fastest.
Arguments:
- records: bfloat16 [12288, 3072], P('rec'), may hold values from -4 to 4
- real_labels: int32 [12288], P('rec'), may hold values from 0 to 255
- frequencies: bfloat16 [3072, 8192], P(None, 'feat'), may hold values from -0.109375 to 0.109375
- class_noise: float32 [256, 2, 8192], P(None, None, 'feat'), may hold values from -48 to 48
- latents: bfloat16 [1024, 128], P('rec'), may hold values from -5 to 5
- syn_labels: int32 [1024], P('rec'), may hold values from 0 to 255
- w_latent: bfloat16 [128, 2048], replicated, may hold values from -0.5 to 0.5
- class_embed: bfloat16 [256, 2048], replicated, may hold values from -5 to 5
- w_out: bfloat16 [2048, 3072], P(None, 'feat'), may hold values from -0.125 to 0.125
Outputs:
- grad_w_out: float32 [2048, 3072], P('rec', 'feat')
- grad_w_latent: float32 [128, 2048], P(None, 'rec')
- grad_embed: float32 [256, 2048], P(None, 'rec')
The draws below stay inside these ranges and needn't reach their ends.
All inputs are finite; a program needn't handle non-finite values.
Results may differ from the reference program's by a relative error of at most 0.0053.
Values may be sent and summed in bfloat16 or wider, within the bound.
No kernel may reach another device: no remote copies, remote signals or barrier semaphores. Data moves between devices by JAX's collectives and lax.ppermute only.
A program may use at most 128 MiB of HBM per device.

```python
import jax
import jax.numpy as jnp
from jax import lax

IMG = 3072
NF = 8192
C = 256
H = 2048
DZ = 128
REC_DEV = 1536
NR = 12288
NS = 1024
N_REC = 8


def plant(array, key, low, largest):
    dims = array.shape
    index_at = [jax.random.randint(jax.random.fold_in(key, axis), (), 0, dims[axis]) for axis in range(len(dims))]
    array = array.at[tuple(index_at)].set(low)
    longest = dims.index(max(dims))
    index_at[longest] = (index_at[longest] + 1) % dims[longest]
    return array.at[tuple(index_at)].set(largest)


def levels(own_key, shape, cuts, least, largest):
    gain = 1.0
    for dim, shards_of in cuts:
        draws = jax.random.uniform(jax.random.fold_in(jax.random.fold_in(own_key, 6), dim), (shards_of,), jnp.float32, least / len(cuts), largest / len(cuts))
        gain = gain * jnp.repeat(jnp.exp(draws), shape[dim] // shards_of).reshape((-1,) + (1,) * (len(shape) - 1 - dim))
    return gain


def normal_values(rng, extent, scale, most, cuts=(), kind=jnp.bfloat16):
    array = scale * jax.random.normal(rng, extent, jnp.float32)
    if cuts:
        array = array * levels(rng, extent, cuts, -0.22, 0.18)
    return jnp.clip(array, -most, most).astype(kind)


def setup_inputs(seed: int = 0) -> dict:
    keys = jax.random.split(jax.random.key(seed), 10)
    return {
        "records": normal_values(keys[0], (NR, IMG), 1.0, 4.0, ((0, 8),)),
        "real_labels": plant(jax.random.randint(keys[1], (NR,), 0, C), jax.random.fold_in(keys[1], 1), 0, C - 1).astype(jnp.int32),
        "frequencies": normal_values(keys[2], (IMG, NF), IMG ** -0.5, 0.109375, ((1, 4),)),
        "class_noise": normal_values(keys[3], (C, 2, NF), 8.0, 48.0, ((2, 4),), jnp.float32),
        "latents": normal_values(keys[4], (NS, DZ), 1.0, 5.0, ((0, 8),)),
        "syn_labels": plant(jax.random.randint(keys[5], (NS,), 0, C), jax.random.fold_in(keys[5], 1), 0, C - 1).astype(jnp.int32),
        "w_latent": normal_values(keys[6], (DZ, H), DZ ** -0.5, 0.5),
        "class_embed": normal_values(keys[7], (C, H), 1.0, 5.0),
        "w_out": normal_values(keys[8], (H, IMG), H ** -0.5, 0.125, ((1, 4),)),
    }


def one_hot(labels, count, dtype):
    return (labels[:, None] == jnp.arange(count, dtype=jnp.int32)[None, :]).astype(dtype)


def class_sums(pre, labels):
    phi = jnp.concatenate([jnp.cos(pre), jnp.sin(pre)], axis=1).astype(jnp.bfloat16)
    table = one_hot(labels, C, jnp.bfloat16)
    return jnp.dot(table.T, phi, preferred_element_type=jnp.float32)


def reference(records, real_labels, frequencies, class_noise, latents, syn_labels, w_latent, class_embed, w_out):
    record_blocks = records.reshape(N_REC, REC_DEV, IMG)
    label_blocks = real_labels.reshape(N_REC, REC_DEV)

    def add_block(total, block):
        pre = jnp.dot(block[0], frequencies, preferred_element_type=jnp.float32)
        return total + class_sums(pre, block[1]), None

    real_sum, _ = lax.scan(add_block, jnp.zeros((C, 2 * NF), jnp.float32), (record_blocks, label_blocks))
    syn_table = one_hot(syn_labels, C, jnp.bfloat16)
    preact = jnp.dot(latents, w_latent, preferred_element_type=jnp.float32) + jnp.dot(syn_table, class_embed, preferred_element_type=jnp.float32)
    hidden = jnp.maximum(preact, 0.0).astype(jnp.bfloat16)
    images = jnp.tanh(jnp.dot(hidden, w_out, preferred_element_type=jnp.float32)).astype(jnp.bfloat16)
    syn_pre = jnp.dot(images, frequencies, preferred_element_type=jnp.float32)
    syn_sum = class_sums(syn_pre, syn_labels)
    noise_flat = class_noise.reshape(C, 2 * NF)
    class_gap = syn_sum / NS - (real_sum + noise_flat) / NR
    feat_grad = 16.0 * jnp.dot(syn_table.astype(jnp.float32), class_gap, precision=lax.Precision.HIGHEST)
    pre_grad = (-jnp.sin(syn_pre) * feat_grad[:, :NF] + jnp.cos(syn_pre) * feat_grad[:, NF:]).astype(jnp.bfloat16)
    image_grad = jnp.dot(pre_grad, frequencies.T, preferred_element_type=jnp.float32)
    out_grad = (image_grad * (1.0 - jnp.square(images.astype(jnp.float32)))).astype(jnp.bfloat16)
    grad_w_out = jnp.dot(hidden.T, out_grad, preferred_element_type=jnp.float32)
    hidden_grad = jnp.dot(out_grad, w_out.T, preferred_element_type=jnp.float32)
    pre_hidden = jnp.where(preact > 0, hidden_grad, 0.0).astype(jnp.bfloat16)
    grad_w_latent = jnp.dot(latents.T, pre_hidden, preferred_element_type=jnp.float32)
    grad_embed = jnp.dot(syn_table.T, pre_hidden, preferred_element_type=jnp.float32)
    return (grad_w_out, grad_w_latent, grad_embed)
```

```python
import functools

import jax
import jax.numpy as jnp
from jax import lax
from jax.experimental import pallas as pl
from jax.experimental.pallas import tpu as pltpu
from jax.sharding import PartitionSpec as P

BF = jnp.bfloat16
F32 = jnp.float32

TURN = 0.15915494309189535
SIN = (4.44286783702217, -7.307441307726672, 3.59477116396636, -0.7843353598850176)
COS = (1.4142134962552275, -6.978850948563815, 5.739460376907241, -1.883557905986894, 0.3106880275267554)


def cos_sin(x):
    turns = x * TURN
    u = turns - jnp.round(turns)
    sq = u * u
    p = SIN[-1]
    for c in SIN[-2::-1]:
        p = p * sq + c
    q = COS[-1]
    for c in COS[-2::-1]:
        q = q * sq + c
    s = u * p
    return 1.0 - s * s, s * q


def one_hot(labels, count, dtype):
    return (labels[:, None] == jnp.arange(count, dtype=jnp.int32)[None, :]).astype(dtype)


def real_kernel(rows, labels_ref, records_ref, freq_ref, out_ref, table_ref):
    total = records_ref.shape[0]
    classes = table_ref.shape[0]
    owners, _, width = out_ref.shape
    part = width // 2

    @pl.when(pl.program_id(0) == 0)
    def _():
        ids = lax.broadcasted_iota(jnp.int32, (classes, total), 0)
        table_ref[...] = jnp.where(ids == labels_ref[...], 1.0, 0.0).astype(BF)

    freq = freq_ref[...]
    block = freq.shape[1]

    def sums(i, pre):
        co, si = cos_sin(pre)
        phi = jnp.concatenate([co.astype(BF), si.astype(BF)], axis=1)
        return jnp.dot(table_ref[:, i * rows : (i + 1) * rows], phi, preferred_element_type=F32)

    acc = None
    before = None
    steps = total // rows
    for i in range(steps + 1):
        pre = None
        if i < steps:
            pre = jnp.dot(records_ref[i * rows : (i + 1) * rows, :], freq, preferred_element_type=F32)
        if i > 0:
            d = sums(i - 1, before)
            acc = d if acc is None else acc + d
        before = pre
    for o in range(owners):
        out_ref[o, :, :part] = acc[:, o * part : (o + 1) * part]
        out_ref[o, :, part:] = acc[:, block + o * part : block + (o + 1) * part]


def real_sums(labels, records, freq, classes, owners):
    m, k = records.shape
    n = freq.shape[1]
    block = min(512, n)
    rows = 512
    part = n // owners
    per = block // part
    return pl.pallas_call(
        functools.partial(real_kernel, rows),
        grid=(n // block,),
        in_specs=[
            pl.BlockSpec((1, m), lambda j: (0, 0)),
            pl.BlockSpec((m, k), lambda j: (0, 0)),
            pl.BlockSpec((k, block), lambda j: (0, j)),
        ],
        out_specs=pl.BlockSpec((per, classes, 2 * part), lambda j: (j, 0, 0)),
        out_shape=jax.ShapeDtypeStruct((owners, classes, 2 * part), F32),
        scratch_shapes=[pltpu.VMEM((classes, m), BF)],
        compiler_params=pltpu.CompilerParams(vmem_limit_bytes=56 * 2**20),
        cost_estimate=pl.CostEstimate(
            flops=2 * m * n * (k + 2 * classes), bytes_accessed=2 * (m * k + k * n), transcendentals=0
        ),
    )(labels.reshape(1, m), records, freq)


def bits_of(n):
    return [1 << b for b in range(n.bit_length() - 1)]


def swap(x, axis, bit):
    n = lax.axis_size(axis)
    return lax.ppermute(x, axis, [(i, i ^ bit) for i in range(n)])


def pick(x, index, dim):
    return lax.dynamic_index_in_dim(x, index, dim, keepdims=False)


def halving(x, axis, order, count):
    me = lax.axis_index(axis)
    nbits = len(order)
    x = x.reshape((2,) * nbits + x.shape[1:])
    left = sorted(order, reverse=True)
    for bit in order:
        dim = left.index(bit)
        left.remove(bit)
        mine = (me // bit) % 2
        got = swap(pick(x, 1 - mine, dim).astype(BF), axis, bit)
        x = pick(x, mine, dim).astype(F32) + got.astype(F32)
    return x


def on_device(
    records, real_labels, frequencies, class_noise, latents, syn_labels, w_latent, class_embed, w_out
):
    classes = class_embed.shape[0]
    hid = class_embed.shape[1]
    groups = lax.axis_size("rec")
    feats = lax.axis_size("feat")
    rec = lax.axis_index("rec")
    nf = frequencies.shape[1]
    part = nf // groups
    rows, dz = latents.shape
    cols = w_out.shape[1]
    real_total = records.shape[0] * groups
    syn_total = rows * groups

    label_row = jnp.zeros((16, dz), BF).at[0, :].set(syn_labels.astype(BF))
    packed = jnp.concatenate([latents, label_row], axis=0)
    packed = lax.all_to_all(
        jnp.broadcast_to(packed[None], (groups,) + packed.shape), "rec", 0, 0, tiled=True
    )
    all_latents = packed[:, :rows].reshape(syn_total, dz)
    all_labels = packed[:, rows].reshape(syn_total).astype(jnp.int32)
    all_table = one_hot(all_labels, classes, BF)

    table = one_hot(syn_labels, classes, BF)
    preact = jnp.dot(latents, w_latent, preferred_element_type=F32) + jnp.dot(
        table, class_embed, preferred_element_type=F32
    )
    hidden = jnp.maximum(preact, 0.0).astype(BF)
    own_images = jnp.tanh(jnp.dot(hidden, w_out, preferred_element_type=F32)).astype(BF)
    images = lax.all_gather(own_images, "feat", axis=0)
    images = images.transpose(1, 0, 2).reshape(rows, feats * cols)
    syn_pre = jnp.dot(images, frequencies, preferred_element_type=F32)
    syn_cos, syn_sin = cos_sin(syn_pre)
    syn_phi = jnp.concatenate(
        [syn_cos.reshape(rows, groups, part), syn_sin.reshape(rows, groups, part)], axis=2
    ).astype(BF)
    syn_sum = lax.dot_general(
        table, syn_phi.reshape(rows, 2 * nf), (((0,), (0,)), ((), ())), preferred_element_type=F32
    )
    syn_sum = syn_sum.reshape(classes, groups, 2 * part).transpose(1, 0, 2)

    real_sum = real_sums(real_labels, records, frequencies, classes, groups)
    gap = syn_sum * (1.0 / syn_total) - real_sum * (1.0 / real_total)
    half = classes // 2
    order = bits_of(groups)
    other = [order[1], order[0]] + order[2:]
    gap = jnp.concatenate(
        [halving(gap[:, :half], "rec", order, groups), halving(gap[:, half:], "rec", other, groups)], axis=0
    )
    noise = lax.dynamic_slice_in_dim(class_noise, rec * part, part, 2).reshape(classes, 2 * part)
    gap = (16.0 * (gap - noise * (1.0 / real_total))).astype(BF)

    feat_grad = jnp.dot(all_table, gap, preferred_element_type=F32).astype(BF)
    feat_grad = lax.all_to_all(feat_grad.reshape(groups, rows, 2 * part), "rec", 0, 0, tiled=True)
    feat_grad = feat_grad.transpose(1, 0, 2).astype(F32)
    pre_grad = (
        -syn_sin.reshape(rows, groups, part) * feat_grad[:, :, :part]
        + syn_cos.reshape(rows, groups, part) * feat_grad[:, :, part:]
    )
    pre_grad = pre_grad.astype(BF).reshape(rows, nf)
    image_grad = lax.dot_general(
        frequencies, pre_grad, (((1,), (1,)), ((), ())), preferred_element_type=F32
    )
    image_grad = halving(image_grad.reshape(feats, cols, rows), "feat", bits_of(feats), feats)
    image_grad = image_grad.T
    out_grad = (image_grad * (1.0 - jnp.square(own_images.astype(F32)))).astype(BF)

    out_grad = lax.all_to_all(
        jnp.broadcast_to(out_grad[None], (groups, rows, cols)), "rec", 0, 0, tiled=True
    ).reshape(syn_total, cols)

    mine = hid // groups
    start = rec * mine
    all_preact = jnp.dot(
        all_latents, lax.dynamic_slice_in_dim(w_latent, start, mine, 1), preferred_element_type=F32
    ) + jnp.dot(
        all_table, lax.dynamic_slice_in_dim(class_embed, start, mine, 1), preferred_element_type=F32
    )
    all_hidden = jnp.maximum(all_preact, 0.0).astype(BF)
    grad_w_out = lax.dot_general(
        all_hidden, out_grad, (((0,), (0,)), ((), ())), preferred_element_type=F32
    )
    hidden_grad = lax.dot_general(
        out_grad,
        lax.dynamic_slice_in_dim(w_out, start, mine, 0),
        (((1,), (1,)), ((), ())),
        preferred_element_type=F32,
    )
    core = lax.axis_index("feat") % 2
    half = syn_total // 2
    hidden_grad = hidden_grad.reshape(2, half, mine)
    got = swap(pick(hidden_grad, 1 - core, 0).astype(BF), "feat", 1)
    hidden_grad = pick(hidden_grad, core, 0) + got.astype(F32)
    for bit in bits_of(feats)[1:]:
        send = hidden_grad.astype(BF)
        hidden_grad = send.astype(F32) + swap(send, "feat", bit).astype(F32)
    my_preact = lax.dynamic_slice_in_dim(all_preact, core * half, half, 0)
    pre_hidden = jnp.where(my_preact > 0, hidden_grad, 0.0).astype(BF)
    lhs = jnp.concatenate([all_latents, all_table], axis=1)
    lhs = lax.dynamic_slice_in_dim(lhs, core * half, half, 0)
    grads = lax.dot_general(lhs, pre_hidden, (((0,), (0,)), ((), ())), preferred_element_type=F32)
    grads = grads + swap(grads, "feat", 1)
    return grad_w_out, grads[:dz], grads[dz:]


def solution(mesh):
    in_specs = (
        P("rec", None),
        P("rec"),
        P(None, "feat"),
        P(None, None, "feat"),
        P("rec", None),
        P("rec"),
        P(),
        P(),
        P(None, "feat"),
    )
    out_specs = (P("rec", "feat"), P(None, "rec"), P(None, "rec"))
    return jax.shard_map(
        on_device, mesh=mesh, in_specs=in_specs, out_specs=out_specs, check_vma=False
    )
```

```python
import functools

import jax
import jax.numpy as jnp
from jax import lax
from jax.experimental import pallas as pl
from jax.experimental.pallas import tpu as pltpu
from jax.sharding import PartitionSpec as P

BF = jnp.bfloat16
F32 = jnp.float32

TURN = 0.15915494309189535
SIN = (4.44286783702217, -7.307441307726672, 3.59477116396636, -0.7843353598850176)
COS = (1.4142134962552275, -6.978850948563815, 5.739460376907241, -1.883557905986894, 0.3106880275267554)


def cos_sin(x):
    turns = x * TURN
    u = turns - jnp.round(turns)
    sq = u * u
    p = SIN[-1]
    for c in SIN[-2::-1]:
        p = p * sq + c
    q = COS[-1]
    for c in COS[-2::-1]:
        q = q * sq + c
    s = u * p
    return 1.0 - s * s, s * q


def one_hot(labels, count, dtype):
    return (labels[:, None] == jnp.arange(count, dtype=jnp.int32)[None, :]).astype(dtype)


def real_kernel(rows, labels_ref, records_ref, freq_ref, out_ref, table_ref):
    total = records_ref.shape[0]
    classes = table_ref.shape[0]
    owners, _, width = out_ref.shape
    part = width // 2

    @pl.when(pl.program_id(0) == 0)
    def _():
        ids = lax.broadcasted_iota(jnp.int32, (classes, total), 0)
        table_ref[...] = jnp.where(ids == labels_ref[...], 1.0, 0.0).astype(BF)

    freq = freq_ref[...]
    block = freq.shape[1]

    def sums(i, pre):
        co, si = cos_sin(pre)
        phi = jnp.concatenate([co.astype(BF), si.astype(BF)], axis=1)
        return jnp.dot(table_ref[:, i * rows : (i + 1) * rows], phi, preferred_element_type=F32)

    acc = None
    before = None
    steps = total // rows
    for i in range(steps + 1):
        pre = None
        if i < steps:
            pre = jnp.dot(records_ref[i * rows : (i + 1) * rows, :], freq, preferred_element_type=F32)
        if i > 0:
            d = sums(i - 1, before)
            acc = d if acc is None else acc + d
        before = pre
    for o in range(owners):
        out_ref[o, :, :part] = acc[:, o * part : (o + 1) * part]
        out_ref[o, :, part:] = acc[:, block + o * part : block + (o + 1) * part]


def real_sums(labels, records, freq, classes, owners):
    m, k = records.shape
    n = freq.shape[1]
    block = min(512, n)
    rows = 512
    part = n // owners
    per = block // part
    return pl.pallas_call(
        functools.partial(real_kernel, rows),
        grid=(n // block,),
        in_specs=[
            pl.BlockSpec((1, m), lambda j: (0, 0)),
            pl.BlockSpec((m, k), lambda j: (0, 0)),
            pl.BlockSpec((k, block), lambda j: (0, j)),
        ],
        out_specs=pl.BlockSpec((per, classes, 2 * part), lambda j: (j, 0, 0)),
        out_shape=jax.ShapeDtypeStruct((owners, classes, 2 * part), F32),
        scratch_shapes=[pltpu.VMEM((classes, m), BF)],
        compiler_params=pltpu.CompilerParams(vmem_limit_bytes=56 * 2**20),
        cost_estimate=pl.CostEstimate(
            flops=2 * m * n * (k + 2 * classes), bytes_accessed=2 * (m * k + k * n), transcendentals=0
        ),
    )(labels.reshape(1, m), records, freq)


def bits_of(n):
    return [1 << b for b in range(n.bit_length() - 1)]


def swap(x, axis, bit):
    n = lax.axis_size(axis)
    return lax.ppermute(x, axis, [(i, i ^ bit) for i in range(n)])


def pick(x, index, dim):
    return lax.dynamic_index_in_dim(x, index, dim, keepdims=False)


def halving(x, axis, order, count):
    me = lax.axis_index(axis)
    nbits = len(order)
    x = x.reshape((2,) * nbits + x.shape[1:])
    left = sorted(order, reverse=True)
    for bit in order:
        dim = left.index(bit)
        left.remove(bit)
        mine = (me // bit) % 2
        got = swap(pick(x, 1 - mine, dim).astype(BF), axis, bit)
        x = pick(x, mine, dim).astype(F32) + got.astype(F32)
    return x


def general(
    records, real_labels, frequencies, class_noise, latents, syn_labels, w_latent, class_embed, w_out
):
    classes = class_embed.shape[0]
    hid = class_embed.shape[1]
    groups = lax.axis_size("rec")
    feats = lax.axis_size("feat")
    rec = lax.axis_index("rec")
    nf = frequencies.shape[1]
    part = nf // groups
    rows, dz = latents.shape
    cols = w_out.shape[1]
    real_total = records.shape[0] * groups
    syn_total = rows * groups

    label_row = jnp.zeros((16, dz), BF).at[0, :].set(syn_labels.astype(BF))
    packed = jnp.concatenate([latents, label_row], axis=0)
    packed = lax.all_to_all(
        jnp.broadcast_to(packed[None], (groups,) + packed.shape), "rec", 0, 0, tiled=True
    )
    all_latents = packed[:, :rows].reshape(syn_total, dz)
    all_labels = packed[:, rows].reshape(syn_total).astype(jnp.int32)
    all_table = one_hot(all_labels, classes, BF)

    table = one_hot(syn_labels, classes, BF)
    preact = jnp.dot(latents, w_latent, preferred_element_type=F32) + jnp.dot(
        table, class_embed, preferred_element_type=F32
    )
    hidden = jnp.maximum(preact, 0.0).astype(BF)
    own_images = jnp.tanh(jnp.dot(hidden, w_out, preferred_element_type=F32)).astype(BF)
    images = lax.all_gather(own_images, "feat", axis=0)
    images = images.transpose(1, 0, 2).reshape(rows, feats * cols)
    syn_pre = jnp.dot(images, frequencies, preferred_element_type=F32)
    syn_cos, syn_sin = cos_sin(syn_pre)
    syn_phi = jnp.concatenate(
        [syn_cos.reshape(rows, groups, part), syn_sin.reshape(rows, groups, part)], axis=2
    ).astype(BF)
    syn_sum = lax.dot_general(
        table, syn_phi.reshape(rows, 2 * nf), (((0,), (0,)), ((), ())), preferred_element_type=F32
    )
    syn_sum = syn_sum.reshape(classes, groups, 2 * part).transpose(1, 0, 2)

    real_sum = real_sums(real_labels, records, frequencies, classes, groups)
    gap = syn_sum * (1.0 / syn_total) - real_sum * (1.0 / real_total)
    half = classes // 2
    order = bits_of(groups)
    other = [order[1], order[0]] + order[2:]
    gap = jnp.concatenate(
        [halving(gap[:, :half], "rec", order, groups), halving(gap[:, half:], "rec", other, groups)], axis=0
    )
    noise = lax.dynamic_slice_in_dim(class_noise, rec * part, part, 2).reshape(classes, 2 * part)
    gap = (16.0 * (gap - noise * (1.0 / real_total))).astype(BF)

    feat_grad = jnp.dot(all_table, gap, preferred_element_type=F32).astype(BF)
    feat_grad = lax.all_to_all(feat_grad.reshape(groups, rows, 2 * part), "rec", 0, 0, tiled=True)
    feat_grad = feat_grad.transpose(1, 0, 2).astype(F32)
    pre_grad = (
        -syn_sin.reshape(rows, groups, part) * feat_grad[:, :, :part]
        + syn_cos.reshape(rows, groups, part) * feat_grad[:, :, part:]
    )
    pre_grad = pre_grad.astype(BF).reshape(rows, nf)
    image_grad = lax.dot_general(
        frequencies, pre_grad, (((1,), (1,)), ((), ())), preferred_element_type=F32
    )
    image_grad = halving(image_grad.reshape(feats, cols, rows), "feat", bits_of(feats), feats)
    image_grad = image_grad.T
    out_grad = (image_grad * (1.0 - jnp.square(own_images.astype(F32)))).astype(BF)

    out_grad = lax.all_to_all(
        jnp.broadcast_to(out_grad[None], (groups, rows, cols)), "rec", 0, 0, tiled=True
    ).reshape(syn_total, cols)

    mine = hid // groups
    start = rec * mine
    all_preact = jnp.dot(
        all_latents, lax.dynamic_slice_in_dim(w_latent, start, mine, 1), preferred_element_type=F32
    ) + jnp.dot(
        all_table, lax.dynamic_slice_in_dim(class_embed, start, mine, 1), preferred_element_type=F32
    )
    all_hidden = jnp.maximum(all_preact, 0.0).astype(BF)
    grad_w_out = lax.dot_general(
        all_hidden, out_grad, (((0,), (0,)), ((), ())), preferred_element_type=F32
    )
    hidden_grad = lax.dot_general(
        out_grad,
        lax.dynamic_slice_in_dim(w_out, start, mine, 0),
        (((1,), (1,)), ((), ())),
        preferred_element_type=F32,
    )
    core = lax.axis_index("feat") % 2
    half = syn_total // 2
    hidden_grad = hidden_grad.reshape(2, half, mine)
    got = swap(pick(hidden_grad, 1 - core, 0).astype(BF), "feat", 1)
    hidden_grad = pick(hidden_grad, core, 0) + got.astype(F32)
    for bit in bits_of(feats)[1:]:
        send = hidden_grad.astype(BF)
        hidden_grad = send.astype(F32) + swap(send, "feat", bit).astype(F32)
    my_preact = lax.dynamic_slice_in_dim(all_preact, core * half, half, 0)
    pre_hidden = jnp.where(my_preact > 0, hidden_grad, 0.0).astype(BF)
    lhs = jnp.concatenate([all_latents, all_table], axis=1)
    lhs = lax.dynamic_slice_in_dim(lhs, core * half, half, 0)
    grads = lax.dot_general(lhs, pre_hidden, (((0,), (0,)), ((), ())), preferred_element_type=F32)
    grads = grads + swap(grads, "feat", 1)
    return grad_w_out, grads[:dz], grads[dz:]


def block(shape, index):
    return pl.BlockSpec(shape, index)


def first_kernel(labels_ref, records_ref, freq_ref, out_ref, table_ref):
    classes, total = table_ref.shape

    @pl.when(pl.program_id(0) == 0)
    def _():
        ids = lax.broadcasted_iota(jnp.int32, (classes, total), 0)
        table_ref[...] = jnp.where(ids == labels_ref[...], 1.0, 0.0).astype(BF)

    freq = freq_ref[...]
    half = total // 2
    before = jnp.dot(records_ref[:half, :], freq, preferred_element_type=F32)
    after = jnp.dot(records_ref[half:, :], freq, preferred_element_type=F32)
    acc = sums(table_ref[:, :half], before) + sums(table_ref[:, half:], after)
    out_ref[0] = acc


def sums(table, pre):
    co, si = cos_sin(pre)
    phi = jnp.concatenate([co.astype(BF), si.astype(BF)], axis=1)
    return jnp.dot(table, phi, preferred_element_type=F32)


def first_sums(labels, records, freq, classes, size):
    k = records.shape[1]
    n = freq.shape[1]
    return pl.pallas_call(
        first_kernel,
        grid=(n // 512,),
        in_specs=[
            block((1, size), lambda j: (0, 0)),
            block((size, k), lambda j: (0, 0)),
            block((k, 512), lambda j: (0, j)),
        ],
        out_specs=block((1, classes, 1024), lambda j: (j, 0, 0)),
        out_shape=jax.ShapeDtypeStruct((n // 512, classes, 1024), F32),
        scratch_shapes=[pltpu.VMEM((classes, size), BF)],
        compiler_params=pltpu.CompilerParams(vmem_limit_bytes=48 * 2**20),
        cost_estimate=pl.CostEstimate(
            flops=2 * size * n * (k + 2 * classes), bytes_accessed=2 * (size * k + k * n), transcendentals=0
        ),
    )(labels.reshape(1, -1), records, freq)


def second_kernel(
    masks,
    real_total,
    syn_total,
    me_ref,
    real_labels_ref,
    syn_labels_ref,
    *refs,
):
    count = len(masks)
    images = refs[:count]
    blocks = refs[count : count + 2]
    freq_ref, part_ref, send_a, keep_a, send_b, keep_b, cs_ref, real_table, syn_table = refs[count + 2 :]
    classes, total = real_table.shape
    feat, x, z_low = me_ref[0], me_ref[1], me_ref[2]
    step = pl.program_id(0)

    @pl.when(step == 0)
    def _():
        ids = lax.broadcasted_iota(jnp.int32, (classes, total), 0)
        real_table[...] = jnp.where(ids == real_labels_ref[...], 1.0, 0.0).astype(BF)
        ids = lax.broadcasted_iota(jnp.int32, syn_table.shape, 0)
        syn_table[...] = jnp.where(ids == syn_labels_ref[...], 1.0, 0.0).astype(BF)

    cols = images[0].shape[1]
    syn_pre = None
    for mask, image in zip(masks, images):
        at = pl.multiple_of((feat ^ mask) * cols, 128)
        d = jnp.dot(image[...], freq_ref[pl.ds(at, cols), :], preferred_element_type=F32)
        syn_pre = d if syn_pre is None else syn_pre + d
    freq = freq_ref[...]
    size = total // 2
    pre0 = jnp.dot(blocks[0][...], freq, preferred_element_type=F32)
    co, si = cos_sin(syn_pre)
    cs_ref[0] = co
    cs_ref[1] = si
    phi = jnp.concatenate([co.astype(BF), si.astype(BF)], axis=1)
    syn = jnp.dot(syn_table[...], phi, preferred_element_type=F32)
    pre1 = jnp.dot(blocks[1][...], freq, preferred_element_type=F32)
    acc = part_ref[0] + sums(real_table[:, :size], pre0)
    acc = acc + sums(real_table[:, size:], pre1)
    gap = syn * (1.0 / syn_total) - acc * (1.0 / real_total)
    zero = jnp.concatenate([gap[:, :256], gap[:, 512:768]], axis=1)
    one = jnp.concatenate([gap[:, 256:512], gap[:, 768:]], axis=1)
    half = classes // 2
    keep_a[0] = jnp.where(x == 0, zero[:half], one[:half])
    send_a[0] = jnp.where(x == 0, one[:half], zero[:half]).astype(BF)
    high = step // 2

    @pl.when(step % 2 == z_low)
    def _():
        keep_b[high, 0] = zero[half:]
        keep_b[high, 1] = one[half:]

    @pl.when(step % 2 != z_low)
    def _():
        send_b[high, 0] = zero[half:].astype(BF)
        send_b[high, 1] = one[half:].astype(BF)


def second_sums(me, real_labels, syn_labels, masks, images, records, size, freq, part, totals):
    k = records.shape[1]
    n = freq.shape[1]
    rows, cols = images[0].shape
    classes = part.shape[1]
    half = classes // 2
    grid_spec = pltpu.PrefetchScalarGridSpec(
        num_scalar_prefetch=1,
        grid=(n // 512,),
        in_specs=[
            block((1, 2 * size), lambda j, me: (0, 0)),
            block((1, rows), lambda j, me: (0, 0)),
        ]
        + [block((rows, cols), lambda j, me: (0, 0)) for _ in images]
        + [
            block((size, k), lambda j, me: (1, 0)),
            block((size, k), lambda j, me: (2, 0)),
            block((k, 512), lambda j, me: (0, j)),
            block((1, classes, 1024), lambda j, me: (j, 0, 0)),
        ],
        out_specs=[
            block((1, half, 512), lambda j, me: (j, 0, 0)),
            block((1, half, 512), lambda j, me: (j, 0, 0)),
            block((2, 2, half, 512), lambda j, me: (0, 0, 0, 0)),
            block((2, 2, half, 512), lambda j, me: (0, 0, 0, 0)),
            block((2, rows, 512), lambda j, me: (0, 0, j)),
        ],
        scratch_shapes=[pltpu.VMEM((classes, 2 * size), BF), pltpu.VMEM((classes, rows), BF)],
    )
    return pl.pallas_call(
        functools.partial(second_kernel, masks, *totals),
        grid_spec=grid_spec,
        out_shape=[
            jax.ShapeDtypeStruct((4, half, 512), BF),
            jax.ShapeDtypeStruct((4, half, 512), F32),
            jax.ShapeDtypeStruct((2, 2, half, 512), BF),
            jax.ShapeDtypeStruct((2, 2, half, 512), F32),
            jax.ShapeDtypeStruct((2, rows, n), F32),
        ],
        compiler_params=pltpu.CompilerParams(vmem_limit_bytes=56 * 2**20),
        cost_estimate=pl.CostEstimate(
            flops=2 * (2 * size + rows) * n * (k + 2 * classes),
            bytes_accessed=2 * (2 * size * k + k * n) + 4 * classes * n * 2,
            transcendentals=0,
        ),
    )(me, real_labels.reshape(1, -1), syn_labels.reshape(1, -1), *images, records, records, freq, part)


def stage_two_kernel(me_ref, ka_s, ka_k, ra_s, ra_k, kb_s, kb_k, rb_s, rb_k, sa, na, sb, nb):
    sa[0] = (ka_s[0, 0] + ra_s[0, 0].astype(F32)).astype(BF)
    na[0] = ka_k[0, 0] + ra_k[0, 0].astype(F32)
    sb[0] = (kb_s[0, 0] + rb_s[0, 0].astype(F32)).astype(BF)
    nb[0] = kb_k[0, 0] + rb_k[0, 0].astype(F32)


def stage_two(me, keep_a, got_a, keep_b, got_b):
    half, width = keep_b.shape[2:]
    shape = (1, 1, half, width)
    keep_a = keep_a.reshape(2, 2, half, width)
    got_a = got_a.reshape(2, 2, half, width)
    low = lambda flip: block(shape, lambda h, me: (h, me[2] ^ flip, 0, 0))
    xs = lambda flip: block(shape, lambda h, me: (h, me[1] ^ flip, 0, 0))
    out = block((1, half, width), lambda h, me: (h, 0, 0))
    spec = pltpu.PrefetchScalarGridSpec(
        num_scalar_prefetch=1,
        grid=(2,),
        in_specs=[low(1), low(0), low(1), low(0), xs(1), xs(0), xs(1), xs(0)],
        out_specs=[out] * 4,
    )
    kinds = [BF, F32, BF, F32]
    return pl.pallas_call(
        stage_two_kernel,
        grid_spec=spec,
        out_shape=[jax.ShapeDtypeStruct((2, half, width), t) for t in kinds],
        cost_estimate=pl.CostEstimate(flops=0, bytes_accessed=4 * 2**20, transcendentals=0),
    )(me, keep_a, keep_a, got_a, got_a, keep_b, keep_b, got_b, got_b)


def stage_three_kernel(me_ref, na_s, na_k, ga_s, ga_k, nb_s, nb_k, gb_s, gb_k, send, keep):
    half = na_s.shape[1]
    send[:half] = (na_s[0] + ga_s[0].astype(F32)).astype(BF)
    keep[:half] = na_k[0] + ga_k[0].astype(F32)
    send[half:] = (nb_s[0] + gb_s[0].astype(F32)).astype(BF)
    keep[half:] = nb_k[0] + gb_k[0].astype(F32)


def stage_three(me, next_a, got_a, next_b, got_b):
    _, half, width = next_a.shape
    high = lambda flip: block((1, half, width), lambda h, me: (me[3] ^ flip, 0, 0))
    out = block((2 * half, width), lambda h, me: (0, 0))
    spec = pltpu.PrefetchScalarGridSpec(
        num_scalar_prefetch=1,
        grid=(1,),
        in_specs=[high(1), high(0)] * 4,
        out_specs=[out, out],
    )
    return pl.pallas_call(
        stage_three_kernel,
        grid_spec=spec,
        out_shape=[jax.ShapeDtypeStruct((2 * half, width), t) for t in (BF, F32)],
        cost_estimate=pl.CostEstimate(flops=0, bytes_accessed=3 * 2**20, transcendentals=0),
    )(me, next_a, next_a, got_a, got_a, next_b, next_b, got_b, got_b)


def gap_kernel(real_total, me_ref, keep_ref, got_ref, noise_ref, labels_ref, out_ref):
    classes = keep_ref.shape[0]
    part = noise_ref.shape[2]
    noise = jnp.concatenate([noise_ref[:, 0, :], noise_ref[:, 1, :]], axis=1)
    gap = keep_ref[...] + got_ref[...].astype(F32) - noise * (1.0 / real_total)
    gap = (16.0 * gap).astype(BF)
    ids = lax.broadcasted_iota(jnp.int32, (labels_ref.shape[0], classes), 1)
    table = jnp.where(ids == labels_ref[...], 1.0, 0.0).astype(BF)
    out_ref[...] = jnp.dot(table, gap, preferred_element_type=F32).astype(BF)


def gap_rows(me, keep, got, noise, labels, real_total):
    classes, width = keep.shape
    total = labels.shape[0]
    spec = pltpu.PrefetchScalarGridSpec(
        num_scalar_prefetch=1,
        grid=(1,),
        in_specs=[
            block((classes, width), lambda h, me: (0, 0)),
            block((classes, width), lambda h, me: (0, 0)),
            block((classes, 2, width // 2), lambda h, me: (0, 0, me[4])),
            block((total, 1), lambda h, me: (0, 0)),
        ],
        out_specs=block((total, width), lambda h, me: (0, 0)),
    )
    return pl.pallas_call(
        functools.partial(gap_kernel, real_total),
        grid_spec=spec,
        out_shape=jax.ShapeDtypeStruct((total, width), BF),
        cost_estimate=pl.CostEstimate(
            flops=2 * total * classes * width, bytes_accessed=3 * 2**20, transcendentals=0
        ),
    )(me, keep, got, noise, labels.reshape(total, 1))


NT = (((1,), (1,)), ((), ()))


def image_kernel(me_ref, cs_ref, rows_ref, freq_ref, send_ref, keep_ref, pre_ref):
    step = pl.program_id(0)
    owners, _, width = rows_ref.shape
    part = width // 2

    @pl.when(step == 0)
    def _():
        for o in range(owners):
            at = slice(o * part, (o + 1) * part)
            grad = rows_ref[o].astype(F32)
            pre = cs_ref[0, :, at] * grad[:, part:] - cs_ref[1, :, at] * grad[:, :part]
            pre_ref[:, at] = pre.astype(BF)

    out = lax.dot_general(freq_ref[...], pre_ref[...], NT, preferred_element_type=F32)

    @pl.when(step < 2)
    def _():
        send_ref[0] = out.astype(BF)

    @pl.when(step >= 2)
    def _():
        keep_ref[0] = out


def image_grads(me, cs, feat_rows, freq, cols):
    k, n = freq.shape
    owners, rows, width = feat_rows.shape
    spec = pltpu.PrefetchScalarGridSpec(
        num_scalar_prefetch=1,
        grid=(4,),
        in_specs=[
            block((2, rows, n), lambda s, me: (0, 0, 0)),
            block((owners, rows, width), lambda s, me: (0, 0, 0)),
            block((cols, n), lambda s, me: ((s % 2) * 2 + ((me[0] % 2) ^ (1 - s // 2)), 0)),
        ],
        out_specs=[
            block((1, cols, rows), lambda s, me: (jnp.minimum(s, 1), 0, 0)),
            block((1, cols, rows), lambda s, me: (jnp.maximum(s - 2, 0), 0, 0)),
        ],
        scratch_shapes=[pltpu.VMEM((rows, n), BF)],
    )
    return pl.pallas_call(
        image_kernel,
        grid_spec=spec,
        out_shape=[jax.ShapeDtypeStruct((2, cols, rows), t) for t in (BF, F32)],
        compiler_params=pltpu.CompilerParams(vmem_limit_bytes=40 * 2**20),
        cost_estimate=pl.CostEstimate(flops=2 * k * n * rows, bytes_accessed=2 * k * n, transcendentals=0),
    )(me, cs, feat_rows, freq)


def split_y_kernel(me_ref, keep_s, keep_k, got_s, got_k, send, keep):
    send[...] = (keep_s[0] + got_s[0].astype(F32)).astype(BF)
    keep[...] = keep_k[0] + got_k[0].astype(F32)


def split_y(me, keep, got):
    _, cols, rows = keep.shape
    at = lambda flip: block((1, cols, rows), lambda h, me: ((me[0] // 2) ^ flip, 0, 0))
    out = block((cols, rows), lambda h, me: (0, 0))
    spec = pltpu.PrefetchScalarGridSpec(
        num_scalar_prefetch=1, grid=(1,), in_specs=[at(1), at(0)] * 2, out_specs=[out, out]
    )
    return pl.pallas_call(
        split_y_kernel,
        grid_spec=spec,
        out_shape=[jax.ShapeDtypeStruct((cols, rows), t) for t in (BF, F32)],
        cost_estimate=pl.CostEstimate(flops=0, bytes_accessed=2**20, transcendentals=0),
    )(me, keep, keep, got, got)


def out_kernel(keep, got, image, out):
    grad = (keep[...] + got[...].astype(F32)).T
    grad = grad * (1.0 - jnp.square(image[...].astype(F32)))
    grad = grad.astype(BF)
    for r in range(out.shape[0]):
        out[r] = grad


def out_grads(keep, got, image, copies):
    rows, cols = image.shape
    return pl.pallas_call(
        out_kernel,
        out_shape=jax.ShapeDtypeStruct((copies, rows, cols), BF),
        cost_estimate=pl.CostEstimate(flops=0, bytes_accessed=2**20, transcendentals=0),
    )(keep, got, image)


def hidden_kernel(me_ref, w_ref, grad_ref, send, keep):
    core = me_ref[0] % 2
    out = lax.dot_general(w_ref[...], grad_ref[0], NT, preferred_element_type=F32)
    half = out.shape[0] // 2
    keep[0] = jnp.where(core == 0, out[:half], out[half:])
    send[0] = jnp.where(core == 0, out[half:], out[:half]).astype(BF)


def hidden_grads(me, w_out, out_grad):
    groups, rows, cols = out_grad.shape
    hid = w_out.shape[0]
    mine = hid // groups
    out = block((1, mine // 2, rows), lambda r, me: (r, 0, 0))
    spec = pltpu.PrefetchScalarGridSpec(
        num_scalar_prefetch=1,
        grid=(groups,),
        in_specs=[
            block((mine, cols), lambda r, me: (r, 0)),
            block((1, rows, cols), lambda r, me: (0, 0, 0)),
        ],
        out_specs=[out, out],
    )
    return pl.pallas_call(
        hidden_kernel,
        grid_spec=spec,
        out_shape=[jax.ShapeDtypeStruct((groups, mine // 2, rows), t) for t in (BF, F32)],
        cost_estimate=pl.CostEstimate(
            flops=2 * hid * cols * rows, bytes_accessed=2 * hid * cols, transcendentals=0
        ),
    )(me, w_out, out_grad)


def add_kernel(a, b, out):
    out[...] = (a[...].astype(F32) + b[...].astype(F32)).astype(out.dtype)


def add(a, b, kind):
    return pl.pallas_call(
        add_kernel,
        out_shape=jax.ShapeDtypeStruct(a.shape, kind),
        cost_estimate=pl.CostEstimate(flops=0, bytes_accessed=2**20, transcendentals=0),
    )(a, b)


def weight_kernel(hidden_ref, grad_ref, out_ref):
    groups, rows, cols = grad_ref.shape
    out_ref[...] = jnp.dot(
        hidden_ref[...], grad_ref[...].reshape(groups * rows, cols), preferred_element_type=F32
    )


def weight_grads(hidden, grad):
    groups, rows, cols = grad.shape
    mine = hidden.shape[0]
    return pl.pallas_call(
        weight_kernel,
        out_shape=jax.ShapeDtypeStruct((mine, cols), F32),
        cost_estimate=pl.CostEstimate(
            flops=2 * mine * groups * rows * cols, bytes_accessed=4 * 2**20, transcendentals=0
        ),
    )(hidden, grad)


def last_kernel(me_ref, got_ref, preact_ref, lhs_ref, out_ref):
    groups, width, rows = got_ref.shape
    acc = None
    for g in range(groups):
        at = slice(g * rows, (g + 1) * rows)
        grad = jnp.where(preact_ref[:, at] > 0, got_ref[g].astype(F32), 0.0).astype(BF)
        d = lax.dot_general(lhs_ref[:, at], grad, NT, preferred_element_type=F32)
        acc = d if acc is None else acc + d
    out_ref[...] = acc


def last_grads(me, got, preact, lhs):
    groups, width, rows = got.shape
    count, total = lhs.shape
    spec = pltpu.PrefetchScalarGridSpec(
        num_scalar_prefetch=1,
        grid=(1,),
        in_specs=[
            block((groups, width, rows), lambda h, me: (0, 0, 0)),
            block((width, total), lambda h, me: (me[0] % 2, 0)),
            block((count, total), lambda h, me: (0, 0)),
        ],
        out_specs=block((count, width), lambda h, me: (0, 0)),
    )
    return pl.pallas_call(
        last_kernel,
        grid_spec=spec,
        out_shape=jax.ShapeDtypeStruct((count, width), F32),
        cost_estimate=pl.CostEstimate(
            flops=2 * total * count * width, bytes_accessed=2 * 2**20, transcendentals=0
        ),
    )(me, got, preact, lhs)


def eight_by_four(
    records, real_labels, frequencies, class_noise, latents, syn_labels, w_latent, class_embed, w_out
):
    classes, hid = class_embed.shape
    groups = lax.axis_size("rec")
    rec = lax.axis_index("rec")
    feat = lax.axis_index("feat")
    rows, dz = latents.shape
    cols = w_out.shape[1]
    real_total = records.shape[0] * groups
    syn_total = rows * groups
    me = jnp.stack([feat, rec % 2, (rec // 2) % 2, rec // 4, rec]).astype(jnp.int32)

    table = one_hot(syn_labels, classes, BF)
    preact = jnp.dot(latents, w_latent, preferred_element_type=F32) + jnp.dot(
        table, class_embed, preferred_element_type=F32
    )
    hidden = jnp.maximum(preact, 0.0).astype(BF)
    own = jnp.tanh(jnp.dot(hidden, w_out, preferred_element_type=F32)).astype(BF)
    far = swap(own, "feat", 2)
    images = [own, far, swap(own, "feat", 1), swap(far, "feat", 1)]

    label_row = jnp.zeros((16, dz), BF).at[0, :].set(syn_labels.astype(BF))
    packed = jnp.concatenate([latents, label_row], axis=0)
    packed = lax.all_to_all(
        jnp.broadcast_to(packed[None], (groups,) + packed.shape), "rec", 0, 0, tiled=True
    )

    size = records.shape[0] // 3
    part = first_sums(real_labels[:size], records, frequencies, classes, size)
    send_a, keep_a, send_b, keep_b, cs = second_sums(
        me, real_labels[size:], syn_labels, (0, 2, 1, 3), images, records, size, frequencies, part,
        (real_total, syn_total),
    )
    got_a = swap(send_a, "rec", 1)
    got_b = swap(send_b, "rec", 2)

    all_latents = packed[:, :rows].reshape(syn_total, dz)
    all_labels = packed[:, rows].reshape(syn_total).astype(jnp.int32)
    all_table = one_hot(all_labels, classes, BF)
    mine = hid // groups
    lhs = jnp.concatenate([all_latents, all_table], axis=1).T
    w = jnp.concatenate(
        [
            lax.dynamic_slice_in_dim(w_latent, rec * mine, mine, 1),
            lax.dynamic_slice_in_dim(class_embed, rec * mine, mine, 1),
        ],
        axis=0,
    )
    all_preact = lax.dot_general(w, lhs, (((0,), (0,)), ((), ())), preferred_element_type=F32)
    all_hidden = jnp.maximum(all_preact, 0.0).astype(BF)

    send_a, next_a, send_b, next_b = stage_two(me, keep_a, got_a, keep_b, got_b)
    got_a = swap(send_a, "rec", 2)
    got_b = swap(send_b, "rec", 1)
    send, keep = stage_three(me, next_a, got_a, next_b, got_b)
    got = swap(send, "rec", 4)
    feat_grad = gap_rows(me, keep, got, class_noise, all_labels, real_total)
    feat_grad = lax.all_to_all(feat_grad.reshape(groups, rows, -1), "rec", 0, 0, tiled=True)

    send, keep = image_grads(me, cs, feat_grad, frequencies, cols)
    send, keep = split_y(me, keep, swap(send, "feat", 1))
    out_grad = out_grads(keep, swap(send, "feat", 2), own, groups)

    all_grad = lax.all_to_all(out_grad, "rec", 0, 0, tiled=True)
    send, keep = hidden_grads(me, w_out, out_grad)
    part_grad = add(keep, swap(send, "feat", 1), BF)
    part_grad = add(part_grad, swap(part_grad, "feat", 2), BF)
    part_grad = lax.all_to_all(part_grad, "rec", 0, 0, tiled=True)
    grads = last_grads(me, part_grad, all_preact, lhs)
    other = swap(grads, "feat", 1)
    core = feat % 2
    grads = jnp.concatenate(
        [jnp.where(core == 0, grads, other), jnp.where(core == 0, other, grads)], axis=1
    )
    grad_w_out = weight_grads(all_hidden, all_grad)
    return grad_w_out, grads[:dz], grads[dz:]


def solution(mesh):
    shape = (mesh.shape["rec"], mesh.shape["feat"])
    in_specs = (
        P("rec", None),
        P("rec"),
        P(None, "feat"),
        P(None, None, "feat"),
        P("rec", None),
        P("rec"),
        P(),
        P(),
        P(None, "feat"),
    )
    out_specs = (P("rec", "feat"), P(None, "rec"), P(None, "rec"))
    return jax.shard_map(
        eight_by_four if shape == (8, 4) else general, mesh=mesh, in_specs=in_specs, out_specs=out_specs, check_vma=False
    )
```

```python
import functools

import jax
import jax.numpy as jnp
from jax import lax
from jax.experimental import pallas as pl
from jax.experimental.pallas import tpu as pltpu
from jax.sharding import PartitionSpec as P

BF = jnp.bfloat16
F32 = jnp.float32

TURN = 0.15915494309189535
SIN = (4.44286783702217, -7.307441307726672, 3.59477116396636, -0.7843353598850176)
COS = (1.4142134962552275, -6.978850948563815, 5.739460376907241, -1.883557905986894, 0.3106880275267554)


def cos_sin(x):
    turns = x * TURN
    u = turns - jnp.round(turns)
    sq = u * u
    p = SIN[-1]
    for c in SIN[-2::-1]:
        p = p * sq + c
    q = COS[-1]
    for c in COS[-2::-1]:
        q = q * sq + c
    s = u * p
    return 1.0 - s * s, s * q


def one_hot(labels, count, dtype):
    return (labels[:, None] == jnp.arange(count, dtype=jnp.int32)[None, :]).astype(dtype)


def real_kernel(rows, labels_ref, records_ref, freq_ref, out_ref, table_ref):
    total = records_ref.shape[0]
    classes = table_ref.shape[0]
    owners, _, width = out_ref.shape
    part = width // 2

    @pl.when(pl.program_id(0) == 0)
    def _():
        ids = lax.broadcasted_iota(jnp.int32, (classes, total), 0)
        table_ref[...] = jnp.where(ids == labels_ref[...], 1.0, 0.0).astype(BF)

    freq = freq_ref[...]
    block = freq.shape[1]

    def sums(i, pre):
        co, si = cos_sin(pre)
        phi = jnp.concatenate([co.astype(BF), si.astype(BF)], axis=1)
        return jnp.dot(table_ref[:, i * rows : (i + 1) * rows], phi, preferred_element_type=F32)

    acc = None
    before = None
    steps = total // rows
    for i in range(steps + 1):
        pre = None
        if i < steps:
            pre = jnp.dot(records_ref[i * rows : (i + 1) * rows, :], freq, preferred_element_type=F32)
        if i > 0:
            d = sums(i - 1, before)
            acc = d if acc is None else acc + d
        before = pre
    for o in range(owners):
        out_ref[o, :, :part] = acc[:, o * part : (o + 1) * part]
        out_ref[o, :, part:] = acc[:, block + o * part : block + (o + 1) * part]


def real_sums(labels, records, freq, classes, owners):
    m, k = records.shape
    n = freq.shape[1]
    block = min(512, n)
    rows = 512
    part = n // owners
    per = block // part
    return pl.pallas_call(
        functools.partial(real_kernel, rows),
        grid=(n // block,),
        in_specs=[
            pl.BlockSpec((1, m), lambda j: (0, 0)),
            pl.BlockSpec((m, k), lambda j: (0, 0)),
            pl.BlockSpec((k, block), lambda j: (0, j)),
        ],
        out_specs=pl.BlockSpec((per, classes, 2 * part), lambda j: (j, 0, 0)),
        out_shape=jax.ShapeDtypeStruct((owners, classes, 2 * part), F32),
        scratch_shapes=[pltpu.VMEM((classes, m), BF)],
        compiler_params=pltpu.CompilerParams(vmem_limit_bytes=56 * 2**20),
        cost_estimate=pl.CostEstimate(
            flops=2 * m * n * (k + 2 * classes), bytes_accessed=2 * (m * k + k * n), transcendentals=0
        ),
    )(labels.reshape(1, m), records, freq)


def bits_of(n):
    return [1 << b for b in range(n.bit_length() - 1)]


def swap(x, axis, bit):
    n = lax.axis_size(axis)
    return lax.ppermute(x, axis, [(i, i ^ bit) for i in range(n)])


def pick(x, index, dim):
    return lax.dynamic_index_in_dim(x, index, dim, keepdims=False)


def halving(x, axis, order, count):
    me = lax.axis_index(axis)
    nbits = len(order)
    x = x.reshape((2,) * nbits + x.shape[1:])
    left = sorted(order, reverse=True)
    for bit in order:
        dim = left.index(bit)
        left.remove(bit)
        mine = (me // bit) % 2
        got = swap(pick(x, 1 - mine, dim).astype(BF), axis, bit)
        x = pick(x, mine, dim).astype(F32) + got.astype(F32)
    return x


def general(
    records, real_labels, frequencies, class_noise, latents, syn_labels, w_latent, class_embed, w_out
):
    classes = class_embed.shape[0]
    hid = class_embed.shape[1]
    groups = lax.axis_size("rec")
    feats = lax.axis_size("feat")
    rec = lax.axis_index("rec")
    nf = frequencies.shape[1]
    part = nf // groups
    rows, dz = latents.shape
    cols = w_out.shape[1]
    real_total = records.shape[0] * groups
    syn_total = rows * groups

    label_row = jnp.zeros((16, dz), BF).at[0, :].set(syn_labels.astype(BF))
    packed = jnp.concatenate([latents, label_row], axis=0)
    packed = lax.all_to_all(
        jnp.broadcast_to(packed[None], (groups,) + packed.shape), "rec", 0, 0, tiled=True
    )
    all_latents = packed[:, :rows].reshape(syn_total, dz)
    all_labels = packed[:, rows].reshape(syn_total).astype(jnp.int32)
    all_table = one_hot(all_labels, classes, BF)

    table = one_hot(syn_labels, classes, BF)
    preact = jnp.dot(latents, w_latent, preferred_element_type=F32) + jnp.dot(
        table, class_embed, preferred_element_type=F32
    )
    hidden = jnp.maximum(preact, 0.0).astype(BF)
    own_images = jnp.tanh(jnp.dot(hidden, w_out, preferred_element_type=F32)).astype(BF)
    images = lax.all_gather(own_images, "feat", axis=0)
    images = images.transpose(1, 0, 2).reshape(rows, feats * cols)
    syn_pre = jnp.dot(images, frequencies, preferred_element_type=F32)
    syn_cos, syn_sin = cos_sin(syn_pre)
    syn_phi = jnp.concatenate(
        [syn_cos.reshape(rows, groups, part), syn_sin.reshape(rows, groups, part)], axis=2
    ).astype(BF)
    syn_sum = lax.dot_general(
        table, syn_phi.reshape(rows, 2 * nf), (((0,), (0,)), ((), ())), preferred_element_type=F32
    )
    syn_sum = syn_sum.reshape(classes, groups, 2 * part).transpose(1, 0, 2)

    real_sum = real_sums(real_labels, records, frequencies, classes, groups)
    gap = syn_sum * (1.0 / syn_total) - real_sum * (1.0 / real_total)
    half = classes // 2
    order = bits_of(groups)
    other = [order[1], order[0]] + order[2:]
    gap = jnp.concatenate(
        [halving(gap[:, :half], "rec", order, groups), halving(gap[:, half:], "rec", other, groups)], axis=0
    )
    noise = lax.dynamic_slice_in_dim(class_noise, rec * part, part, 2).reshape(classes, 2 * part)
    gap = (16.0 * (gap - noise * (1.0 / real_total))).astype(BF)

    feat_grad = jnp.dot(all_table, gap, preferred_element_type=F32).astype(BF)
    feat_grad = lax.all_to_all(feat_grad.reshape(groups, rows, 2 * part), "rec", 0, 0, tiled=True)
    feat_grad = feat_grad.transpose(1, 0, 2).astype(F32)
    pre_grad = (
        -syn_sin.reshape(rows, groups, part) * feat_grad[:, :, :part]
        + syn_cos.reshape(rows, groups, part) * feat_grad[:, :, part:]
    )
    pre_grad = pre_grad.astype(BF).reshape(rows, nf)
    image_grad = lax.dot_general(
        frequencies, pre_grad, (((1,), (1,)), ((), ())), preferred_element_type=F32
    )
    image_grad = halving(image_grad.reshape(feats, cols, rows), "feat", bits_of(feats), feats)
    image_grad = image_grad.T
    out_grad = (image_grad * (1.0 - jnp.square(own_images.astype(F32)))).astype(BF)

    out_grad = lax.all_to_all(
        jnp.broadcast_to(out_grad[None], (groups, rows, cols)), "rec", 0, 0, tiled=True
    ).reshape(syn_total, cols)

    mine = hid // groups
    start = rec * mine
    all_preact = jnp.dot(
        all_latents, lax.dynamic_slice_in_dim(w_latent, start, mine, 1), preferred_element_type=F32
    ) + jnp.dot(
        all_table, lax.dynamic_slice_in_dim(class_embed, start, mine, 1), preferred_element_type=F32
    )
    all_hidden = jnp.maximum(all_preact, 0.0).astype(BF)
    grad_w_out = lax.dot_general(
        all_hidden, out_grad, (((0,), (0,)), ((), ())), preferred_element_type=F32
    )
    hidden_grad = lax.dot_general(
        out_grad,
        lax.dynamic_slice_in_dim(w_out, start, mine, 0),
        (((1,), (1,)), ((), ())),
        preferred_element_type=F32,
    )
    core = lax.axis_index("feat") % 2
    half = syn_total // 2
    hidden_grad = hidden_grad.reshape(2, half, mine)
    got = swap(pick(hidden_grad, 1 - core, 0).astype(BF), "feat", 1)
    hidden_grad = pick(hidden_grad, core, 0) + got.astype(F32)
    for bit in bits_of(feats)[1:]:
        send = hidden_grad.astype(BF)
        hidden_grad = send.astype(F32) + swap(send, "feat", bit).astype(F32)
    my_preact = lax.dynamic_slice_in_dim(all_preact, core * half, half, 0)
    pre_hidden = jnp.where(my_preact > 0, hidden_grad, 0.0).astype(BF)
    lhs = jnp.concatenate([all_latents, all_table], axis=1)
    lhs = lax.dynamic_slice_in_dim(lhs, core * half, half, 0)
    grads = lax.dot_general(lhs, pre_hidden, (((0,), (0,)), ((), ())), preferred_element_type=F32)
    grads = grads + swap(grads, "feat", 1)
    return grad_w_out, grads[:dz], grads[dz:]


def block(shape, index):
    return pl.BlockSpec(shape, index)


def sums(table, pre):
    co, si = cos_sin(pre)
    phi = jnp.concatenate([co.astype(BF), si.astype(BF)], axis=1)
    return jnp.dot(table, phi, preferred_element_type=F32)


def features_kernel(masks, size, real_total, syn_total, me_ref, real_labels_ref, syn_labels_ref, *refs):
    count = len(masks)
    images = refs[:count]
    records_hbm, freq_ref, send_a, keep_a, send_b, keep_b, cs_ref = refs[count : count + 7]
    records, real_table, syn_table, sem = refs[count + 7 :]
    classes, total = real_table.shape
    steps = total // size
    feat, x, z_low = me_ref[0], me_ref[1], me_ref[2]
    step = pl.program_id(0)
    cols = images[0].shape[1]

    def copy(i):
        at = pl.ds(i * size, size)
        return pltpu.make_async_copy(records_hbm.at[at, :], records.at[at, :], sem.at[i])

    def body(wait):
        syn_pre = None
        for mask, image in zip(masks, images):
            at = pl.multiple_of((feat ^ mask) * cols, 128)
            d = jnp.dot(image[...], freq_ref[pl.ds(at, cols), :], preferred_element_type=F32)
            syn_pre = d if syn_pre is None else syn_pre + d
        freq = freq_ref[...]
        acc = None
        before = None
        for i in range(steps + 1):
            if i < steps:
                if wait:
                    copy(i).wait()
                pre = jnp.dot(records[i * size : (i + 1) * size, :], freq, preferred_element_type=F32)
            if i == 0:
                co, si = cos_sin(syn_pre)
                cs_ref[0] = co
                cs_ref[1] = si
                phi = jnp.concatenate([co.astype(BF), si.astype(BF)], axis=1)
                syn = jnp.dot(syn_table[...], phi, preferred_element_type=F32)
            else:
                d = sums(real_table[:, (i - 1) * size : i * size], before)
                acc = d if acc is None else acc + d
            before = pre
        gap = syn * (1.0 / syn_total) - acc * (1.0 / real_total)
        zero = jnp.concatenate([gap[:, :256], gap[:, 512:768]], axis=1)
        one = jnp.concatenate([gap[:, 256:512], gap[:, 768:]], axis=1)
        half = classes // 2
        keep_a[0] = jnp.where(x == 0, zero[:half], one[:half])
        send_a[0] = jnp.where(x == 0, one[:half], zero[:half]).astype(BF)
        high = step // 2

        @pl.when(step % 2 == z_low)
        def _():
            keep_b[high, 0] = zero[half:]
            keep_b[high, 1] = one[half:]

        @pl.when(step % 2 != z_low)
        def _():
            send_b[high, 0] = zero[half:].astype(BF)
            send_b[high, 1] = one[half:].astype(BF)

    @pl.when(step == 0)
    def _():
        for i in range(steps):
            copy(i).start()
        ids = lax.broadcasted_iota(jnp.int32, (classes, total), 0)
        real_table[...] = jnp.where(ids == real_labels_ref[...], 1.0, 0.0).astype(BF)
        ids = lax.broadcasted_iota(jnp.int32, syn_table.shape, 0)
        syn_table[...] = jnp.where(ids == syn_labels_ref[...], 1.0, 0.0).astype(BF)
        body(True)

    @pl.when(step > 0)
    def _():
        body(False)


def feature_sums(me, real_labels, syn_labels, masks, images, records, freq, classes, totals):
    total, k = records.shape
    n = freq.shape[1]
    rows, cols = images[0].shape
    half = classes // 2
    size = 512
    grid_spec = pltpu.PrefetchScalarGridSpec(
        num_scalar_prefetch=1,
        grid=(n // 512,),
        in_specs=[
            block((1, total), lambda j, me: (0, 0)),
            block((1, rows), lambda j, me: (0, 0)),
        ]
        + [block((rows, cols), lambda j, me: (0, 0)) for _ in images]
        + [
            pl.BlockSpec(memory_space=pl.ANY),
            block((k, 512), lambda j, me: (0, j)),
        ],
        out_specs=[
            block((1, half, 512), lambda j, me: (j, 0, 0)),
            block((1, half, 512), lambda j, me: (j, 0, 0)),
            block((2, 2, half, 512), lambda j, me: (0, 0, 0, 0)),
            block((2, 2, half, 512), lambda j, me: (0, 0, 0, 0)),
            block((2, rows, 512), lambda j, me: (0, 0, j)),
        ],
        scratch_shapes=[
            pltpu.VMEM((total, k), BF),
            pltpu.VMEM((classes, total), BF),
            pltpu.VMEM((classes, rows), BF),
            pltpu.SemaphoreType.DMA((total // size,)),
        ],
    )
    return pl.pallas_call(
        functools.partial(features_kernel, masks, size, *totals),
        grid_spec=grid_spec,
        out_shape=[
            jax.ShapeDtypeStruct((4, half, 512), BF),
            jax.ShapeDtypeStruct((4, half, 512), F32),
            jax.ShapeDtypeStruct((2, 2, half, 512), BF),
            jax.ShapeDtypeStruct((2, 2, half, 512), F32),
            jax.ShapeDtypeStruct((2, rows, n), F32),
        ],
        compiler_params=pltpu.CompilerParams(vmem_limit_bytes=50 * 2**20),
        cost_estimate=pl.CostEstimate(
            flops=2 * (total + rows) * n * (k + 2 * classes),
            bytes_accessed=2 * (total * k + k * n) + 4 * classes * n * 2,
            transcendentals=0,
        ),
    )(me, real_labels.reshape(1, -1), syn_labels.reshape(1, -1), *images, records, freq)


def stage_two_kernel(me_ref, ka_s, ka_k, ra_s, ra_k, kb_s, kb_k, rb_s, rb_k, sa, na, sb, nb):
    sa[0] = (ka_s[0, 0] + ra_s[0, 0].astype(F32)).astype(BF)
    na[0] = ka_k[0, 0] + ra_k[0, 0].astype(F32)
    sb[0] = (kb_s[0, 0] + rb_s[0, 0].astype(F32)).astype(BF)
    nb[0] = kb_k[0, 0] + rb_k[0, 0].astype(F32)


def stage_two(me, keep_a, got_a, keep_b, got_b):
    half, width = keep_b.shape[2:]
    shape = (1, 1, half, width)
    keep_a = keep_a.reshape(2, 2, half, width)
    got_a = got_a.reshape(2, 2, half, width)
    low = lambda flip: block(shape, lambda h, me: (h, me[2] ^ flip, 0, 0))
    xs = lambda flip: block(shape, lambda h, me: (h, me[1] ^ flip, 0, 0))
    out = block((1, half, width), lambda h, me: (h, 0, 0))
    spec = pltpu.PrefetchScalarGridSpec(
        num_scalar_prefetch=1,
        grid=(2,),
        in_specs=[low(1), low(0), low(1), low(0), xs(1), xs(0), xs(1), xs(0)],
        out_specs=[out] * 4,
    )
    kinds = [BF, F32, BF, F32]
    return pl.pallas_call(
        stage_two_kernel,
        grid_spec=spec,
        out_shape=[jax.ShapeDtypeStruct((2, half, width), t) for t in kinds],
        compiler_params=pltpu.CompilerParams(vmem_limit_bytes=8 * 2**20),
        cost_estimate=pl.CostEstimate(flops=0, bytes_accessed=4 * 2**20, transcendentals=0),
    )(me, keep_a, keep_a, got_a, got_a, keep_b, keep_b, got_b, got_b)


def stage_three_kernel(me_ref, na_s, na_k, ga_s, ga_k, nb_s, nb_k, gb_s, gb_k, send, keep):
    half = na_s.shape[1]
    send[:half] = (na_s[0] + ga_s[0].astype(F32)).astype(BF)
    keep[:half] = na_k[0] + ga_k[0].astype(F32)
    send[half:] = (nb_s[0] + gb_s[0].astype(F32)).astype(BF)
    keep[half:] = nb_k[0] + gb_k[0].astype(F32)


def stage_three(me, next_a, got_a, next_b, got_b):
    _, half, width = next_a.shape
    high = lambda flip: block((1, half, width), lambda h, me: (me[3] ^ flip, 0, 0))
    out = block((2 * half, width), lambda h, me: (0, 0))
    spec = pltpu.PrefetchScalarGridSpec(
        num_scalar_prefetch=1,
        grid=(1,),
        in_specs=[high(1), high(0)] * 4,
        out_specs=[out, out],
    )
    return pl.pallas_call(
        stage_three_kernel,
        grid_spec=spec,
        out_shape=[jax.ShapeDtypeStruct((2 * half, width), t) for t in (BF, F32)],
        compiler_params=pltpu.CompilerParams(vmem_limit_bytes=8 * 2**20),
        cost_estimate=pl.CostEstimate(flops=0, bytes_accessed=3 * 2**20, transcendentals=0),
    )(me, next_a, next_a, got_a, got_a, next_b, next_b, got_b, got_b)


def gap_kernel(real_total, me_ref, keep_ref, got_ref, noise_ref, labels_ref, out_ref):
    classes = keep_ref.shape[0]
    part = noise_ref.shape[2]
    noise = jnp.concatenate([noise_ref[:, 0, :], noise_ref[:, 1, :]], axis=1)
    gap = keep_ref[...] + got_ref[...].astype(F32) - noise * (1.0 / real_total)
    gap = (16.0 * gap).astype(BF)
    ids = lax.broadcasted_iota(jnp.int32, (labels_ref.shape[0], classes), 1)
    table = jnp.where(ids == labels_ref[...], 1.0, 0.0).astype(BF)
    out_ref[...] = jnp.dot(table, gap, preferred_element_type=F32).astype(BF)


def gap_rows(me, keep, got, noise, labels, real_total):
    classes, width = keep.shape
    total = labels.shape[0]
    spec = pltpu.PrefetchScalarGridSpec(
        num_scalar_prefetch=1,
        grid=(1,),
        in_specs=[
            block((classes, width), lambda h, me: (0, 0)),
            block((classes, width), lambda h, me: (0, 0)),
            block((classes, 2, width // 2), lambda h, me: (0, 0, me[4])),
            block((total, 1), lambda h, me: (0, 0)),
        ],
        out_specs=block((total, width), lambda h, me: (0, 0)),
    )
    return pl.pallas_call(
        functools.partial(gap_kernel, real_total),
        grid_spec=spec,
        out_shape=jax.ShapeDtypeStruct((total, width), BF),
        compiler_params=pltpu.CompilerParams(vmem_limit_bytes=14 * 2**20),
        cost_estimate=pl.CostEstimate(
            flops=2 * total * classes * width, bytes_accessed=3 * 2**20, transcendentals=0
        ),
    )(me, keep, got, noise, labels.reshape(total, 1))


NT = (((1,), (1,)), ((), ()))


def image_kernel(me_ref, cs_ref, rows_ref, freq_ref, send_ref, keep_ref, pre_ref):
    step = pl.program_id(0)
    owners, _, width = rows_ref.shape
    part = width // 2

    @pl.when(step == 0)
    def _():
        for o in range(owners):
            at = slice(o * part, (o + 1) * part)
            grad = rows_ref[o].astype(F32)
            pre = cs_ref[0, :, at] * grad[:, part:] - cs_ref[1, :, at] * grad[:, :part]
            pre_ref[:, at] = pre.astype(BF)

    out = lax.dot_general(freq_ref[...], pre_ref[...], NT, preferred_element_type=F32)

    @pl.when(step < 2)
    def _():
        send_ref[0] = out.astype(BF)

    @pl.when(step >= 2)
    def _():
        keep_ref[0] = out


def image_grads(me, cs, feat_rows, freq, cols):
    k, n = freq.shape
    owners, rows, width = feat_rows.shape
    spec = pltpu.PrefetchScalarGridSpec(
        num_scalar_prefetch=1,
        grid=(4,),
        in_specs=[
            block((2, rows, n), lambda s, me: (0, 0, 0)),
            block((owners, rows, width), lambda s, me: (0, 0, 0)),
            block((cols, n), lambda s, me: ((s % 2) * 2 + ((me[0] % 2) ^ (1 - s // 2)), 0)),
        ],
        out_specs=[
            block((1, cols, rows), lambda s, me: (jnp.minimum(s, 1), 0, 0)),
            block((1, cols, rows), lambda s, me: (jnp.maximum(s - 2, 0), 0, 0)),
        ],
        scratch_shapes=[pltpu.VMEM((rows, n), BF)],
    )
    return pl.pallas_call(
        image_kernel,
        grid_spec=spec,
        out_shape=[jax.ShapeDtypeStruct((2, cols, rows), t) for t in (BF, F32)],
        compiler_params=pltpu.CompilerParams(vmem_limit_bytes=24 * 2**20),
        cost_estimate=pl.CostEstimate(flops=2 * k * n * rows, bytes_accessed=2 * k * n, transcendentals=0),
    )(me, cs, feat_rows, freq)


def split_y_kernel(me_ref, keep_s, keep_k, got_s, got_k, send, keep):
    send[...] = (keep_s[0] + got_s[0].astype(F32)).astype(BF)
    keep[...] = keep_k[0] + got_k[0].astype(F32)


def split_y(me, keep, got):
    _, cols, rows = keep.shape
    at = lambda flip: block((1, cols, rows), lambda h, me: ((me[0] // 2) ^ flip, 0, 0))
    out = block((cols, rows), lambda h, me: (0, 0))
    spec = pltpu.PrefetchScalarGridSpec(
        num_scalar_prefetch=1, grid=(1,), in_specs=[at(1), at(0)] * 2, out_specs=[out, out]
    )
    return pl.pallas_call(
        split_y_kernel,
        grid_spec=spec,
        out_shape=[jax.ShapeDtypeStruct((cols, rows), t) for t in (BF, F32)],
        compiler_params=pltpu.CompilerParams(vmem_limit_bytes=8 * 2**20),
        cost_estimate=pl.CostEstimate(flops=0, bytes_accessed=2**20, transcendentals=0),
    )(me, keep, keep, got, got)


def out_kernel(keep, got, image, out, flipped):
    grad = (keep[...] + got[...].astype(F32)).T
    grad = grad * (1.0 - jnp.square(image[...].astype(F32)))
    out[...] = grad.astype(BF)
    flipped[...] = grad.T.astype(BF)


def out_grads(keep, got, image):
    rows, cols = image.shape
    return pl.pallas_call(
        out_kernel,
        out_shape=[jax.ShapeDtypeStruct((rows, cols), BF), jax.ShapeDtypeStruct((cols, rows), BF)],
        compiler_params=pltpu.CompilerParams(vmem_limit_bytes=8 * 2**20),
        cost_estimate=pl.CostEstimate(flops=0, bytes_accessed=2**20, transcendentals=0),
    )(keep, got, image)


def hidden_kernel(me_ref, w_ref, grad_ref, send, keep):
    core = me_ref[0] % 2
    out = jnp.dot(w_ref[...], grad_ref[...], preferred_element_type=F32)
    count, half, rows = send.shape
    out = out.reshape(count, 2, half, rows)
    keep[...] = jnp.where(core == 0, out[:, 0], out[:, 1])
    send[...] = jnp.where(core == 0, out[:, 1], out[:, 0]).astype(BF)


def hidden_grads(me, w_out, flipped, groups):
    cols, rows = flipped.shape
    hid = w_out.shape[0]
    mine = hid // groups
    out = block((2, mine // 2, rows), lambda r, me: (r, 0, 0))
    spec = pltpu.PrefetchScalarGridSpec(
        num_scalar_prefetch=1,
        grid=(groups // 2,),
        in_specs=[
            block((2 * mine, cols), lambda r, me: (r, 0)),
            block((cols, rows), lambda r, me: (0, 0)),
        ],
        out_specs=[out, out],
    )
    return pl.pallas_call(
        hidden_kernel,
        grid_spec=spec,
        out_shape=[jax.ShapeDtypeStruct((groups, mine // 2, rows), t) for t in (BF, F32)],
        compiler_params=pltpu.CompilerParams(vmem_limit_bytes=8 * 2**20),
        cost_estimate=pl.CostEstimate(
            flops=2 * hid * cols * rows, bytes_accessed=2 * hid * cols, transcendentals=0
        ),
    )(me, w_out, flipped)


def add_kernel(a, b, out):
    out[...] = (a[...].astype(F32) + b[...].astype(F32)).astype(out.dtype)


def add(a, b, kind):
    return pl.pallas_call(
        add_kernel,
        out_shape=jax.ShapeDtypeStruct(a.shape, kind),
        compiler_params=pltpu.CompilerParams(vmem_limit_bytes=8 * 2**20),
        cost_estimate=pl.CostEstimate(flops=0, bytes_accessed=2**20, transcendentals=0),
    )(a, b)


def weight_kernel(me_ref, hidden_ref, *refs):
    out_ref = refs[-1]
    acc = None
    for mask, grad in enumerate(refs[:-1]):
        rows = grad.shape[0]
        at = pl.multiple_of((me_ref[4] ^ mask) * rows, 128)
        d = jnp.dot(hidden_ref[:, pl.ds(at, rows)], grad[...], preferred_element_type=F32)
        acc = d if acc is None else acc + d
    out_ref[...] = acc


def weight_grads(me, hidden, grads):
    rows, cols = grads[0].shape
    mine, total = hidden.shape
    spec = pltpu.PrefetchScalarGridSpec(
        num_scalar_prefetch=1,
        grid=(1,),
        in_specs=[block((mine, total), lambda h, me: (0, 0))]
        + [block((rows, cols), lambda h, me: (0, 0)) for _ in grads],
        out_specs=block((mine, cols), lambda h, me: (0, 0)),
    )
    return pl.pallas_call(
        weight_kernel,
        grid_spec=spec,
        out_shape=jax.ShapeDtypeStruct((mine, cols), F32),
        compiler_params=pltpu.CompilerParams(vmem_limit_bytes=12 * 2**20),
        cost_estimate=pl.CostEstimate(
            flops=2 * mine * total * cols, bytes_accessed=4 * 2**20, transcendentals=0
        ),
    )(me, hidden, *grads)


def last_kernel(me_ref, got_ref, preact_ref, lhs_ref, out_ref):
    groups, width, rows = got_ref.shape
    acc = None
    for g in range(groups):
        at = slice(g * rows, (g + 1) * rows)
        grad = jnp.where(preact_ref[:, at] > 0, got_ref[g].astype(F32), 0.0).astype(BF)
        d = lax.dot_general(lhs_ref[:, at], grad, NT, preferred_element_type=F32)
        acc = d if acc is None else acc + d
    out_ref[...] = acc


def last_grads(me, got, preact, lhs):
    groups, width, rows = got.shape
    count, total = lhs.shape
    spec = pltpu.PrefetchScalarGridSpec(
        num_scalar_prefetch=1,
        grid=(1,),
        in_specs=[
            block((groups, width, rows), lambda h, me: (0, 0, 0)),
            block((width, total), lambda h, me: (me[0] % 2, 0)),
            block((count, total), lambda h, me: (0, 0)),
        ],
        out_specs=block((count, width), lambda h, me: (0, 0)),
    )
    return pl.pallas_call(
        last_kernel,
        grid_spec=spec,
        out_shape=jax.ShapeDtypeStruct((count, width), F32),
        compiler_params=pltpu.CompilerParams(vmem_limit_bytes=12 * 2**20),
        cost_estimate=pl.CostEstimate(
            flops=2 * total * count * width, bytes_accessed=2 * 2**20, transcendentals=0
        ),
    )(me, got, preact, lhs)


def eight_by_four(
    records, real_labels, frequencies, class_noise, latents, syn_labels, w_latent, class_embed, w_out
):
    classes, hid = class_embed.shape
    groups = lax.axis_size("rec")
    rec = lax.axis_index("rec")
    feat = lax.axis_index("feat")
    rows, dz = latents.shape
    cols = w_out.shape[1]
    real_total = records.shape[0] * groups
    syn_total = rows * groups
    me = jnp.stack([feat, rec % 2, (rec // 2) % 2, rec // 4, rec]).astype(jnp.int32)

    table = one_hot(syn_labels, classes, BF)
    preact = jnp.dot(latents, w_latent, preferred_element_type=F32) + jnp.dot(
        table, class_embed, preferred_element_type=F32
    )
    hidden = jnp.maximum(preact, 0.0).astype(BF)
    own = jnp.tanh(jnp.dot(hidden, w_out, preferred_element_type=F32)).astype(BF)
    far = swap(own, "feat", 2)
    images = [own, far, swap(own, "feat", 1), swap(far, "feat", 1)]

    label_row = jnp.zeros((16, dz), BF).at[0, :].set(syn_labels.astype(BF))
    packed = jnp.concatenate([latents, label_row], axis=0)
    packed = lax.all_to_all(
        jnp.broadcast_to(packed[None], (groups,) + packed.shape), "rec", 0, 0, tiled=True
    )

    send_a, keep_a, send_b, keep_b, cs = feature_sums(
        me, real_labels, syn_labels, (0, 2, 1, 3), images, records, frequencies, classes,
        (real_total, syn_total),
    )
    got_a = swap(send_a, "rec", 1)
    got_b = swap(send_b, "rec", 2)

    all_latents = packed[:, :rows].reshape(syn_total, dz)
    all_labels = packed[:, rows].reshape(syn_total).astype(jnp.int32)
    all_table = one_hot(all_labels, classes, BF)
    mine = hid // groups
    lhs = jnp.concatenate([all_latents, all_table], axis=1).T
    w = jnp.concatenate(
        [
            lax.dynamic_slice_in_dim(w_latent, rec * mine, mine, 1),
            lax.dynamic_slice_in_dim(class_embed, rec * mine, mine, 1),
        ],
        axis=0,
    )
    all_preact = lax.dot_general(w, lhs, (((0,), (0,)), ((), ())), preferred_element_type=F32)
    all_hidden = jnp.maximum(all_preact, 0.0).astype(BF)

    send_a, next_a, send_b, next_b = stage_two(me, keep_a, got_a, keep_b, got_b)
    got_a = swap(send_a, "rec", 2)
    got_b = swap(send_b, "rec", 1)
    send, keep = stage_three(me, next_a, got_a, next_b, got_b)
    got = swap(send, "rec", 4)
    feat_grad = gap_rows(me, keep, got, class_noise, all_labels, real_total)
    feat_grad = lax.all_to_all(feat_grad.reshape(groups, rows, -1), "rec", 0, 0, tiled=True)

    send, keep = image_grads(me, cs, feat_grad, frequencies, cols)
    send, keep = split_y(me, keep, swap(send, "feat", 1))
    out_grad, flipped = out_grads(keep, swap(send, "feat", 2), own)

    by = {0: out_grad}
    by[1] = swap(out_grad, "rec", 1)
    by[2] = swap(out_grad, "rec", 2)
    by[4] = swap(out_grad, "rec", 4)
    by[3] = swap(by[2], "rec", 1)
    by[6] = swap(by[4], "rec", 2)
    by[5] = swap(by[4], "rec", 1)
    by[7] = swap(by[6], "rec", 1)

    send, keep = hidden_grads(me, w_out, flipped, groups)
    part_grad = add(keep, swap(send, "feat", 1), BF)
    part_grad = add(part_grad, swap(part_grad, "feat", 2), BF)
    part_grad = lax.all_to_all(part_grad, "rec", 0, 0, tiled=True)
    grads = last_grads(me, part_grad, all_preact, lhs)
    other = swap(grads, "feat", 1)
    core = feat % 2
    grads = jnp.concatenate(
        [jnp.where(core == 0, grads, other), jnp.where(core == 0, other, grads)], axis=1
    )
    grad_w_out = weight_grads(me, all_hidden, [by[mask] for mask in range(groups)])
    return grad_w_out, grads[:dz], grads[dz:]


def solution(mesh):
    shape = (mesh.shape["rec"], mesh.shape["feat"])
    in_specs = (
        P("rec", None),
        P("rec"),
        P(None, "feat"),
        P(None, None, "feat"),
        P("rec", None),
        P("rec"),
        P(),
        P(),
        P(None, "feat"),
    )
    out_specs = (P("rec", "feat"), P(None, "rec"), P(None, "rec"))
    return jax.shard_map(
        eight_by_four if shape == (8, 4) else general, mesh=mesh, in_specs=in_specs, out_specs=out_specs, check_vma=False
    )
```

```python
import functools

import jax
import jax.numpy as jnp
from jax import lax
from jax.experimental import pallas as pl
from jax.experimental.pallas import tpu as pltpu
from jax.sharding import PartitionSpec as P

BF = jnp.bfloat16
F32 = jnp.float32

TURN = 0.15915494309189535
SIN = (4.44286783702217, -7.307441307726672, 3.59477116396636, -0.7843353598850176)
COS = (1.4142134962552275, -6.978850948563815, 5.739460376907241, -1.883557905986894, 0.3106880275267554)


def cos_sin(x):
    turns = x * TURN
    u = turns - jnp.round(turns)
    sq = u * u
    p = SIN[-1]
    for c in SIN[-2::-1]:
        p = p * sq + c
    q = COS[-1]
    for c in COS[-2::-1]:
        q = q * sq + c
    s = u * p
    return 1.0 - s * s, s * q


def one_hot(labels, count, dtype):
    return (labels[:, None] == jnp.arange(count, dtype=jnp.int32)[None, :]).astype(dtype)


def real_kernel(rows, labels_ref, records_ref, freq_ref, out_ref, table_ref):
    total = records_ref.shape[0]
    classes = table_ref.shape[0]
    owners, _, width = out_ref.shape
    part = width // 2

    @pl.when(pl.program_id(0) == 0)
    def _():
        ids = lax.broadcasted_iota(jnp.int32, (classes, total), 0)
        table_ref[...] = jnp.where(ids == labels_ref[...], 1.0, 0.0).astype(BF)

    freq = freq_ref[...]
    block = freq.shape[1]

    def sums(i, pre):
        co, si = cos_sin(pre)
        phi = jnp.concatenate([co.astype(BF), si.astype(BF)], axis=1)
        return jnp.dot(table_ref[:, i * rows : (i + 1) * rows], phi, preferred_element_type=F32)

    acc = None
    before = None
    steps = total // rows
    for i in range(steps + 1):
        pre = None
        if i < steps:
            pre = jnp.dot(records_ref[i * rows : (i + 1) * rows, :], freq, preferred_element_type=F32)
        if i > 0:
            d = sums(i - 1, before)
            acc = d if acc is None else acc + d
        before = pre
    for o in range(owners):
        out_ref[o, :, :part] = acc[:, o * part : (o + 1) * part]
        out_ref[o, :, part:] = acc[:, block + o * part : block + (o + 1) * part]


def real_sums(labels, records, freq, classes, owners):
    m, k = records.shape
    n = freq.shape[1]
    block = min(512, n)
    rows = 512
    part = n // owners
    per = block // part
    return pl.pallas_call(
        functools.partial(real_kernel, rows),
        grid=(n // block,),
        in_specs=[
            pl.BlockSpec((1, m), lambda j: (0, 0)),
            pl.BlockSpec((m, k), lambda j: (0, 0)),
            pl.BlockSpec((k, block), lambda j: (0, j)),
        ],
        out_specs=pl.BlockSpec((per, classes, 2 * part), lambda j: (j, 0, 0)),
        out_shape=jax.ShapeDtypeStruct((owners, classes, 2 * part), F32),
        scratch_shapes=[pltpu.VMEM((classes, m), BF)],
        compiler_params=pltpu.CompilerParams(vmem_limit_bytes=56 * 2**20),
        cost_estimate=pl.CostEstimate(
            flops=2 * m * n * (k + 2 * classes), bytes_accessed=2 * (m * k + k * n), transcendentals=0
        ),
    )(labels.reshape(1, m), records, freq)


def bits_of(n):
    return [1 << b for b in range(n.bit_length() - 1)]


def swap(x, axis, bit):
    n = lax.axis_size(axis)
    return lax.ppermute(x, axis, [(i, i ^ bit) for i in range(n)])


def pick(x, index, dim):
    return lax.dynamic_index_in_dim(x, index, dim, keepdims=False)


def halving(x, axis, order, count):
    me = lax.axis_index(axis)
    nbits = len(order)
    x = x.reshape((2,) * nbits + x.shape[1:])
    left = sorted(order, reverse=True)
    for bit in order:
        dim = left.index(bit)
        left.remove(bit)
        mine = (me // bit) % 2
        got = swap(pick(x, 1 - mine, dim).astype(BF), axis, bit)
        x = pick(x, mine, dim).astype(F32) + got.astype(F32)
    return x


def general(
    records, real_labels, frequencies, class_noise, latents, syn_labels, w_latent, class_embed, w_out
):
    classes = class_embed.shape[0]
    hid = class_embed.shape[1]
    groups = lax.axis_size("rec")
    feats = lax.axis_size("feat")
    rec = lax.axis_index("rec")
    nf = frequencies.shape[1]
    part = nf // groups
    rows, dz = latents.shape
    cols = w_out.shape[1]
    real_total = records.shape[0] * groups
    syn_total = rows * groups

    label_row = jnp.zeros((16, dz), BF).at[0, :].set(syn_labels.astype(BF))
    packed = jnp.concatenate([latents, label_row], axis=0)
    packed = lax.all_to_all(
        jnp.broadcast_to(packed[None], (groups,) + packed.shape), "rec", 0, 0, tiled=True
    )
    all_latents = packed[:, :rows].reshape(syn_total, dz)
    all_labels = packed[:, rows].reshape(syn_total).astype(jnp.int32)
    all_table = one_hot(all_labels, classes, BF)

    table = one_hot(syn_labels, classes, BF)
    preact = jnp.dot(latents, w_latent, preferred_element_type=F32) + jnp.dot(
        table, class_embed, preferred_element_type=F32
    )
    hidden = jnp.maximum(preact, 0.0).astype(BF)
    own_images = jnp.tanh(jnp.dot(hidden, w_out, preferred_element_type=F32)).astype(BF)
    images = lax.all_gather(own_images, "feat", axis=0)
    images = images.transpose(1, 0, 2).reshape(rows, feats * cols)
    syn_pre = jnp.dot(images, frequencies, preferred_element_type=F32)
    syn_cos, syn_sin = cos_sin(syn_pre)
    syn_phi = jnp.concatenate(
        [syn_cos.reshape(rows, groups, part), syn_sin.reshape(rows, groups, part)], axis=2
    ).astype(BF)
    syn_sum = lax.dot_general(
        table, syn_phi.reshape(rows, 2 * nf), (((0,), (0,)), ((), ())), preferred_element_type=F32
    )
    syn_sum = syn_sum.reshape(classes, groups, 2 * part).transpose(1, 0, 2)

    real_sum = real_sums(real_labels, records, frequencies, classes, groups)
    gap = syn_sum * (1.0 / syn_total) - real_sum * (1.0 / real_total)
    half = classes // 2
    order = bits_of(groups)
    other = [order[1], order[0]] + order[2:]
    gap = jnp.concatenate(
        [halving(gap[:, :half], "rec", order, groups), halving(gap[:, half:], "rec", other, groups)], axis=0
    )
    noise = lax.dynamic_slice_in_dim(class_noise, rec * part, part, 2).reshape(classes, 2 * part)
    gap = (16.0 * (gap - noise * (1.0 / real_total))).astype(BF)

    feat_grad = jnp.dot(all_table, gap, preferred_element_type=F32).astype(BF)
    feat_grad = lax.all_to_all(feat_grad.reshape(groups, rows, 2 * part), "rec", 0, 0, tiled=True)
    feat_grad = feat_grad.transpose(1, 0, 2).astype(F32)
    pre_grad = (
        -syn_sin.reshape(rows, groups, part) * feat_grad[:, :, :part]
        + syn_cos.reshape(rows, groups, part) * feat_grad[:, :, part:]
    )
    pre_grad = pre_grad.astype(BF).reshape(rows, nf)
    image_grad = lax.dot_general(
        frequencies, pre_grad, (((1,), (1,)), ((), ())), preferred_element_type=F32
    )
    image_grad = halving(image_grad.reshape(feats, cols, rows), "feat", bits_of(feats), feats)
    image_grad = image_grad.T
    out_grad = (image_grad * (1.0 - jnp.square(own_images.astype(F32)))).astype(BF)

    out_grad = lax.all_to_all(
        jnp.broadcast_to(out_grad[None], (groups, rows, cols)), "rec", 0, 0, tiled=True
    ).reshape(syn_total, cols)

    mine = hid // groups
    start = rec * mine
    all_preact = jnp.dot(
        all_latents, lax.dynamic_slice_in_dim(w_latent, start, mine, 1), preferred_element_type=F32
    ) + jnp.dot(
        all_table, lax.dynamic_slice_in_dim(class_embed, start, mine, 1), preferred_element_type=F32
    )
    all_hidden = jnp.maximum(all_preact, 0.0).astype(BF)
    grad_w_out = lax.dot_general(
        all_hidden, out_grad, (((0,), (0,)), ((), ())), preferred_element_type=F32
    )
    hidden_grad = lax.dot_general(
        out_grad,
        lax.dynamic_slice_in_dim(w_out, start, mine, 0),
        (((1,), (1,)), ((), ())),
        preferred_element_type=F32,
    )
    core = lax.axis_index("feat") % 2
    half = syn_total // 2
    hidden_grad = hidden_grad.reshape(2, half, mine)
    got = swap(pick(hidden_grad, 1 - core, 0).astype(BF), "feat", 1)
    hidden_grad = pick(hidden_grad, core, 0) + got.astype(F32)
    for bit in bits_of(feats)[1:]:
        send = hidden_grad.astype(BF)
        hidden_grad = send.astype(F32) + swap(send, "feat", bit).astype(F32)
    my_preact = lax.dynamic_slice_in_dim(all_preact, core * half, half, 0)
    pre_hidden = jnp.where(my_preact > 0, hidden_grad, 0.0).astype(BF)
    lhs = jnp.concatenate([all_latents, all_table], axis=1)
    lhs = lax.dynamic_slice_in_dim(lhs, core * half, half, 0)
    grads = lax.dot_general(lhs, pre_hidden, (((0,), (0,)), ((), ())), preferred_element_type=F32)
    grads = grads + swap(grads, "feat", 1)
    return grad_w_out, grads[:dz], grads[dz:]


def block(shape, index):
    return pl.BlockSpec(shape, index)


def sums(table, pre):
    co, si = cos_sin(pre)
    phi = jnp.concatenate([co.astype(BF), si.astype(BF)], axis=1)
    return jnp.dot(table, phi, preferred_element_type=F32)


def features_kernel(
    masks, last, real_total, syn_total, me_ref, real_labels_ref, syn_labels_ref, *refs
):
    count = len(masks)
    images = refs[:count]
    records_hbm, freq_ref = refs[count : count + 2]
    outs = refs[count + 2 : -4]
    records, real_table, syn_table, sem = refs[-4:]
    classes, total = real_table.shape
    size = 512
    steps = total // size
    step = pl.program_id(0)
    cols = images[0].shape[1]
    half = classes // 2

    def copy(i):
        at = pl.ds(i * size, size)
        return pltpu.make_async_copy(records_hbm.at[at, :], records.at[at, :], sem.at[i])

    def work(wait):
        if wait:
            for i in range(steps):
                copy(i).start()
            ids = lax.broadcasted_iota(jnp.int32, (classes, total), 0)
            real_table[...] = jnp.where(ids == real_labels_ref[...], 1.0, 0.0).astype(BF)
            ids = lax.broadcasted_iota(jnp.int32, syn_table.shape, 0)
            syn_table[...] = jnp.where(ids == syn_labels_ref[...], 1.0, 0.0).astype(BF)
        syn_pre = None
        for mask, image in zip(masks, images):
            at = pl.multiple_of((me_ref[0] ^ mask) * cols, 128)
            d = jnp.dot(image[...], freq_ref[pl.ds(at, cols), :], preferred_element_type=F32)
            syn_pre = d if syn_pre is None else syn_pre + d
        freq = freq_ref[...]
        acc = None
        before = None
        for i in range(steps + 1):
            if i < steps:
                if wait:
                    copy(i).wait()
                pre = jnp.dot(records[i * size : (i + 1) * size, :], freq, preferred_element_type=F32)
            if i == 0:
                co, si = cos_sin(syn_pre)
                outs[-1][0, 0] = co
                outs[-1][0, 1] = si
                phi = jnp.concatenate([co.astype(BF), si.astype(BF)], axis=1)
                syn = jnp.dot(syn_table[...], phi, preferred_element_type=F32)
            else:
                d = sums(real_table[:, (i - 1) * size : i * size], before)
                acc = d if acc is None else acc + d
            before = pre
        gap = syn * (1.0 / syn_total) - acc * (1.0 / real_total)
        width = gap.shape[1] // 4
        return [
            jnp.concatenate(
                [gap[:, h * width : (h + 1) * width], gap[:, (h + 2) * width : (h + 3) * width]], axis=1
            )
            for h in range(2)
        ]

    if last:
        parts = work(True)
        for h in range(2):
            outs[0][h] = parts[h][:half]
            outs[1][h] = parts[h][half:]
        return
    send_a, keep_a, send_b, keep_b = outs[:4]

    @pl.when(step == 0)
    def _():
        parts = work(True)
        for h in range(2):
            send_a[0, h] = parts[h][:half].astype(BF)
            send_b[0, h] = parts[h][half:].astype(BF)

    @pl.when(step > 0)
    def _():
        parts = work(False)

        @pl.when(step == 1)
        def _():
            for h in range(2):
                send_a[0, h] = parts[h][:half].astype(BF)
                keep_b[h] = parts[h][half:]

        @pl.when(step == 2)
        def _():
            for h in range(2):
                keep_a[h] = parts[h][:half]
                send_b[0, h] = parts[h][half:].astype(BF)


def feature_sums(last, me, real_labels, syn_labels, masks, images, records, freq, classes, totals):
    total, k = records.shape
    n = freq.shape[1]
    rows, cols = images[0].shape
    half = classes // 2
    tile = n // 4
    tiles = 1 if last else 3
    whole = lambda shape: block(shape, lambda j, me: (0,) * len(shape))
    kept = jax.ShapeDtypeStruct((2, half, tile), F32)
    sent = jax.ShapeDtypeStruct((2, 2, half, tile), BF)
    wave = jax.ShapeDtypeStruct((tiles, 2, rows, tile), F32)
    wave_spec = block((1, 2, rows, tile), lambda j, me: (j, 0, 0, 0))
    if last:
        shapes = [kept, kept, wave]
        specs = [whole(kept.shape), whole(kept.shape), wave_spec]
    else:
        shapes = [sent, kept, sent, kept, wave]
        specs = [
            block((1, 2, half, tile), lambda j, me: (jnp.minimum(j, 1), 0, 0, 0)),
            whole(kept.shape),
            block((1, 2, half, tile), lambda j, me: (j // 2, 0, 0, 0)),
            whole(kept.shape),
            wave_spec,
        ]
    grid_spec = pltpu.PrefetchScalarGridSpec(
        num_scalar_prefetch=1,
        grid=(tiles,),
        in_specs=[whole((1, total)), whole((1, rows))]
        + [whole((rows, cols)) for _ in images]
        + [
            pl.BlockSpec(memory_space=pl.ANY),
            block((k, tile), lambda j, me: (0, me[5] ^ (0 if last else 3 - j))),
        ],
        out_specs=specs,
        scratch_shapes=[
            pltpu.VMEM((total, k), BF),
            pltpu.VMEM((classes, total), BF),
            pltpu.VMEM((classes, rows), BF),
            pltpu.SemaphoreType.DMA((total // 512,)),
        ],
    )
    return pl.pallas_call(
        functools.partial(features_kernel, masks, last, *totals),
        grid_spec=grid_spec,
        out_shape=shapes,
        compiler_params=pltpu.CompilerParams(vmem_limit_bytes=44 * 2**20),
        cost_estimate=pl.CostEstimate(
            flops=2 * (total + rows) * tiles * tile * (k + 2 * classes),
            bytes_accessed=2 * (total * k + k * tiles * tile),
            transcendentals=0,
        ),
    )(me, real_labels.reshape(1, -1), syn_labels.reshape(1, -1), *images, records, freq)


def stage_two_send_kernel(ka, ga, kb, gb, sa, sb):
    sa[...] = (ka[...] + ga[0].astype(F32)).astype(BF)
    sb[...] = (kb[...] + gb[0].astype(F32)).astype(BF)


def stage_two_send(keep_a, got_a, keep_b, got_b):
    return pl.pallas_call(
        stage_two_send_kernel,
        out_shape=[jax.ShapeDtypeStruct(keep_a.shape, BF)] * 2,
        compiler_params=pltpu.CompilerParams(vmem_limit_bytes=10 * 2**20),
        cost_estimate=pl.CostEstimate(flops=0, bytes_accessed=3 * 2**20, transcendentals=0),
    )(keep_a, got_a, keep_b, got_b)


def stage_three_kernel(me_ref, na, fa, ga, nb, fb, gb, send, keep):
    high = me_ref[3]
    half = na.shape[1]
    for flip, out in ((1, send), (0, keep)):
        at = high ^ flip
        out[:half] = (na[at] + fa[1, at].astype(F32) + ga[at].astype(F32)).astype(out.dtype)
        out[half:] = (nb[at] + fb[1, at].astype(F32) + gb[at].astype(F32)).astype(out.dtype)


def stage_three(me, keep_a, first_a, got_a, keep_b, first_b, got_b):
    _, half, width = keep_a.shape
    args = (keep_a, first_a, got_a, keep_b, first_b, got_b)
    whole = lambda shape: block(shape, lambda h, me: (0,) * len(shape))
    spec = pltpu.PrefetchScalarGridSpec(
        num_scalar_prefetch=1,
        grid=(1,),
        in_specs=[whole(x.shape) for x in args],
        out_specs=[whole((2 * half, width))] * 2,
    )
    return pl.pallas_call(
        stage_three_kernel,
        grid_spec=spec,
        out_shape=[jax.ShapeDtypeStruct((2 * half, width), t) for t in (BF, F32)],
        compiler_params=pltpu.CompilerParams(vmem_limit_bytes=12 * 2**20),
        cost_estimate=pl.CostEstimate(flops=0, bytes_accessed=3 * 2**20, transcendentals=0),
    )(me, *args)


def gap_kernel(real_total, keep_ref, got_ref, noise_ref, labels_ref, out_ref):
    classes = keep_ref.shape[0]
    gap = keep_ref[...] + got_ref[...].astype(F32) - noise_ref[...] * (1.0 / real_total)
    gap = (16.0 * gap).astype(BF)
    ids = lax.broadcasted_iota(jnp.int32, (labels_ref.shape[0], classes), 1)
    table = jnp.where(ids == labels_ref[...], 1.0, 0.0).astype(BF)
    out_ref[...] = jnp.dot(table, gap, preferred_element_type=F32).astype(BF)


def gap_rows(keep, got, noise, labels, real_total):
    classes, width = keep.shape
    total = labels.shape[0]
    return pl.pallas_call(
        functools.partial(gap_kernel, real_total),
        out_shape=jax.ShapeDtypeStruct((total, width), BF),
        compiler_params=pltpu.CompilerParams(vmem_limit_bytes=14 * 2**20),
        cost_estimate=pl.CostEstimate(
            flops=2 * total * classes * width, bytes_accessed=3 * 2**20, transcendentals=0
        ),
    )(keep, got, noise, labels.reshape(total, 1))


NT = (((1,), (1,)), ((), ()))


def image_kernel(me_ref, three_ref, last_ref, rows_ref, freq_ref, send_ref, keep_ref, pre_ref):
    step = pl.program_id(0)
    cols = send_ref.shape[1]
    tile = three_ref.shape[3]
    part = tile // 2

    @pl.when(step == 0)
    def _():
        for t in range(4):
            place = me_ref[5] ^ (3 - t)
            wave = last_ref.at[0] if t == 3 else three_ref.at[t]
            for h in range(2):
                grad = rows_ref[4 * h + 2 * (place % 2) + place // 2].astype(F32)
                lanes = slice(h * part, (h + 1) * part)
                pre = wave[0, :, lanes] * grad[:, part:] - wave[1, :, lanes] * grad[:, :part]
                at = pl.multiple_of(place * tile + h * part, 128)
                pre_ref[:, pl.ds(at, part)] = pre.astype(BF)

    out = lax.dot_general(freq_ref[...], pre_ref[...], NT, preferred_element_type=F32)
    steps = pl.num_programs(0) // 2

    @pl.when(step < steps)
    def _():
        send_ref[0] = out.astype(BF)

    @pl.when(step >= steps)
    def _():
        keep_ref[0] = out


def image_grads(me, three, last, feat_rows, freq, cols):
    k, n = freq.shape
    owners, rows, width = feat_rows.shape
    whole = lambda x: block(x.shape, lambda s, me: (0,) * x.ndim)

    def source(s, me):
        owner = 2 * ((s // 2) % 2) + ((me[0] % 2) ^ (1 - s // 4))
        return 2 * owner + s % 2, 0

    spec = pltpu.PrefetchScalarGridSpec(
        num_scalar_prefetch=1,
        grid=(8,),
        in_specs=[whole(three), whole(last), whole(feat_rows), block((cols // 2, n), source)],
        out_specs=[
            block((1, cols // 2, rows), lambda s, me: (jnp.minimum(s, 3) // 2, jnp.minimum(s, 3) % 2, 0)),
            block((1, cols // 2, rows), lambda s, me: (jnp.maximum(s - 4, 0) // 2, jnp.maximum(s - 4, 0) % 2, 0)),
        ],
        scratch_shapes=[pltpu.VMEM((rows, n), BF)],
    )
    return pl.pallas_call(
        image_kernel,
        grid_spec=spec,
        out_shape=[jax.ShapeDtypeStruct((2, cols, rows), t) for t in (BF, F32)],
        compiler_params=pltpu.CompilerParams(vmem_limit_bytes=56 * 2**20),
        cost_estimate=pl.CostEstimate(flops=2 * k * n * rows, bytes_accessed=2 * k * n, transcendentals=0),
    )(me, three, last, feat_rows, freq)


def split_y_kernel(me_ref, keep_s, keep_k, got_s, got_k, send, keep):
    send[...] = (keep_s[0] + got_s[0].astype(F32)).astype(BF)
    keep[...] = keep_k[0] + got_k[0].astype(F32)


def split_y(me, keep, got):
    _, cols, rows = keep.shape
    at = lambda flip: block((1, cols, rows), lambda h, me: ((me[0] // 2) ^ flip, 0, 0))
    out = block((cols, rows), lambda h, me: (0, 0))
    spec = pltpu.PrefetchScalarGridSpec(
        num_scalar_prefetch=1, grid=(1,), in_specs=[at(1), at(0)] * 2, out_specs=[out, out]
    )
    return pl.pallas_call(
        split_y_kernel,
        grid_spec=spec,
        out_shape=[jax.ShapeDtypeStruct((cols, rows), t) for t in (BF, F32)],
        compiler_params=pltpu.CompilerParams(vmem_limit_bytes=8 * 2**20),
        cost_estimate=pl.CostEstimate(flops=0, bytes_accessed=2**20, transcendentals=0),
    )(me, keep, keep, got, got)


def out_kernel(keep, got, image, out, flipped):
    grad = (keep[...] + got[...].astype(F32)).T
    grad = grad * (1.0 - jnp.square(image[...].astype(F32)))
    out[...] = grad.astype(BF)
    flipped[...] = grad.T.astype(BF)


def out_grads(keep, got, image):
    rows, cols = image.shape
    return pl.pallas_call(
        out_kernel,
        out_shape=[jax.ShapeDtypeStruct((rows, cols), BF), jax.ShapeDtypeStruct((cols, rows), BF)],
        compiler_params=pltpu.CompilerParams(vmem_limit_bytes=8 * 2**20),
        cost_estimate=pl.CostEstimate(flops=0, bytes_accessed=2**20, transcendentals=0),
    )(keep, got, image)


def hidden_kernel(me_ref, w_ref, grad_ref, send, keep):
    core = me_ref[0] % 2
    out = jnp.dot(w_ref[...], grad_ref[...], preferred_element_type=F32)
    count, half, rows = send.shape
    out = out.reshape(count, 2, half, rows)
    keep[...] = jnp.where(core == 0, out[:, 0], out[:, 1])
    send[...] = jnp.where(core == 0, out[:, 1], out[:, 0]).astype(BF)


def hidden_grads(me, w_out, flipped, groups):
    cols, rows = flipped.shape
    hid = w_out.shape[0]
    mine = hid // groups
    out = block((2, mine // 2, rows), lambda r, me: (r, 0, 0))
    spec = pltpu.PrefetchScalarGridSpec(
        num_scalar_prefetch=1,
        grid=(groups // 2,),
        in_specs=[
            block((2 * mine, cols), lambda r, me: (r, 0)),
            block((cols, rows), lambda r, me: (0, 0)),
        ],
        out_specs=[out, out],
    )
    return pl.pallas_call(
        hidden_kernel,
        grid_spec=spec,
        out_shape=[jax.ShapeDtypeStruct((groups, mine // 2, rows), t) for t in (BF, F32)],
        compiler_params=pltpu.CompilerParams(vmem_limit_bytes=8 * 2**20),
        cost_estimate=pl.CostEstimate(
            flops=2 * hid * cols * rows, bytes_accessed=2 * hid * cols, transcendentals=0
        ),
    )(me, w_out, flipped)


def add_kernel(a, b, out):
    out[...] = (a[...].astype(F32) + b[...].astype(F32)).astype(out.dtype)


def add(a, b, kind):
    return pl.pallas_call(
        add_kernel,
        out_shape=jax.ShapeDtypeStruct(a.shape, kind),
        compiler_params=pltpu.CompilerParams(vmem_limit_bytes=8 * 2**20),
        cost_estimate=pl.CostEstimate(flops=0, bytes_accessed=2**20, transcendentals=0),
    )(a, b)


def weight_kernel(me_ref, hidden_ref, *refs):
    out_ref = refs[-1]
    acc = None
    for mask, grad in enumerate(refs[:-1]):
        rows = grad.shape[0]
        at = pl.multiple_of((me_ref[4] ^ mask) * rows, 128)
        d = jnp.dot(hidden_ref[:, pl.ds(at, rows)], grad[...], preferred_element_type=F32)
        acc = d if acc is None else acc + d
    out_ref[...] = acc


def weight_grads(me, hidden, grads):
    rows, cols = grads[0].shape
    mine, total = hidden.shape
    spec = pltpu.PrefetchScalarGridSpec(
        num_scalar_prefetch=1,
        grid=(1,),
        in_specs=[block((mine, total), lambda h, me: (0, 0))]
        + [block((rows, cols), lambda h, me: (0, 0)) for _ in grads],
        out_specs=block((mine, cols), lambda h, me: (0, 0)),
    )
    return pl.pallas_call(
        weight_kernel,
        grid_spec=spec,
        out_shape=jax.ShapeDtypeStruct((mine, cols), F32),
        compiler_params=pltpu.CompilerParams(vmem_limit_bytes=12 * 2**20),
        cost_estimate=pl.CostEstimate(
            flops=2 * mine * total * cols, bytes_accessed=4 * 2**20, transcendentals=0
        ),
    )(me, hidden, *grads)


def last_kernel(me_ref, got_ref, preact_ref, lhs_ref, out_ref):
    groups, width, rows = got_ref.shape
    acc = None
    for g in range(groups):
        at = slice(g * rows, (g + 1) * rows)
        grad = jnp.where(preact_ref[:, at] > 0, got_ref[g].astype(F32), 0.0).astype(BF)
        d = lax.dot_general(lhs_ref[:, at], grad, NT, preferred_element_type=F32)
        acc = d if acc is None else acc + d
    out_ref[...] = acc


def last_grads(me, got, preact, lhs):
    groups, width, rows = got.shape
    count, total = lhs.shape
    spec = pltpu.PrefetchScalarGridSpec(
        num_scalar_prefetch=1,
        grid=(1,),
        in_specs=[
            block((groups, width, rows), lambda h, me: (0, 0, 0)),
            block((width, total), lambda h, me: (me[0] % 2, 0)),
            block((count, total), lambda h, me: (0, 0)),
        ],
        out_specs=block((count, width), lambda h, me: (0, 0)),
    )
    return pl.pallas_call(
        last_kernel,
        grid_spec=spec,
        out_shape=jax.ShapeDtypeStruct((count, width), F32),
        compiler_params=pltpu.CompilerParams(vmem_limit_bytes=12 * 2**20),
        cost_estimate=pl.CostEstimate(
            flops=2 * total * count * width, bytes_accessed=2 * 2**20, transcendentals=0
        ),
    )(me, got, preact, lhs)


def outputs_kernel(dz, me_ref, own, other, latent, embed):
    width = own.shape[1]
    mine = pl.multiple_of((me_ref[0] % 2) * width, 128)
    theirs = pl.multiple_of((1 - me_ref[0] % 2) * width, 128)
    for x, at in ((own, mine), (other, theirs)):
        latent[:, pl.ds(at, width)] = x[:dz]
        embed[:, pl.ds(at, width)] = x[dz:]


def outputs(me, own, other, dz):
    count, width = own.shape
    whole = lambda shape: block(shape, lambda h, me: (0,) * len(shape))
    spec = pltpu.PrefetchScalarGridSpec(
        num_scalar_prefetch=1,
        grid=(1,),
        in_specs=[whole(own.shape), whole(own.shape)],
        out_specs=[whole((dz, 2 * width)), whole((count - dz, 2 * width))],
    )
    return pl.pallas_call(
        functools.partial(outputs_kernel, dz),
        grid_spec=spec,
        out_shape=[jax.ShapeDtypeStruct((c, 2 * width), F32) for c in (dz, count - dz)],
        compiler_params=pltpu.CompilerParams(vmem_limit_bytes=8 * 2**20),
        cost_estimate=pl.CostEstimate(flops=0, bytes_accessed=2**20, transcendentals=0),
    )(me, own, other)


def tie(first, later):
    return lax.optimization_barrier((first, later))


def eight_by_four(
    records, real_labels, frequencies, class_noise, latents, syn_labels, w_latent, class_embed, w_out
):
    classes, hid = class_embed.shape
    groups = lax.axis_size("rec")
    rec = lax.axis_index("rec")
    feat = lax.axis_index("feat")
    rows, dz = latents.shape
    cols = w_out.shape[1]
    real_total = records.shape[0] * groups
    syn_total = rows * groups
    x, z_low, z_high = rec % 2, (rec // 2) % 2, rec // 4
    place = 2 * x + z_low
    me = jnp.stack([feat, x, z_low, z_high, rec, place]).astype(jnp.int32)

    table = one_hot(syn_labels, classes, BF)
    preact = jnp.dot(latents, w_latent, preferred_element_type=F32) + jnp.dot(
        table, class_embed, preferred_element_type=F32
    )
    hidden = jnp.maximum(preact, 0.0).astype(BF)
    own = jnp.tanh(jnp.dot(hidden, w_out, preferred_element_type=F32)).astype(BF)
    far = swap(own, "feat", 2)
    images = [own, far, swap(own, "feat", 1), swap(far, "feat", 1)]

    label_row = jnp.zeros((16, dz), BF).at[0, :].set(syn_labels.astype(BF))
    packed = jnp.concatenate([latents, label_row], axis=0)
    packed = lax.all_to_all(
        jnp.broadcast_to(packed[None], (groups,) + packed.shape), "rec", 0, 0, tiled=True
    )

    images, packed = tie(images, packed)
    args = (me, real_labels, syn_labels, (0, 2, 1, 3), images, records, frequencies, classes)
    totals = (real_total, syn_total)
    send_a, keep_a, send_b, keep_b, three = feature_sums(False, *args, totals)
    first_a = swap(send_a, "rec", 1)
    first_b = swap(send_b, "rec", 2)
    last_a, last_b, last = feature_sums(True, *args, totals)
    last_a, (first_a, first_b) = tie(last_a, (first_a, first_b))

    all_latents = packed[:, :rows].reshape(syn_total, dz)
    all_labels = packed[:, rows].reshape(syn_total).astype(jnp.int32)
    all_table = one_hot(all_labels, classes, BF)
    mine = hid // groups
    lhs = jnp.concatenate([all_latents, all_table], axis=1).T
    w = jnp.concatenate(
        [
            lax.dynamic_slice_in_dim(w_latent, rec * mine, mine, 1),
            lax.dynamic_slice_in_dim(class_embed, rec * mine, mine, 1),
        ],
        axis=0,
    )
    all_preact = lax.dot_general(w, lhs, (((0,), (0,)), ((), ())), preferred_element_type=F32)
    all_hidden = jnp.maximum(all_preact, 0.0).astype(BF)

    send_a, send_b = stage_two_send(keep_a, first_a, keep_b, first_b)
    got_a = swap(send_a, "rec", 2)
    got_b = swap(send_b, "rec", 1)
    part = frequencies.shape[1] // groups
    noise = lax.dynamic_slice_in_dim(class_noise, (2 * place + z_high) * part, part, 2)
    noise = noise.reshape(classes, 2 * part)
    got_a, noise = tie(got_a, noise)
    send, keep = stage_three(me, last_a, first_a, got_a, last_b, first_b, got_b)
    got = swap(send, "rec", 4)
    feat_grad = gap_rows(keep, got, noise, all_labels, real_total)
    feat_grad = lax.all_to_all(feat_grad.reshape(groups, rows, -1), "rec", 0, 0, tiled=True)

    send, keep = image_grads(me, three, last, feat_grad, frequencies, cols)
    send, keep = split_y(me, keep, swap(send, "feat", 1))
    out_grad, flipped = out_grads(keep, swap(send, "feat", 2), own)

    by = {0: out_grad}
    by[1] = swap(out_grad, "rec", 1)
    by[2] = swap(out_grad, "rec", 2)
    by[4] = swap(out_grad, "rec", 4)
    send, keep = hidden_grads(me, w_out, flipped, groups)
    part_grad = add(keep, swap(send, "feat", 1), BF)
    part_grad, (by[1], by[2]) = tie(part_grad, (by[1], by[2]))
    by[3] = swap(by[2], "rec", 1)
    far_grad = swap(part_grad, "feat", 2)
    far_grad, by[4] = tie(far_grad, by[4])
    by[6] = swap(by[4], "rec", 2)
    by[5] = swap(by[4], "rec", 1)
    part_grad = add(part_grad, far_grad, BF)
    part_grad = lax.all_to_all(part_grad, "rec", 0, 0, tiled=True)
    part_grad, (by[3], by[6]) = tie(part_grad, (by[3], by[6]))
    by[7] = swap(by[6], "rec", 1)
    grads = last_grads(me, part_grad, all_preact, lhs)
    grad_w_latent, grad_embed = outputs(me, grads, swap(grads, "feat", 1), dz)
    grad_w_out = weight_grads(me, all_hidden, [by[mask] for mask in range(groups)])
    return grad_w_out, grad_w_latent, grad_embed


def solution(mesh):
    shape = (mesh.shape["rec"], mesh.shape["feat"])
    in_specs = (
        P("rec", None),
        P("rec"),
        P(None, "feat"),
        P(None, None, "feat"),
        P("rec", None),
        P("rec"),
        P(),
        P(),
        P(None, "feat"),
    )
    out_specs = (P("rec", "feat"), P(None, "rec"), P(None, "rec"))
    return jax.shard_map(
        eight_by_four if shape == (8, 4) else general, mesh=mesh, in_specs=in_specs, out_specs=out_specs, check_vma=False
    )
```

```python
import functools

import jax
import jax.numpy as jnp
from jax import lax
from jax.experimental import pallas as pl
from jax.experimental.pallas import tpu as pltpu
from jax.sharding import PartitionSpec as P

BF = jnp.bfloat16
F32 = jnp.float32

TURN = 0.15915494309189535
SIN = (4.44286783702217, -7.307441307726672, 3.59477116396636, -0.7843353598850176)
COS = (1.4142134962552275, -6.978850948563815, 5.739460376907241, -1.883557905986894, 0.3106880275267554)


def cos_sin(x):
    turns = x * TURN
    u = turns - jnp.round(turns)
    sq = u * u
    p = SIN[-1]
    for c in SIN[-2::-1]:
        p = p * sq + c
    q = COS[-1]
    for c in COS[-2::-1]:
        q = q * sq + c
    s = u * p
    return 1.0 - s * s, s * q


def one_hot(labels, count, dtype):
    return (labels[:, None] == jnp.arange(count, dtype=jnp.int32)[None, :]).astype(dtype)


def real_kernel(rows, labels_ref, records_ref, freq_ref, out_ref, table_ref):
    total = records_ref.shape[0]
    classes = table_ref.shape[0]
    owners, _, width = out_ref.shape
    part = width // 2

    @pl.when(pl.program_id(0) == 0)
    def _():
        ids = lax.broadcasted_iota(jnp.int32, (classes, total), 0)
        table_ref[...] = jnp.where(ids == labels_ref[...], 1.0, 0.0).astype(BF)

    freq = freq_ref[...]
    block = freq.shape[1]

    def sums(i, pre):
        co, si = cos_sin(pre)
        phi = jnp.concatenate([co.astype(BF), si.astype(BF)], axis=1)
        return jnp.dot(table_ref[:, i * rows : (i + 1) * rows], phi, preferred_element_type=F32)

    acc = None
    before = None
    steps = total // rows
    for i in range(steps + 1):
        pre = None
        if i < steps:
            pre = jnp.dot(records_ref[i * rows : (i + 1) * rows, :], freq, preferred_element_type=F32)
        if i > 0:
            d = sums(i - 1, before)
            acc = d if acc is None else acc + d
        before = pre
    for o in range(owners):
        out_ref[o, :, :part] = acc[:, o * part : (o + 1) * part]
        out_ref[o, :, part:] = acc[:, block + o * part : block + (o + 1) * part]


def real_sums(labels, records, freq, classes, owners):
    m, k = records.shape
    n = freq.shape[1]
    block = min(512, n)
    rows = 512
    part = n // owners
    per = block // part
    return pl.pallas_call(
        functools.partial(real_kernel, rows),
        grid=(n // block,),
        in_specs=[
            pl.BlockSpec((1, m), lambda j: (0, 0)),
            pl.BlockSpec((m, k), lambda j: (0, 0)),
            pl.BlockSpec((k, block), lambda j: (0, j)),
        ],
        out_specs=pl.BlockSpec((per, classes, 2 * part), lambda j: (j, 0, 0)),
        out_shape=jax.ShapeDtypeStruct((owners, classes, 2 * part), F32),
        scratch_shapes=[pltpu.VMEM((classes, m), BF)],
        compiler_params=pltpu.CompilerParams(vmem_limit_bytes=56 * 2**20),
        cost_estimate=pl.CostEstimate(
            flops=2 * m * n * (k + 2 * classes), bytes_accessed=2 * (m * k + k * n), transcendentals=0
        ),
    )(labels.reshape(1, m), records, freq)


def bits_of(n):
    return [1 << b for b in range(n.bit_length() - 1)]


def swap(x, axis, bit):
    n = lax.axis_size(axis)
    return lax.ppermute(x, axis, [(i, i ^ bit) for i in range(n)])


def pick(x, index, dim):
    return lax.dynamic_index_in_dim(x, index, dim, keepdims=False)


def halving(x, axis, order, count):
    me = lax.axis_index(axis)
    nbits = len(order)
    x = x.reshape((2,) * nbits + x.shape[1:])
    left = sorted(order, reverse=True)
    for bit in order:
        dim = left.index(bit)
        left.remove(bit)
        mine = (me // bit) % 2
        got = swap(pick(x, 1 - mine, dim).astype(BF), axis, bit)
        x = pick(x, mine, dim).astype(F32) + got.astype(F32)
    return x


def general(
    records, real_labels, frequencies, class_noise, latents, syn_labels, w_latent, class_embed, w_out
):
    classes = class_embed.shape[0]
    hid = class_embed.shape[1]
    groups = lax.axis_size("rec")
    feats = lax.axis_size("feat")
    rec = lax.axis_index("rec")
    nf = frequencies.shape[1]
    part = nf // groups
    rows, dz = latents.shape
    cols = w_out.shape[1]
    real_total = records.shape[0] * groups
    syn_total = rows * groups

    label_row = jnp.zeros((16, dz), BF).at[0, :].set(syn_labels.astype(BF))
    packed = jnp.concatenate([latents, label_row], axis=0)
    packed = lax.all_to_all(
        jnp.broadcast_to(packed[None], (groups,) + packed.shape), "rec", 0, 0, tiled=True
    )
    all_latents = packed[:, :rows].reshape(syn_total, dz)
    all_labels = packed[:, rows].reshape(syn_total).astype(jnp.int32)
    all_table = one_hot(all_labels, classes, BF)

    table = one_hot(syn_labels, classes, BF)
    preact = jnp.dot(latents, w_latent, preferred_element_type=F32) + jnp.dot(
        table, class_embed, preferred_element_type=F32
    )
    hidden = jnp.maximum(preact, 0.0).astype(BF)
    own_images = jnp.tanh(jnp.dot(hidden, w_out, preferred_element_type=F32)).astype(BF)
    images = lax.all_gather(own_images, "feat", axis=0)
    images = images.transpose(1, 0, 2).reshape(rows, feats * cols)
    syn_pre = jnp.dot(images, frequencies, preferred_element_type=F32)
    syn_cos, syn_sin = cos_sin(syn_pre)
    syn_phi = jnp.concatenate(
        [syn_cos.reshape(rows, groups, part), syn_sin.reshape(rows, groups, part)], axis=2
    ).astype(BF)
    syn_sum = lax.dot_general(
        table, syn_phi.reshape(rows, 2 * nf), (((0,), (0,)), ((), ())), preferred_element_type=F32
    )
    syn_sum = syn_sum.reshape(classes, groups, 2 * part).transpose(1, 0, 2)

    real_sum = real_sums(real_labels, records, frequencies, classes, groups)
    gap = syn_sum * (1.0 / syn_total) - real_sum * (1.0 / real_total)
    half = classes // 2
    order = bits_of(groups)
    other = [order[1], order[0]] + order[2:]
    gap = jnp.concatenate(
        [halving(gap[:, :half], "rec", order, groups), halving(gap[:, half:], "rec", other, groups)], axis=0
    )
    noise = lax.dynamic_slice_in_dim(class_noise, rec * part, part, 2).reshape(classes, 2 * part)
    gap = (16.0 * (gap - noise * (1.0 / real_total))).astype(BF)

    feat_grad = jnp.dot(all_table, gap, preferred_element_type=F32).astype(BF)
    feat_grad = lax.all_to_all(feat_grad.reshape(groups, rows, 2 * part), "rec", 0, 0, tiled=True)
    feat_grad = feat_grad.transpose(1, 0, 2).astype(F32)
    pre_grad = (
        -syn_sin.reshape(rows, groups, part) * feat_grad[:, :, :part]
        + syn_cos.reshape(rows, groups, part) * feat_grad[:, :, part:]
    )
    pre_grad = pre_grad.astype(BF).reshape(rows, nf)
    image_grad = lax.dot_general(
        frequencies, pre_grad, (((1,), (1,)), ((), ())), preferred_element_type=F32
    )
    image_grad = halving(image_grad.reshape(feats, cols, rows), "feat", bits_of(feats), feats)
    image_grad = image_grad.T
    out_grad = (image_grad * (1.0 - jnp.square(own_images.astype(F32)))).astype(BF)

    out_grad = lax.all_to_all(
        jnp.broadcast_to(out_grad[None], (groups, rows, cols)), "rec", 0, 0, tiled=True
    ).reshape(syn_total, cols)

    mine = hid // groups
    start = rec * mine
    all_preact = jnp.dot(
        all_latents, lax.dynamic_slice_in_dim(w_latent, start, mine, 1), preferred_element_type=F32
    ) + jnp.dot(
        all_table, lax.dynamic_slice_in_dim(class_embed, start, mine, 1), preferred_element_type=F32
    )
    all_hidden = jnp.maximum(all_preact, 0.0).astype(BF)
    grad_w_out = lax.dot_general(
        all_hidden, out_grad, (((0,), (0,)), ((), ())), preferred_element_type=F32
    )
    hidden_grad = lax.dot_general(
        out_grad,
        lax.dynamic_slice_in_dim(w_out, start, mine, 0),
        (((1,), (1,)), ((), ())),
        preferred_element_type=F32,
    )
    core = lax.axis_index("feat") % 2
    half = syn_total // 2
    hidden_grad = hidden_grad.reshape(2, half, mine)
    got = swap(pick(hidden_grad, 1 - core, 0).astype(BF), "feat", 1)
    hidden_grad = pick(hidden_grad, core, 0) + got.astype(F32)
    for bit in bits_of(feats)[1:]:
        send = hidden_grad.astype(BF)
        hidden_grad = send.astype(F32) + swap(send, "feat", bit).astype(F32)
    my_preact = lax.dynamic_slice_in_dim(all_preact, core * half, half, 0)
    pre_hidden = jnp.where(my_preact > 0, hidden_grad, 0.0).astype(BF)
    lhs = jnp.concatenate([all_latents, all_table], axis=1)
    lhs = lax.dynamic_slice_in_dim(lhs, core * half, half, 0)
    grads = lax.dot_general(lhs, pre_hidden, (((0,), (0,)), ((), ())), preferred_element_type=F32)
    grads = grads + swap(grads, "feat", 1)
    return grad_w_out, grads[:dz], grads[dz:]


def block(shape, index):
    return pl.BlockSpec(shape, index)


def sums(table, pre):
    co, si = cos_sin(pre)
    phi = jnp.concatenate([co.astype(BF), si.astype(BF)], axis=1)
    return jnp.dot(table, phi, preferred_element_type=F32)


def features_kernel(
    masks, last, real_total, syn_total, me_ref, real_labels_ref, syn_labels_ref, *refs
):
    count = len(masks)
    images = refs[:count]
    records_hbm, freq_ref = refs[count : count + 2]
    outs = refs[count + 2 : -4]
    records, real_table, syn_table, sem = refs[-4:]
    classes, total = real_table.shape
    size = 512
    steps = total // size
    step = pl.program_id(0)
    cols = images[0].shape[1]
    half = classes // 2

    def copy(i):
        at = pl.ds(i * size, size)
        return pltpu.make_async_copy(records_hbm.at[at, :], records.at[at, :], sem.at[i])

    def work(wait):
        if wait:
            for i in range(steps):
                copy(i).start()
            ids = lax.broadcasted_iota(jnp.int32, (classes, total), 0)
            real_table[...] = jnp.where(ids == real_labels_ref[...], 1.0, 0.0).astype(BF)
            ids = lax.broadcasted_iota(jnp.int32, syn_table.shape, 0)
            syn_table[...] = jnp.where(ids == syn_labels_ref[...], 1.0, 0.0).astype(BF)
        syn_pre = None
        for mask, image in zip(masks, images):
            at = pl.multiple_of((me_ref[0] ^ mask) * cols, 128)
            d = jnp.dot(image[...], freq_ref[pl.ds(at, cols), :], preferred_element_type=F32)
            syn_pre = d if syn_pre is None else syn_pre + d
        freq = freq_ref[...]
        acc = None
        before = None
        for i in range(steps + 1):
            if i < steps:
                if wait:
                    copy(i).wait()
                pre = jnp.dot(records[i * size : (i + 1) * size, :], freq, preferred_element_type=F32)
            if i == 0:
                co, si = cos_sin(syn_pre)
                outs[-1][0, 0] = co
                outs[-1][0, 1] = si
                phi = jnp.concatenate([co.astype(BF), si.astype(BF)], axis=1)
                syn = jnp.dot(syn_table[...], phi, preferred_element_type=F32)
            else:
                d = sums(real_table[:, (i - 1) * size : i * size], before)
                acc = d if acc is None else acc + d
            before = pre
        gap = syn * (1.0 / syn_total) - acc * (1.0 / real_total)
        width = gap.shape[1] // 4
        return [
            jnp.concatenate(
                [gap[:, h * width : (h + 1) * width], gap[:, (h + 2) * width : (h + 3) * width]], axis=1
            )
            for h in range(2)
        ]

    if last:
        parts = work(True)
        for h in range(2):
            outs[0][h] = parts[h][:half]
            outs[1][h] = parts[h][half:]
        return
    send_a, keep_a, send_b, keep_b = outs[:4]

    @pl.when(step == 0)
    def _():
        parts = work(True)
        for h in range(2):
            send_a[0, h] = parts[h][:half].astype(BF)
            send_b[0, h] = parts[h][half:].astype(BF)

    @pl.when(step > 0)
    def _():
        parts = work(False)

        @pl.when(step == 1)
        def _():
            for h in range(2):
                send_a[0, h] = parts[h][:half].astype(BF)
                keep_b[h] = parts[h][half:]

        @pl.when(step == 2)
        def _():
            for h in range(2):
                keep_a[h] = parts[h][:half]
                send_b[0, h] = parts[h][half:].astype(BF)


def feature_sums(last, me, real_labels, syn_labels, masks, images, records, freq, classes, totals):
    total, k = records.shape
    n = freq.shape[1]
    rows, cols = images[0].shape
    half = classes // 2
    tile = n // 4
    tiles = 1 if last else 3
    whole = lambda shape: block(shape, lambda j, me: (0,) * len(shape))
    kept = jax.ShapeDtypeStruct((2, half, tile), F32)
    sent = jax.ShapeDtypeStruct((2, 2, half, tile), BF)
    wave = jax.ShapeDtypeStruct((tiles, 2, rows, tile), F32)
    wave_spec = block((1, 2, rows, tile), lambda j, me: (j, 0, 0, 0))
    if last:
        shapes = [kept, kept, wave]
        specs = [whole(kept.shape), whole(kept.shape), wave_spec]
    else:
        shapes = [sent, kept, sent, kept, wave]
        specs = [
            block((1, 2, half, tile), lambda j, me: (jnp.minimum(j, 1), 0, 0, 0)),
            whole(kept.shape),
            block((1, 2, half, tile), lambda j, me: (j // 2, 0, 0, 0)),
            whole(kept.shape),
            wave_spec,
        ]
    grid_spec = pltpu.PrefetchScalarGridSpec(
        num_scalar_prefetch=1,
        grid=(tiles,),
        in_specs=[whole((1, total)), whole((1, rows))]
        + [whole((rows, cols)) for _ in images]
        + [
            pl.BlockSpec(memory_space=pl.ANY),
            block((k, tile), lambda j, me: (0, me[5] ^ (0 if last else 3 - j))),
        ],
        out_specs=specs,
        scratch_shapes=[
            pltpu.VMEM((total, k), BF),
            pltpu.VMEM((classes, total), BF),
            pltpu.VMEM((classes, rows), BF),
            pltpu.SemaphoreType.DMA((total // 512,)),
        ],
    )
    return pl.pallas_call(
        functools.partial(features_kernel, masks, last, *totals),
        grid_spec=grid_spec,
        out_shape=shapes,
        compiler_params=pltpu.CompilerParams(vmem_limit_bytes=44 * 2**20),
        cost_estimate=pl.CostEstimate(
            flops=2 * (total + rows) * tiles * tile * (k + 2 * classes),
            bytes_accessed=2 * (total * k + k * tiles * tile),
            transcendentals=0,
        ),
    )(me, real_labels.reshape(1, -1), syn_labels.reshape(1, -1), *images, records, freq)


def stage_two_send_kernel(ka, ga, kb, gb, sa, sb):
    sa[...] = (ka[...] + ga[0].astype(F32)).astype(BF)
    sb[...] = (kb[...] + gb[0].astype(F32)).astype(BF)


def stage_two_send(keep_a, got_a, keep_b, got_b):
    return pl.pallas_call(
        stage_two_send_kernel,
        out_shape=[jax.ShapeDtypeStruct(keep_a.shape, BF)] * 2,
        compiler_params=pltpu.CompilerParams(vmem_limit_bytes=10 * 2**20),
        cost_estimate=pl.CostEstimate(flops=0, bytes_accessed=3 * 2**20, transcendentals=0),
    )(keep_a, got_a, keep_b, got_b)


def stage_three_kernel(me_ref, na, fa, ga, nb, fb, gb, send, keep):
    high = me_ref[3]
    half = na.shape[1]
    for flip, out in ((1, send), (0, keep)):
        at = high ^ flip
        out[:half] = (na[at] + fa[1, at].astype(F32) + ga[at].astype(F32)).astype(out.dtype)
        out[half:] = (nb[at] + fb[1, at].astype(F32) + gb[at].astype(F32)).astype(out.dtype)


def stage_three(me, keep_a, first_a, got_a, keep_b, first_b, got_b):
    _, half, width = keep_a.shape
    args = (keep_a, first_a, got_a, keep_b, first_b, got_b)
    whole = lambda shape: block(shape, lambda h, me: (0,) * len(shape))
    spec = pltpu.PrefetchScalarGridSpec(
        num_scalar_prefetch=1,
        grid=(1,),
        in_specs=[whole(x.shape) for x in args],
        out_specs=[whole((2 * half, width))] * 2,
    )
    return pl.pallas_call(
        stage_three_kernel,
        grid_spec=spec,
        out_shape=[jax.ShapeDtypeStruct((2 * half, width), t) for t in (BF, F32)],
        compiler_params=pltpu.CompilerParams(vmem_limit_bytes=12 * 2**20),
        cost_estimate=pl.CostEstimate(flops=0, bytes_accessed=3 * 2**20, transcendentals=0),
    )(me, *args)


def gap_kernel(real_total, keep_ref, got_ref, noise_ref, labels_ref, out_ref):
    classes = keep_ref.shape[0]
    gap = keep_ref[...] + got_ref[...].astype(F32) - noise_ref[...] * (1.0 / real_total)
    gap = (16.0 * gap).astype(BF)
    ids = lax.broadcasted_iota(jnp.int32, (labels_ref.shape[0], classes), 1)
    table = jnp.where(ids == labels_ref[...], 1.0, 0.0).astype(BF)
    out_ref[...] = jnp.dot(table, gap, preferred_element_type=F32).astype(BF)


def gap_rows(keep, got, noise, labels, real_total):
    classes, width = keep.shape
    total = labels.shape[0]
    return pl.pallas_call(
        functools.partial(gap_kernel, real_total),
        out_shape=jax.ShapeDtypeStruct((total, width), BF),
        compiler_params=pltpu.CompilerParams(vmem_limit_bytes=14 * 2**20),
        cost_estimate=pl.CostEstimate(
            flops=2 * total * classes * width, bytes_accessed=3 * 2**20, transcendentals=0
        ),
    )(keep, got, noise, labels.reshape(total, 1))


NT = (((1,), (1,)), ((), ()))


def image_kernel(me_ref, three_ref, last_ref, rows_ref, freq_ref, send_ref, keep_ref, pre_ref):
    step = pl.program_id(0)
    cols = send_ref.shape[1]
    tile = three_ref.shape[3]
    part = tile // 2

    @pl.when(step == 0)
    def _():
        for t in range(4):
            place = me_ref[5] ^ (3 - t)
            wave = last_ref.at[0] if t == 3 else three_ref.at[t]
            for h in range(2):
                grad = rows_ref[4 * h + 2 * (place % 2) + place // 2].astype(F32)
                lanes = slice(h * part, (h + 1) * part)
                pre = wave[0, :, lanes] * grad[:, part:] - wave[1, :, lanes] * grad[:, :part]
                at = pl.multiple_of(place * tile + h * part, 128)
                pre_ref[:, pl.ds(at, part)] = pre.astype(BF)

    out = lax.dot_general(freq_ref[...], pre_ref[...], NT, preferred_element_type=F32)
    steps = pl.num_programs(0) // 2

    @pl.when(step < steps)
    def _():
        send_ref[0] = out.astype(BF)

    @pl.when(step >= steps)
    def _():
        keep_ref[0] = out


def image_grads(me, three, last, feat_rows, freq, cols):
    k, n = freq.shape
    owners, rows, width = feat_rows.shape
    whole = lambda x: block(x.shape, lambda s, me: (0,) * x.ndim)

    def source(s, me):
        return 2 * (s % 2) + ((me[0] % 2) ^ (1 - s // 2)), 0

    spec = pltpu.PrefetchScalarGridSpec(
        num_scalar_prefetch=1,
        grid=(4,),
        in_specs=[whole(three), whole(last), whole(feat_rows), block((cols, n), source)],
        out_specs=[
            block((1, cols, rows), lambda s, me: (jnp.minimum(s, 1), 0, 0)),
            block((1, cols, rows), lambda s, me: (jnp.maximum(s - 2, 0), 0, 0)),
        ],
        scratch_shapes=[pltpu.VMEM((rows, n), BF)],
    )
    return pl.pallas_call(
        image_kernel,
        grid_spec=spec,
        out_shape=[jax.ShapeDtypeStruct((2, cols, rows), t) for t in (BF, F32)],
        compiler_params=pltpu.CompilerParams(vmem_limit_bytes=56 * 2**20),
        cost_estimate=pl.CostEstimate(flops=2 * k * n * rows, bytes_accessed=2 * k * n, transcendentals=0),
    )(me, three, last, feat_rows, freq)


def split_y_kernel(me_ref, keep_s, keep_k, got_s, got_k, send, keep):
    send[...] = (keep_s[0] + got_s[0].astype(F32)).astype(BF)
    keep[...] = keep_k[0] + got_k[0].astype(F32)


def split_y(me, keep, got):
    _, cols, rows = keep.shape
    at = lambda flip: block((1, cols, rows), lambda h, me: ((me[0] // 2) ^ flip, 0, 0))
    out = block((cols, rows), lambda h, me: (0, 0))
    spec = pltpu.PrefetchScalarGridSpec(
        num_scalar_prefetch=1, grid=(1,), in_specs=[at(1), at(0)] * 2, out_specs=[out, out]
    )
    return pl.pallas_call(
        split_y_kernel,
        grid_spec=spec,
        out_shape=[jax.ShapeDtypeStruct((cols, rows), t) for t in (BF, F32)],
        compiler_params=pltpu.CompilerParams(vmem_limit_bytes=8 * 2**20),
        cost_estimate=pl.CostEstimate(flops=0, bytes_accessed=2**20, transcendentals=0),
    )(me, keep, keep, got, got)


def out_kernel(keep, got, image, out):
    grad = (keep[...] + got[...].astype(F32)).T
    grad = grad * (1.0 - jnp.square(image[...].astype(F32)))
    out[...] = grad.astype(BF)


def out_grads(keep, got, image):
    return pl.pallas_call(
        out_kernel,
        out_shape=jax.ShapeDtypeStruct(image.shape, BF),
        compiler_params=pltpu.CompilerParams(vmem_limit_bytes=8 * 2**20),
        cost_estimate=pl.CostEstimate(flops=0, bytes_accessed=2**20, transcendentals=0),
    )(keep, got, image)


def hidden_kernel(me_ref, w_ref, *refs):
    grads = refs[:4]
    send, keep = refs[4:]
    core = me_ref[0] % 2
    out = [lax.dot_general(w_ref[...], g[...], NT, preferred_element_type=F32) for g in grads]
    for i in range(2):
        keep[i] = jnp.where(core == 0, out[2 * i], out[2 * i + 1])
        send[i] = jnp.where(core == 0, out[2 * i + 1], out[2 * i]).astype(BF)


def hidden_grads(me, w_out, grads, mine):
    rows, cols = grads[0].shape
    whole = lambda shape: block(shape, lambda r, me: (0,) * len(shape))
    spec = pltpu.PrefetchScalarGridSpec(
        num_scalar_prefetch=1,
        grid=(1,),
        in_specs=[block((mine, cols), lambda r, me: (me[4], 0))] + [whole((rows, cols))] * 4,
        out_specs=[whole((2, mine, rows))] * 2,
    )
    return pl.pallas_call(
        hidden_kernel,
        grid_spec=spec,
        out_shape=[jax.ShapeDtypeStruct((2, mine, rows), t) for t in (BF, F32)],
        compiler_params=pltpu.CompilerParams(vmem_limit_bytes=8 * 2**20),
        cost_estimate=pl.CostEstimate(
            flops=8 * mine * cols * rows, bytes_accessed=2 * 5 * mine * cols, transcendentals=0
        ),
    )(me, w_out, *grads)


def add_kernel(a, b, out):
    out[...] = (a[...].astype(F32) + b[...].astype(F32)).astype(out.dtype)


def add(a, b, kind):
    return pl.pallas_call(
        add_kernel,
        out_shape=jax.ShapeDtypeStruct(a.shape, kind),
        compiler_params=pltpu.CompilerParams(vmem_limit_bytes=8 * 2**20),
        cost_estimate=pl.CostEstimate(flops=0, bytes_accessed=2**20, transcendentals=0),
    )(a, b)


def weight_kernel(me_ref, hidden_ref, *refs):
    out_ref = refs[-1]
    acc = None
    for mask, grad in enumerate(refs[:-1]):
        rows = grad.shape[0]
        at = pl.multiple_of((me_ref[4] ^ mask) * rows, 128)
        d = jnp.dot(hidden_ref[:, pl.ds(at, rows)], grad[...], preferred_element_type=F32)
        acc = d if acc is None else acc + d
    out_ref[...] = acc


def weight_grads(me, hidden, grads):
    rows, cols = grads[0].shape
    mine, total = hidden.shape
    spec = pltpu.PrefetchScalarGridSpec(
        num_scalar_prefetch=1,
        grid=(1,),
        in_specs=[block((mine, total), lambda h, me: (0, 0))]
        + [block((rows, cols), lambda h, me: (0, 0)) for _ in grads],
        out_specs=block((mine, cols), lambda h, me: (0, 0)),
    )
    return pl.pallas_call(
        weight_kernel,
        grid_spec=spec,
        out_shape=jax.ShapeDtypeStruct((mine, cols), F32),
        compiler_params=pltpu.CompilerParams(vmem_limit_bytes=12 * 2**20),
        cost_estimate=pl.CostEstimate(
            flops=2 * mine * total * cols, bytes_accessed=4 * 2**20, transcendentals=0
        ),
    )(me, hidden, *grads)


def last_kernel(me_ref, preact_ref, lhs_ref, p0, q0, p1, q1, out_ref):
    rows = p0.shape[2]
    acc = None
    for h, (p, q) in enumerate(((p0, q0), (p1, q1))):
        for i in range(2):
            mask = 4 * h + 2 * i + me_ref[0] % 2
            at = pl.ds(pl.multiple_of((me_ref[4] ^ mask) * rows, 128), rows)
            grad = p[i].astype(F32) + q[i].astype(F32)
            grad = jnp.where(preact_ref[:, at] > 0, grad, 0.0).astype(BF)
            d = lax.dot_general(lhs_ref[:, at], grad, NT, preferred_element_type=F32)
            acc = d if acc is None else acc + d
    out_ref[...] = acc


def last_grads(me, preact, lhs, parts):
    count, total = lhs.shape
    mine = preact.shape[0]
    args = (preact, lhs, *parts)
    whole = lambda shape: block(shape, lambda h, me: (0,) * len(shape))
    spec = pltpu.PrefetchScalarGridSpec(
        num_scalar_prefetch=1,
        grid=(1,),
        in_specs=[whole(x.shape) for x in args],
        out_specs=whole((count, mine)),
    )
    return pl.pallas_call(
        last_kernel,
        grid_spec=spec,
        out_shape=jax.ShapeDtypeStruct((count, mine), F32),
        compiler_params=pltpu.CompilerParams(vmem_limit_bytes=12 * 2**20),
        cost_estimate=pl.CostEstimate(
            flops=total * count * mine, bytes_accessed=2 * 2**20, transcendentals=0
        ),
    )(me, *args)


def outputs_kernel(own, other, latent, embed):
    dz = latent.shape[0]
    latent[...] = own[:dz] + other[:dz]
    embed[...] = own[dz:] + other[dz:]


def outputs(own, other, dz):
    count, mine = own.shape
    return pl.pallas_call(
        outputs_kernel,
        out_shape=[jax.ShapeDtypeStruct((c, mine), F32) for c in (dz, count - dz)],
        compiler_params=pltpu.CompilerParams(vmem_limit_bytes=8 * 2**20),
        cost_estimate=pl.CostEstimate(flops=0, bytes_accessed=2**20, transcendentals=0),
    )(own, other)


def tie(first, later):
    return lax.optimization_barrier((first, later))


def eight_by_four(
    records, real_labels, frequencies, class_noise, latents, syn_labels, w_latent, class_embed, w_out
):
    classes, hid = class_embed.shape
    groups = lax.axis_size("rec")
    rec = lax.axis_index("rec")
    feat = lax.axis_index("feat")
    rows, dz = latents.shape
    cols = w_out.shape[1]
    real_total = records.shape[0] * groups
    syn_total = rows * groups
    x, z_low, z_high = rec % 2, (rec // 2) % 2, rec // 4
    place = 2 * x + z_low
    me = jnp.stack([feat, x, z_low, z_high, rec, place]).astype(jnp.int32)

    table = one_hot(syn_labels, classes, BF)
    preact = jnp.dot(latents, w_latent, preferred_element_type=F32) + jnp.dot(
        table, class_embed, preferred_element_type=F32
    )
    hidden = jnp.maximum(preact, 0.0).astype(BF)
    own = jnp.tanh(jnp.dot(hidden, w_out, preferred_element_type=F32)).astype(BF)
    far = swap(own, "feat", 2)
    images = [own, far, swap(own, "feat", 1), swap(far, "feat", 1)]

    label_row = jnp.zeros((16, dz), BF).at[0, :].set(syn_labels.astype(BF))
    packed, _ = tie(jnp.concatenate([latents, label_row], axis=0), own)
    packed = lax.all_to_all(
        jnp.broadcast_to(packed[None], (groups,) + packed.shape), "rec", 0, 0, tiled=True
    )

    images, packed = tie(images, packed)
    args = (me, real_labels, syn_labels, (0, 2, 1, 3), images, records, frequencies, classes)
    totals = (real_total, syn_total)
    send_a, keep_a, send_b, keep_b, three = feature_sums(False, *args, totals)
    first_a = swap(send_a, "rec", 1)
    first_b = swap(send_b, "rec", 2)
    last_a, last_b, last = feature_sums(True, *args, totals)
    last_a, (first_a, first_b) = tie(last_a, (first_a, first_b))

    all_latents = packed[:, :rows].reshape(syn_total, dz)
    all_labels = packed[:, rows].reshape(syn_total).astype(jnp.int32)
    all_table = one_hot(all_labels, classes, BF)
    mine = hid // groups
    lhs = jnp.concatenate([all_latents, all_table], axis=1).T
    w = jnp.concatenate(
        [
            lax.dynamic_slice_in_dim(w_latent, rec * mine, mine, 1),
            lax.dynamic_slice_in_dim(class_embed, rec * mine, mine, 1),
        ],
        axis=0,
    )
    all_preact = lax.dot_general(w, lhs, (((0,), (0,)), ((), ())), preferred_element_type=F32)
    all_hidden = jnp.maximum(all_preact, 0.0).astype(BF)

    send_a, send_b = stage_two_send(keep_a, first_a, keep_b, first_b)
    got_a = swap(send_a, "rec", 2)
    got_b = swap(send_b, "rec", 1)
    part = frequencies.shape[1] // groups
    noise = lax.dynamic_slice_in_dim(class_noise, (2 * place + z_high) * part, part, 2)
    noise = noise.reshape(classes, 2 * part)
    got_a, noise = tie(got_a, noise)
    send, keep = stage_three(me, last_a, first_a, got_a, last_b, first_b, got_b)
    got = swap(send, "rec", 4)
    feat_grad = gap_rows(keep, got, noise, all_labels, real_total)
    feat_grad = lax.all_to_all(feat_grad.reshape(groups, rows, -1), "rec", 0, 0, tiled=True)
    feat_grad, (all_preact, all_hidden, lhs) = tie(feat_grad, (all_preact, all_hidden, lhs))

    send, keep = image_grads(me, three, last, feat_grad, frequencies, cols)
    send, keep = split_y(me, keep, swap(send, "feat", 1))
    out_grad = out_grads(keep, swap(send, "feat", 2), own)

    by = {0: out_grad}
    by[4] = swap(out_grad, "rec", 4)
    by[2] = swap(out_grad, "rec", 2)
    by[1] = swap(out_grad, "rec", 1)
    by[4], (by[2], by[1]) = tie(by[4], (by[2], by[1]))
    by[3] = swap(by[2], "rec", 1)
    by[6] = swap(by[4], "rec", 2)
    by[5] = swap(by[4], "rec", 1)

    def reduced(send, keep):
        part = add(keep, swap(send, "feat", 1), BF)
        return [part, swap(part, "feat", 2)]

    send, keep = hidden_grads(me, w_out, [by[i] for i in range(4)], mine)
    by[6], send = tie(by[6], send)
    by[7] = swap(by[6], "rec", 1)
    parts = reduced(send, keep)
    by[7], parts = tie(by[7], parts)
    parts += reduced(*hidden_grads(me, w_out, [by[4 + i] for i in range(4)], mine))
    grad_w_out = weight_grads(me, all_hidden, [by[mask] for mask in range(groups)])
    parts[3], grad_w_out = tie(parts[3], grad_w_out)
    grads = last_grads(me, all_preact, lhs, parts)
    grad_w_latent, grad_embed = outputs(grads, swap(grads, "feat", 1), dz)
    return grad_w_out, grad_w_latent, grad_embed


def solution(mesh):
    shape = (mesh.shape["rec"], mesh.shape["feat"])
    in_specs = (
        P("rec", None),
        P("rec"),
        P(None, "feat"),
        P(None, None, "feat"),
        P("rec", None),
        P("rec"),
        P(),
        P(),
        P(None, "feat"),
    )
    out_specs = (P("rec", "feat"), P(None, "rec"), P(None, "rec"))
    return jax.shard_map(
        eight_by_four if shape == (8, 4) else general, mesh=mesh, in_specs=in_specs, out_specs=out_specs, check_vma=False
    )
```

```python
import functools

import jax
import jax.numpy as jnp
from jax import lax
from jax.experimental import pallas as pl
from jax.experimental.pallas import tpu as pltpu
from jax.sharding import PartitionSpec as P

BF = jnp.bfloat16
F32 = jnp.float32

TURN = 0.15915494309189535
SIN = (4.44286783702217, -7.307441307726672, 3.59477116396636, -0.7843353598850176)
COS = (1.4142134962552275, -6.978850948563815, 5.739460376907241, -1.883557905986894, 0.3106880275267554)


def cos_sin(x):
    turns = x * TURN
    u = turns - jnp.round(turns)
    sq = u * u
    p = SIN[-1]
    for c in SIN[-2::-1]:
        p = p * sq + c
    q = COS[-1]
    for c in COS[-2::-1]:
        q = q * sq + c
    s = u * p
    return 1.0 - s * s, s * q


def one_hot(labels, count, dtype):
    return (labels[:, None] == jnp.arange(count, dtype=jnp.int32)[None, :]).astype(dtype)


def real_kernel(rows, labels_ref, records_ref, freq_ref, out_ref, table_ref):
    total = records_ref.shape[0]
    classes = table_ref.shape[0]
    owners, _, width = out_ref.shape
    part = width // 2

    @pl.when(pl.program_id(0) == 0)
    def _():
        ids = lax.broadcasted_iota(jnp.int32, (classes, total), 0)
        table_ref[...] = jnp.where(ids == labels_ref[...], 1.0, 0.0).astype(BF)

    freq = freq_ref[...]
    block = freq.shape[1]

    def sums(i, pre):
        co, si = cos_sin(pre)
        phi = jnp.concatenate([co.astype(BF), si.astype(BF)], axis=1)
        return jnp.dot(table_ref[:, i * rows : (i + 1) * rows], phi, preferred_element_type=F32)

    acc = None
    before = None
    steps = total // rows
    for i in range(steps + 1):
        pre = None
        if i < steps:
            pre = jnp.dot(records_ref[i * rows : (i + 1) * rows, :], freq, preferred_element_type=F32)
        if i > 0:
            d = sums(i - 1, before)
            acc = d if acc is None else acc + d
        before = pre
    for o in range(owners):
        out_ref[o, :, :part] = acc[:, o * part : (o + 1) * part]
        out_ref[o, :, part:] = acc[:, block + o * part : block + (o + 1) * part]


def real_sums(labels, records, freq, classes, owners):
    m, k = records.shape
    n = freq.shape[1]
    block = min(512, n)
    rows = 512
    part = n // owners
    per = block // part
    return pl.pallas_call(
        functools.partial(real_kernel, rows),
        grid=(n // block,),
        in_specs=[
            pl.BlockSpec((1, m), lambda j: (0, 0)),
            pl.BlockSpec((m, k), lambda j: (0, 0)),
            pl.BlockSpec((k, block), lambda j: (0, j)),
        ],
        out_specs=pl.BlockSpec((per, classes, 2 * part), lambda j: (j, 0, 0)),
        out_shape=jax.ShapeDtypeStruct((owners, classes, 2 * part), F32),
        scratch_shapes=[pltpu.VMEM((classes, m), BF)],
        compiler_params=pltpu.CompilerParams(vmem_limit_bytes=56 * 2**20),
        cost_estimate=pl.CostEstimate(
            flops=2 * m * n * (k + 2 * classes), bytes_accessed=2 * (m * k + k * n), transcendentals=0
        ),
    )(labels.reshape(1, m), records, freq)


def bits_of(n):
    return [1 << b for b in range(n.bit_length() - 1)]


def swap(x, axis, bit):
    n = lax.axis_size(axis)
    return lax.ppermute(x, axis, [(i, i ^ bit) for i in range(n)])


def pick(x, index, dim):
    return lax.dynamic_index_in_dim(x, index, dim, keepdims=False)


def halving(x, axis, order, count):
    me = lax.axis_index(axis)
    nbits = len(order)
    x = x.reshape((2,) * nbits + x.shape[1:])
    left = sorted(order, reverse=True)
    for bit in order:
        dim = left.index(bit)
        left.remove(bit)
        mine = (me // bit) % 2
        got = swap(pick(x, 1 - mine, dim).astype(BF), axis, bit)
        x = pick(x, mine, dim).astype(F32) + got.astype(F32)
    return x


def general(
    records, real_labels, frequencies, class_noise, latents, syn_labels, w_latent, class_embed, w_out
):
    classes = class_embed.shape[0]
    hid = class_embed.shape[1]
    groups = lax.axis_size("rec")
    feats = lax.axis_size("feat")
    rec = lax.axis_index("rec")
    nf = frequencies.shape[1]
    part = nf // groups
    rows, dz = latents.shape
    cols = w_out.shape[1]
    real_total = records.shape[0] * groups
    syn_total = rows * groups

    label_row = jnp.zeros((16, dz), BF).at[0, :].set(syn_labels.astype(BF))
    packed = jnp.concatenate([latents, label_row], axis=0)
    packed = lax.all_to_all(
        jnp.broadcast_to(packed[None], (groups,) + packed.shape), "rec", 0, 0, tiled=True
    )
    all_latents = packed[:, :rows].reshape(syn_total, dz)
    all_labels = packed[:, rows].reshape(syn_total).astype(jnp.int32)
    all_table = one_hot(all_labels, classes, BF)

    table = one_hot(syn_labels, classes, BF)
    preact = jnp.dot(latents, w_latent, preferred_element_type=F32) + jnp.dot(
        table, class_embed, preferred_element_type=F32
    )
    hidden = jnp.maximum(preact, 0.0).astype(BF)
    own_images = jnp.tanh(jnp.dot(hidden, w_out, preferred_element_type=F32)).astype(BF)
    images = lax.all_gather(own_images, "feat", axis=0)
    images = images.transpose(1, 0, 2).reshape(rows, feats * cols)
    syn_pre = jnp.dot(images, frequencies, preferred_element_type=F32)
    syn_cos, syn_sin = cos_sin(syn_pre)
    syn_phi = jnp.concatenate(
        [syn_cos.reshape(rows, groups, part), syn_sin.reshape(rows, groups, part)], axis=2
    ).astype(BF)
    syn_sum = lax.dot_general(
        table, syn_phi.reshape(rows, 2 * nf), (((0,), (0,)), ((), ())), preferred_element_type=F32
    )
    syn_sum = syn_sum.reshape(classes, groups, 2 * part).transpose(1, 0, 2)

    real_sum = real_sums(real_labels, records, frequencies, classes, groups)
    gap = syn_sum * (1.0 / syn_total) - real_sum * (1.0 / real_total)
    half = classes // 2
    order = bits_of(groups)
    other = [order[1], order[0]] + order[2:]
    gap = jnp.concatenate(
        [halving(gap[:, :half], "rec", order, groups), halving(gap[:, half:], "rec", other, groups)], axis=0
    )
    noise = lax.dynamic_slice_in_dim(class_noise, rec * part, part, 2).reshape(classes, 2 * part)
    gap = (16.0 * (gap - noise * (1.0 / real_total))).astype(BF)

    feat_grad = jnp.dot(all_table, gap, preferred_element_type=F32).astype(BF)
    feat_grad = lax.all_to_all(feat_grad.reshape(groups, rows, 2 * part), "rec", 0, 0, tiled=True)
    feat_grad = feat_grad.transpose(1, 0, 2).astype(F32)
    pre_grad = (
        -syn_sin.reshape(rows, groups, part) * feat_grad[:, :, :part]
        + syn_cos.reshape(rows, groups, part) * feat_grad[:, :, part:]
    )
    pre_grad = pre_grad.astype(BF).reshape(rows, nf)
    image_grad = lax.dot_general(
        frequencies, pre_grad, (((1,), (1,)), ((), ())), preferred_element_type=F32
    )
    image_grad = halving(image_grad.reshape(feats, cols, rows), "feat", bits_of(feats), feats)
    image_grad = image_grad.T
    out_grad = (image_grad * (1.0 - jnp.square(own_images.astype(F32)))).astype(BF)

    out_grad = lax.all_to_all(
        jnp.broadcast_to(out_grad[None], (groups, rows, cols)), "rec", 0, 0, tiled=True
    ).reshape(syn_total, cols)

    mine = hid // groups
    start = rec * mine
    all_preact = jnp.dot(
        all_latents, lax.dynamic_slice_in_dim(w_latent, start, mine, 1), preferred_element_type=F32
    ) + jnp.dot(
        all_table, lax.dynamic_slice_in_dim(class_embed, start, mine, 1), preferred_element_type=F32
    )
    all_hidden = jnp.maximum(all_preact, 0.0).astype(BF)
    grad_w_out = lax.dot_general(
        all_hidden, out_grad, (((0,), (0,)), ((), ())), preferred_element_type=F32
    )
    hidden_grad = lax.dot_general(
        out_grad,
        lax.dynamic_slice_in_dim(w_out, start, mine, 0),
        (((1,), (1,)), ((), ())),
        preferred_element_type=F32,
    )
    core = lax.axis_index("feat") % 2
    half = syn_total // 2
    hidden_grad = hidden_grad.reshape(2, half, mine)
    got = swap(pick(hidden_grad, 1 - core, 0).astype(BF), "feat", 1)
    hidden_grad = pick(hidden_grad, core, 0) + got.astype(F32)
    for bit in bits_of(feats)[1:]:
        send = hidden_grad.astype(BF)
        hidden_grad = send.astype(F32) + swap(send, "feat", bit).astype(F32)
    my_preact = lax.dynamic_slice_in_dim(all_preact, core * half, half, 0)
    pre_hidden = jnp.where(my_preact > 0, hidden_grad, 0.0).astype(BF)
    lhs = jnp.concatenate([all_latents, all_table], axis=1)
    lhs = lax.dynamic_slice_in_dim(lhs, core * half, half, 0)
    grads = lax.dot_general(lhs, pre_hidden, (((0,), (0,)), ((), ())), preferred_element_type=F32)
    grads = grads + swap(grads, "feat", 1)
    return grad_w_out, grads[:dz], grads[dz:]


def block(shape, index):
    return pl.BlockSpec(shape, index)


def sums(table, pre):
    co, si = cos_sin(pre)
    phi = jnp.concatenate([co.astype(BF), si.astype(BF)], axis=1)
    return jnp.dot(table, phi, preferred_element_type=F32)


def features_kernel(
    masks, last, real_total, syn_total, me_ref, real_labels_ref, syn_labels_ref, *refs
):
    count = len(masks)
    images = refs[:count]
    records_hbm, freq_ref = refs[count : count + 2]
    outs = refs[count + 3 : -4]
    records, real_table, syn_table, sem = refs[-4:]
    classes, total = real_table.shape
    size = 512
    steps = total // size
    step = pl.program_id(0)
    cols = images[0].shape[1]
    half = classes // 2

    def copy(i):
        at = pl.ds(i * size, size)
        return pltpu.make_async_copy(records_hbm.at[at, :], records.at[at, :], sem.at[i])

    def work(wait):
        if wait:
            for i in range(steps):
                copy(i).start()
            ids = lax.broadcasted_iota(jnp.int32, (classes, total), 0)
            real_table[...] = jnp.where(ids == real_labels_ref[...], 1.0, 0.0).astype(BF)
            ids = lax.broadcasted_iota(jnp.int32, syn_table.shape, 0)
            syn_table[...] = jnp.where(ids == syn_labels_ref[...], 1.0, 0.0).astype(BF)
        freq = freq_ref[...]
        acc = None
        before = None
        for i in range(steps + 1):
            if i < steps:
                if wait:
                    copy(i).wait()
                pre = jnp.dot(records[i * size : (i + 1) * size, :], freq, preferred_element_type=F32)
            else:
                syn_pre = None
                for mask, image in zip(masks, images):
                    at = pl.multiple_of((me_ref[0] ^ mask) * cols, 128)
                    d = jnp.dot(image[...], freq_ref[pl.ds(at, cols), :], preferred_element_type=F32)
                    syn_pre = d if syn_pre is None else syn_pre + d
            if i > 0:
                d = sums(real_table[:, (i - 1) * size : i * size], before)
                acc = d if acc is None else acc + d
            before = pre
        co, si = cos_sin(syn_pre)
        outs[-1][0, 0] = co
        outs[-1][0, 1] = si
        phi = jnp.concatenate([co.astype(BF), si.astype(BF)], axis=1)
        syn = jnp.dot(syn_table[...], phi, preferred_element_type=F32)
        gap = syn * (1.0 / syn_total) - acc * (1.0 / real_total)
        width = gap.shape[1] // 4
        return [
            jnp.concatenate(
                [gap[:, h * width : (h + 1) * width], gap[:, (h + 2) * width : (h + 3) * width]], axis=1
            )
            for h in range(2)
        ]

    if last:
        parts = work(True)
        for h in range(2):
            outs[0][h] = parts[h][:half]
            outs[1][h] = parts[h][half:]
        return
    send_a, keep_a, send_b, keep_b = outs[:4]

    @pl.when(step == 0)
    def _():
        parts = work(True)
        for h in range(2):
            send_a[0, h] = parts[h][:half].astype(BF)
            send_b[0, h] = parts[h][half:].astype(BF)

    @pl.when(step > 0)
    def _():
        parts = work(False)

        @pl.when(step == 1)
        def _():
            for h in range(2):
                send_a[0, h] = parts[h][:half].astype(BF)
                keep_b[h] = parts[h][half:]

        @pl.when(step == 2)
        def _():
            for h in range(2):
                keep_a[h] = parts[h][:half]
                send_b[0, h] = parts[h][half:].astype(BF)


def feature_sums(last, me, real_labels, syn_labels, masks, images, records, freq, classes, totals, after):
    total, k = records.shape
    n = freq.shape[1]
    rows, cols = images[0].shape
    half = classes // 2
    tile = n // 4
    tiles = 1 if last else 3
    whole = lambda shape: block(shape, lambda j, me: (0,) * len(shape))
    kept = jax.ShapeDtypeStruct((2, half, tile), F32)
    sent = jax.ShapeDtypeStruct((2, 2, half, tile), BF)
    wave = pltpu.HBM((tiles, 2, rows, tile), F32)
    wave_spec = block((1, 2, rows, tile), lambda j, me: (j, 0, 0, 0))
    if last:
        shapes = [kept, kept, wave]
        specs = [whole(kept.shape), whole(kept.shape), wave_spec]
    else:
        shapes = [sent, kept, sent, kept, wave]
        specs = [
            block((1, 2, half, tile), lambda j, me: (jnp.minimum(j, 1), 0, 0, 0)),
            whole(kept.shape),
            block((1, 2, half, tile), lambda j, me: (j // 2, 0, 0, 0)),
            whole(kept.shape),
            wave_spec,
        ]
    grid_spec = pltpu.PrefetchScalarGridSpec(
        num_scalar_prefetch=1,
        grid=(tiles,),
        in_specs=[whole((1, total)), whole((1, rows))]
        + [whole((rows, cols)) for _ in images]
        + [
            pl.BlockSpec(memory_space=pl.ANY),
            block((k, tile), lambda j, me: (0, me[5] ^ (0 if last else 3 - j))),
            pl.BlockSpec(memory_space=pl.ANY),
        ],
        out_specs=specs,
        scratch_shapes=[
            pltpu.VMEM((total, k), BF),
            pltpu.VMEM((classes, total), BF),
            pltpu.VMEM((classes, rows), BF),
            pltpu.SemaphoreType.DMA((total // 512,)),
        ],
    )
    return pl.pallas_call(
        functools.partial(features_kernel, masks, last, *totals),
        grid_spec=grid_spec,
        out_shape=shapes,
        compiler_params=pltpu.CompilerParams(vmem_limit_bytes=44 * 2**20),
        cost_estimate=pl.CostEstimate(
            flops=2 * (total + rows) * tiles * tile * (k + 2 * classes),
            bytes_accessed=2 * (total * k + k * tiles * tile),
            transcendentals=0,
        ),
    )(me, real_labels.reshape(1, -1), syn_labels.reshape(1, -1), *images, records, freq, after)


def stage_two_send_kernel(ka, ga, kb, gb, after, sa, sb):
    sa[...] = (ka[...] + ga[0].astype(F32)).astype(BF)
    sb[...] = (kb[...] + gb[0].astype(F32)).astype(BF)


def stage_two_send(keep_a, got_a, keep_b, got_b, after):
    return pl.pallas_call(
        stage_two_send_kernel,
        in_specs=[pl.BlockSpec()] * 4 + [pl.BlockSpec(memory_space=pl.ANY)],
        out_shape=[jax.ShapeDtypeStruct(keep_a.shape, BF)] * 2,
        compiler_params=pltpu.CompilerParams(vmem_limit_bytes=10 * 2**20),
        cost_estimate=pl.CostEstimate(flops=0, bytes_accessed=3 * 2**20, transcendentals=0),
    )(keep_a, got_a, keep_b, got_b, after)


def stage_three_kernel(me_ref, na, fa, ga, nb, fb, gb, after, behind, send, keep):
    high = me_ref[3]
    half = na.shape[1]
    for flip, out in ((1, send), (0, keep)):
        at = high ^ flip
        out[:half] = (na[at] + fa[1, at].astype(F32) + ga[at].astype(F32)).astype(out.dtype)
        out[half:] = (nb[at] + fb[1, at].astype(F32) + gb[at].astype(F32)).astype(out.dtype)


def stage_three(me, keep_a, first_a, got_a, keep_b, first_b, got_b, after):
    _, half, width = keep_a.shape
    args = (keep_a, first_a, got_a, keep_b, first_b, got_b)
    whole = lambda shape: block(shape, lambda h, me: (0,) * len(shape))
    spec = pltpu.PrefetchScalarGridSpec(
        num_scalar_prefetch=1,
        grid=(1,),
        in_specs=[whole(x.shape) for x in args] + [pl.BlockSpec(memory_space=pl.ANY)] * 2,
        out_specs=[whole((2 * half, width))] * 2,
    )
    return pl.pallas_call(
        stage_three_kernel,
        grid_spec=spec,
        out_shape=[jax.ShapeDtypeStruct((2 * half, width), t) for t in (BF, F32)],
        compiler_params=pltpu.CompilerParams(vmem_limit_bytes=12 * 2**20),
        cost_estimate=pl.CostEstimate(flops=0, bytes_accessed=3 * 2**20, transcendentals=0),
    )(me, *args, *after)


def gap_kernel(real_total, me_ref, keep_ref, got_ref, noise_ref, labels_ref, out_ref):
    classes = keep_ref.shape[0]
    rows = labels_ref.shape[1]
    gap = keep_ref[...] + got_ref[...].astype(F32) - noise_ref[...] * (1.0 / real_total)
    gap = (16.0 * gap).astype(BF)
    ids = lax.broadcasted_iota(jnp.int32, (classes, rows), 0)
    for mask in range(labels_ref.shape[0]):
        table = jnp.where(ids == labels_ref[mask : mask + 1, :], 1.0, 0.0).astype(BF)
        out = lax.dot_general(table, gap, (((0,), (0,)), ((), ())), preferred_element_type=F32)
        out_ref[me_ref[4] ^ mask] = out.astype(BF)


def gap_rows(me, keep, got, noise, labels, real_total):
    classes, width = keep.shape
    groups, rows = labels.shape
    whole = lambda shape: block(shape, lambda h, me: (0,) * len(shape))
    spec = pltpu.PrefetchScalarGridSpec(
        num_scalar_prefetch=1,
        grid=(1,),
        in_specs=[whole(x.shape) for x in (keep, got, noise, labels)],
        out_specs=whole((groups, rows, width)),
    )
    return pl.pallas_call(
        functools.partial(gap_kernel, real_total),
        grid_spec=spec,
        out_shape=jax.ShapeDtypeStruct((groups, rows, width), BF),
        compiler_params=pltpu.CompilerParams(vmem_limit_bytes=14 * 2**20),
        cost_estimate=pl.CostEstimate(
            flops=2 * groups * rows * classes * width, bytes_accessed=3 * 2**20, transcendentals=0
        ),
    )(me, keep, got, noise, labels)


NT = (((1,), (1,)), ((), ()))


def image_kernel(
    me_ref, three_ref, last_ref, rows_ref, freq_hbm, a, b, c, send_ref, keep_ref, freq_ref, pre_ref, sem
):
    cols = send_ref.shape[1]
    tile = three_ref.shape[3]
    part = tile // 2
    core = me_ref[0] % 2
    copies = []
    for s in range(4):
        first = (2 * (s % 2) + (core ^ (1 - s // 2))) * cols
        source = freq_hbm.at[pl.ds(pl.multiple_of(first, 128), cols), :]
        copies.append(pltpu.make_async_copy(source, freq_ref.at[s], sem.at[s]))
        copies[-1].start()
    for t in range(4):
        place = me_ref[5] ^ (3 - t)
        wave = last_ref.at[0] if t == 3 else three_ref.at[t]
        for h in range(2):
            grad = rows_ref[4 * h + 2 * (place % 2) + place // 2].astype(F32)
            lanes = slice(h * part, (h + 1) * part)
            pre = wave[0, :, lanes] * grad[:, part:] - wave[1, :, lanes] * grad[:, :part]
            at = pl.multiple_of(place * tile + h * part, 128)
            pre_ref[:, pl.ds(at, part)] = pre.astype(BF)
    for s in range(4):
        copies[s].wait()
        out = lax.dot_general(freq_ref[s], pre_ref[...], NT, preferred_element_type=F32)
        if s < 2:
            send_ref[s] = out.astype(BF)
        else:
            keep_ref[s - 2] = out


def image_grads(me, three, last, feat_rows, freq, cols, after):
    k, n = freq.shape
    owners, rows, width = feat_rows.shape
    whole = lambda shape: block(shape, lambda s, me: (0,) * len(shape))
    spec = pltpu.PrefetchScalarGridSpec(
        num_scalar_prefetch=1,
        grid=(1,),
        in_specs=[whole(three.shape), whole(last.shape), whole(feat_rows.shape)]
        + [pl.BlockSpec(memory_space=pl.ANY)] * 4,
        out_specs=[whole((2, cols, rows))] * 2,
        scratch_shapes=[
            pltpu.VMEM((4, cols, n), BF),
            pltpu.VMEM((rows, n), BF),
            pltpu.SemaphoreType.DMA((4,)),
        ],
    )
    return pl.pallas_call(
        image_kernel,
        grid_spec=spec,
        out_shape=[jax.ShapeDtypeStruct((2, cols, rows), t) for t in (BF, F32)],
        compiler_params=pltpu.CompilerParams(vmem_limit_bytes=52 * 2**20),
        cost_estimate=pl.CostEstimate(flops=2 * k * n * rows, bytes_accessed=2 * k * n, transcendentals=0),
    )(me, three, last, feat_rows, freq, *after)


def split_y_kernel(me_ref, keep_s, keep_k, got_s, got_k, send, keep):
    send[...] = (keep_s[0] + got_s[0].astype(F32)).astype(BF)
    keep[...] = keep_k[0] + got_k[0].astype(F32)


def split_y(me, keep, got):
    _, cols, rows = keep.shape
    at = lambda flip: block((1, cols, rows), lambda h, me: ((me[0] // 2) ^ flip, 0, 0))
    out = block((cols, rows), lambda h, me: (0, 0))
    spec = pltpu.PrefetchScalarGridSpec(
        num_scalar_prefetch=1, grid=(1,), in_specs=[at(1), at(0)] * 2, out_specs=[out, out]
    )
    return pl.pallas_call(
        split_y_kernel,
        grid_spec=spec,
        out_shape=[jax.ShapeDtypeStruct((cols, rows), t) for t in (BF, F32)],
        compiler_params=pltpu.CompilerParams(vmem_limit_bytes=8 * 2**20),
        cost_estimate=pl.CostEstimate(flops=0, bytes_accessed=2**20, transcendentals=0),
    )(me, keep, keep, got, got)


def out_kernel(keep, got, image, out):
    grad = (keep[...] + got[...].astype(F32)).T
    grad = grad * (1.0 - jnp.square(image[...].astype(F32)))
    out[...] = grad.astype(BF)


def out_grads(keep, got, image):
    return pl.pallas_call(
        out_kernel,
        out_shape=jax.ShapeDtypeStruct(image.shape, BF),
        compiler_params=pltpu.CompilerParams(vmem_limit_bytes=8 * 2**20),
        cost_estimate=pl.CostEstimate(flops=0, bytes_accessed=2**20, transcendentals=0),
    )(keep, got, image)


def hidden_kernel(me_ref, w_ref, *refs):
    grads = refs[:4]
    send, keep = refs[5:]
    core = me_ref[0] % 2
    out = [lax.dot_general(w_ref[...], g[...], NT, preferred_element_type=F32) for g in grads]
    for i in range(2):
        keep[i] = jnp.where(core == 0, out[2 * i], out[2 * i + 1])
        send[i] = jnp.where(core == 0, out[2 * i + 1], out[2 * i]).astype(BF)


def hidden_grads(me, w_out, grads, mine, after):
    rows, cols = grads[0].shape
    whole = lambda shape: block(shape, lambda r, me: (0,) * len(shape))
    spec = pltpu.PrefetchScalarGridSpec(
        num_scalar_prefetch=1,
        grid=(1,),
        in_specs=[block((mine, cols), lambda r, me: (me[4], 0))] + [whole((rows, cols))] * 4
        + [pl.BlockSpec(memory_space=pl.ANY)],
        out_specs=[whole((2, mine, rows))] * 2,
    )
    return pl.pallas_call(
        hidden_kernel,
        grid_spec=spec,
        out_shape=[jax.ShapeDtypeStruct((2, mine, rows), t) for t in (BF, F32)],
        compiler_params=pltpu.CompilerParams(vmem_limit_bytes=8 * 2**20),
        cost_estimate=pl.CostEstimate(
            flops=8 * mine * cols * rows, bytes_accessed=2 * 5 * mine * cols, transcendentals=0
        ),
    )(me, w_out, *grads, after)


def add_kernel(a, b, out):
    out[...] = (a[...].astype(F32) + b[...].astype(F32)).astype(out.dtype)


def add(a, b, kind):
    return pl.pallas_call(
        add_kernel,
        out_shape=jax.ShapeDtypeStruct(a.shape, kind),
        compiler_params=pltpu.CompilerParams(vmem_limit_bytes=8 * 2**20),
        cost_estimate=pl.CostEstimate(flops=0, bytes_accessed=2**20, transcendentals=0),
    )(a, b)


def weight_kernel(me_ref, hidden_ref, *refs):
    out_ref = refs[-1]
    acc = None
    for mask, grad in enumerate(refs[:-1]):
        rows = grad.shape[0]
        at = slice(mask * rows, (mask + 1) * rows)
        d = jnp.dot(hidden_ref[:, at], grad[...], preferred_element_type=F32)
        acc = d if acc is None else acc + d
    out_ref[...] = acc


def weight_grads(me, hidden, grads):
    rows, cols = grads[0].shape
    mine, total = hidden.shape
    spec = pltpu.PrefetchScalarGridSpec(
        num_scalar_prefetch=1,
        grid=(1,),
        in_specs=[block((mine, total), lambda h, me: (0, 0))]
        + [block((rows, cols), lambda h, me: (0, 0)) for _ in grads],
        out_specs=block((mine, cols), lambda h, me: (0, 0)),
    )
    return pl.pallas_call(
        weight_kernel,
        grid_spec=spec,
        out_shape=jax.ShapeDtypeStruct((mine, cols), F32),
        compiler_params=pltpu.CompilerParams(vmem_limit_bytes=12 * 2**20),
        cost_estimate=pl.CostEstimate(
            flops=2 * mine * total * cols, bytes_accessed=4 * 2**20, transcendentals=0
        ),
    )(me, hidden, *grads)


def last_kernel(me_ref, preact_ref, lhs_ref, p0, q0, p1, q1, after, out_ref):
    rows = p0.shape[2]
    acc = None
    for h, (p, q) in enumerate(((p0, q0), (p1, q1))):
        for i in range(2):
            mask = 4 * h + 2 * i + me_ref[0] % 2
            at = pl.ds(pl.multiple_of(mask * rows, 128), rows)
            grad = p[i].astype(F32) + q[i].astype(F32)
            grad = jnp.where(preact_ref[:, at] > 0, grad, 0.0).astype(BF)
            d = lax.dot_general(lhs_ref[:, at], grad, NT, preferred_element_type=F32)
            acc = d if acc is None else acc + d
    out_ref[...] = acc


def last_grads(me, preact, lhs, parts, after):
    count, total = lhs.shape
    mine = preact.shape[0]
    args = (preact, lhs, *parts)
    whole = lambda shape: block(shape, lambda h, me: (0,) * len(shape))
    spec = pltpu.PrefetchScalarGridSpec(
        num_scalar_prefetch=1,
        grid=(1,),
        in_specs=[whole(x.shape) for x in args] + [pl.BlockSpec(memory_space=pl.ANY)],
        out_specs=whole((count, mine)),
    )
    return pl.pallas_call(
        last_kernel,
        grid_spec=spec,
        out_shape=jax.ShapeDtypeStruct((count, mine), F32),
        compiler_params=pltpu.CompilerParams(vmem_limit_bytes=12 * 2**20),
        cost_estimate=pl.CostEstimate(
            flops=total * count * mine, bytes_accessed=2 * 2**20, transcendentals=0
        ),
    )(me, *args, after)


def outputs_kernel(own, other, latent, embed):
    dz = latent.shape[0]
    latent[...] = own[:dz] + other[:dz]
    embed[...] = own[dz:] + other[dz:]


def outputs(own, other, dz):
    count, mine = own.shape
    return pl.pallas_call(
        outputs_kernel,
        out_shape=[jax.ShapeDtypeStruct((c, mine), F32) for c in (dz, count - dz)],
        compiler_params=pltpu.CompilerParams(vmem_limit_bytes=8 * 2**20),
        cost_estimate=pl.CostEstimate(flops=0, bytes_accessed=2**20, transcendentals=0),
    )(own, other)


def tie(first, later):
    return lax.optimization_barrier((first, later))


def eight_by_four(
    records, real_labels, frequencies, class_noise, latents, syn_labels, w_latent, class_embed, w_out
):
    classes, hid = class_embed.shape
    groups = lax.axis_size("rec")
    rec = lax.axis_index("rec")
    feat = lax.axis_index("feat")
    rows, dz = latents.shape
    cols = w_out.shape[1]
    real_total = records.shape[0] * groups
    syn_total = rows * groups
    x, z_low, z_high = rec % 2, (rec // 2) % 2, rec // 4
    place = 2 * x + z_low
    me = jnp.stack([feat, x, z_low, z_high, rec, place]).astype(jnp.int32)

    table = one_hot(syn_labels, classes, BF)
    preact = jnp.dot(latents, w_latent, preferred_element_type=F32) + jnp.dot(
        table, class_embed, preferred_element_type=F32
    )
    hidden = jnp.maximum(preact, 0.0).astype(BF)
    own = jnp.tanh(jnp.dot(hidden, w_out, preferred_element_type=F32)).astype(BF)
    far = swap(own, "feat", 2)
    images = [own, far, swap(own, "feat", 1), swap(far, "feat", 1)]

    label_row = jnp.zeros((16, dz), BF).at[0, :].set(syn_labels.astype(BF))
    packed = jnp.concatenate([latents, label_row], axis=0)[None]
    packed = jnp.concatenate([packed, swap(packed, "rec", 1)], axis=0)
    quad = jnp.concatenate([packed, swap(packed, "rec", 2)], axis=0)
    args = (me, real_labels, syn_labels, (0, 2, 1, 3), images, records, frequencies, classes)
    totals = (real_total, syn_total)
    send_a, keep_a, send_b, keep_b, three = feature_sums(False, *args, totals, packed)
    eight = jnp.concatenate([quad, swap(quad, "rec", 4)], axis=0)
    first_a = swap(send_a, "rec", 1)
    first_b = swap(send_b, "rec", 2)
    last_a, last_b, last = feature_sums(True, *args, totals, quad)

    all_latents = eight[:, :rows].reshape(syn_total, dz)
    all_labels = eight[:, rows].reshape(syn_total).astype(jnp.int32)
    all_table = one_hot(all_labels, classes, BF)
    mine = hid // groups
    lhs = jnp.concatenate([all_latents, all_table], axis=1).T
    w = jnp.concatenate(
        [
            lax.dynamic_slice_in_dim(w_latent, rec * mine, mine, 1),
            lax.dynamic_slice_in_dim(class_embed, rec * mine, mine, 1),
        ],
        axis=0,
    )
    all_preact = lax.dot_general(w, lhs, (((0,), (0,)), ((), ())), preferred_element_type=F32)
    all_hidden = jnp.maximum(all_preact, 0.0).astype(BF)

    send_a, send_b = stage_two_send(keep_a, first_a, keep_b, first_b, last)
    got_a = swap(send_a, "rec", 2)
    got_b = swap(send_b, "rec", 1)
    part = frequencies.shape[1] // groups
    noise = lax.dynamic_slice_in_dim(class_noise, (2 * place + z_high) * part, part, 2)
    noise = noise.reshape(classes, 2 * part)
    send, keep = stage_three(me, last_a, first_a, got_a, last_b, first_b, got_b, (noise, eight))
    got = swap(send, "rec", 4)
    feat_grad = gap_rows(me, keep, got, noise, all_labels.reshape(groups, rows), real_total)
    feat_grad = lax.all_to_all(feat_grad, "rec", 0, 0, tiled=True)

    send, keep = image_grads(
        me, three, last, feat_grad, frequencies, cols, (all_preact, all_hidden, lhs)
    )
    send, keep = split_y(me, keep, swap(send, "feat", 1))
    out_grad = out_grads(keep, swap(send, "feat", 2), own)

    by = {0: out_grad}
    by[4] = swap(out_grad, "rec", 4)
    by[2] = swap(out_grad, "rec", 2)
    by[1] = swap(out_grad, "rec", 1)
    by[4], (by[2], by[1]) = tie(by[4], (by[2], by[1]))
    by[3] = swap(by[2], "rec", 1)
    by[6] = swap(by[4], "rec", 2)
    by[5] = swap(by[4], "rec", 1)

    def reduced(send, keep):
        part = add(keep, swap(send, "feat", 1), BF)
        return [part, swap(part, "feat", 2)]

    by[7] = swap(by[6], "rec", 1)
    send, keep = hidden_grads(me, w_out, [by[i] for i in range(4)], mine, by[5])
    parts = reduced(send, keep)
    parts += reduced(*hidden_grads(me, w_out, [by[4 + i] for i in range(4)], mine, parts[0]))
    grad_w_out = weight_grads(me, all_hidden, [by[mask] for mask in range(groups)])
    grads = last_grads(me, all_preact, lhs, parts, grad_w_out)
    grad_w_latent, grad_embed = outputs(grads, swap(grads, "feat", 1), dz)
    return grad_w_out, grad_w_latent, grad_embed


def solution(mesh):
    shape = (mesh.shape["rec"], mesh.shape["feat"])
    in_specs = (
        P("rec", None),
        P("rec"),
        P(None, "feat"),
        P(None, None, "feat"),
        P("rec", None),
        P("rec"),
        P(),
        P(),
        P(None, "feat"),
    )
    out_specs = (P("rec", "feat"), P(None, "rec"), P(None, "rec"))
    return jax.shard_map(
        eight_by_four if shape == (8, 4) else general, mesh=mesh, in_specs=in_specs, out_specs=out_specs, check_vma=False
    )
```

```python
import functools

import jax
import jax.numpy as jnp
from jax import lax
from jax.experimental import pallas as pl
from jax.experimental.pallas import tpu as pltpu
from jax.sharding import PartitionSpec as P

BF = jnp.bfloat16
F32 = jnp.float32

TURN = 0.15915494309189535
SIN = (4.44286783702217, -7.307441307726672, 3.59477116396636, -0.7843353598850176)
COS = (1.4142134962552275, -6.978850948563815, 5.739460376907241, -1.883557905986894, 0.3106880275267554)


def cos_sin(x):
    turns = x * TURN
    u = turns - jnp.round(turns)
    sq = u * u
    p = SIN[-1]
    for c in SIN[-2::-1]:
        p = p * sq + c
    q = COS[-1]
    for c in COS[-2::-1]:
        q = q * sq + c
    s = u * p
    return 1.0 - s * s, s * q


def one_hot(labels, count, dtype):
    return (labels[:, None] == jnp.arange(count, dtype=jnp.int32)[None, :]).astype(dtype)


def real_kernel(rows, labels_ref, records_ref, freq_ref, out_ref, table_ref):
    total = records_ref.shape[0]
    classes = table_ref.shape[0]
    owners, _, width = out_ref.shape
    part = width // 2

    @pl.when(pl.program_id(0) == 0)
    def _():
        ids = lax.broadcasted_iota(jnp.int32, (classes, total), 0)
        table_ref[...] = jnp.where(ids == labels_ref[...], 1.0, 0.0).astype(BF)

    freq = freq_ref[...]
    block = freq.shape[1]

    def sums(i, pre):
        co, si = cos_sin(pre)
        phi = jnp.concatenate([co.astype(BF), si.astype(BF)], axis=1)
        return jnp.dot(table_ref[:, i * rows : (i + 1) * rows], phi, preferred_element_type=F32)

    acc = None
    before = None
    steps = total // rows
    for i in range(steps + 1):
        pre = None
        if i < steps:
            pre = jnp.dot(records_ref[i * rows : (i + 1) * rows, :], freq, preferred_element_type=F32)
        if i > 0:
            d = sums(i - 1, before)
            acc = d if acc is None else acc + d
        before = pre
    for o in range(owners):
        out_ref[o, :, :part] = acc[:, o * part : (o + 1) * part]
        out_ref[o, :, part:] = acc[:, block + o * part : block + (o + 1) * part]


def real_sums(labels, records, freq, classes, owners):
    m, k = records.shape
    n = freq.shape[1]
    block = min(512, n)
    rows = 512
    part = n // owners
    per = block // part
    return pl.pallas_call(
        functools.partial(real_kernel, rows),
        grid=(n // block,),
        in_specs=[
            pl.BlockSpec((1, m), lambda j: (0, 0)),
            pl.BlockSpec((m, k), lambda j: (0, 0)),
            pl.BlockSpec((k, block), lambda j: (0, j)),
        ],
        out_specs=pl.BlockSpec((per, classes, 2 * part), lambda j: (j, 0, 0)),
        out_shape=jax.ShapeDtypeStruct((owners, classes, 2 * part), F32),
        scratch_shapes=[pltpu.VMEM((classes, m), BF)],
        compiler_params=pltpu.CompilerParams(vmem_limit_bytes=56 * 2**20),
        cost_estimate=pl.CostEstimate(
            flops=2 * m * n * (k + 2 * classes), bytes_accessed=2 * (m * k + k * n), transcendentals=0
        ),
    )(labels.reshape(1, m), records, freq)


def bits_of(n):
    return [1 << b for b in range(n.bit_length() - 1)]


def swap(x, axis, bit):
    n = lax.axis_size(axis)
    return lax.ppermute(x, axis, [(i, i ^ bit) for i in range(n)])


def pick(x, index, dim):
    return lax.dynamic_index_in_dim(x, index, dim, keepdims=False)


def halving(x, axis, order, count):
    me = lax.axis_index(axis)
    nbits = len(order)
    x = x.reshape((2,) * nbits + x.shape[1:])
    left = sorted(order, reverse=True)
    for bit in order:
        dim = left.index(bit)
        left.remove(bit)
        mine = (me // bit) % 2
        got = swap(pick(x, 1 - mine, dim).astype(BF), axis, bit)
        x = pick(x, mine, dim).astype(F32) + got.astype(F32)
    return x


def general(
    records, real_labels, frequencies, class_noise, latents, syn_labels, w_latent, class_embed, w_out
):
    classes = class_embed.shape[0]
    hid = class_embed.shape[1]
    groups = lax.axis_size("rec")
    feats = lax.axis_size("feat")
    rec = lax.axis_index("rec")
    nf = frequencies.shape[1]
    part = nf // groups
    rows, dz = latents.shape
    cols = w_out.shape[1]
    real_total = records.shape[0] * groups
    syn_total = rows * groups

    label_row = jnp.zeros((16, dz), BF).at[0, :].set(syn_labels.astype(BF))
    packed = jnp.concatenate([latents, label_row], axis=0)
    packed = lax.all_to_all(
        jnp.broadcast_to(packed[None], (groups,) + packed.shape), "rec", 0, 0, tiled=True
    )
    all_latents = packed[:, :rows].reshape(syn_total, dz)
    all_labels = packed[:, rows].reshape(syn_total).astype(jnp.int32)
    all_table = one_hot(all_labels, classes, BF)

    table = one_hot(syn_labels, classes, BF)
    preact = jnp.dot(latents, w_latent, preferred_element_type=F32) + jnp.dot(
        table, class_embed, preferred_element_type=F32
    )
    hidden = jnp.maximum(preact, 0.0).astype(BF)
    own_images = jnp.tanh(jnp.dot(hidden, w_out, preferred_element_type=F32)).astype(BF)
    images = lax.all_gather(own_images, "feat", axis=0)
    images = images.transpose(1, 0, 2).reshape(rows, feats * cols)
    syn_pre = jnp.dot(images, frequencies, preferred_element_type=F32)
    syn_cos, syn_sin = cos_sin(syn_pre)
    syn_phi = jnp.concatenate(
        [syn_cos.reshape(rows, groups, part), syn_sin.reshape(rows, groups, part)], axis=2
    ).astype(BF)
    syn_sum = lax.dot_general(
        table, syn_phi.reshape(rows, 2 * nf), (((0,), (0,)), ((), ())), preferred_element_type=F32
    )
    syn_sum = syn_sum.reshape(classes, groups, 2 * part).transpose(1, 0, 2)

    real_sum = real_sums(real_labels, records, frequencies, classes, groups)
    gap = syn_sum * (1.0 / syn_total) - real_sum * (1.0 / real_total)
    half = classes // 2
    order = bits_of(groups)
    other = [order[1], order[0]] + order[2:]
    gap = jnp.concatenate(
        [halving(gap[:, :half], "rec", order, groups), halving(gap[:, half:], "rec", other, groups)], axis=0
    )
    noise = lax.dynamic_slice_in_dim(class_noise, rec * part, part, 2).reshape(classes, 2 * part)
    gap = (16.0 * (gap - noise * (1.0 / real_total))).astype(BF)

    feat_grad = jnp.dot(all_table, gap, preferred_element_type=F32).astype(BF)
    feat_grad = lax.all_to_all(feat_grad.reshape(groups, rows, 2 * part), "rec", 0, 0, tiled=True)
    feat_grad = feat_grad.transpose(1, 0, 2).astype(F32)
    pre_grad = (
        -syn_sin.reshape(rows, groups, part) * feat_grad[:, :, :part]
        + syn_cos.reshape(rows, groups, part) * feat_grad[:, :, part:]
    )
    pre_grad = pre_grad.astype(BF).reshape(rows, nf)
    image_grad = lax.dot_general(
        frequencies, pre_grad, (((1,), (1,)), ((), ())), preferred_element_type=F32
    )
    image_grad = halving(image_grad.reshape(feats, cols, rows), "feat", bits_of(feats), feats)
    image_grad = image_grad.T
    out_grad = (image_grad * (1.0 - jnp.square(own_images.astype(F32)))).astype(BF)

    out_grad = lax.all_to_all(
        jnp.broadcast_to(out_grad[None], (groups, rows, cols)), "rec", 0, 0, tiled=True
    ).reshape(syn_total, cols)

    mine = hid // groups
    start = rec * mine
    all_preact = jnp.dot(
        all_latents, lax.dynamic_slice_in_dim(w_latent, start, mine, 1), preferred_element_type=F32
    ) + jnp.dot(
        all_table, lax.dynamic_slice_in_dim(class_embed, start, mine, 1), preferred_element_type=F32
    )
    all_hidden = jnp.maximum(all_preact, 0.0).astype(BF)
    grad_w_out = lax.dot_general(
        all_hidden, out_grad, (((0,), (0,)), ((), ())), preferred_element_type=F32
    )
    hidden_grad = lax.dot_general(
        out_grad,
        lax.dynamic_slice_in_dim(w_out, start, mine, 0),
        (((1,), (1,)), ((), ())),
        preferred_element_type=F32,
    )
    core = lax.axis_index("feat") % 2
    half = syn_total // 2
    hidden_grad = hidden_grad.reshape(2, half, mine)
    got = swap(pick(hidden_grad, 1 - core, 0).astype(BF), "feat", 1)
    hidden_grad = pick(hidden_grad, core, 0) + got.astype(F32)
    for bit in bits_of(feats)[1:]:
        send = hidden_grad.astype(BF)
        hidden_grad = send.astype(F32) + swap(send, "feat", bit).astype(F32)
    my_preact = lax.dynamic_slice_in_dim(all_preact, core * half, half, 0)
    pre_hidden = jnp.where(my_preact > 0, hidden_grad, 0.0).astype(BF)
    lhs = jnp.concatenate([all_latents, all_table], axis=1)
    lhs = lax.dynamic_slice_in_dim(lhs, core * half, half, 0)
    grads = lax.dot_general(lhs, pre_hidden, (((0,), (0,)), ((), ())), preferred_element_type=F32)
    grads = grads + swap(grads, "feat", 1)
    return grad_w_out, grads[:dz], grads[dz:]


def block(shape, index):
    return pl.BlockSpec(shape, index)


def sums(table, pre):
    co, si = cos_sin(pre)
    phi = jnp.concatenate([co.astype(BF), si.astype(BF)], axis=1)
    return jnp.dot(table, phi, preferred_element_type=F32)


def features_kernel(
    masks, last, real_total, syn_total, me_ref, real_labels_ref, syn_labels_ref, *refs
):
    count = 1 if last else len(masks)
    images = [refs[0].at[i] for i in range(len(masks))] if last else refs[:count]
    records_hbm, freq_ref = refs[count : count + 2]
    outs = refs[count + (4 if last else 3) : -4]
    wave, token = outs[-2:]
    records, real_table, syn_table, sem = refs[-4:]
    classes, total = real_table.shape
    size = 512
    steps = total // size
    step = pl.program_id(0)
    cols = images[0].shape[1]
    half = classes // 2
    token[...] = jnp.zeros_like(token)

    def copy(i):
        at = pl.ds(i * size, size)
        return pltpu.make_async_copy(records_hbm.at[at, :], records.at[at, :], sem.at[i])

    def work(wait):
        if wait:
            for i in range(steps):
                copy(i).start()
            ids = lax.broadcasted_iota(jnp.int32, (classes, total), 0)
            real_table[...] = jnp.where(ids == real_labels_ref[...], 1.0, 0.0).astype(BF)
            ids = lax.broadcasted_iota(jnp.int32, syn_table.shape, 0)
            syn_table[...] = jnp.where(ids == syn_labels_ref[...], 1.0, 0.0).astype(BF)
        syn_pre = None
        for mask, image in zip(masks, images):
            at = pl.multiple_of((me_ref[0] ^ mask) * cols, 128)
            d = jnp.dot(image[...], freq_ref[pl.ds(at, cols), :], preferred_element_type=F32)
            syn_pre = d if syn_pre is None else syn_pre + d
        freq = freq_ref[...]
        acc = None
        before = None
        for i in range(steps + 1):
            if i < steps:
                if wait:
                    copy(i).wait()
                pre = jnp.dot(records[i * size : (i + 1) * size, :], freq, preferred_element_type=F32)
            if i == 0:
                co, si = cos_sin(syn_pre)
                wave[0, 0] = co
                wave[0, 1] = si
                phi = jnp.concatenate([co.astype(BF), si.astype(BF)], axis=1)
                syn = jnp.dot(syn_table[...], phi, preferred_element_type=F32)
            else:
                d = sums(real_table[:, (i - 1) * size : i * size], before)
                acc = d if acc is None else acc + d
            before = pre
        gap = syn * (1.0 / syn_total) - acc * (1.0 / real_total)
        width = gap.shape[1] // 4
        return [
            jnp.concatenate(
                [gap[:, h * width : (h + 1) * width], gap[:, (h + 2) * width : (h + 3) * width]], axis=1
            )
            for h in range(2)
        ]

    if last:
        parts = work(True)
        for h in range(2):
            outs[0][h] = parts[h][:half]
            outs[1][h] = parts[h][half:]
        return
    send_a, keep_a, send_b, keep_b, both = outs[:5]

    @pl.when(step == 0)
    def _():
        for i in range(count):
            both[i] = images[i][...]
        parts = work(True)
        for h in range(2):
            send_a[0, h] = parts[h][:half].astype(BF)
            send_b[0, h] = parts[h][half:].astype(BF)

    @pl.when(step > 0)
    def _():
        parts = work(False)

        @pl.when(step == 1)
        def _():
            for h in range(2):
                send_a[0, h] = parts[h][:half].astype(BF)
                keep_b[h] = parts[h][half:]

        @pl.when(step == 2)
        def _():
            for h in range(2):
                keep_a[h] = parts[h][:half]
                send_b[0, h] = parts[h][half:].astype(BF)


def feature_sums(
    last, me, real_labels, syn_labels, masks, images, records, freq, classes, totals, after, waves=None
):
    total, k = records.shape
    n = freq.shape[1]
    rows, cols = images.shape[1:] if last else images[0].shape
    half = classes // 2
    tile = n // 4
    tiles = 1 if last else 3
    whole = lambda shape: block(shape, lambda j, me: (0,) * len(shape))
    kept = jax.ShapeDtypeStruct((2, half, tile), F32)
    sent = jax.ShapeDtypeStruct((2, 2, half, tile), BF)
    both = (len(masks), rows, cols)
    place = lambda j, me: me[5] ^ (0 if last else 3 - j)
    anywhere = pl.BlockSpec(memory_space=pl.ANY)
    shapes = [pltpu.HBM((4, 2, rows, tile), F32), jax.ShapeDtypeStruct((8, 128), F32)]
    specs = [block((1, 2, rows, tile), lambda j, me: (place(j, me), 0, 0, 0)), whole((8, 128))]
    if last:
        shapes = [kept, kept] + shapes
        specs = [whole(kept.shape), whole(kept.shape)] + specs
        images = (images,)
        extra = (after, waves)
    else:
        shapes = [sent, kept, sent, kept, pltpu.HBM(both, BF)] + shapes
        specs = [
            block((1, 2, half, tile), lambda j, me: (jnp.minimum(j, 1), 0, 0, 0)),
            whole(kept.shape),
            block((1, 2, half, tile), lambda j, me: (j // 2, 0, 0, 0)),
            whole(kept.shape),
            whole(both),
        ] + specs
        extra = (after,)
    grid_spec = pltpu.PrefetchScalarGridSpec(
        num_scalar_prefetch=1,
        grid=(tiles,),
        in_specs=[whole((1, total)), whole((1, rows))]
        + [whole(image.shape) for image in images]
        + [anywhere, block((k, tile), lambda j, me: (0, place(j, me)))]
        + [anywhere] * len(extra),
        out_specs=specs,
        scratch_shapes=[
            pltpu.VMEM((total, k), BF),
            pltpu.VMEM((classes, total), BF),
            pltpu.VMEM((classes, rows), BF),
            pltpu.SemaphoreType.DMA((total // 512,)),
        ],
    )
    return pl.pallas_call(
        functools.partial(features_kernel, masks, last, *totals),
        grid_spec=grid_spec,
        out_shape=shapes,
        input_output_aliases={7: 2} if last else {},
        compiler_params=pltpu.CompilerParams(vmem_limit_bytes=44 * 2**20),
        cost_estimate=pl.CostEstimate(
            flops=2 * (total + rows) * tiles * tile * (k + 2 * classes),
            bytes_accessed=2 * (total * k + k * tiles * tile),
            transcendentals=0,
        ),
    )(me, real_labels.reshape(1, -1), syn_labels.reshape(1, -1), *images, records, freq, *extra)


def stage_two_send_kernel(ka, ga, kb, gb, after, sa, sb):
    sa[...] = (ka[...] + ga[0].astype(F32)).astype(BF)
    sb[...] = (kb[...] + gb[0].astype(F32)).astype(BF)


def stage_two_send(keep_a, got_a, keep_b, got_b, after):
    return pl.pallas_call(
        stage_two_send_kernel,
        in_specs=[pl.BlockSpec()] * 4 + [pl.BlockSpec(memory_space=pl.ANY)],
        out_shape=[jax.ShapeDtypeStruct(keep_a.shape, BF)] * 2,
        compiler_params=pltpu.CompilerParams(vmem_limit_bytes=10 * 2**20),
        cost_estimate=pl.CostEstimate(flops=0, bytes_accessed=3 * 2**20, transcendentals=0),
    )(keep_a, got_a, keep_b, got_b, after)


def stage_three_kernel(me_ref, na, fa, ga, nb, fb, gb, a, b, c, send, keep):
    high = me_ref[3]
    half = na.shape[1]
    for flip, out in ((1, send), (0, keep)):
        at = high ^ flip
        out[:half] = (na[at] + fa[1, at].astype(F32) + ga[at].astype(F32)).astype(out.dtype)
        out[half:] = (nb[at] + fb[1, at].astype(F32) + gb[at].astype(F32)).astype(out.dtype)


def stage_three(me, keep_a, first_a, got_a, keep_b, first_b, got_b, after):
    _, half, width = keep_a.shape
    args = (keep_a, first_a, got_a, keep_b, first_b, got_b)
    whole = lambda shape: block(shape, lambda h, me: (0,) * len(shape))
    spec = pltpu.PrefetchScalarGridSpec(
        num_scalar_prefetch=1,
        grid=(1,),
        in_specs=[whole(x.shape) for x in args] + [pl.BlockSpec(memory_space=pl.ANY)] * 3,
        out_specs=[whole((2 * half, width))] * 2,
    )
    return pl.pallas_call(
        stage_three_kernel,
        grid_spec=spec,
        out_shape=[jax.ShapeDtypeStruct((2 * half, width), t) for t in (BF, F32)],
        compiler_params=pltpu.CompilerParams(vmem_limit_bytes=12 * 2**20),
        cost_estimate=pl.CostEstimate(flops=0, bytes_accessed=3 * 2**20, transcendentals=0),
    )(me, *args, *after)


def gap_kernel(real_total, me_ref, keep_ref, got_ref, noise_ref, labels_ref, out_ref):
    classes = keep_ref.shape[0]
    rows = labels_ref.shape[1]
    gap = keep_ref[...] + got_ref[...].astype(F32) - noise_ref[...] * (1.0 / real_total)
    gap = (16.0 * gap).astype(BF)
    ids = lax.broadcasted_iota(jnp.int32, (classes, rows), 0)
    for mask in range(labels_ref.shape[0]):
        table = jnp.where(ids == labels_ref[mask : mask + 1, :], 1.0, 0.0).astype(BF)
        out = lax.dot_general(table, gap, (((0,), (0,)), ((), ())), preferred_element_type=F32)
        out_ref[me_ref[4] ^ mask] = out.astype(BF)


def gap_rows(me, keep, got, noise, labels, real_total):
    classes, width = keep.shape
    groups, rows = labels.shape
    whole = lambda shape: block(shape, lambda h, me: (0,) * len(shape))
    spec = pltpu.PrefetchScalarGridSpec(
        num_scalar_prefetch=1,
        grid=(1,),
        in_specs=[whole(x.shape) for x in (keep, got, noise, labels)],
        out_specs=whole((groups, rows, width)),
    )
    return pl.pallas_call(
        functools.partial(gap_kernel, real_total),
        grid_spec=spec,
        out_shape=jax.ShapeDtypeStruct((groups, rows, width), BF),
        compiler_params=pltpu.CompilerParams(vmem_limit_bytes=14 * 2**20),
        cost_estimate=pl.CostEstimate(
            flops=2 * groups * rows * classes * width, bytes_accessed=3 * 2**20, transcendentals=0
        ),
    )(me, keep, got, noise, labels)


NT = (((1,), (1,)), ((), ()))


def image_kernel(me_ref, wave_ref, rows_ref, freq_ref, a, b, c, send_ref, keep_ref, pre_ref):
    step = pl.program_id(0)
    tile = wave_ref.shape[3]
    part = tile // 2

    @pl.when(step == 0)
    def _():
        for place in range(4):
            for h in range(2):
                grad = rows_ref[4 * h + 2 * (place % 2) + place // 2].astype(F32)
                lanes = slice(h * part, (h + 1) * part)
                pre = wave_ref[place, 0, :, lanes] * grad[:, part:]
                pre = pre - wave_ref[place, 1, :, lanes] * grad[:, :part]
                at = place * tile + h * part
                pre_ref[:, at : at + part] = pre.astype(BF)

    out = lax.dot_general(freq_ref[...], pre_ref[...], NT, preferred_element_type=F32)

    @pl.when(step < 2)
    def _():
        send_ref[0] = out.astype(BF)

    @pl.when(step >= 2)
    def _():
        keep_ref[0] = out


def image_grads(me, waves, feat_rows, freq, cols, after):
    k, n = freq.shape
    owners, rows, width = feat_rows.shape
    whole = lambda shape: block(shape, lambda s, me: (0,) * len(shape))

    def source(s, me):
        return 2 * (s % 2) + ((me[0] % 2) ^ (1 - s // 2)), 0

    spec = pltpu.PrefetchScalarGridSpec(
        num_scalar_prefetch=1,
        grid=(4,),
        in_specs=[whole(waves.shape), whole(feat_rows.shape), block((cols, n), source)]
        + [pl.BlockSpec(memory_space=pl.ANY)] * 3,
        out_specs=[
            block((1, cols, rows), lambda s, me: (jnp.minimum(s, 1), 0, 0)),
            block((1, cols, rows), lambda s, me: (jnp.maximum(s - 2, 0), 0, 0)),
        ],
        scratch_shapes=[pltpu.VMEM((rows, n), BF)],
    )
    return pl.pallas_call(
        image_kernel,
        grid_spec=spec,
        out_shape=[jax.ShapeDtypeStruct((2, cols, rows), BF), pltpu.HBM((2, cols, rows), F32)],
        compiler_params=pltpu.CompilerParams(vmem_limit_bytes=52 * 2**20),
        cost_estimate=pl.CostEstimate(flops=2 * k * n * rows, bytes_accessed=2 * k * n, transcendentals=0),
    )(me, waves, feat_rows, freq, *after)


def split_y_kernel(me_ref, keep_s, keep_k, got_s, got_k, send, keep):
    send[...] = (keep_s[0] + got_s[0].astype(F32)).astype(BF)
    keep[...] = keep_k[0] + got_k[0].astype(F32)


def split_y(me, keep, got):
    _, cols, rows = keep.shape
    at = lambda flip: block((1, cols, rows), lambda h, me: ((me[0] // 2) ^ flip, 0, 0))
    out = block((cols, rows), lambda h, me: (0, 0))
    spec = pltpu.PrefetchScalarGridSpec(
        num_scalar_prefetch=1, grid=(1,), in_specs=[at(1), at(0)] * 2, out_specs=[out, out]
    )
    return pl.pallas_call(
        split_y_kernel,
        grid_spec=spec,
        out_shape=[jax.ShapeDtypeStruct((cols, rows), t) for t in (BF, F32)],
        compiler_params=pltpu.CompilerParams(vmem_limit_bytes=8 * 2**20),
        cost_estimate=pl.CostEstimate(flops=0, bytes_accessed=2**20, transcendentals=0),
    )(me, keep, keep, got, got)


def out_kernel(keep, got, image, out):
    grad = (keep[...] + got[...].astype(F32)).T
    grad = grad * (1.0 - jnp.square(image[...].astype(F32)))
    out[...] = grad.astype(BF)


def out_grads(keep, got, image):
    return pl.pallas_call(
        out_kernel,
        out_shape=jax.ShapeDtypeStruct(image.shape, BF),
        compiler_params=pltpu.CompilerParams(vmem_limit_bytes=8 * 2**20),
        cost_estimate=pl.CostEstimate(flops=0, bytes_accessed=2**20, transcendentals=0),
    )(keep, got, image)


def hidden_kernel(me_ref, w_ref, *refs):
    grads = refs[:4]
    send, keep = refs[5:]
    core = me_ref[0] % 2
    out = [lax.dot_general(w_ref[...], g[...], NT, preferred_element_type=F32) for g in grads]
    for i in range(2):
        keep[i] = jnp.where(core == 0, out[2 * i], out[2 * i + 1])
        send[i] = jnp.where(core == 0, out[2 * i + 1], out[2 * i]).astype(BF)


def hidden_grads(me, w_out, grads, mine, after):
    rows, cols = grads[0].shape
    whole = lambda shape: block(shape, lambda r, me: (0,) * len(shape))
    spec = pltpu.PrefetchScalarGridSpec(
        num_scalar_prefetch=1,
        grid=(1,),
        in_specs=[block((mine, cols), lambda r, me: (me[4], 0))] + [whole((rows, cols))] * 4
        + [pl.BlockSpec(memory_space=pl.ANY)],
        out_specs=[whole((2, mine, rows))] * 2,
    )
    return pl.pallas_call(
        hidden_kernel,
        grid_spec=spec,
        out_shape=[jax.ShapeDtypeStruct((2, mine, rows), t) for t in (BF, F32)],
        compiler_params=pltpu.CompilerParams(vmem_limit_bytes=8 * 2**20),
        cost_estimate=pl.CostEstimate(
            flops=8 * mine * cols * rows, bytes_accessed=2 * 5 * mine * cols, transcendentals=0
        ),
    )(me, w_out, *grads, after)


def add_kernel(a, b, out):
    out[...] = (a[...].astype(F32) + b[...].astype(F32)).astype(out.dtype)


def add(a, b, kind):
    return pl.pallas_call(
        add_kernel,
        out_shape=jax.ShapeDtypeStruct(a.shape, kind),
        compiler_params=pltpu.CompilerParams(vmem_limit_bytes=8 * 2**20),
        cost_estimate=pl.CostEstimate(flops=0, bytes_accessed=2**20, transcendentals=0),
    )(a, b)


def weight_kernel(me_ref, hidden_ref, *refs):
    out_ref = refs[-1]
    acc = None
    for mask, grad in enumerate(refs[:-1]):
        rows = grad.shape[0]
        at = slice(mask * rows, (mask + 1) * rows)
        d = jnp.dot(hidden_ref[:, at], grad[...], preferred_element_type=F32)
        acc = d if acc is None else acc + d
    out_ref[...] = acc


def weight_grads(me, hidden, grads):
    rows, cols = grads[0].shape
    mine, total = hidden.shape
    spec = pltpu.PrefetchScalarGridSpec(
        num_scalar_prefetch=1,
        grid=(1,),
        in_specs=[block((mine, total), lambda h, me: (0, 0))]
        + [block((rows, cols), lambda h, me: (0, 0)) for _ in grads],
        out_specs=block((mine, cols), lambda h, me: (0, 0)),
    )
    return pl.pallas_call(
        weight_kernel,
        grid_spec=spec,
        out_shape=pltpu.HBM((mine, cols), F32),
        compiler_params=pltpu.CompilerParams(vmem_limit_bytes=12 * 2**20),
        cost_estimate=pl.CostEstimate(
            flops=2 * mine * total * cols, bytes_accessed=4 * 2**20, transcendentals=0
        ),
    )(me, hidden, *grads)


def last_kernel(me_ref, preact_ref, lhs_ref, p0, q0, p1, q1, after, out_ref):
    rows = p0.shape[2]
    acc = None
    for h, (p, q) in enumerate(((p0, q0), (p1, q1))):
        for i in range(2):
            mask = 4 * h + 2 * i + me_ref[0] % 2
            at = pl.ds(pl.multiple_of(mask * rows, 128), rows)
            grad = p[i].astype(F32) + q[i].astype(F32)
            grad = jnp.where(preact_ref[:, at] > 0, grad, 0.0).astype(BF)
            d = lax.dot_general(lhs_ref[:, at], grad, NT, preferred_element_type=F32)
            acc = d if acc is None else acc + d
    out_ref[...] = acc


def last_grads(me, preact, lhs, parts, after):
    count, total = lhs.shape
    mine = preact.shape[0]
    args = (preact, lhs, *parts)
    whole = lambda shape: block(shape, lambda h, me: (0,) * len(shape))
    spec = pltpu.PrefetchScalarGridSpec(
        num_scalar_prefetch=1,
        grid=(1,),
        in_specs=[whole(x.shape) for x in args] + [pl.BlockSpec(memory_space=pl.ANY)],
        out_specs=whole((count, mine)),
    )
    return pl.pallas_call(
        last_kernel,
        grid_spec=spec,
        out_shape=jax.ShapeDtypeStruct((count, mine), F32),
        compiler_params=pltpu.CompilerParams(vmem_limit_bytes=12 * 2**20),
        cost_estimate=pl.CostEstimate(
            flops=total * count * mine, bytes_accessed=2 * 2**20, transcendentals=0
        ),
    )(me, *args, after)


def outputs_kernel(own, other, latent, embed):
    dz = latent.shape[0]
    latent[...] = own[:dz] + other[:dz]
    embed[...] = own[dz:] + other[dz:]


def outputs(own, other, dz):
    count, mine = own.shape
    return pl.pallas_call(
        outputs_kernel,
        out_shape=[jax.ShapeDtypeStruct((c, mine), F32) for c in (dz, count - dz)],
        compiler_params=pltpu.CompilerParams(vmem_limit_bytes=8 * 2**20),
        cost_estimate=pl.CostEstimate(flops=0, bytes_accessed=2**20, transcendentals=0),
    )(own, other)


def tie(first, later):
    return lax.optimization_barrier((first, later))


def eight_by_four(
    records, real_labels, frequencies, class_noise, latents, syn_labels, w_latent, class_embed, w_out
):
    classes, hid = class_embed.shape
    groups = lax.axis_size("rec")
    rec = lax.axis_index("rec")
    feat = lax.axis_index("feat")
    rows, dz = latents.shape
    cols = w_out.shape[1]
    real_total = records.shape[0] * groups
    syn_total = rows * groups
    x, z_low, z_high = rec % 2, (rec // 2) % 2, rec // 4
    place = 2 * x + z_low
    me = jnp.stack([feat, x, z_low, z_high, rec, place]).astype(jnp.int32)

    table = one_hot(syn_labels, classes, BF)
    preact = jnp.dot(latents, w_latent, preferred_element_type=F32) + jnp.dot(
        table, class_embed, preferred_element_type=F32
    )
    hidden = jnp.maximum(preact, 0.0).astype(BF)
    own = jnp.tanh(jnp.dot(hidden, w_out, preferred_element_type=F32)).astype(BF)
    far = swap(own, "feat", 2)
    images = [own, far, swap(own, "feat", 1), swap(far, "feat", 1)]

    label_row = jnp.zeros((16, dz), BF).at[0, :].set(syn_labels.astype(BF))
    packed = jnp.concatenate([latents, label_row], axis=0)[None]
    packed = jnp.concatenate([packed, swap(packed, "rec", 1)], axis=0)
    pair = swap(packed, "rec", 2)
    masks = (0, 2, 1, 3)
    totals = (real_total, syn_total)
    send_a, keep_a, send_b, keep_b, both, waves, token = feature_sums(
        False, me, real_labels, syn_labels, masks, images, records, frequencies, classes, totals, packed
    )
    first_a = swap(send_a, "rec", 1)
    first_b = swap(send_b, "rec", 2)
    pair, token = tie(pair, token)
    quad = jnp.concatenate([packed, pair], axis=0)
    eight = jnp.concatenate([quad, swap(quad, "rec", 4)], axis=0)
    first_token = token
    last_a, last_b, waves, token = feature_sums(
        True, me, real_labels, syn_labels, masks, both, records, frequencies, classes, totals, quad, waves
    )

    all_latents = eight[:, :rows].reshape(syn_total, dz)
    all_labels = eight[:, rows].reshape(syn_total).astype(jnp.int32)
    all_table = one_hot(all_labels, classes, BF)
    mine = hid // groups
    lhs = jnp.concatenate([all_latents, all_table], axis=1).T
    w = jnp.concatenate(
        [
            lax.dynamic_slice_in_dim(w_latent, rec * mine, mine, 1),
            lax.dynamic_slice_in_dim(class_embed, rec * mine, mine, 1),
        ],
        axis=0,
    )
    all_preact = lax.dot_general(w, lhs, (((0,), (0,)), ((), ())), preferred_element_type=F32)
    all_hidden = jnp.maximum(all_preact, 0.0).astype(BF)

    send_a, send_b = stage_two_send(keep_a, first_a, keep_b, first_b, token)
    got_a = swap(send_a, "rec", 2)
    got_b = swap(send_b, "rec", 1)
    part = frequencies.shape[1] // groups
    noise = lax.dynamic_slice_in_dim(class_noise, (2 * place + z_high) * part, part, 2)
    noise = noise.reshape(classes, 2 * part)
    send, keep = stage_three(me, last_a, first_a, got_a, last_b, first_b, got_b, (noise, eight, first_token))
    got = swap(send, "rec", 4)
    feat_grad = gap_rows(me, keep, got, noise, all_labels.reshape(groups, rows), real_total)
    feat_grad = lax.all_to_all(feat_grad, "rec", 0, 0, tiled=True)

    send, keep = image_grads(
        me, waves, feat_grad, frequencies, cols, (all_preact, all_hidden, lhs)
    )
    send, keep = split_y(me, keep, swap(send, "feat", 1))
    out_grad = out_grads(keep, swap(send, "feat", 2), own)

    by = {0: out_grad}
    by[4] = swap(out_grad, "rec", 4)
    by[2] = swap(out_grad, "rec", 2)
    by[1] = swap(out_grad, "rec", 1)
    by[4], (by[2], by[1]) = tie(by[4], (by[2], by[1]))
    by[3] = swap(by[2], "rec", 1)
    by[6] = swap(by[4], "rec", 2)
    by[5] = swap(by[4], "rec", 1)

    def reduced(send, keep):
        part = add(keep, swap(send, "feat", 1), BF)
        return [part, swap(part, "feat", 2)]

    by[7] = swap(by[6], "rec", 1)
    send, keep = hidden_grads(me, w_out, [by[i] for i in range(4)], mine, by[5])
    parts = reduced(send, keep)
    parts += reduced(*hidden_grads(me, w_out, [by[4 + i] for i in range(4)], mine, parts[0]))
    grad_w_out = weight_grads(me, all_hidden, [by[mask] for mask in range(groups)])
    grads = last_grads(me, all_preact, lhs, parts, grad_w_out)
    grad_w_latent, grad_embed = outputs(grads, swap(grads, "feat", 1), dz)
    return grad_w_out, grad_w_latent, grad_embed


def solution(mesh):
    shape = (mesh.shape["rec"], mesh.shape["feat"])
    in_specs = (
        P("rec", None),
        P("rec"),
        P(None, "feat"),
        P(None, None, "feat"),
        P("rec", None),
        P("rec"),
        P(),
        P(),
        P(None, "feat"),
    )
    out_specs = (P("rec", "feat"), P(None, "rec"), P(None, "rec"))
    return jax.shard_map(
        eight_by_four if shape == (8, 4) else general, mesh=mesh, in_specs=in_specs, out_specs=out_specs, check_vma=False
    )
```

```python
import functools

import jax
import jax.numpy as jnp
from jax import lax
from jax.experimental import pallas as pl
from jax.experimental.pallas import tpu as pltpu
from jax.sharding import PartitionSpec as P

BF = jnp.bfloat16
F32 = jnp.float32

TURN = 0.15915494309189535
SIN = (4.44286783702217, -7.307441307726672, 3.59477116396636, -0.7843353598850176)
COS = (1.4142134962552275, -6.978850948563815, 5.739460376907241, -1.883557905986894, 0.3106880275267554)


def cos_sin(x):
    turns = x * TURN
    u = turns - jnp.round(turns)
    sq = u * u
    p = SIN[-1]
    for c in SIN[-2::-1]:
        p = p * sq + c
    q = COS[-1]
    for c in COS[-2::-1]:
        q = q * sq + c
    s = u * p
    return 1.0 - s * s, s * q


def one_hot(labels, count, dtype):
    return (labels[:, None] == jnp.arange(count, dtype=jnp.int32)[None, :]).astype(dtype)


def real_kernel(rows, labels_ref, records_ref, freq_ref, out_ref, table_ref):
    total = records_ref.shape[0]
    classes = table_ref.shape[0]
    owners, _, width = out_ref.shape
    part = width // 2

    @pl.when(pl.program_id(0) == 0)
    def _():
        ids = lax.broadcasted_iota(jnp.int32, (classes, total), 0)
        table_ref[...] = jnp.where(ids == labels_ref[...], 1.0, 0.0).astype(BF)

    freq = freq_ref[...]
    block = freq.shape[1]

    def sums(i, pre):
        co, si = cos_sin(pre)
        phi = jnp.concatenate([co.astype(BF), si.astype(BF)], axis=1)
        return jnp.dot(table_ref[:, i * rows : (i + 1) * rows], phi, preferred_element_type=F32)

    acc = None
    before = None
    steps = total // rows
    for i in range(steps + 1):
        pre = None
        if i < steps:
            pre = jnp.dot(records_ref[i * rows : (i + 1) * rows, :], freq, preferred_element_type=F32)
        if i > 0:
            d = sums(i - 1, before)
            acc = d if acc is None else acc + d
        before = pre
    for o in range(owners):
        out_ref[o, :, :part] = acc[:, o * part : (o + 1) * part]
        out_ref[o, :, part:] = acc[:, block + o * part : block + (o + 1) * part]


def real_sums(labels, records, freq, classes, owners):
    m, k = records.shape
    n = freq.shape[1]
    block = min(512, n)
    rows = 512
    part = n // owners
    per = block // part
    return pl.pallas_call(
        functools.partial(real_kernel, rows),
        grid=(n // block,),
        in_specs=[
            pl.BlockSpec((1, m), lambda j: (0, 0)),
            pl.BlockSpec((m, k), lambda j: (0, 0)),
            pl.BlockSpec((k, block), lambda j: (0, j)),
        ],
        out_specs=pl.BlockSpec((per, classes, 2 * part), lambda j: (j, 0, 0)),
        out_shape=jax.ShapeDtypeStruct((owners, classes, 2 * part), F32),
        scratch_shapes=[pltpu.VMEM((classes, m), BF)],
        compiler_params=pltpu.CompilerParams(vmem_limit_bytes=56 * 2**20),
        cost_estimate=pl.CostEstimate(
            flops=2 * m * n * (k + 2 * classes), bytes_accessed=2 * (m * k + k * n), transcendentals=0
        ),
    )(labels.reshape(1, m), records, freq)


def bits_of(n):
    return [1 << b for b in range(n.bit_length() - 1)]


def swap(x, axis, bit):
    n = lax.axis_size(axis)
    return lax.ppermute(x, axis, [(i, i ^ bit) for i in range(n)])


def pick(x, index, dim):
    return lax.dynamic_index_in_dim(x, index, dim, keepdims=False)


def halving(x, axis, order, count):
    me = lax.axis_index(axis)
    nbits = len(order)
    x = x.reshape((2,) * nbits + x.shape[1:])
    left = sorted(order, reverse=True)
    for bit in order:
        dim = left.index(bit)
        left.remove(bit)
        mine = (me // bit) % 2
        got = swap(pick(x, 1 - mine, dim).astype(BF), axis, bit)
        x = pick(x, mine, dim).astype(F32) + got.astype(F32)
    return x


def general(
    records, real_labels, frequencies, class_noise, latents, syn_labels, w_latent, class_embed, w_out
):
    classes = class_embed.shape[0]
    hid = class_embed.shape[1]
    groups = lax.axis_size("rec")
    feats = lax.axis_size("feat")
    rec = lax.axis_index("rec")
    nf = frequencies.shape[1]
    part = nf // groups
    rows, dz = latents.shape
    cols = w_out.shape[1]
    real_total = records.shape[0] * groups
    syn_total = rows * groups

    label_row = jnp.zeros((16, dz), BF).at[0, :].set(syn_labels.astype(BF))
    packed = jnp.concatenate([latents, label_row], axis=0)
    packed = lax.all_to_all(
        jnp.broadcast_to(packed[None], (groups,) + packed.shape), "rec", 0, 0, tiled=True
    )
    all_latents = packed[:, :rows].reshape(syn_total, dz)
    all_labels = packed[:, rows].reshape(syn_total).astype(jnp.int32)
    all_table = one_hot(all_labels, classes, BF)

    table = one_hot(syn_labels, classes, BF)
    preact = jnp.dot(latents, w_latent, preferred_element_type=F32) + jnp.dot(
        table, class_embed, preferred_element_type=F32
    )
    hidden = jnp.maximum(preact, 0.0).astype(BF)
    own_images = jnp.tanh(jnp.dot(hidden, w_out, preferred_element_type=F32)).astype(BF)
    images = lax.all_gather(own_images, "feat", axis=0)
    images = images.transpose(1, 0, 2).reshape(rows, feats * cols)
    syn_pre = jnp.dot(images, frequencies, preferred_element_type=F32)
    syn_cos, syn_sin = cos_sin(syn_pre)
    syn_phi = jnp.concatenate(
        [syn_cos.reshape(rows, groups, part), syn_sin.reshape(rows, groups, part)], axis=2
    ).astype(BF)
    syn_sum = lax.dot_general(
        table, syn_phi.reshape(rows, 2 * nf), (((0,), (0,)), ((), ())), preferred_element_type=F32
    )
    syn_sum = syn_sum.reshape(classes, groups, 2 * part).transpose(1, 0, 2)

    real_sum = real_sums(real_labels, records, frequencies, classes, groups)
    gap = syn_sum * (1.0 / syn_total) - real_sum * (1.0 / real_total)
    half = classes // 2
    order = bits_of(groups)
    other = [order[1], order[0]] + order[2:]
    gap = jnp.concatenate(
        [halving(gap[:, :half], "rec", order, groups), halving(gap[:, half:], "rec", other, groups)], axis=0
    )
    noise = lax.dynamic_slice_in_dim(class_noise, rec * part, part, 2).reshape(classes, 2 * part)
    gap = (16.0 * (gap - noise * (1.0 / real_total))).astype(BF)

    feat_grad = jnp.dot(all_table, gap, preferred_element_type=F32).astype(BF)
    feat_grad = lax.all_to_all(feat_grad.reshape(groups, rows, 2 * part), "rec", 0, 0, tiled=True)
    feat_grad = feat_grad.transpose(1, 0, 2).astype(F32)
    pre_grad = (
        -syn_sin.reshape(rows, groups, part) * feat_grad[:, :, :part]
        + syn_cos.reshape(rows, groups, part) * feat_grad[:, :, part:]
    )
    pre_grad = pre_grad.astype(BF).reshape(rows, nf)
    image_grad = lax.dot_general(
        frequencies, pre_grad, (((1,), (1,)), ((), ())), preferred_element_type=F32
    )
    image_grad = halving(image_grad.reshape(feats, cols, rows), "feat", bits_of(feats), feats)
    image_grad = image_grad.T
    out_grad = (image_grad * (1.0 - jnp.square(own_images.astype(F32)))).astype(BF)

    out_grad = lax.all_to_all(
        jnp.broadcast_to(out_grad[None], (groups, rows, cols)), "rec", 0, 0, tiled=True
    ).reshape(syn_total, cols)

    mine = hid // groups
    start = rec * mine
    all_preact = jnp.dot(
        all_latents, lax.dynamic_slice_in_dim(w_latent, start, mine, 1), preferred_element_type=F32
    ) + jnp.dot(
        all_table, lax.dynamic_slice_in_dim(class_embed, start, mine, 1), preferred_element_type=F32
    )
    all_hidden = jnp.maximum(all_preact, 0.0).astype(BF)
    grad_w_out = lax.dot_general(
        all_hidden, out_grad, (((0,), (0,)), ((), ())), preferred_element_type=F32
    )
    hidden_grad = lax.dot_general(
        out_grad,
        lax.dynamic_slice_in_dim(w_out, start, mine, 0),
        (((1,), (1,)), ((), ())),
        preferred_element_type=F32,
    )
    core = lax.axis_index("feat") % 2
    half = syn_total // 2
    hidden_grad = hidden_grad.reshape(2, half, mine)
    got = swap(pick(hidden_grad, 1 - core, 0).astype(BF), "feat", 1)
    hidden_grad = pick(hidden_grad, core, 0) + got.astype(F32)
    for bit in bits_of(feats)[1:]:
        send = hidden_grad.astype(BF)
        hidden_grad = send.astype(F32) + swap(send, "feat", bit).astype(F32)
    my_preact = lax.dynamic_slice_in_dim(all_preact, core * half, half, 0)
    pre_hidden = jnp.where(my_preact > 0, hidden_grad, 0.0).astype(BF)
    lhs = jnp.concatenate([all_latents, all_table], axis=1)
    lhs = lax.dynamic_slice_in_dim(lhs, core * half, half, 0)
    grads = lax.dot_general(lhs, pre_hidden, (((0,), (0,)), ((), ())), preferred_element_type=F32)
    grads = grads + swap(grads, "feat", 1)
    return grad_w_out, grads[:dz], grads[dz:]


def block(shape, index):
    return pl.BlockSpec(shape, index)


def sums(table, pre):
    co, si = cos_sin(pre)
    phi = jnp.concatenate([co.astype(BF), si.astype(BF)], axis=1)
    return jnp.dot(table, phi, preferred_element_type=F32)


def features_kernel(
    masks, last, real_total, syn_total, me_ref, real_labels_ref, syn_labels_ref, *refs
):
    count = 1 if last else len(masks)
    images = [refs[0].at[i] for i in range(len(masks))] if last else refs[:count]
    records_hbm, freq_ref = refs[count : count + 2]
    outs = refs[count + (4 if last else 3) : -4]
    wave, token = outs[-2:]
    records, real_table, syn_table, sem = refs[-4:]
    classes, total = real_table.shape
    size = 512
    steps = total // size
    step = pl.program_id(0)
    cols = images[0].shape[1]
    half = classes // 2
    token[...] = jnp.zeros_like(token)

    def copy(i):
        at = pl.ds(i * size, size)
        return pltpu.make_async_copy(records_hbm.at[at, :], records.at[at, :], sem.at[i])

    def work(wait):
        if wait:
            for i in range(steps):
                copy(i).start()
            ids = lax.broadcasted_iota(jnp.int32, (classes, total), 0)
            real_table[...] = jnp.where(ids == real_labels_ref[...], 1.0, 0.0).astype(BF)
            ids = lax.broadcasted_iota(jnp.int32, syn_table.shape, 0)
            syn_table[...] = jnp.where(ids == syn_labels_ref[...], 1.0, 0.0).astype(BF)
        syn_pre = None
        for mask, image in zip(masks, images):
            at = pl.multiple_of((me_ref[0] ^ mask) * cols, 128)
            d = jnp.dot(image[...], freq_ref[pl.ds(at, cols), :], preferred_element_type=F32)
            syn_pre = d if syn_pre is None else syn_pre + d
        freq = freq_ref[...]
        acc = None
        before = None
        for i in range(steps + 1):
            if i < steps:
                if wait:
                    copy(i).wait()
                pre = jnp.dot(records[i * size : (i + 1) * size, :], freq, preferred_element_type=F32)
            if i == 0:
                co, si = cos_sin(syn_pre)
                wave[0, 0] = co
                wave[0, 1] = si
                phi = jnp.concatenate([co.astype(BF), si.astype(BF)], axis=1)
                syn = jnp.dot(syn_table[...], phi, preferred_element_type=F32)
            else:
                d = sums(real_table[:, (i - 1) * size : i * size], before)
                acc = d if acc is None else acc + d
            before = pre
        gap = syn * (1.0 / syn_total) - acc * (1.0 / real_total)
        width = gap.shape[1] // 4
        return [
            jnp.concatenate(
                [gap[:, h * width : (h + 1) * width], gap[:, (h + 2) * width : (h + 3) * width]], axis=1
            )
            for h in range(2)
        ]

    if last:
        parts = work(True)
        for h in range(2):
            outs[0][h] = parts[h][:half]
            outs[1][h] = parts[h][half:]
        return
    send_a, keep_a, send_b, keep_b, both = outs[:5]

    @pl.when(step == 0)
    def _():
        for i in range(count):
            both[i] = images[i][...]
        parts = work(True)
        for h in range(2):
            send_a[0, h] = parts[h][:half].astype(BF)
            send_b[0, h] = parts[h][half:].astype(BF)

    @pl.when(step > 0)
    def _():
        parts = work(False)

        @pl.when(step == 1)
        def _():
            for h in range(2):
                send_a[0, h] = parts[h][:half].astype(BF)
                keep_b[h] = parts[h][half:]

        @pl.when(step == 2)
        def _():
            for h in range(2):
                keep_a[h] = parts[h][:half]
                send_b[0, h] = parts[h][half:].astype(BF)


def feature_sums(
    last, me, real_labels, syn_labels, masks, images, records, freq, classes, totals, after, waves=None
):
    total, k = records.shape
    n = freq.shape[1]
    rows, cols = images.shape[1:] if last else images[0].shape
    half = classes // 2
    tile = n // 4
    tiles = 1 if last else 3
    whole = lambda shape: block(shape, lambda j, me: (0,) * len(shape))
    kept = jax.ShapeDtypeStruct((2, half, tile), F32)
    sent = jax.ShapeDtypeStruct((2, 2, half, tile), BF)
    both = (len(masks), rows, cols)
    place = lambda j, me: me[5] ^ (0 if last else 3 - j)
    anywhere = pl.BlockSpec(memory_space=pl.ANY)
    shapes = [pltpu.HBM((4, 2, rows, tile), F32), jax.ShapeDtypeStruct((8, 128), F32)]
    specs = [block((1, 2, rows, tile), lambda j, me: (place(j, me), 0, 0, 0)), whole((8, 128))]
    if last:
        shapes = [kept, kept] + shapes
        specs = [whole(kept.shape), whole(kept.shape)] + specs
        images = (images,)
        extra = (after, waves)
    else:
        shapes = [sent, kept, sent, kept, pltpu.HBM(both, BF)] + shapes
        specs = [
            block((1, 2, half, tile), lambda j, me: (jnp.minimum(j, 1), 0, 0, 0)),
            whole(kept.shape),
            block((1, 2, half, tile), lambda j, me: (j // 2, 0, 0, 0)),
            whole(kept.shape),
            whole(both),
        ] + specs
        extra = (after,)
    grid_spec = pltpu.PrefetchScalarGridSpec(
        num_scalar_prefetch=1,
        grid=(tiles,),
        in_specs=[whole((1, total)), whole((1, rows))]
        + [whole(image.shape) for image in images]
        + [anywhere, block((k, tile), lambda j, me: (0, place(j, me)))]
        + [anywhere] * len(extra),
        out_specs=specs,
        scratch_shapes=[
            pltpu.VMEM((total, k), BF),
            pltpu.VMEM((classes, total), BF),
            pltpu.VMEM((classes, rows), BF),
            pltpu.SemaphoreType.DMA((total // 512,)),
        ],
    )
    return pl.pallas_call(
        functools.partial(features_kernel, masks, last, *totals),
        grid_spec=grid_spec,
        out_shape=shapes,
        input_output_aliases={7: 2} if last else {},
        compiler_params=pltpu.CompilerParams(vmem_limit_bytes=44 * 2**20),
        cost_estimate=pl.CostEstimate(
            flops=2 * (total + rows) * tiles * tile * (k + 2 * classes),
            bytes_accessed=2 * (total * k + k * tiles * tile),
            transcendentals=0,
        ),
    )(me, real_labels.reshape(1, -1), syn_labels.reshape(1, -1), *images, records, freq, *extra)


def stage_two_send_kernel(ka, ga, kb, gb, after, sa, sb, token):
    token[...] = jnp.zeros_like(token)
    sa[...] = (ka[...] + ga[0].astype(F32)).astype(BF)
    sb[...] = (kb[...] + gb[0].astype(F32)).astype(BF)


def stage_two_send(keep_a, got_a, keep_b, got_b, after):
    return pl.pallas_call(
        stage_two_send_kernel,
        in_specs=[pl.BlockSpec()] * 4 + [pl.BlockSpec(memory_space=pl.ANY)],
        out_shape=[jax.ShapeDtypeStruct(keep_a.shape, BF)] * 2 + [jax.ShapeDtypeStruct((8, 128), F32)],
        compiler_params=pltpu.CompilerParams(vmem_limit_bytes=10 * 2**20),
        cost_estimate=pl.CostEstimate(flops=0, bytes_accessed=3 * 2**20, transcendentals=0),
    )(keep_a, got_a, keep_b, got_b, after)


def stage_three_kernel(me_ref, na, fa, ga, nb, fb, gb, a, b, c, send, keep, token):
    token[...] = jnp.zeros_like(token)
    high = me_ref[3]
    half = na.shape[1]
    for flip, out in ((1, send), (0, keep)):
        at = high ^ flip
        out[:half] = (na[at] + fa[1, at].astype(F32) + ga[at].astype(F32)).astype(out.dtype)
        out[half:] = (nb[at] + fb[1, at].astype(F32) + gb[at].astype(F32)).astype(out.dtype)


def stage_three(me, keep_a, first_a, got_a, keep_b, first_b, got_b, after):
    _, half, width = keep_a.shape
    args = (keep_a, first_a, got_a, keep_b, first_b, got_b)
    whole = lambda shape: block(shape, lambda h, me: (0,) * len(shape))
    spec = pltpu.PrefetchScalarGridSpec(
        num_scalar_prefetch=1,
        grid=(1,),
        in_specs=[whole(x.shape) for x in args] + [pl.BlockSpec(memory_space=pl.ANY)] * 3,
        out_specs=[whole((2 * half, width))] * 2 + [whole((8, 128))],
    )
    return pl.pallas_call(
        stage_three_kernel,
        grid_spec=spec,
        out_shape=[jax.ShapeDtypeStruct((2 * half, width), t) for t in (BF, F32)]
        + [jax.ShapeDtypeStruct((8, 128), F32)],
        compiler_params=pltpu.CompilerParams(vmem_limit_bytes=12 * 2**20),
        cost_estimate=pl.CostEstimate(flops=0, bytes_accessed=3 * 2**20, transcendentals=0),
    )(me, *args, *after)


def gap_kernel(real_total, order, me_ref, keep_ref, got_ref, noise_ref, labels_ref, after, out_ref):
    classes = keep_ref.shape[0]
    rows = labels_ref.shape[1]
    gap = keep_ref[...] + got_ref[...].astype(F32) - noise_ref[...] * (1.0 / real_total)
    gap = (16.0 * gap).astype(BF)
    ids = lax.broadcasted_iota(jnp.int32, (classes, rows), 0)
    for i, mask in enumerate(order):
        table = jnp.where(ids == labels_ref[i : i + 1, :], 1.0, 0.0).astype(BF)
        out = lax.dot_general(table, gap, (((0,), (0,)), ((), ())), preferred_element_type=F32)
        out_ref[me_ref[4] ^ mask] = out.astype(BF)


def gap_rows(me, keep, got, noise, labels, real_total, order, after):
    classes, width = keep.shape
    groups, rows = labels.shape
    whole = lambda shape: block(shape, lambda h, me: (0,) * len(shape))
    spec = pltpu.PrefetchScalarGridSpec(
        num_scalar_prefetch=1,
        grid=(1,),
        in_specs=[whole(x.shape) for x in (keep, got, noise, labels)]
        + [pl.BlockSpec(memory_space=pl.ANY)],
        out_specs=whole((groups, rows, width)),
    )
    return pl.pallas_call(
        functools.partial(gap_kernel, real_total, order),
        grid_spec=spec,
        out_shape=jax.ShapeDtypeStruct((groups, rows, width), BF),
        compiler_params=pltpu.CompilerParams(vmem_limit_bytes=14 * 2**20),
        cost_estimate=pl.CostEstimate(
            flops=2 * groups * rows * classes * width, bytes_accessed=3 * 2**20, transcendentals=0
        ),
    )(me, keep, got, noise, labels, after)


NT = (((1,), (1,)), ((), ()))


def image_kernel(me_ref, wave_ref, rows_ref, freq_ref, a, b, c, send_ref, keep_ref, pre_ref):
    step = pl.program_id(0)
    tile = wave_ref.shape[3]
    part = tile // 2

    @pl.when(step == 0)
    def _():
        for place in range(4):
            for h in range(2):
                grad = rows_ref[4 * h + 2 * (place % 2) + place // 2].astype(F32)
                lanes = slice(h * part, (h + 1) * part)
                pre = wave_ref[place, 0, :, lanes] * grad[:, part:]
                pre = pre - wave_ref[place, 1, :, lanes] * grad[:, :part]
                at = place * tile + h * part
                pre_ref[:, at : at + part] = pre.astype(BF)

    out = lax.dot_general(freq_ref[...], pre_ref[...], NT, preferred_element_type=F32)

    @pl.when(step < 2)
    def _():
        send_ref[0] = out.astype(BF)

    @pl.when(step >= 2)
    def _():
        keep_ref[0] = out


def image_grads(me, waves, feat_rows, freq, cols, after):
    k, n = freq.shape
    owners, rows, width = feat_rows.shape
    whole = lambda shape: block(shape, lambda s, me: (0,) * len(shape))

    def source(s, me):
        return 2 * (s % 2) + ((me[0] % 2) ^ (1 - s // 2)), 0

    spec = pltpu.PrefetchScalarGridSpec(
        num_scalar_prefetch=1,
        grid=(4,),
        in_specs=[whole(waves.shape), whole(feat_rows.shape), block((cols, n), source)]
        + [pl.BlockSpec(memory_space=pl.ANY)] * 3,
        out_specs=[
            block((1, cols, rows), lambda s, me: (jnp.minimum(s, 1), 0, 0)),
            block((1, cols, rows), lambda s, me: (jnp.maximum(s - 2, 0), 0, 0)),
        ],
        scratch_shapes=[pltpu.VMEM((rows, n), BF)],
    )
    return pl.pallas_call(
        image_kernel,
        grid_spec=spec,
        out_shape=[jax.ShapeDtypeStruct((2, cols, rows), BF), pltpu.HBM((2, cols, rows), F32)],
        compiler_params=pltpu.CompilerParams(vmem_limit_bytes=52 * 2**20),
        cost_estimate=pl.CostEstimate(flops=2 * k * n * rows, bytes_accessed=2 * k * n, transcendentals=0),
    )(me, waves, feat_rows, freq, *after)


def split_y_kernel(me_ref, keep_s, keep_k, got_s, got_k, send, keep):
    send[...] = (keep_s[0] + got_s[0].astype(F32)).astype(BF)
    keep[...] = keep_k[0] + got_k[0].astype(F32)


def split_y(me, keep, got):
    _, cols, rows = keep.shape
    at = lambda flip: block((1, cols, rows), lambda h, me: ((me[0] // 2) ^ flip, 0, 0))
    out = block((cols, rows), lambda h, me: (0, 0))
    spec = pltpu.PrefetchScalarGridSpec(
        num_scalar_prefetch=1, grid=(1,), in_specs=[at(1), at(0)] * 2, out_specs=[out, out]
    )
    return pl.pallas_call(
        split_y_kernel,
        grid_spec=spec,
        out_shape=[jax.ShapeDtypeStruct((cols, rows), t) for t in (BF, F32)],
        compiler_params=pltpu.CompilerParams(vmem_limit_bytes=8 * 2**20),
        cost_estimate=pl.CostEstimate(flops=0, bytes_accessed=2**20, transcendentals=0),
    )(me, keep, keep, got, got)


def out_kernel(keep, got, image, out):
    grad = (keep[...] + got[...].astype(F32)).T
    grad = grad * (1.0 - jnp.square(image[...].astype(F32)))
    out[...] = grad.astype(BF)


def out_grads(keep, got, image):
    return pl.pallas_call(
        out_kernel,
        out_shape=jax.ShapeDtypeStruct(image.shape, BF),
        compiler_params=pltpu.CompilerParams(vmem_limit_bytes=8 * 2**20),
        cost_estimate=pl.CostEstimate(flops=0, bytes_accessed=2**20, transcendentals=0),
    )(keep, got, image)


def hidden_kernel(me_ref, w_ref, *refs):
    grads = refs[:4]
    send, keep = refs[5:]
    core = me_ref[0] % 2
    out = [lax.dot_general(w_ref[...], g[...], NT, preferred_element_type=F32) for g in grads]
    for i in range(2):
        keep[i] = jnp.where(core == 0, out[2 * i], out[2 * i + 1])
        send[i] = jnp.where(core == 0, out[2 * i + 1], out[2 * i]).astype(BF)


def hidden_grads(me, w_out, grads, mine, after):
    rows, cols = grads[0].shape
    whole = lambda shape: block(shape, lambda r, me: (0,) * len(shape))
    spec = pltpu.PrefetchScalarGridSpec(
        num_scalar_prefetch=1,
        grid=(1,),
        in_specs=[block((mine, cols), lambda r, me: (me[4], 0))] + [whole((rows, cols))] * 4
        + [pl.BlockSpec(memory_space=pl.ANY)],
        out_specs=[whole((2, mine, rows))] * 2,
    )
    return pl.pallas_call(
        hidden_kernel,
        grid_spec=spec,
        out_shape=[jax.ShapeDtypeStruct((2, mine, rows), t) for t in (BF, F32)],
        compiler_params=pltpu.CompilerParams(vmem_limit_bytes=8 * 2**20),
        cost_estimate=pl.CostEstimate(
            flops=8 * mine * cols * rows, bytes_accessed=2 * 5 * mine * cols, transcendentals=0
        ),
    )(me, w_out, *grads, after)


def add_kernel(a, b, out):
    out[...] = (a[...].astype(F32) + b[...].astype(F32)).astype(out.dtype)


def add(a, b, kind):
    return pl.pallas_call(
        add_kernel,
        out_shape=jax.ShapeDtypeStruct(a.shape, kind),
        compiler_params=pltpu.CompilerParams(vmem_limit_bytes=8 * 2**20),
        cost_estimate=pl.CostEstimate(flops=0, bytes_accessed=2**20, transcendentals=0),
    )(a, b)


def weight_kernel(me_ref, hidden_ref, *refs):
    out_ref = refs[-1]
    acc = None
    for mask, grad in enumerate(refs[:-1]):
        rows = grad.shape[0]
        at = slice(mask * rows, (mask + 1) * rows)
        d = jnp.dot(hidden_ref[:, at], grad[...], preferred_element_type=F32)
        acc = d if acc is None else acc + d
    out_ref[...] = acc


def weight_grads(me, hidden, grads):
    rows, cols = grads[0].shape
    mine, total = hidden.shape
    spec = pltpu.PrefetchScalarGridSpec(
        num_scalar_prefetch=1,
        grid=(1,),
        in_specs=[block((mine, total), lambda h, me: (0, 0))]
        + [block((rows, cols), lambda h, me: (0, 0)) for _ in grads],
        out_specs=block((mine, cols), lambda h, me: (0, 0)),
    )
    return pl.pallas_call(
        weight_kernel,
        grid_spec=spec,
        out_shape=pltpu.HBM((mine, cols), F32),
        compiler_params=pltpu.CompilerParams(vmem_limit_bytes=12 * 2**20),
        cost_estimate=pl.CostEstimate(
            flops=2 * mine * total * cols, bytes_accessed=4 * 2**20, transcendentals=0
        ),
    )(me, hidden, *grads)


def last_kernel(me_ref, preact_ref, lhs_ref, p0, q0, p1, q1, after, out_ref):
    rows = p0.shape[2]
    acc = None
    for h, (p, q) in enumerate(((p0, q0), (p1, q1))):
        for i in range(2):
            place = 4 * (me_ref[0] % 2) + 2 * i + h
            at = pl.ds(pl.multiple_of(place * rows, 128), rows)
            grad = p[i].astype(F32) + q[i].astype(F32)
            grad = jnp.where(preact_ref[:, at] > 0, grad, 0.0).astype(BF)
            d = lax.dot_general(lhs_ref[:, at], grad, NT, preferred_element_type=F32)
            acc = d if acc is None else acc + d
    out_ref[...] = acc


def last_grads(me, preact, lhs, parts, after):
    count, total = lhs.shape
    mine = preact.shape[0]
    args = (preact, lhs, *parts)
    whole = lambda shape: block(shape, lambda h, me: (0,) * len(shape))
    spec = pltpu.PrefetchScalarGridSpec(
        num_scalar_prefetch=1,
        grid=(1,),
        in_specs=[whole(x.shape) for x in args] + [pl.BlockSpec(memory_space=pl.ANY)],
        out_specs=whole((count, mine)),
    )
    return pl.pallas_call(
        last_kernel,
        grid_spec=spec,
        out_shape=jax.ShapeDtypeStruct((count, mine), F32),
        compiler_params=pltpu.CompilerParams(vmem_limit_bytes=12 * 2**20),
        cost_estimate=pl.CostEstimate(
            flops=total * count * mine, bytes_accessed=2 * 2**20, transcendentals=0
        ),
    )(me, *args, after)


def outputs_kernel(own, other, latent, embed):
    dz = latent.shape[0]
    latent[...] = own[:dz] + other[:dz]
    embed[...] = own[dz:] + other[dz:]


def outputs(own, other, dz):
    count, mine = own.shape
    return pl.pallas_call(
        outputs_kernel,
        out_shape=[jax.ShapeDtypeStruct((c, mine), F32) for c in (dz, count - dz)],
        compiler_params=pltpu.CompilerParams(vmem_limit_bytes=8 * 2**20),
        cost_estimate=pl.CostEstimate(flops=0, bytes_accessed=2**20, transcendentals=0),
    )(own, other)


def tie(first, later):
    return lax.optimization_barrier((first, later))


def eight_by_four(
    records, real_labels, frequencies, class_noise, latents, syn_labels, w_latent, class_embed, w_out
):
    classes, hid = class_embed.shape
    groups = lax.axis_size("rec")
    rec = lax.axis_index("rec")
    feat = lax.axis_index("feat")
    rows, dz = latents.shape
    cols = w_out.shape[1]
    real_total = records.shape[0] * groups
    syn_total = rows * groups
    x, z_low, z_high = rec % 2, (rec // 2) % 2, rec // 4
    place = 2 * x + z_low
    me = jnp.stack([feat, x, z_low, z_high, rec, place]).astype(jnp.int32)

    table = one_hot(syn_labels, classes, BF)
    preact = jnp.dot(latents, w_latent, preferred_element_type=F32) + jnp.dot(
        table, class_embed, preferred_element_type=F32
    )
    hidden = jnp.maximum(preact, 0.0).astype(BF)
    own = jnp.tanh(jnp.dot(hidden, w_out, preferred_element_type=F32)).astype(BF)
    far = swap(own, "feat", 2)

    order = (0, 4, 2, 6, 1, 5, 3, 7)
    label_row = jnp.zeros((16, dz), BF).at[0, :].set(syn_labels.astype(BF))
    packed = jnp.concatenate([latents, label_row], axis=0)[None]
    far, pair = tie(far, swap(packed, "rec", 4))
    images = [own, far, swap(own, "feat", 1), swap(far, "feat", 1)]
    packed, real_labels = tie(jnp.concatenate([packed, pair], axis=0), real_labels)
    pair = swap(packed, "rec", 2)

    masks = (0, 2, 1, 3)
    totals = (real_total, syn_total)
    send_a, keep_a, send_b, keep_b, both, waves, token = feature_sums(
        False, me, real_labels, syn_labels, masks, images, records, frequencies, classes, totals, me
    )
    first_a = swap(send_a, "rec", 1)
    first_b = swap(send_b, "rec", 2)
    pair, token = tie(pair, token)
    last_a, last_b, waves, token = feature_sums(
        True, me, real_labels, syn_labels, masks, both, records, frequencies, classes, totals, token, waves
    )

    send_a, send_b, token = stage_two_send(keep_a, first_a, keep_b, first_b, token)
    got_a = swap(send_a, "rec", 2)
    got_b = swap(send_b, "rec", 1)
    part = frequencies.shape[1] // groups
    noise = lax.dynamic_slice_in_dim(class_noise, (2 * place + z_high) * part, part, 2)
    noise = noise.reshape(classes, 2 * part)
    send, keep, token = stage_three(me, last_a, first_a, got_a, last_b, first_b, got_b, (noise, token, token))
    got = swap(send, "rec", 4)
    pair, token = tie(pair, token)
    quad = jnp.concatenate([packed, pair], axis=0)
    eight = jnp.concatenate([quad, swap(quad, "rec", 1)], axis=0)
    all_latents = eight[:, :rows].reshape(syn_total, dz)
    all_labels = eight[:, rows].reshape(syn_total).astype(jnp.int32)
    all_table = one_hot(all_labels, classes, BF)
    mine = hid // groups
    lhs = jnp.concatenate([all_latents, all_table], axis=1).T
    w = jnp.concatenate(
        [
            lax.dynamic_slice_in_dim(w_latent, rec * mine, mine, 1),
            lax.dynamic_slice_in_dim(class_embed, rec * mine, mine, 1),
        ],
        axis=0,
    )
    all_preact = lax.dot_general(w, lhs, (((0,), (0,)), ((), ())), preferred_element_type=F32)
    all_hidden = jnp.maximum(all_preact, 0.0).astype(BF)

    feat_grad = gap_rows(me, keep, got, noise, all_labels.reshape(groups, rows), real_total, order, token)
    feat_grad = lax.all_to_all(feat_grad, "rec", 0, 0, tiled=True)

    send, keep = image_grads(
        me, waves, feat_grad, frequencies, cols, (all_preact, all_hidden, lhs)
    )
    send, keep = split_y(me, keep, swap(send, "feat", 1))
    out_grad = out_grads(keep, swap(send, "feat", 2), own)

    by = {0: out_grad}
    by[4] = swap(out_grad, "rec", 4)
    by[2] = swap(out_grad, "rec", 2)
    by[1] = swap(out_grad, "rec", 1)
    by[4], (by[2], by[1]) = tie(by[4], (by[2], by[1]))
    by[3] = swap(by[2], "rec", 1)
    by[6] = swap(by[4], "rec", 2)
    by[5] = swap(by[4], "rec", 1)

    def reduced(send, keep):
        part = add(keep, swap(send, "feat", 1), BF)
        return [part, swap(part, "feat", 2)]

    by[7] = swap(by[6], "rec", 1)
    send, keep = hidden_grads(me, w_out, [by[i] for i in range(4)], mine, by[5])
    parts = reduced(send, keep)
    parts += reduced(*hidden_grads(me, w_out, [by[4 + i] for i in range(4)], mine, parts[0]))
    grad_w_out = weight_grads(me, all_hidden, [by[mask] for mask in order])
    grads = last_grads(me, all_preact, lhs, parts, grad_w_out)
    grad_w_latent, grad_embed = outputs(grads, swap(grads, "feat", 1), dz)
    return grad_w_out, grad_w_latent, grad_embed


def solution(mesh):
    shape = (mesh.shape["rec"], mesh.shape["feat"])
    in_specs = (
        P("rec", None),
        P("rec"),
        P(None, "feat"),
        P(None, None, "feat"),
        P("rec", None),
        P("rec"),
        P(),
        P(),
        P(None, "feat"),
    )
    out_specs = (P("rec", "feat"), P(None, "rec"), P(None, "rec"))
    return jax.shard_map(
        eight_by_four if shape == (8, 4) else general, mesh=mesh, in_specs=in_specs, out_specs=out_specs, check_vma=False
    )
```

```python
import functools

import jax
import jax.numpy as jnp
from jax import lax
from jax.experimental import pallas as pl
from jax.experimental.pallas import tpu as pltpu
from jax.sharding import PartitionSpec as P

BF = jnp.bfloat16
F32 = jnp.float32

TURN = 0.15915494309189535
SIN = (4.44286783702217, -7.307441307726672, 3.59477116396636, -0.7843353598850176)
COS = (1.4142134962552275, -6.978850948563815, 5.739460376907241, -1.883557905986894, 0.3106880275267554)


def cos_sin(x):
    turns = x * TURN
    u = turns - jnp.round(turns)
    sq = u * u
    p = SIN[-1]
    for c in SIN[-2::-1]:
        p = p * sq + c
    q = COS[-1]
    for c in COS[-2::-1]:
        q = q * sq + c
    s = u * p
    return 1.0 - s * s, s * q


def one_hot(labels, count, dtype):
    return (labels[:, None] == jnp.arange(count, dtype=jnp.int32)[None, :]).astype(dtype)


def real_kernel(rows, labels_ref, records_ref, freq_ref, out_ref, table_ref):
    total = records_ref.shape[0]
    classes = table_ref.shape[0]
    owners, _, width = out_ref.shape
    part = width // 2

    @pl.when(pl.program_id(0) == 0)
    def _():
        ids = lax.broadcasted_iota(jnp.int32, (classes, total), 0)
        table_ref[...] = jnp.where(ids == labels_ref[...], 1.0, 0.0).astype(BF)

    freq = freq_ref[...]
    block = freq.shape[1]

    def sums(i, pre):
        co, si = cos_sin(pre)
        phi = jnp.concatenate([co.astype(BF), si.astype(BF)], axis=1)
        return jnp.dot(table_ref[:, i * rows : (i + 1) * rows], phi, preferred_element_type=F32)

    acc = None
    before = None
    steps = total // rows
    for i in range(steps + 1):
        pre = None
        if i < steps:
            pre = jnp.dot(records_ref[i * rows : (i + 1) * rows, :], freq, preferred_element_type=F32)
        if i > 0:
            d = sums(i - 1, before)
            acc = d if acc is None else acc + d
        before = pre
    for o in range(owners):
        out_ref[o, :, :part] = acc[:, o * part : (o + 1) * part]
        out_ref[o, :, part:] = acc[:, block + o * part : block + (o + 1) * part]


def real_sums(labels, records, freq, classes, owners):
    m, k = records.shape
    n = freq.shape[1]
    block = min(512, n)
    rows = 512
    part = n // owners
    per = block // part
    return pl.pallas_call(
        functools.partial(real_kernel, rows),
        grid=(n // block,),
        in_specs=[
            pl.BlockSpec((1, m), lambda j: (0, 0)),
            pl.BlockSpec((m, k), lambda j: (0, 0)),
            pl.BlockSpec((k, block), lambda j: (0, j)),
        ],
        out_specs=pl.BlockSpec((per, classes, 2 * part), lambda j: (j, 0, 0)),
        out_shape=jax.ShapeDtypeStruct((owners, classes, 2 * part), F32),
        scratch_shapes=[pltpu.VMEM((classes, m), BF)],
        compiler_params=pltpu.CompilerParams(vmem_limit_bytes=56 * 2**20),
        cost_estimate=pl.CostEstimate(
            flops=2 * m * n * (k + 2 * classes), bytes_accessed=2 * (m * k + k * n), transcendentals=0
        ),
    )(labels.reshape(1, m), records, freq)


def bits_of(n):
    return [1 << b for b in range(n.bit_length() - 1)]


def swap(x, axis, bit):
    n = lax.axis_size(axis)
    return lax.ppermute(x, axis, [(i, i ^ bit) for i in range(n)])


def pick(x, index, dim):
    return lax.dynamic_index_in_dim(x, index, dim, keepdims=False)


def halving(x, axis, order, count):
    me = lax.axis_index(axis)
    nbits = len(order)
    x = x.reshape((2,) * nbits + x.shape[1:])
    left = sorted(order, reverse=True)
    for bit in order:
        dim = left.index(bit)
        left.remove(bit)
        mine = (me // bit) % 2
        got = swap(pick(x, 1 - mine, dim).astype(BF), axis, bit)
        x = pick(x, mine, dim).astype(F32) + got.astype(F32)
    return x


def general(
    records, real_labels, frequencies, class_noise, latents, syn_labels, w_latent, class_embed, w_out
):
    classes = class_embed.shape[0]
    hid = class_embed.shape[1]
    groups = lax.axis_size("rec")
    feats = lax.axis_size("feat")
    rec = lax.axis_index("rec")
    nf = frequencies.shape[1]
    part = nf // groups
    rows, dz = latents.shape
    cols = w_out.shape[1]
    real_total = records.shape[0] * groups
    syn_total = rows * groups

    label_row = jnp.zeros((16, dz), BF).at[0, :].set(syn_labels.astype(BF))
    packed = jnp.concatenate([latents, label_row], axis=0)
    packed = lax.all_to_all(
        jnp.broadcast_to(packed[None], (groups,) + packed.shape), "rec", 0, 0, tiled=True
    )
    all_latents = packed[:, :rows].reshape(syn_total, dz)
    all_labels = packed[:, rows].reshape(syn_total).astype(jnp.int32)
    all_table = one_hot(all_labels, classes, BF)

    table = one_hot(syn_labels, classes, BF)
    preact = jnp.dot(latents, w_latent, preferred_element_type=F32) + jnp.dot(
        table, class_embed, preferred_element_type=F32
    )
    hidden = jnp.maximum(preact, 0.0).astype(BF)
    own_images = jnp.tanh(jnp.dot(hidden, w_out, preferred_element_type=F32)).astype(BF)
    images = lax.all_gather(own_images, "feat", axis=0)
    images = images.transpose(1, 0, 2).reshape(rows, feats * cols)
    syn_pre = jnp.dot(images, frequencies, preferred_element_type=F32)
    syn_cos, syn_sin = cos_sin(syn_pre)
    syn_phi = jnp.concatenate(
        [syn_cos.reshape(rows, groups, part), syn_sin.reshape(rows, groups, part)], axis=2
    ).astype(BF)
    syn_sum = lax.dot_general(
        table, syn_phi.reshape(rows, 2 * nf), (((0,), (0,)), ((), ())), preferred_element_type=F32
    )
    syn_sum = syn_sum.reshape(classes, groups, 2 * part).transpose(1, 0, 2)

    real_sum = real_sums(real_labels, records, frequencies, classes, groups)
    gap = syn_sum * (1.0 / syn_total) - real_sum * (1.0 / real_total)
    half = classes // 2
    order = bits_of(groups)
    other = [order[1], order[0]] + order[2:]
    gap = jnp.concatenate(
        [halving(gap[:, :half], "rec", order, groups), halving(gap[:, half:], "rec", other, groups)], axis=0
    )
    noise = lax.dynamic_slice_in_dim(class_noise, rec * part, part, 2).reshape(classes, 2 * part)
    gap = (16.0 * (gap - noise * (1.0 / real_total))).astype(BF)

    feat_grad = jnp.dot(all_table, gap, preferred_element_type=F32).astype(BF)
    feat_grad = lax.all_to_all(feat_grad.reshape(groups, rows, 2 * part), "rec", 0, 0, tiled=True)
    feat_grad = feat_grad.transpose(1, 0, 2).astype(F32)
    pre_grad = (
        -syn_sin.reshape(rows, groups, part) * feat_grad[:, :, :part]
        + syn_cos.reshape(rows, groups, part) * feat_grad[:, :, part:]
    )
    pre_grad = pre_grad.astype(BF).reshape(rows, nf)
    image_grad = lax.dot_general(
        frequencies, pre_grad, (((1,), (1,)), ((), ())), preferred_element_type=F32
    )
    image_grad = halving(image_grad.reshape(feats, cols, rows), "feat", bits_of(feats), feats)
    image_grad = image_grad.T
    out_grad = (image_grad * (1.0 - jnp.square(own_images.astype(F32)))).astype(BF)

    out_grad = lax.all_to_all(
        jnp.broadcast_to(out_grad[None], (groups, rows, cols)), "rec", 0, 0, tiled=True
    ).reshape(syn_total, cols)

    mine = hid // groups
    start = rec * mine
    all_preact = jnp.dot(
        all_latents, lax.dynamic_slice_in_dim(w_latent, start, mine, 1), preferred_element_type=F32
    ) + jnp.dot(
        all_table, lax.dynamic_slice_in_dim(class_embed, start, mine, 1), preferred_element_type=F32
    )
    all_hidden = jnp.maximum(all_preact, 0.0).astype(BF)
    grad_w_out = lax.dot_general(
        all_hidden, out_grad, (((0,), (0,)), ((), ())), preferred_element_type=F32
    )
    hidden_grad = lax.dot_general(
        out_grad,
        lax.dynamic_slice_in_dim(w_out, start, mine, 0),
        (((1,), (1,)), ((), ())),
        preferred_element_type=F32,
    )
    core = lax.axis_index("feat") % 2
    half = syn_total // 2
    hidden_grad = hidden_grad.reshape(2, half, mine)
    got = swap(pick(hidden_grad, 1 - core, 0).astype(BF), "feat", 1)
    hidden_grad = pick(hidden_grad, core, 0) + got.astype(F32)
    for bit in bits_of(feats)[1:]:
        send = hidden_grad.astype(BF)
        hidden_grad = send.astype(F32) + swap(send, "feat", bit).astype(F32)
    my_preact = lax.dynamic_slice_in_dim(all_preact, core * half, half, 0)
    pre_hidden = jnp.where(my_preact > 0, hidden_grad, 0.0).astype(BF)
    lhs = jnp.concatenate([all_latents, all_table], axis=1)
    lhs = lax.dynamic_slice_in_dim(lhs, core * half, half, 0)
    grads = lax.dot_general(lhs, pre_hidden, (((0,), (0,)), ((), ())), preferred_element_type=F32)
    grads = grads + swap(grads, "feat", 1)
    return grad_w_out, grads[:dz], grads[dz:]


def block(shape, index):
    return pl.BlockSpec(shape, index)


def sums(table, pre):
    co, si = cos_sin(pre)
    phi = jnp.concatenate([co.astype(BF), si.astype(BF)], axis=1)
    return jnp.dot(table, phi, preferred_element_type=F32)


def features_kernel(
    masks, last, real_total, syn_total, me_ref, real_labels_ref, syn_labels_ref, *refs
):
    count = 1 if last else len(masks)
    images = [refs[0].at[i] for i in range(len(masks))] if last else refs[:count]
    records_hbm, freq_ref = refs[count : count + 2]
    outs = refs[count + (4 if last else 3) : -4]
    wave, token = outs[-2:]
    records, real_table, syn_table, sem = refs[-4:]
    classes, total = real_table.shape
    size = 512
    steps = total // size
    step = pl.program_id(0)
    cols = images[0].shape[1]
    half = classes // 2
    token[...] = jnp.zeros_like(token)

    def copy(i):
        at = pl.ds(i * size, size)
        return pltpu.make_async_copy(records_hbm.at[at, :], records.at[at, :], sem.at[i])

    def work(wait):
        if wait:
            for i in range(steps):
                copy(i).start()
            ids = lax.broadcasted_iota(jnp.int32, (classes, total), 0)
            real_table[...] = jnp.where(ids == real_labels_ref[...], 1.0, 0.0).astype(BF)
            ids = lax.broadcasted_iota(jnp.int32, syn_table.shape, 0)
            syn_table[...] = jnp.where(ids == syn_labels_ref[...], 1.0, 0.0).astype(BF)
        syn_pre = None
        for mask, image in zip(masks, images):
            at = pl.multiple_of((me_ref[0] ^ mask) * cols, 128)
            d = jnp.dot(image[...], freq_ref[pl.ds(at, cols), :], preferred_element_type=F32)
            syn_pre = d if syn_pre is None else syn_pre + d
        freq = freq_ref[...]
        acc = None
        before = None
        for i in range(steps + 1):
            if i < steps:
                if wait:
                    copy(i).wait()
                pre = jnp.dot(records[i * size : (i + 1) * size, :], freq, preferred_element_type=F32)
            if i == 0:
                co, si = cos_sin(syn_pre)
                wave[0, 0] = co
                wave[0, 1] = si
                phi = jnp.concatenate([co.astype(BF), si.astype(BF)], axis=1)
                syn = jnp.dot(syn_table[...], phi, preferred_element_type=F32)
            else:
                d = sums(real_table[:, (i - 1) * size : i * size], before)
                acc = d if acc is None else acc + d
            before = pre
        gap = syn * (1.0 / syn_total) - acc * (1.0 / real_total)
        width = gap.shape[1] // 4
        return [
            jnp.concatenate(
                [gap[:, h * width : (h + 1) * width], gap[:, (h + 2) * width : (h + 3) * width]], axis=1
            )
            for h in range(2)
        ]

    if last:
        parts = work(True)
        for h in range(2):
            outs[0][h] = parts[h][:half]
            outs[1][h] = parts[h][half:]
        return
    send_a, keep_a, send_b, keep_b, both = outs[:5]

    @pl.when(step == 0)
    def _():
        for i in range(count):
            both[i] = images[i][...]
        parts = work(True)
        for h in range(2):
            send_a[0, h] = parts[h][:half].astype(BF)
            send_b[0, h] = parts[h][half:].astype(BF)

    @pl.when(step > 0)
    def _():
        parts = work(False)

        @pl.when(step == 1)
        def _():
            for h in range(2):
                send_a[0, h] = parts[h][:half].astype(BF)
                keep_b[h] = parts[h][half:]

        @pl.when(step == 2)
        def _():
            for h in range(2):
                keep_a[h] = parts[h][:half]
                send_b[0, h] = parts[h][half:].astype(BF)


def feature_sums(
    last, me, real_labels, syn_labels, masks, images, records, freq, classes, totals, after, waves=None
):
    total, k = records.shape
    n = freq.shape[1]
    rows, cols = images.shape[1:] if last else images[0].shape
    half = classes // 2
    tile = n // 4
    tiles = 1 if last else 3
    whole = lambda shape: block(shape, lambda j, me: (0,) * len(shape))
    kept = jax.ShapeDtypeStruct((2, half, tile), F32)
    sent = jax.ShapeDtypeStruct((2, 2, half, tile), BF)
    both = (len(masks), rows, cols)
    place = lambda j, me: me[5] ^ (0 if last else 3 - j)
    anywhere = pl.BlockSpec(memory_space=pl.ANY)
    shapes = [pltpu.HBM((4, 2, rows, tile), F32), jax.ShapeDtypeStruct((8, 128), F32)]
    specs = [block((1, 2, rows, tile), lambda j, me: (place(j, me), 0, 0, 0)), whole((8, 128))]
    if last:
        shapes = [kept, kept] + shapes
        specs = [whole(kept.shape), whole(kept.shape)] + specs
        images = (images,)
        extra = (after, waves)
    else:
        shapes = [sent, kept, sent, kept, pltpu.HBM(both, BF)] + shapes
        specs = [
            block((1, 2, half, tile), lambda j, me: (jnp.minimum(j, 1), 0, 0, 0)),
            whole(kept.shape),
            block((1, 2, half, tile), lambda j, me: (j // 2, 0, 0, 0)),
            whole(kept.shape),
            whole(both),
        ] + specs
        extra = (after,)
    grid_spec = pltpu.PrefetchScalarGridSpec(
        num_scalar_prefetch=1,
        grid=(tiles,),
        in_specs=[whole((1, total)), whole((1, rows))]
        + [whole(image.shape) for image in images]
        + [anywhere, block((k, tile), lambda j, me: (0, place(j, me)))]
        + [anywhere] * len(extra),
        out_specs=specs,
        scratch_shapes=[
            pltpu.VMEM((total, k), BF),
            pltpu.VMEM((classes, total), BF),
            pltpu.VMEM((classes, rows), BF),
            pltpu.SemaphoreType.DMA((total // 512,)),
        ],
    )
    return pl.pallas_call(
        functools.partial(features_kernel, masks, last, *totals),
        grid_spec=grid_spec,
        out_shape=shapes,
        input_output_aliases={7: 2} if last else {},
        compiler_params=pltpu.CompilerParams(vmem_limit_bytes=44 * 2**20),
        cost_estimate=pl.CostEstimate(
            flops=2 * (total + rows) * tiles * tile * (k + 2 * classes),
            bytes_accessed=2 * (total * k + k * tiles * tile),
            transcendentals=0,
        ),
    )(me, real_labels.reshape(1, -1), syn_labels.reshape(1, -1), *images, records, freq, *extra)


def stage_two_send_kernel(ka, ga, kb, gb, after, sa, sb, token):
    token[...] = jnp.zeros_like(token)
    sa[...] = (ka[...] + ga[0].astype(F32)).astype(BF)
    sb[...] = (kb[...] + gb[0].astype(F32)).astype(BF)


def stage_two_send(keep_a, got_a, keep_b, got_b, after):
    return pl.pallas_call(
        stage_two_send_kernel,
        in_specs=[pl.BlockSpec()] * 4 + [pl.BlockSpec(memory_space=pl.ANY)],
        out_shape=[jax.ShapeDtypeStruct(keep_a.shape, BF)] * 2 + [jax.ShapeDtypeStruct((8, 128), F32)],
        compiler_params=pltpu.CompilerParams(vmem_limit_bytes=10 * 2**20),
        cost_estimate=pl.CostEstimate(flops=0, bytes_accessed=3 * 2**20, transcendentals=0),
    )(keep_a, got_a, keep_b, got_b, after)


def stage_three_kernel(me_ref, na, fa, ga, nb, fb, gb, a, b, c, send, keep, token):
    token[...] = jnp.zeros_like(token)
    high = me_ref[3]
    half = na.shape[1]
    for flip, out in ((1, send), (0, keep)):
        at = high ^ flip
        out[:half] = (na[at] + fa[1, at].astype(F32) + ga[at].astype(F32)).astype(out.dtype)
        out[half:] = (nb[at] + fb[1, at].astype(F32) + gb[at].astype(F32)).astype(out.dtype)


def stage_three(me, keep_a, first_a, got_a, keep_b, first_b, got_b, after):
    _, half, width = keep_a.shape
    args = (keep_a, first_a, got_a, keep_b, first_b, got_b)
    whole = lambda shape: block(shape, lambda h, me: (0,) * len(shape))
    spec = pltpu.PrefetchScalarGridSpec(
        num_scalar_prefetch=1,
        grid=(1,),
        in_specs=[whole(x.shape) for x in args] + [pl.BlockSpec(memory_space=pl.ANY)] * 3,
        out_specs=[whole((2 * half, width))] * 2 + [whole((8, 128))],
    )
    return pl.pallas_call(
        stage_three_kernel,
        grid_spec=spec,
        out_shape=[jax.ShapeDtypeStruct((2 * half, width), t) for t in (BF, F32)]
        + [jax.ShapeDtypeStruct((8, 128), F32)],
        compiler_params=pltpu.CompilerParams(vmem_limit_bytes=12 * 2**20),
        cost_estimate=pl.CostEstimate(flops=0, bytes_accessed=3 * 2**20, transcendentals=0),
    )(me, *args, *after)


def gap_kernel(real_total, order, me_ref, keep_ref, got_ref, noise_ref, labels_ref, after, out_ref):
    classes = keep_ref.shape[0]
    rows = labels_ref.shape[1]
    gap = keep_ref[...] + got_ref[...].astype(F32) - noise_ref[...] * (1.0 / real_total)
    gap = (16.0 * gap).astype(BF)
    ids = lax.broadcasted_iota(jnp.int32, (classes, rows), 0)
    for i, mask in enumerate(order):
        table = jnp.where(ids == labels_ref[i : i + 1, :], 1.0, 0.0).astype(BF)
        out = lax.dot_general(table, gap, (((0,), (0,)), ((), ())), preferred_element_type=F32)
        out_ref[me_ref[4] ^ mask] = out.astype(BF)


def gap_rows(me, keep, got, noise, labels, real_total, order, after):
    classes, width = keep.shape
    groups, rows = labels.shape
    whole = lambda shape: block(shape, lambda h, me: (0,) * len(shape))
    spec = pltpu.PrefetchScalarGridSpec(
        num_scalar_prefetch=1,
        grid=(1,),
        in_specs=[whole(x.shape) for x in (keep, got, noise, labels)]
        + [pl.BlockSpec(memory_space=pl.ANY)],
        out_specs=whole((groups, rows, width)),
    )
    return pl.pallas_call(
        functools.partial(gap_kernel, real_total, order),
        grid_spec=spec,
        out_shape=jax.ShapeDtypeStruct((groups, rows, width), BF),
        compiler_params=pltpu.CompilerParams(vmem_limit_bytes=14 * 2**20),
        cost_estimate=pl.CostEstimate(
            flops=2 * groups * rows * classes * width, bytes_accessed=3 * 2**20, transcendentals=0
        ),
    )(me, keep, got, noise, labels, after)


NT = (((1,), (1,)), ((), ()))


def image_kernel(me_ref, wave_ref, rows_ref, freq_ref, a, b, c, send_ref, keep_ref, pre_ref):
    step = pl.program_id(0)
    tile = wave_ref.shape[3]
    part = tile // 2

    @pl.when(step == 0)
    def _():
        for place in range(4):
            for h in range(2):
                grad = rows_ref[4 * h + 2 * (place % 2) + place // 2].astype(F32)
                lanes = slice(h * part, (h + 1) * part)
                pre = wave_ref[place, 0, :, lanes] * grad[:, part:]
                pre = pre - wave_ref[place, 1, :, lanes] * grad[:, :part]
                at = place * tile + h * part
                pre_ref[:, at : at + part] = pre.astype(BF)

    out = lax.dot_general(freq_ref[...], pre_ref[...], NT, preferred_element_type=F32)

    @pl.when(step < 2)
    def _():
        send_ref[0] = out.astype(BF)

    @pl.when(step >= 2)
    def _():
        keep_ref[0] = out


def image_grads(me, waves, feat_rows, freq, cols, after):
    k, n = freq.shape
    owners, rows, width = feat_rows.shape
    whole = lambda shape: block(shape, lambda s, me: (0,) * len(shape))

    def source(s, me):
        return 2 * (s % 2) + ((me[0] % 2) ^ (1 - s // 2)), 0

    spec = pltpu.PrefetchScalarGridSpec(
        num_scalar_prefetch=1,
        grid=(4,),
        in_specs=[whole(waves.shape), whole(feat_rows.shape), block((cols, n), source)]
        + [pl.BlockSpec(memory_space=pl.ANY)] * 3,
        out_specs=[
            block((1, cols, rows), lambda s, me: (jnp.minimum(s, 1), 0, 0)),
            block((1, cols, rows), lambda s, me: (jnp.maximum(s - 2, 0), 0, 0)),
        ],
        scratch_shapes=[pltpu.VMEM((rows, n), BF)],
    )
    return pl.pallas_call(
        image_kernel,
        grid_spec=spec,
        out_shape=[jax.ShapeDtypeStruct((2, cols, rows), BF), pltpu.HBM((2, cols, rows), F32)],
        compiler_params=pltpu.CompilerParams(vmem_limit_bytes=52 * 2**20),
        cost_estimate=pl.CostEstimate(flops=2 * k * n * rows, bytes_accessed=2 * k * n, transcendentals=0),
    )(me, waves, feat_rows, freq, *after)


def split_y_kernel(me_ref, keep_s, keep_k, got_s, got_k, send, keep):
    send[...] = (keep_s[0] + got_s[0].astype(F32)).astype(BF)
    keep[...] = keep_k[0] + got_k[0].astype(F32)


def split_y(me, keep, got):
    _, cols, rows = keep.shape
    at = lambda flip: block((1, cols, rows), lambda h, me: ((me[0] // 2) ^ flip, 0, 0))
    out = block((cols, rows), lambda h, me: (0, 0))
    spec = pltpu.PrefetchScalarGridSpec(
        num_scalar_prefetch=1, grid=(1,), in_specs=[at(1), at(0)] * 2, out_specs=[out, out]
    )
    return pl.pallas_call(
        split_y_kernel,
        grid_spec=spec,
        out_shape=[jax.ShapeDtypeStruct((cols, rows), t) for t in (BF, F32)],
        compiler_params=pltpu.CompilerParams(vmem_limit_bytes=8 * 2**20),
        cost_estimate=pl.CostEstimate(flops=0, bytes_accessed=2**20, transcendentals=0),
    )(me, keep, keep, got, got)


def out_kernel(keep, got, image, out):
    grad = (keep[...] + got[...].astype(F32)).T
    grad = grad * (1.0 - jnp.square(image[...].astype(F32)))
    out[...] = grad.astype(BF)


def out_grads(keep, got, image):
    return pl.pallas_call(
        out_kernel,
        out_shape=jax.ShapeDtypeStruct(image.shape, BF),
        compiler_params=pltpu.CompilerParams(vmem_limit_bytes=8 * 2**20),
        cost_estimate=pl.CostEstimate(flops=0, bytes_accessed=2**20, transcendentals=0),
    )(keep, got, image)


def hidden_kernel(me_ref, w_ref, *refs):
    grads = refs[:4]
    send, keep = refs[5:]
    core = me_ref[0] % 2
    out = [lax.dot_general(w_ref[...], g[...], NT, preferred_element_type=F32) for g in grads]
    for i in range(2):
        keep[i] = jnp.where(core == 0, out[2 * i], out[2 * i + 1])
        send[i] = jnp.where(core == 0, out[2 * i + 1], out[2 * i]).astype(BF)


def hidden_grads(me, w_out, grads, mine, after):
    rows, cols = grads[0].shape
    whole = lambda shape: block(shape, lambda r, me: (0,) * len(shape))
    spec = pltpu.PrefetchScalarGridSpec(
        num_scalar_prefetch=1,
        grid=(1,),
        in_specs=[block((mine, cols), lambda r, me: (me[4], 0))] + [whole((rows, cols))] * 4
        + [pl.BlockSpec(memory_space=pl.ANY)],
        out_specs=[whole((2, mine, rows))] * 2,
    )
    return pl.pallas_call(
        hidden_kernel,
        grid_spec=spec,
        out_shape=[jax.ShapeDtypeStruct((2, mine, rows), t) for t in (BF, F32)],
        compiler_params=pltpu.CompilerParams(vmem_limit_bytes=8 * 2**20),
        cost_estimate=pl.CostEstimate(
            flops=8 * mine * cols * rows, bytes_accessed=2 * 5 * mine * cols, transcendentals=0
        ),
    )(me, w_out, *grads, after)


def add_kernel(a, b, out):
    out[...] = (a[...].astype(F32) + b[...].astype(F32)).astype(out.dtype)


def add(a, b, kind):
    return pl.pallas_call(
        add_kernel,
        out_shape=jax.ShapeDtypeStruct(a.shape, kind),
        compiler_params=pltpu.CompilerParams(vmem_limit_bytes=8 * 2**20),
        cost_estimate=pl.CostEstimate(flops=0, bytes_accessed=2**20, transcendentals=0),
    )(a, b)


def weight_kernel(me_ref, hidden_ref, *refs):
    out_ref, token = refs[-2:]
    token[...] = jnp.zeros_like(token)
    acc = None
    for mask, grad in enumerate(refs[:-2]):
        rows = grad.shape[0]
        at = slice(mask * rows, (mask + 1) * rows)
        d = jnp.dot(hidden_ref[:, at], grad[...], preferred_element_type=F32)
        acc = d if acc is None else acc + d
    out_ref[...] = acc


def weight_grads(me, hidden, grads):
    rows, cols = grads[0].shape
    mine, total = hidden.shape
    spec = pltpu.PrefetchScalarGridSpec(
        num_scalar_prefetch=1,
        grid=(1,),
        in_specs=[block((mine, total), lambda h, me: (0, 0))]
        + [block((rows, cols), lambda h, me: (0, 0)) for _ in grads],
        out_specs=[block((mine, cols), lambda h, me: (0, 0)), block((8, 128), lambda h, me: (0, 0))],
    )
    return pl.pallas_call(
        weight_kernel,
        grid_spec=spec,
        out_shape=[pltpu.HBM((mine, cols), F32), jax.ShapeDtypeStruct((8, 128), F32)],
        compiler_params=pltpu.CompilerParams(vmem_limit_bytes=12 * 2**20),
        cost_estimate=pl.CostEstimate(
            flops=2 * mine * total * cols, bytes_accessed=4 * 2**20, transcendentals=0
        ),
    )(me, hidden, *grads)


def last_kernel(me_ref, gate_ref, lhs_ref, p0, q0, p1, q1, after, out_ref):
    rows = p0.shape[2]
    acc = None
    for h, (p, q) in enumerate(((p0, q0), (p1, q1))):
        for i in range(2):
            place = 4 * (me_ref[0] % 2) + 2 * i + h
            at = pl.ds(pl.multiple_of(place * rows, 128), rows)
            grad = p[i].astype(F32) + q[i].astype(F32)
            grad = jnp.where(gate_ref[:, at].astype(F32) > 0, grad, 0.0).astype(BF)
            d = lax.dot_general(lhs_ref[:, at], grad, NT, preferred_element_type=F32)
            acc = d if acc is None else acc + d
    out_ref[...] = acc


def last_grads(me, gate, lhs, parts, after):
    count, total = lhs.shape
    mine = gate.shape[0]
    args = (gate, lhs, *parts)
    whole = lambda shape: block(shape, lambda h, me: (0,) * len(shape))
    spec = pltpu.PrefetchScalarGridSpec(
        num_scalar_prefetch=1,
        grid=(1,),
        in_specs=[whole(x.shape) for x in args] + [pl.BlockSpec(memory_space=pl.ANY)],
        out_specs=whole((count, mine)),
    )
    return pl.pallas_call(
        last_kernel,
        grid_spec=spec,
        out_shape=jax.ShapeDtypeStruct((count, mine), F32),
        compiler_params=pltpu.CompilerParams(vmem_limit_bytes=12 * 2**20),
        cost_estimate=pl.CostEstimate(
            flops=total * count * mine, bytes_accessed=2 * 2**20, transcendentals=0
        ),
    )(me, *args, after)


def outputs_kernel(own, other, latent, embed):
    dz = latent.shape[0]
    latent[...] = own[:dz] + other[:dz]
    embed[...] = own[dz:] + other[dz:]


def outputs(own, other, dz):
    count, mine = own.shape
    return pl.pallas_call(
        outputs_kernel,
        out_shape=[jax.ShapeDtypeStruct((c, mine), F32) for c in (dz, count - dz)],
        compiler_params=pltpu.CompilerParams(vmem_limit_bytes=8 * 2**20),
        cost_estimate=pl.CostEstimate(flops=0, bytes_accessed=2**20, transcendentals=0),
    )(own, other)


def tie(first, later):
    return lax.optimization_barrier((first, later))


def eight_by_four(
    records, real_labels, frequencies, class_noise, latents, syn_labels, w_latent, class_embed, w_out
):
    classes, hid = class_embed.shape
    groups = lax.axis_size("rec")
    rec = lax.axis_index("rec")
    feat = lax.axis_index("feat")
    rows, dz = latents.shape
    cols = w_out.shape[1]
    real_total = records.shape[0] * groups
    syn_total = rows * groups
    x, z_low, z_high = rec % 2, (rec // 2) % 2, rec // 4
    place = 2 * x + z_low
    me = jnp.stack([feat, x, z_low, z_high, rec, place]).astype(jnp.int32)

    table = one_hot(syn_labels, classes, BF)
    preact = jnp.dot(latents, w_latent, preferred_element_type=F32) + jnp.dot(
        table, class_embed, preferred_element_type=F32
    )
    hidden = jnp.maximum(preact, 0.0).astype(BF)
    own = jnp.tanh(jnp.dot(hidden, w_out, preferred_element_type=F32)).astype(BF)
    far = swap(own, "feat", 2)

    order = (0, 4, 2, 6, 1, 5, 3, 7)
    label_row = jnp.zeros((16, dz), BF).at[0, :].set(syn_labels.astype(BF))
    packed = jnp.concatenate([latents, label_row], axis=0)[None]
    far, pair = tie(far, swap(packed, "rec", 4))
    images = [own, far, swap(own, "feat", 1), swap(far, "feat", 1)]
    packed, real_labels = tie(jnp.concatenate([packed, pair], axis=0), real_labels)
    pair = swap(packed, "rec", 2)

    masks = (0, 2, 1, 3)
    totals = (real_total, syn_total)
    send_a, keep_a, send_b, keep_b, both, waves, token = feature_sums(
        False, me, real_labels, syn_labels, masks, images, records, frequencies, classes, totals, me
    )
    first_a = swap(send_a, "rec", 1)
    first_b = swap(send_b, "rec", 2)
    pair, token = tie(pair, token)
    last_a, last_b, waves, token = feature_sums(
        True, me, real_labels, syn_labels, masks, both, records, frequencies, classes, totals, token, waves
    )

    send_a, send_b, token = stage_two_send(keep_a, first_a, keep_b, first_b, token)
    got_a = swap(send_a, "rec", 2)
    got_b = swap(send_b, "rec", 1)
    part = frequencies.shape[1] // groups
    noise = lax.dynamic_slice_in_dim(class_noise, (2 * place + z_high) * part, part, 2)
    noise = noise.reshape(classes, 2 * part)
    send, keep, token = stage_three(me, last_a, first_a, got_a, last_b, first_b, got_b, (noise, token, token))
    got = swap(send, "rec", 4)
    pair, token = tie(pair, token)
    quad = jnp.concatenate([packed, pair], axis=0)
    eight = jnp.concatenate([quad, swap(quad, "rec", 1)], axis=0)
    all_latents = eight[:, :rows].reshape(syn_total, dz)
    all_labels = eight[:, rows].reshape(syn_total).astype(jnp.int32)
    all_table = one_hot(all_labels, classes, BF)
    mine = hid // groups
    lhs = jnp.concatenate([all_latents, all_table], axis=1).T
    w = jnp.concatenate(
        [
            lax.dynamic_slice_in_dim(w_latent, rec * mine, mine, 1),
            lax.dynamic_slice_in_dim(class_embed, rec * mine, mine, 1),
        ],
        axis=0,
    )
    all_preact = lax.dot_general(w, lhs, (((0,), (0,)), ((), ())), preferred_element_type=F32)
    all_hidden = jnp.maximum(all_preact, 0.0).astype(BF)
    gate = (all_preact > 0).astype(BF)

    feat_grad = gap_rows(me, keep, got, noise, all_labels.reshape(groups, rows), real_total, order, token)
    feat_grad = lax.all_to_all(feat_grad, "rec", 0, 0, tiled=True)

    send, keep = image_grads(
        me, waves, feat_grad, frequencies, cols, (gate, all_hidden, lhs)
    )
    send, keep = split_y(me, keep, swap(send, "feat", 1))
    out_grad = out_grads(keep, swap(send, "feat", 2), own)

    by = {0: out_grad}
    by[4] = swap(out_grad, "rec", 4)
    by[2] = swap(out_grad, "rec", 2)
    by[1] = swap(out_grad, "rec", 1)
    by[2], by[1] = tie(by[2], by[1])
    by[3] = swap(by[2], "rec", 1)
    by[6] = swap(by[4], "rec", 2)
    by[5] = swap(by[4], "rec", 1)

    def reduced(send, keep):
        part = add(keep, swap(send, "feat", 1), BF)
        return [part, swap(part, "feat", 2)]

    by[7] = swap(by[6], "rec", 1)
    send, keep = hidden_grads(me, w_out, [by[i] for i in range(4)], mine, by[5])
    parts = reduced(send, keep)
    parts += reduced(*hidden_grads(me, w_out, [by[4 + i] for i in range(4)], mine, parts[0]))
    grad_w_out, token = weight_grads(me, all_hidden, [by[mask] for mask in order])
    grads = last_grads(me, gate, lhs, parts, token)
    grad_w_latent, grad_embed = outputs(grads, swap(grads, "feat", 1), dz)
    return grad_w_out, grad_w_latent, grad_embed


def solution(mesh):
    shape = (mesh.shape["rec"], mesh.shape["feat"])
    in_specs = (
        P("rec", None),
        P("rec"),
        P(None, "feat"),
        P(None, None, "feat"),
        P("rec", None),
        P("rec"),
        P(),
        P(),
        P(None, "feat"),
    )
    out_specs = (P("rec", "feat"), P(None, "rec"), P(None, "rec"))
    return jax.shard_map(
        eight_by_four if shape == (8, 4) else general, mesh=mesh, in_specs=in_specs, out_specs=out_specs, check_vma=False
    )
```

```python
import functools

import jax
import jax.numpy as jnp
from jax import lax
from jax.experimental import pallas as pl
from jax.experimental.pallas import tpu as pltpu
from jax.sharding import PartitionSpec as P

BF = jnp.bfloat16
F32 = jnp.float32

TURN = 0.15915494309189535
SIN = (4.44286783702217, -7.307441307726672, 3.59477116396636, -0.7843353598850176)
COS = (1.4142134962552275, -6.978850948563815, 5.739460376907241, -1.883557905986894, 0.3106880275267554)


def cos_sin(x):
    turns = x * TURN
    u = turns - jnp.round(turns)
    sq = u * u
    p = SIN[-1]
    for c in SIN[-2::-1]:
        p = p * sq + c
    q = COS[-1]
    for c in COS[-2::-1]:
        q = q * sq + c
    s = u * p
    return 1.0 - s * s, s * q


def one_hot(labels, count, dtype):
    return (labels[:, None] == jnp.arange(count, dtype=jnp.int32)[None, :]).astype(dtype)


def real_kernel(rows, labels_ref, records_ref, freq_ref, out_ref, table_ref):
    total = records_ref.shape[0]
    classes = table_ref.shape[0]
    owners, _, width = out_ref.shape
    part = width // 2

    @pl.when(pl.program_id(0) == 0)
    def _():
        ids = lax.broadcasted_iota(jnp.int32, (classes, total), 0)
        table_ref[...] = jnp.where(ids == labels_ref[...], 1.0, 0.0).astype(BF)

    freq = freq_ref[...]
    block = freq.shape[1]

    def sums(i, pre):
        co, si = cos_sin(pre)
        phi = jnp.concatenate([co.astype(BF), si.astype(BF)], axis=1)
        return jnp.dot(table_ref[:, i * rows : (i + 1) * rows], phi, preferred_element_type=F32)

    acc = None
    before = None
    steps = total // rows
    for i in range(steps + 1):
        pre = None
        if i < steps:
            pre = jnp.dot(records_ref[i * rows : (i + 1) * rows, :], freq, preferred_element_type=F32)
        if i > 0:
            d = sums(i - 1, before)
            acc = d if acc is None else acc + d
        before = pre
    for o in range(owners):
        out_ref[o, :, :part] = acc[:, o * part : (o + 1) * part]
        out_ref[o, :, part:] = acc[:, block + o * part : block + (o + 1) * part]


def real_sums(labels, records, freq, classes, owners):
    m, k = records.shape
    n = freq.shape[1]
    block = min(512, n)
    rows = 512
    part = n // owners
    per = block // part
    return pl.pallas_call(
        functools.partial(real_kernel, rows),
        grid=(n // block,),
        in_specs=[
            pl.BlockSpec((1, m), lambda j: (0, 0)),
            pl.BlockSpec((m, k), lambda j: (0, 0)),
            pl.BlockSpec((k, block), lambda j: (0, j)),
        ],
        out_specs=pl.BlockSpec((per, classes, 2 * part), lambda j: (j, 0, 0)),
        out_shape=jax.ShapeDtypeStruct((owners, classes, 2 * part), F32),
        scratch_shapes=[pltpu.VMEM((classes, m), BF)],
        compiler_params=pltpu.CompilerParams(vmem_limit_bytes=56 * 2**20),
        cost_estimate=pl.CostEstimate(
            flops=2 * m * n * (k + 2 * classes), bytes_accessed=2 * (m * k + k * n), transcendentals=0
        ),
    )(labels.reshape(1, m), records, freq)


def bits_of(n):
    return [1 << b for b in range(n.bit_length() - 1)]


def swap(x, axis, bit):
    n = lax.axis_size(axis)
    return lax.ppermute(x, axis, [(i, i ^ bit) for i in range(n)])


def pick(x, index, dim):
    return lax.dynamic_index_in_dim(x, index, dim, keepdims=False)


def halving(x, axis, order, count):
    me = lax.axis_index(axis)
    nbits = len(order)
    x = x.reshape((2,) * nbits + x.shape[1:])
    left = sorted(order, reverse=True)
    for bit in order:
        dim = left.index(bit)
        left.remove(bit)
        mine = (me // bit) % 2
        got = swap(pick(x, 1 - mine, dim).astype(BF), axis, bit)
        x = pick(x, mine, dim).astype(F32) + got.astype(F32)
    return x


def general(
    records, real_labels, frequencies, class_noise, latents, syn_labels, w_latent, class_embed, w_out
):
    classes = class_embed.shape[0]
    hid = class_embed.shape[1]
    groups = lax.axis_size("rec")
    feats = lax.axis_size("feat")
    rec = lax.axis_index("rec")
    nf = frequencies.shape[1]
    part = nf // groups
    rows, dz = latents.shape
    cols = w_out.shape[1]
    real_total = records.shape[0] * groups
    syn_total = rows * groups

    label_row = jnp.zeros((16, dz), BF).at[0, :].set(syn_labels.astype(BF))
    packed = jnp.concatenate([latents, label_row], axis=0)
    packed = lax.all_to_all(
        jnp.broadcast_to(packed[None], (groups,) + packed.shape), "rec", 0, 0, tiled=True
    )
    all_latents = packed[:, :rows].reshape(syn_total, dz)
    all_labels = packed[:, rows].reshape(syn_total).astype(jnp.int32)
    all_table = one_hot(all_labels, classes, BF)

    table = one_hot(syn_labels, classes, BF)
    preact = jnp.dot(latents, w_latent, preferred_element_type=F32) + jnp.dot(
        table, class_embed, preferred_element_type=F32
    )
    hidden = jnp.maximum(preact, 0.0).astype(BF)
    own_images = jnp.tanh(jnp.dot(hidden, w_out, preferred_element_type=F32)).astype(BF)
    images = lax.all_gather(own_images, "feat", axis=0)
    images = images.transpose(1, 0, 2).reshape(rows, feats * cols)
    syn_pre = jnp.dot(images, frequencies, preferred_element_type=F32)
    syn_cos, syn_sin = cos_sin(syn_pre)
    syn_phi = jnp.concatenate(
        [syn_cos.reshape(rows, groups, part), syn_sin.reshape(rows, groups, part)], axis=2
    ).astype(BF)
    syn_sum = lax.dot_general(
        table, syn_phi.reshape(rows, 2 * nf), (((0,), (0,)), ((), ())), preferred_element_type=F32
    )
    syn_sum = syn_sum.reshape(classes, groups, 2 * part).transpose(1, 0, 2)

    real_sum = real_sums(real_labels, records, frequencies, classes, groups)
    gap = syn_sum * (1.0 / syn_total) - real_sum * (1.0 / real_total)
    half = classes // 2
    order = bits_of(groups)
    other = [order[1], order[0]] + order[2:]
    gap = jnp.concatenate(
        [halving(gap[:, :half], "rec", order, groups), halving(gap[:, half:], "rec", other, groups)], axis=0
    )
    noise = lax.dynamic_slice_in_dim(class_noise, rec * part, part, 2).reshape(classes, 2 * part)
    gap = (16.0 * (gap - noise * (1.0 / real_total))).astype(BF)

    feat_grad = jnp.dot(all_table, gap, preferred_element_type=F32).astype(BF)
    feat_grad = lax.all_to_all(feat_grad.reshape(groups, rows, 2 * part), "rec", 0, 0, tiled=True)
    feat_grad = feat_grad.transpose(1, 0, 2).astype(F32)
    pre_grad = (
        -syn_sin.reshape(rows, groups, part) * feat_grad[:, :, :part]
        + syn_cos.reshape(rows, groups, part) * feat_grad[:, :, part:]
    )
    pre_grad = pre_grad.astype(BF).reshape(rows, nf)
    image_grad = lax.dot_general(
        frequencies, pre_grad, (((1,), (1,)), ((), ())), preferred_element_type=F32
    )
    image_grad = halving(image_grad.reshape(feats, cols, rows), "feat", bits_of(feats), feats)
    image_grad = image_grad.T
    out_grad = (image_grad * (1.0 - jnp.square(own_images.astype(F32)))).astype(BF)

    out_grad = lax.all_to_all(
        jnp.broadcast_to(out_grad[None], (groups, rows, cols)), "rec", 0, 0, tiled=True
    ).reshape(syn_total, cols)

    mine = hid // groups
    start = rec * mine
    all_preact = jnp.dot(
        all_latents, lax.dynamic_slice_in_dim(w_latent, start, mine, 1), preferred_element_type=F32
    ) + jnp.dot(
        all_table, lax.dynamic_slice_in_dim(class_embed, start, mine, 1), preferred_element_type=F32
    )
    all_hidden = jnp.maximum(all_preact, 0.0).astype(BF)
    grad_w_out = lax.dot_general(
        all_hidden, out_grad, (((0,), (0,)), ((), ())), preferred_element_type=F32
    )
    hidden_grad = lax.dot_general(
        out_grad,
        lax.dynamic_slice_in_dim(w_out, start, mine, 0),
        (((1,), (1,)), ((), ())),
        preferred_element_type=F32,
    )
    core = lax.axis_index("feat") % 2
    half = syn_total // 2
    hidden_grad = hidden_grad.reshape(2, half, mine)
    got = swap(pick(hidden_grad, 1 - core, 0).astype(BF), "feat", 1)
    hidden_grad = pick(hidden_grad, core, 0) + got.astype(F32)
    for bit in bits_of(feats)[1:]:
        send = hidden_grad.astype(BF)
        hidden_grad = send.astype(F32) + swap(send, "feat", bit).astype(F32)
    my_preact = lax.dynamic_slice_in_dim(all_preact, core * half, half, 0)
    pre_hidden = jnp.where(my_preact > 0, hidden_grad, 0.0).astype(BF)
    lhs = jnp.concatenate([all_latents, all_table], axis=1)
    lhs = lax.dynamic_slice_in_dim(lhs, core * half, half, 0)
    grads = lax.dot_general(lhs, pre_hidden, (((0,), (0,)), ((), ())), preferred_element_type=F32)
    grads = grads + swap(grads, "feat", 1)
    return grad_w_out, grads[:dz], grads[dz:]


def block(shape, index):
    return pl.BlockSpec(shape, index)


def sums(table, pre):
    co, si = cos_sin(pre)
    phi = jnp.concatenate([co.astype(BF), si.astype(BF)], axis=1)
    return jnp.dot(table, phi, preferred_element_type=F32)


def features_kernel(
    masks, last, real_total, syn_total, me_ref, real_labels_ref, syn_labels_ref, *refs
):
    count = 1 if last else len(masks)
    images = [refs[0].at[i] for i in range(len(masks))] if last else refs[:count]
    records_hbm, freq_ref = refs[count : count + 2]
    outs = refs[count + (4 if last else 3) : -4]
    wave, token = outs[-2:]
    records, real_table, syn_table, sem = refs[-4:]
    classes, total = real_table.shape
    size = 512
    steps = total // size
    step = pl.program_id(0)
    cols = images[0].shape[1]
    half = classes // 2
    token[...] = jnp.zeros_like(token)

    def copy(i):
        at = pl.ds(i * size, size)
        return pltpu.make_async_copy(records_hbm.at[at, :], records.at[at, :], sem.at[i])

    def work(wait):
        if wait:
            for i in range(steps):
                copy(i).start()
            ids = lax.broadcasted_iota(jnp.int32, (classes, total), 0)
            real_table[...] = jnp.where(ids == real_labels_ref[...], 1.0, 0.0).astype(BF)
            ids = lax.broadcasted_iota(jnp.int32, syn_table.shape, 0)
            syn_table[...] = jnp.where(ids == syn_labels_ref[...], 1.0, 0.0).astype(BF)
        syn_pre = None
        for mask, image in zip(masks, images):
            at = pl.multiple_of((me_ref[0] ^ mask) * cols, 128)
            d = jnp.dot(image[...], freq_ref[pl.ds(at, cols), :], preferred_element_type=F32)
            syn_pre = d if syn_pre is None else syn_pre + d
        freq = freq_ref[...]
        acc = None
        before = None
        for i in range(steps + 1):
            if i < steps:
                if wait:
                    copy(i).wait()
                pre = jnp.dot(records[i * size : (i + 1) * size, :], freq, preferred_element_type=F32)
            if i == 0:
                co, si = cos_sin(syn_pre)
                wave[0, 0] = co
                wave[0, 1] = si
                phi = jnp.concatenate([co.astype(BF), si.astype(BF)], axis=1)
                syn = jnp.dot(syn_table[...], phi, preferred_element_type=F32)
            else:
                d = sums(real_table[:, (i - 1) * size : i * size], before)
                acc = d if acc is None else acc + d
            before = pre
        gap = syn * (1.0 / syn_total) - acc * (1.0 / real_total)
        width = gap.shape[1] // 4
        return [
            jnp.concatenate(
                [gap[:, h * width : (h + 1) * width], gap[:, (h + 2) * width : (h + 3) * width]], axis=1
            )
            for h in range(2)
        ]

    if last:
        parts = work(True)
        for h in range(2):
            outs[0][h] = parts[h][:half]
            outs[1][h] = parts[h][half:]
        return
    send_a, keep_a, send_b, keep_b, both = outs[:5]

    @pl.when(step == 0)
    def _():
        for i in range(count):
            both[i] = images[i][...]
        parts = work(True)
        for h in range(2):
            send_a[0, h] = parts[h][:half].astype(BF)
            send_b[0, h] = parts[h][half:].astype(BF)

    @pl.when(step > 0)
    def _():
        parts = work(False)

        @pl.when(step == 1)
        def _():
            for h in range(2):
                send_a[0, h] = parts[h][:half].astype(BF)
                keep_b[h] = parts[h][half:]

        @pl.when(step == 2)
        def _():
            for h in range(2):
                keep_a[h] = parts[h][:half]
                send_b[0, h] = parts[h][half:].astype(BF)


def feature_sums(
    last, me, real_labels, syn_labels, masks, images, records, freq, classes, totals, after, waves=None
):
    total, k = records.shape
    n = freq.shape[1]
    rows, cols = images.shape[1:] if last else images[0].shape
    half = classes // 2
    tile = n // 4
    tiles = 1 if last else 3
    whole = lambda shape: block(shape, lambda j, me: (0,) * len(shape))
    kept = jax.ShapeDtypeStruct((2, half, tile), F32)
    sent = jax.ShapeDtypeStruct((2, 2, half, tile), BF)
    both = (len(masks), rows, cols)
    place = lambda j, me: me[5] ^ (0 if last else 3 - j)
    anywhere = pl.BlockSpec(memory_space=pl.ANY)
    shapes = [pltpu.HBM((4, 2, rows, tile), F32), jax.ShapeDtypeStruct((8, 128), F32)]
    specs = [block((1, 2, rows, tile), lambda j, me: (place(j, me), 0, 0, 0)), whole((8, 128))]
    if last:
        shapes = [kept, kept] + shapes
        specs = [whole(kept.shape), whole(kept.shape)] + specs
        images = (images,)
        extra = (after, waves)
    else:
        shapes = [sent, kept, sent, kept, pltpu.HBM(both, BF)] + shapes
        specs = [
            block((1, 2, half, tile), lambda j, me: (jnp.minimum(j, 1), 0, 0, 0)),
            whole(kept.shape),
            block((1, 2, half, tile), lambda j, me: (j // 2, 0, 0, 0)),
            whole(kept.shape),
            whole(both),
        ] + specs
        extra = (after,)
    grid_spec = pltpu.PrefetchScalarGridSpec(
        num_scalar_prefetch=1,
        grid=(tiles,),
        in_specs=[whole((1, total)), whole((1, rows))]
        + [whole(image.shape) for image in images]
        + [anywhere, block((k, tile), lambda j, me: (0, place(j, me)))]
        + [anywhere] * len(extra),
        out_specs=specs,
        scratch_shapes=[
            pltpu.VMEM((total, k), BF),
            pltpu.VMEM((classes, total), BF),
            pltpu.VMEM((classes, rows), BF),
            pltpu.SemaphoreType.DMA((total // 512,)),
        ],
    )
    return pl.pallas_call(
        functools.partial(features_kernel, masks, last, *totals),
        grid_spec=grid_spec,
        out_shape=shapes,
        input_output_aliases={7: 2} if last else {},
        compiler_params=pltpu.CompilerParams(vmem_limit_bytes=44 * 2**20),
        cost_estimate=pl.CostEstimate(
            flops=2 * (total + rows) * tiles * tile * (k + 2 * classes),
            bytes_accessed=2 * (total * k + k * tiles * tile),
            transcendentals=0,
        ),
    )(me, real_labels.reshape(1, -1), syn_labels.reshape(1, -1), *images, records, freq, *extra)


def stage_two_send_kernel(ka, ga, kb, gb, after, sa, sb, token):
    token[...] = jnp.zeros_like(token)
    sa[...] = (ka[...] + ga[0].astype(F32)).astype(BF)
    sb[...] = (kb[...] + gb[0].astype(F32)).astype(BF)


def stage_two_send(keep_a, got_a, keep_b, got_b, after):
    return pl.pallas_call(
        stage_two_send_kernel,
        in_specs=[pl.BlockSpec()] * 4 + [pl.BlockSpec(memory_space=pl.ANY)],
        out_shape=[jax.ShapeDtypeStruct(keep_a.shape, BF)] * 2 + [jax.ShapeDtypeStruct((8, 128), F32)],
        compiler_params=pltpu.CompilerParams(vmem_limit_bytes=10 * 2**20),
        cost_estimate=pl.CostEstimate(flops=0, bytes_accessed=3 * 2**20, transcendentals=0),
    )(keep_a, got_a, keep_b, got_b, after)


def stage_three_kernel(me_ref, na, fa, ga, nb, fb, gb, a, b, c, send, keep, token):
    token[...] = jnp.zeros_like(token)
    high = me_ref[3]
    half = na.shape[1]
    for flip, out in ((1, send), (0, keep)):
        at = high ^ flip
        out[:half] = (na[at] + fa[1, at].astype(F32) + ga[at].astype(F32)).astype(out.dtype)
        out[half:] = (nb[at] + fb[1, at].astype(F32) + gb[at].astype(F32)).astype(out.dtype)


def stage_three(me, keep_a, first_a, got_a, keep_b, first_b, got_b, after):
    _, half, width = keep_a.shape
    args = (keep_a, first_a, got_a, keep_b, first_b, got_b)
    whole = lambda shape: block(shape, lambda h, me: (0,) * len(shape))
    spec = pltpu.PrefetchScalarGridSpec(
        num_scalar_prefetch=1,
        grid=(1,),
        in_specs=[whole(x.shape) for x in args] + [pl.BlockSpec(memory_space=pl.ANY)] * 3,
        out_specs=[whole((2 * half, width))] * 2 + [whole((8, 128))],
    )
    return pl.pallas_call(
        stage_three_kernel,
        grid_spec=spec,
        out_shape=[jax.ShapeDtypeStruct((2 * half, width), t) for t in (BF, F32)]
        + [jax.ShapeDtypeStruct((8, 128), F32)],
        compiler_params=pltpu.CompilerParams(vmem_limit_bytes=12 * 2**20),
        cost_estimate=pl.CostEstimate(flops=0, bytes_accessed=3 * 2**20, transcendentals=0),
    )(me, *args, *after)


def gap_kernel(real_total, order, me_ref, keep_ref, got_ref, noise_ref, labels_ref, after, out_ref):
    classes = keep_ref.shape[0]
    rows = labels_ref.shape[1]
    gap = keep_ref[...] + got_ref[...].astype(F32) - noise_ref[...] * (1.0 / real_total)
    gap = (16.0 * gap).astype(BF)
    ids = lax.broadcasted_iota(jnp.int32, (classes, rows), 0)
    for i, mask in enumerate(order):
        table = jnp.where(ids == labels_ref[i : i + 1, :], 1.0, 0.0).astype(BF)
        out = lax.dot_general(table, gap, (((0,), (0,)), ((), ())), preferred_element_type=F32)
        out_ref[me_ref[4] ^ mask] = out.astype(BF)


def gap_rows(me, keep, got, noise, labels, real_total, order, after):
    classes, width = keep.shape
    groups, rows = labels.shape
    whole = lambda shape: block(shape, lambda h, me: (0,) * len(shape))
    spec = pltpu.PrefetchScalarGridSpec(
        num_scalar_prefetch=1,
        grid=(1,),
        in_specs=[whole(x.shape) for x in (keep, got, noise, labels)]
        + [pl.BlockSpec(memory_space=pl.ANY)],
        out_specs=whole((groups, rows, width)),
    )
    return pl.pallas_call(
        functools.partial(gap_kernel, real_total, order),
        grid_spec=spec,
        out_shape=jax.ShapeDtypeStruct((groups, rows, width), BF),
        compiler_params=pltpu.CompilerParams(vmem_limit_bytes=14 * 2**20),
        cost_estimate=pl.CostEstimate(
            flops=2 * groups * rows * classes * width, bytes_accessed=3 * 2**20, transcendentals=0
        ),
    )(me, keep, got, noise, labels, after)


NT = (((1,), (1,)), ((), ()))


def sent_kernel(me_ref, wave_ref, rows_ref, freq_ref, a, b, c, send_ref, pre_ref):
    tile = wave_ref.shape[3]
    part = tile // 2

    @pl.when(pl.program_id(0) == 0)
    def _():
        for place in range(4):
            for h in range(2):
                grad = rows_ref[4 * h + 2 * (place % 2) + place // 2].astype(F32)
                lanes = slice(h * part, (h + 1) * part)
                pre = wave_ref[place, 0, :, lanes] * grad[:, part:]
                pre = pre - wave_ref[place, 1, :, lanes] * grad[:, :part]
                at = place * tile + h * part
                pre_ref[:, at : at + part] = pre.astype(BF)

    out = lax.dot_general(freq_ref[...], pre_ref[...], NT, preferred_element_type=F32)
    send_ref[0] = out.astype(BF)


def kept_kernel(me_ref, pre_ref, freq_ref, keep_ref):
    keep_ref[0] = lax.dot_general(freq_ref[...], pre_ref[...], NT, preferred_element_type=F32)


def image_grads(me, freq, cols, arrays, after, kept=None):
    k, n = freq.shape
    sent = kept is None
    rows = arrays[1].shape[1] if sent else arrays[0].shape[0]
    count = 2 if sent else 1
    whole = lambda shape: block(shape, lambda s, me: (0,) * len(shape))

    def source(s, me):
        return (me[0] ^ (2 * (1 - s)) ^ 1, 0) if sent else (me[0] ^ (2 * (1 - kept)), 0)

    out = block((1, cols, rows), lambda s, me: (s, 0, 0))
    shape = jax.ShapeDtypeStruct((count, cols, rows), BF if sent else F32)
    pre = jax.ShapeDtypeStruct((rows, n), BF)
    spec = pltpu.PrefetchScalarGridSpec(
        num_scalar_prefetch=1,
        grid=(count,),
        in_specs=[whole(x.shape) for x in arrays]
        + [block((cols, n), source)]
        + [pl.BlockSpec(memory_space=pl.ANY)] * len(after),
        out_specs=[out, whole(pre.shape)] if sent else out,
    )
    return pl.pallas_call(
        sent_kernel if sent else kept_kernel,
        grid_spec=spec,
        out_shape=[shape, pre] if sent else shape,
        compiler_params=pltpu.CompilerParams(vmem_limit_bytes=52 * 2**20),
        cost_estimate=pl.CostEstimate(flops=k * n * rows, bytes_accessed=k * n, transcendentals=0),
    )(me, *arrays, freq, *after)


def first_add_kernel(a, b, out):
    out[...] = (a[0] + b[0].astype(F32)).astype(BF)


def first_add(keep, got):
    _, cols, rows = keep.shape
    one = block((1, cols, rows), lambda h: (0, 0, 0))
    return pl.pallas_call(
        first_add_kernel,
        grid=(1,),
        in_specs=[one, one],
        out_specs=block((cols, rows), lambda h: (0, 0)),
        out_shape=jax.ShapeDtypeStruct((cols, rows), BF),
        compiler_params=pltpu.CompilerParams(vmem_limit_bytes=8 * 2**20),
        cost_estimate=pl.CostEstimate(flops=0, bytes_accessed=2**20, transcendentals=0),
    )(keep, got)


def out_kernel(keep, near, far, image, out):
    grad = (keep[0] + near[0].astype(F32) + far[...].astype(F32)).T
    grad = grad * (1.0 - jnp.square(image[...].astype(F32)))
    out[...] = grad.astype(BF)


def out_grads(keep, near, far, image):
    _, cols, rows = keep.shape
    one = lambda i: block((1, cols, rows), lambda h: (i, 0, 0))
    return pl.pallas_call(
        out_kernel,
        grid=(1,),
        in_specs=[one(0), one(1), block((cols, rows), lambda h: (0, 0)), block((rows, cols), lambda h: (0, 0))],
        out_specs=block((rows, cols), lambda h: (0, 0)),
        out_shape=jax.ShapeDtypeStruct(image.shape, BF),
        compiler_params=pltpu.CompilerParams(vmem_limit_bytes=8 * 2**20),
        cost_estimate=pl.CostEstimate(flops=0, bytes_accessed=2**20, transcendentals=0),
    )(keep, near, far, image)


def hidden_kernel(me_ref, w_ref, *refs):
    grads = refs[:4]
    send, keep = refs[5:]
    core = me_ref[0] % 2
    out = [lax.dot_general(w_ref[...], g[...], NT, preferred_element_type=F32) for g in grads]
    for i in range(2):
        keep[i] = jnp.where(core == 0, out[2 * i], out[2 * i + 1])
        send[i] = jnp.where(core == 0, out[2 * i + 1], out[2 * i]).astype(BF)


def hidden_grads(me, w_out, grads, mine, after):
    rows, cols = grads[0].shape
    whole = lambda shape: block(shape, lambda r, me: (0,) * len(shape))
    spec = pltpu.PrefetchScalarGridSpec(
        num_scalar_prefetch=1,
        grid=(1,),
        in_specs=[block((mine, cols), lambda r, me: (me[4], 0))] + [whole((rows, cols))] * 4
        + [pl.BlockSpec(memory_space=pl.ANY)],
        out_specs=[whole((2, mine, rows))] * 2,
    )
    return pl.pallas_call(
        hidden_kernel,
        grid_spec=spec,
        out_shape=[jax.ShapeDtypeStruct((2, mine, rows), t) for t in (BF, F32)],
        compiler_params=pltpu.CompilerParams(vmem_limit_bytes=8 * 2**20),
        cost_estimate=pl.CostEstimate(
            flops=8 * mine * cols * rows, bytes_accessed=2 * 5 * mine * cols, transcendentals=0
        ),
    )(me, w_out, *grads, after)


def add_kernel(a, b, out):
    out[...] = (a[...].astype(F32) + b[...].astype(F32)).astype(out.dtype)


def add(a, b, kind):
    return pl.pallas_call(
        add_kernel,
        out_shape=jax.ShapeDtypeStruct(a.shape, kind),
        compiler_params=pltpu.CompilerParams(vmem_limit_bytes=8 * 2**20),
        cost_estimate=pl.CostEstimate(flops=0, bytes_accessed=2**20, transcendentals=0),
    )(a, b)


def weight_kernel(me_ref, hidden_ref, *refs):
    out_ref, token = refs[-2:]
    token[...] = jnp.zeros_like(token)
    acc = None
    for mask, grad in enumerate(refs[:-2]):
        rows = grad.shape[0]
        at = slice(mask * rows, (mask + 1) * rows)
        d = jnp.dot(hidden_ref[:, at], grad[...], preferred_element_type=F32)
        acc = d if acc is None else acc + d
    out_ref[...] = acc


def weight_grads(me, hidden, grads):
    rows, cols = grads[0].shape
    mine, total = hidden.shape
    spec = pltpu.PrefetchScalarGridSpec(
        num_scalar_prefetch=1,
        grid=(1,),
        in_specs=[block((mine, total), lambda h, me: (0, 0))]
        + [block((rows, cols), lambda h, me: (0, 0)) for _ in grads],
        out_specs=[block((mine, cols), lambda h, me: (0, 0)), block((8, 128), lambda h, me: (0, 0))],
    )
    return pl.pallas_call(
        weight_kernel,
        grid_spec=spec,
        out_shape=[pltpu.HBM((mine, cols), F32), jax.ShapeDtypeStruct((8, 128), F32)],
        compiler_params=pltpu.CompilerParams(vmem_limit_bytes=12 * 2**20),
        cost_estimate=pl.CostEstimate(
            flops=2 * mine * total * cols, bytes_accessed=4 * 2**20, transcendentals=0
        ),
    )(me, hidden, *grads)


def last_kernel(me_ref, gate_ref, lhs_ref, p0, q0, p1, q1, after, out_ref):
    rows = p0.shape[2]
    acc = None
    for h, (p, q) in enumerate(((p0, q0), (p1, q1))):
        for i in range(2):
            place = 4 * (me_ref[0] % 2) + 2 * i + h
            at = pl.ds(pl.multiple_of(place * rows, 128), rows)
            grad = p[i].astype(F32) + q[i].astype(F32)
            grad = jnp.where(gate_ref[:, at].astype(F32) > 0, grad, 0.0).astype(BF)
            d = lax.dot_general(lhs_ref[:, at], grad, NT, preferred_element_type=F32)
            acc = d if acc is None else acc + d
    out_ref[...] = acc


def last_grads(me, gate, lhs, parts, after):
    count, total = lhs.shape
    mine = gate.shape[0]
    args = (gate, lhs, *parts)
    whole = lambda shape: block(shape, lambda h, me: (0,) * len(shape))
    spec = pltpu.PrefetchScalarGridSpec(
        num_scalar_prefetch=1,
        grid=(1,),
        in_specs=[whole(x.shape) for x in args] + [pl.BlockSpec(memory_space=pl.ANY)],
        out_specs=whole((count, mine)),
    )
    return pl.pallas_call(
        last_kernel,
        grid_spec=spec,
        out_shape=jax.ShapeDtypeStruct((count, mine), F32),
        compiler_params=pltpu.CompilerParams(vmem_limit_bytes=12 * 2**20),
        cost_estimate=pl.CostEstimate(
            flops=total * count * mine, bytes_accessed=2 * 2**20, transcendentals=0
        ),
    )(me, *args, after)


def outputs_kernel(own, other, latent, embed):
    dz = latent.shape[0]
    latent[...] = own[:dz] + other[:dz]
    embed[...] = own[dz:] + other[dz:]


def outputs(own, other, dz):
    count, mine = own.shape
    return pl.pallas_call(
        outputs_kernel,
        out_shape=[jax.ShapeDtypeStruct((c, mine), F32) for c in (dz, count - dz)],
        compiler_params=pltpu.CompilerParams(vmem_limit_bytes=8 * 2**20),
        cost_estimate=pl.CostEstimate(flops=0, bytes_accessed=2**20, transcendentals=0),
    )(own, other)


def tie(first, later):
    return lax.optimization_barrier((first, later))


def eight_by_four(
    records, real_labels, frequencies, class_noise, latents, syn_labels, w_latent, class_embed, w_out
):
    classes, hid = class_embed.shape
    groups = lax.axis_size("rec")
    rec = lax.axis_index("rec")
    feat = lax.axis_index("feat")
    rows, dz = latents.shape
    cols = w_out.shape[1]
    real_total = records.shape[0] * groups
    syn_total = rows * groups
    x, z_low, z_high = rec % 2, (rec // 2) % 2, rec // 4
    place = 2 * x + z_low
    me = jnp.stack([feat, x, z_low, z_high, rec, place]).astype(jnp.int32)

    table = one_hot(syn_labels, classes, BF)
    preact = jnp.dot(latents, w_latent, preferred_element_type=F32) + jnp.dot(
        table, class_embed, preferred_element_type=F32
    )
    hidden = jnp.maximum(preact, 0.0).astype(BF)
    own = jnp.tanh(jnp.dot(hidden, w_out, preferred_element_type=F32)).astype(BF)
    far = swap(own, "feat", 2)

    order = (0, 4, 2, 6, 1, 5, 3, 7)
    label_row = jnp.zeros((16, dz), BF).at[0, :].set(syn_labels.astype(BF))
    packed = jnp.concatenate([latents, label_row], axis=0)[None]
    far, pair = tie(far, swap(packed, "rec", 4))
    images = [own, far, swap(own, "feat", 1), swap(far, "feat", 1)]
    packed, real_labels = tie(jnp.concatenate([packed, pair], axis=0), real_labels)
    pair = swap(packed, "rec", 2)

    masks = (0, 2, 1, 3)
    totals = (real_total, syn_total)
    send_a, keep_a, send_b, keep_b, both, waves, token = feature_sums(
        False, me, real_labels, syn_labels, masks, images, records, frequencies, classes, totals, me
    )
    first_a = swap(send_a, "rec", 1)
    first_b = swap(send_b, "rec", 2)
    pair, token = tie(pair, token)
    last_a, last_b, waves, token = feature_sums(
        True, me, real_labels, syn_labels, masks, both, records, frequencies, classes, totals, token, waves
    )

    send_a, send_b, token = stage_two_send(keep_a, first_a, keep_b, first_b, token)
    got_a = swap(send_a, "rec", 2)
    got_b = swap(send_b, "rec", 1)
    part = frequencies.shape[1] // groups
    noise = lax.dynamic_slice_in_dim(class_noise, (2 * place + z_high) * part, part, 2)
    noise = noise.reshape(classes, 2 * part)
    send, keep, token = stage_three(me, last_a, first_a, got_a, last_b, first_b, got_b, (noise, token, token))
    got = swap(send, "rec", 4)
    pair, token = tie(pair, token)
    quad = jnp.concatenate([packed, pair], axis=0)
    eight = jnp.concatenate([quad, swap(quad, "rec", 1)], axis=0)
    all_latents = eight[:, :rows].reshape(syn_total, dz)
    all_labels = eight[:, rows].reshape(syn_total).astype(jnp.int32)
    all_table = one_hot(all_labels, classes, BF)
    mine = hid // groups
    lhs = jnp.concatenate([all_latents, all_table], axis=1).T
    w = jnp.concatenate(
        [
            lax.dynamic_slice_in_dim(w_latent, rec * mine, mine, 1),
            lax.dynamic_slice_in_dim(class_embed, rec * mine, mine, 1),
        ],
        axis=0,
    )
    all_preact = lax.dot_general(w, lhs, (((0,), (0,)), ((), ())), preferred_element_type=F32)
    all_hidden = jnp.maximum(all_preact, 0.0).astype(BF)
    gate = (all_preact > 0).astype(BF)

    feat_grad = gap_rows(me, keep, got, noise, all_labels.reshape(groups, rows), real_total, order, token)
    feat_grad = lax.all_to_all(feat_grad, "rec", 0, 0, tiled=True)

    send, pre_grad = image_grads(
        me, frequencies, cols, (waves, feat_grad), (gate, all_hidden, lhs)
    )
    near = swap(send, "feat", 1)
    keep = image_grads(me, frequencies, cols, (pre_grad,), (), 0)
    far = swap(first_add(keep, near), "feat", 2)
    keep = image_grads(me, frequencies, cols, (pre_grad,), (), 1)
    out_grad = out_grads(keep, near, far, own)

    by = {0: out_grad}
    by[4] = swap(out_grad, "rec", 4)
    by[2] = swap(out_grad, "rec", 2)
    by[1] = swap(out_grad, "rec", 1)
    by[2], by[1] = tie(by[2], by[1])
    by[3] = swap(by[2], "rec", 1)
    by[6] = swap(by[4], "rec", 2)
    by[5] = swap(by[4], "rec", 1)

    def reduced(send, keep):
        part = add(keep, swap(send, "feat", 1), BF)
        return [part, swap(part, "feat", 2)]

    by[7] = swap(by[6], "rec", 1)
    send, keep = hidden_grads(me, w_out, [by[i] for i in range(4)], mine, by[5])
    parts = reduced(send, keep)
    parts += reduced(*hidden_grads(me, w_out, [by[4 + i] for i in range(4)], mine, parts[0]))
    grad_w_out, token = weight_grads(me, all_hidden, [by[mask] for mask in order])
    grads = last_grads(me, gate, lhs, parts, token)
    grad_w_latent, grad_embed = outputs(grads, swap(grads, "feat", 1), dz)
    return grad_w_out, grad_w_latent, grad_embed


def solution(mesh):
    shape = (mesh.shape["rec"], mesh.shape["feat"])
    in_specs = (
        P("rec", None),
        P("rec"),
        P(None, "feat"),
        P(None, None, "feat"),
        P("rec", None),
        P("rec"),
        P(),
        P(),
        P(None, "feat"),
    )
    out_specs = (P("rec", "feat"), P(None, "rec"), P(None, "rec"))
    return jax.shard_map(
        eight_by_four if shape == (8, 4) else general, mesh=mesh, in_specs=in_specs, out_specs=out_specs, check_vma=False
    )
```

```python
import functools

import jax
import jax.numpy as jnp
from jax import lax
from jax.experimental import pallas as pl
from jax.experimental.pallas import tpu as pltpu
from jax.sharding import PartitionSpec as P

BF = jnp.bfloat16
F32 = jnp.float32

TURN = 0.15915494309189535
SIN = (4.44286783702217, -7.307441307726672, 3.59477116396636, -0.7843353598850176)
COS = (1.4142134962552275, -6.978850948563815, 5.739460376907241, -1.883557905986894, 0.3106880275267554)


def cos_sin(x):
    turns = x * TURN
    u = turns - jnp.round(turns)
    sq = u * u
    p = SIN[-1]
    for c in SIN[-2::-1]:
        p = p * sq + c
    q = COS[-1]
    for c in COS[-2::-1]:
        q = q * sq + c
    s = u * p
    return 1.0 - s * s, s * q


def one_hot(labels, count, dtype):
    return (labels[:, None] == jnp.arange(count, dtype=jnp.int32)[None, :]).astype(dtype)


def real_kernel(rows, labels_ref, records_ref, freq_ref, out_ref, table_ref):
    total = records_ref.shape[0]
    classes = table_ref.shape[0]
    owners, _, width = out_ref.shape
    part = width // 2

    @pl.when(pl.program_id(0) == 0)
    def _():
        ids = lax.broadcasted_iota(jnp.int32, (classes, total), 0)
        table_ref[...] = jnp.where(ids == labels_ref[...], 1.0, 0.0).astype(BF)

    freq = freq_ref[...]
    block = freq.shape[1]

    def sums(i, pre):
        co, si = cos_sin(pre)
        phi = jnp.concatenate([co.astype(BF), si.astype(BF)], axis=1)
        return jnp.dot(table_ref[:, i * rows : (i + 1) * rows], phi, preferred_element_type=F32)

    acc = None
    before = None
    steps = total // rows
    for i in range(steps + 1):
        pre = None
        if i < steps:
            pre = jnp.dot(records_ref[i * rows : (i + 1) * rows, :], freq, preferred_element_type=F32)
        if i > 0:
            d = sums(i - 1, before)
            acc = d if acc is None else acc + d
        before = pre
    for o in range(owners):
        out_ref[o, :, :part] = acc[:, o * part : (o + 1) * part]
        out_ref[o, :, part:] = acc[:, block + o * part : block + (o + 1) * part]


def real_sums(labels, records, freq, classes, owners):
    m, k = records.shape
    n = freq.shape[1]
    block = min(512, n)
    rows = 512
    part = n // owners
    per = block // part
    return pl.pallas_call(
        functools.partial(real_kernel, rows),
        grid=(n // block,),
        in_specs=[
            pl.BlockSpec((1, m), lambda j: (0, 0)),
            pl.BlockSpec((m, k), lambda j: (0, 0)),
            pl.BlockSpec((k, block), lambda j: (0, j)),
        ],
        out_specs=pl.BlockSpec((per, classes, 2 * part), lambda j: (j, 0, 0)),
        out_shape=jax.ShapeDtypeStruct((owners, classes, 2 * part), F32),
        scratch_shapes=[pltpu.VMEM((classes, m), BF)],
        compiler_params=pltpu.CompilerParams(vmem_limit_bytes=56 * 2**20),
        cost_estimate=pl.CostEstimate(
            flops=2 * m * n * (k + 2 * classes), bytes_accessed=2 * (m * k + k * n), transcendentals=0
        ),
    )(labels.reshape(1, m), records, freq)


def bits_of(n):
    return [1 << b for b in range(n.bit_length() - 1)]


def swap(x, axis, bit):
    n = lax.axis_size(axis)
    return lax.ppermute(x, axis, [(i, i ^ bit) for i in range(n)])


def pick(x, index, dim):
    return lax.dynamic_index_in_dim(x, index, dim, keepdims=False)


def halving(x, axis, order, count):
    me = lax.axis_index(axis)
    nbits = len(order)
    x = x.reshape((2,) * nbits + x.shape[1:])
    left = sorted(order, reverse=True)
    for bit in order:
        dim = left.index(bit)
        left.remove(bit)
        mine = (me // bit) % 2
        got = swap(pick(x, 1 - mine, dim).astype(BF), axis, bit)
        x = pick(x, mine, dim).astype(F32) + got.astype(F32)
    return x


def general(
    records, real_labels, frequencies, class_noise, latents, syn_labels, w_latent, class_embed, w_out
):
    classes = class_embed.shape[0]
    hid = class_embed.shape[1]
    groups = lax.axis_size("rec")
    feats = lax.axis_size("feat")
    rec = lax.axis_index("rec")
    nf = frequencies.shape[1]
    part = nf // groups
    rows, dz = latents.shape
    cols = w_out.shape[1]
    real_total = records.shape[0] * groups
    syn_total = rows * groups

    label_row = jnp.zeros((16, dz), BF).at[0, :].set(syn_labels.astype(BF))
    packed = jnp.concatenate([latents, label_row], axis=0)
    packed = lax.all_to_all(
        jnp.broadcast_to(packed[None], (groups,) + packed.shape), "rec", 0, 0, tiled=True
    )
    all_latents = packed[:, :rows].reshape(syn_total, dz)
    all_labels = packed[:, rows].reshape(syn_total).astype(jnp.int32)
    all_table = one_hot(all_labels, classes, BF)

    table = one_hot(syn_labels, classes, BF)
    preact = jnp.dot(latents, w_latent, preferred_element_type=F32) + jnp.dot(
        table, class_embed, preferred_element_type=F32
    )
    hidden = jnp.maximum(preact, 0.0).astype(BF)
    own_images = jnp.tanh(jnp.dot(hidden, w_out, preferred_element_type=F32)).astype(BF)
    images = lax.all_gather(own_images, "feat", axis=0)
    images = images.transpose(1, 0, 2).reshape(rows, feats * cols)
    syn_pre = jnp.dot(images, frequencies, preferred_element_type=F32)
    syn_cos, syn_sin = cos_sin(syn_pre)
    syn_phi = jnp.concatenate(
        [syn_cos.reshape(rows, groups, part), syn_sin.reshape(rows, groups, part)], axis=2
    ).astype(BF)
    syn_sum = lax.dot_general(
        table, syn_phi.reshape(rows, 2 * nf), (((0,), (0,)), ((), ())), preferred_element_type=F32
    )
    syn_sum = syn_sum.reshape(classes, groups, 2 * part).transpose(1, 0, 2)

    real_sum = real_sums(real_labels, records, frequencies, classes, groups)
    gap = syn_sum * (1.0 / syn_total) - real_sum * (1.0 / real_total)
    half = classes // 2
    order = bits_of(groups)
    other = [order[1], order[0]] + order[2:]
    gap = jnp.concatenate(
        [halving(gap[:, :half], "rec", order, groups), halving(gap[:, half:], "rec", other, groups)], axis=0
    )
    noise = lax.dynamic_slice_in_dim(class_noise, rec * part, part, 2).reshape(classes, 2 * part)
    gap = (16.0 * (gap - noise * (1.0 / real_total))).astype(BF)

    feat_grad = jnp.dot(all_table, gap, preferred_element_type=F32).astype(BF)
    feat_grad = lax.all_to_all(feat_grad.reshape(groups, rows, 2 * part), "rec", 0, 0, tiled=True)
    feat_grad = feat_grad.transpose(1, 0, 2).astype(F32)
    pre_grad = (
        -syn_sin.reshape(rows, groups, part) * feat_grad[:, :, :part]
        + syn_cos.reshape(rows, groups, part) * feat_grad[:, :, part:]
    )
    pre_grad = pre_grad.astype(BF).reshape(rows, nf)
    image_grad = lax.dot_general(
        frequencies, pre_grad, (((1,), (1,)), ((), ())), preferred_element_type=F32
    )
    image_grad = halving(image_grad.reshape(feats, cols, rows), "feat", bits_of(feats), feats)
    image_grad = image_grad.T
    out_grad = (image_grad * (1.0 - jnp.square(own_images.astype(F32)))).astype(BF)

    out_grad = lax.all_to_all(
        jnp.broadcast_to(out_grad[None], (groups, rows, cols)), "rec", 0, 0, tiled=True
    ).reshape(syn_total, cols)

    mine = hid // groups
    start = rec * mine
    all_preact = jnp.dot(
        all_latents, lax.dynamic_slice_in_dim(w_latent, start, mine, 1), preferred_element_type=F32
    ) + jnp.dot(
        all_table, lax.dynamic_slice_in_dim(class_embed, start, mine, 1), preferred_element_type=F32
    )
    all_hidden = jnp.maximum(all_preact, 0.0).astype(BF)
    grad_w_out = lax.dot_general(
        all_hidden, out_grad, (((0,), (0,)), ((), ())), preferred_element_type=F32
    )
    hidden_grad = lax.dot_general(
        out_grad,
        lax.dynamic_slice_in_dim(w_out, start, mine, 0),
        (((1,), (1,)), ((), ())),
        preferred_element_type=F32,
    )
    core = lax.axis_index("feat") % 2
    half = syn_total // 2
    hidden_grad = hidden_grad.reshape(2, half, mine)
    got = swap(pick(hidden_grad, 1 - core, 0).astype(BF), "feat", 1)
    hidden_grad = pick(hidden_grad, core, 0) + got.astype(F32)
    for bit in bits_of(feats)[1:]:
        send = hidden_grad.astype(BF)
        hidden_grad = send.astype(F32) + swap(send, "feat", bit).astype(F32)
    my_preact = lax.dynamic_slice_in_dim(all_preact, core * half, half, 0)
    pre_hidden = jnp.where(my_preact > 0, hidden_grad, 0.0).astype(BF)
    lhs = jnp.concatenate([all_latents, all_table], axis=1)
    lhs = lax.dynamic_slice_in_dim(lhs, core * half, half, 0)
    grads = lax.dot_general(lhs, pre_hidden, (((0,), (0,)), ((), ())), preferred_element_type=F32)
    grads = grads + swap(grads, "feat", 1)
    return grad_w_out, grads[:dz], grads[dz:]


def block(shape, index):
    return pl.BlockSpec(shape, index)


def sums(table, pre):
    co, si = cos_sin(pre)
    phi = jnp.concatenate([co.astype(BF), si.astype(BF)], axis=1)
    return jnp.dot(table, phi, preferred_element_type=F32)


def features_kernel(
    masks, last, real_total, syn_total, me_ref, real_labels_ref, syn_labels_ref, *refs
):
    count = 1 if last else len(masks)
    images = [refs[0].at[i] for i in range(len(masks))] if last else refs[:count]
    records_hbm, freq_ref = refs[count : count + 2]
    outs = refs[count + (4 if last else 3) : -4]
    wave, token = outs[-2:]
    records, real_table, syn_table, sem = refs[-4:]
    classes, total = real_table.shape
    size = 512
    steps = total // size
    step = pl.program_id(0)
    cols = images[0].shape[1]
    half = classes // 2
    token[...] = jnp.zeros_like(token)

    def copy(i):
        at = pl.ds(i * size, size)
        return pltpu.make_async_copy(records_hbm.at[at, :], records.at[at, :], sem.at[i])

    def work(wait):
        if wait:
            for i in range(steps):
                copy(i).start()
            ids = lax.broadcasted_iota(jnp.int32, (classes, total), 0)
            real_table[...] = jnp.where(ids == real_labels_ref[...], 1.0, 0.0).astype(BF)
            ids = lax.broadcasted_iota(jnp.int32, syn_table.shape, 0)
            syn_table[...] = jnp.where(ids == syn_labels_ref[...], 1.0, 0.0).astype(BF)
        syn_pre = None
        for mask, image in zip(masks, images):
            at = pl.multiple_of((me_ref[0] ^ mask) * cols, 128)
            d = jnp.dot(image[...], freq_ref[pl.ds(at, cols), :], preferred_element_type=F32)
            syn_pre = d if syn_pre is None else syn_pre + d
        freq = freq_ref[...]
        acc = None
        before = None
        for i in range(steps + 1):
            if i < steps:
                if wait:
                    copy(i).wait()
                pre = jnp.dot(records[i * size : (i + 1) * size, :], freq, preferred_element_type=F32)
            if i == 0:
                co, si = cos_sin(syn_pre)
                wave[0, 0] = co
                wave[0, 1] = si
                phi = jnp.concatenate([co.astype(BF), si.astype(BF)], axis=1)
                syn = jnp.dot(syn_table[...], phi, preferred_element_type=F32)
            else:
                d = sums(real_table[:, (i - 1) * size : i * size], before)
                acc = d if acc is None else acc + d
            before = pre
        gap = syn * (1.0 / syn_total) - acc * (1.0 / real_total)
        width = gap.shape[1] // 4
        return [
            jnp.concatenate(
                [gap[:, h * width : (h + 1) * width], gap[:, (h + 2) * width : (h + 3) * width]], axis=1
            )
            for h in range(2)
        ]

    if last:
        parts = work(True)
        for h in range(2):
            outs[0][h] = parts[h][:half]
            outs[1][h] = parts[h][half:]
        return
    send_a, keep_a, send_b, keep_b, both = outs[:5]

    @pl.when(step == 0)
    def _():
        for i in range(count):
            both[i] = images[i][...]
        parts = work(True)
        for h in range(2):
            send_a[0, h] = parts[h][:half].astype(BF)
            send_b[0, h] = parts[h][half:].astype(BF)

    @pl.when(step > 0)
    def _():
        parts = work(False)

        @pl.when(step == 1)
        def _():
            for h in range(2):
                send_a[0, h] = parts[h][:half].astype(BF)
                keep_b[h] = parts[h][half:]

        @pl.when(step == 2)
        def _():
            for h in range(2):
                keep_a[h] = parts[h][:half]
                send_b[0, h] = parts[h][half:].astype(BF)


def feature_sums(
    last, me, real_labels, syn_labels, masks, images, records, freq, classes, totals, after, waves=None
):
    total, k = records.shape
    n = freq.shape[1]
    rows, cols = images.shape[1:] if last else images[0].shape
    half = classes // 2
    tile = n // 4
    tiles = 1 if last else 3
    whole = lambda shape: block(shape, lambda j, me: (0,) * len(shape))
    kept = jax.ShapeDtypeStruct((2, half, tile), F32)
    sent = jax.ShapeDtypeStruct((2, 2, half, tile), BF)
    both = (len(masks), rows, cols)
    place = lambda j, me: me[5] ^ (0 if last else 3 - j)
    anywhere = pl.BlockSpec(memory_space=pl.ANY)
    shapes = [pltpu.HBM((4, 2, rows, tile), F32), jax.ShapeDtypeStruct((8, 128), F32)]
    specs = [block((1, 2, rows, tile), lambda j, me: (place(j, me), 0, 0, 0)), whole((8, 128))]
    if last:
        shapes = [kept, kept] + shapes
        specs = [whole(kept.shape), whole(kept.shape)] + specs
        images = (images,)
        extra = (after, waves)
    else:
        shapes = [sent, kept, sent, kept, jax.ShapeDtypeStruct(both, BF)] + shapes
        specs = [
            block((1, 2, half, tile), lambda j, me: (jnp.minimum(j, 1), 0, 0, 0)),
            whole(kept.shape),
            block((1, 2, half, tile), lambda j, me: (j // 2, 0, 0, 0)),
            whole(kept.shape),
            whole(both),
        ] + specs
        extra = (after,)
    grid_spec = pltpu.PrefetchScalarGridSpec(
        num_scalar_prefetch=1,
        grid=(tiles,),
        in_specs=[whole((1, total)), whole((1, rows))]
        + [whole(image.shape) for image in images]
        + [anywhere, block((k, tile), lambda j, me: (0, place(j, me)))]
        + [anywhere] * len(extra),
        out_specs=specs,
        scratch_shapes=[
            pltpu.VMEM((total, k), BF),
            pltpu.VMEM((classes, total), BF),
            pltpu.VMEM((classes, rows), BF),
            pltpu.SemaphoreType.DMA((total // 512,)),
        ],
    )
    return pl.pallas_call(
        functools.partial(features_kernel, masks, last, *totals),
        grid_spec=grid_spec,
        out_shape=shapes,
        input_output_aliases={7: 2} if last else {},
        compiler_params=pltpu.CompilerParams(vmem_limit_bytes=44 * 2**20),
        cost_estimate=pl.CostEstimate(
            flops=2 * (total + rows) * tiles * tile * (k + 2 * classes),
            bytes_accessed=2 * (total * k + k * tiles * tile),
            transcendentals=0,
        ),
    )(me, real_labels.reshape(1, -1), syn_labels.reshape(1, -1), *images, records, freq, *extra)


def stage_two_send_kernel(ka, ga, kb, gb, after, sa, sb, token):
    token[...] = jnp.zeros_like(token)
    sa[...] = (ka[...] + ga[0].astype(F32)).astype(BF)
    sb[...] = (kb[...] + gb[0].astype(F32)).astype(BF)


def stage_two_send(keep_a, got_a, keep_b, got_b, after):
    return pl.pallas_call(
        stage_two_send_kernel,
        in_specs=[pl.BlockSpec()] * 4 + [pl.BlockSpec(memory_space=pl.ANY)],
        out_shape=[jax.ShapeDtypeStruct(keep_a.shape, BF)] * 2 + [jax.ShapeDtypeStruct((8, 128), F32)],
        compiler_params=pltpu.CompilerParams(vmem_limit_bytes=10 * 2**20),
        cost_estimate=pl.CostEstimate(flops=0, bytes_accessed=3 * 2**20, transcendentals=0),
    )(keep_a, got_a, keep_b, got_b, after)


def stage_three_kernel(me_ref, na, fa, ga, nb, fb, gb, a, b, c, send, keep, token):
    token[...] = jnp.zeros_like(token)
    high = me_ref[3]
    half = na.shape[1]
    for flip, out in ((1, send), (0, keep)):
        at = high ^ flip
        out[:half] = (na[at] + fa[1, at].astype(F32) + ga[at].astype(F32)).astype(out.dtype)
        out[half:] = (nb[at] + fb[1, at].astype(F32) + gb[at].astype(F32)).astype(out.dtype)


def stage_three(me, keep_a, first_a, got_a, keep_b, first_b, got_b, after):
    _, half, width = keep_a.shape
    args = (keep_a, first_a, got_a, keep_b, first_b, got_b)
    whole = lambda shape: block(shape, lambda h, me: (0,) * len(shape))
    spec = pltpu.PrefetchScalarGridSpec(
        num_scalar_prefetch=1,
        grid=(1,),
        in_specs=[whole(x.shape) for x in args] + [pl.BlockSpec(memory_space=pl.ANY)] * 3,
        out_specs=[whole((2 * half, width))] * 2 + [whole((8, 128))],
    )
    return pl.pallas_call(
        stage_three_kernel,
        grid_spec=spec,
        out_shape=[jax.ShapeDtypeStruct((2 * half, width), t) for t in (BF, F32)]
        + [jax.ShapeDtypeStruct((8, 128), F32)],
        compiler_params=pltpu.CompilerParams(vmem_limit_bytes=12 * 2**20),
        cost_estimate=pl.CostEstimate(flops=0, bytes_accessed=3 * 2**20, transcendentals=0),
    )(me, *args, *after)


def gap_kernel(real_total, order, me_ref, keep_ref, got_ref, noise_ref, labels_ref, after, out_ref):
    classes = keep_ref.shape[0]
    rows = labels_ref.shape[1]
    gap = keep_ref[...] + got_ref[...].astype(F32) - noise_ref[...] * (1.0 / real_total)
    gap = (16.0 * gap).astype(BF)
    ids = lax.broadcasted_iota(jnp.int32, (classes, rows), 0)
    for i, mask in enumerate(order):
        table = jnp.where(ids == labels_ref[i : i + 1, :], 1.0, 0.0).astype(BF)
        out = lax.dot_general(table, gap, (((0,), (0,)), ((), ())), preferred_element_type=F32)
        out_ref[me_ref[4] ^ mask] = out.astype(BF)


def gap_rows(me, keep, got, noise, labels, real_total, order, after):
    classes, width = keep.shape
    groups, rows = labels.shape
    whole = lambda shape: block(shape, lambda h, me: (0,) * len(shape))
    spec = pltpu.PrefetchScalarGridSpec(
        num_scalar_prefetch=1,
        grid=(1,),
        in_specs=[whole(x.shape) for x in (keep, got, noise, labels)]
        + [pl.BlockSpec(memory_space=pl.ANY)],
        out_specs=whole((groups, rows, width)),
    )
    return pl.pallas_call(
        functools.partial(gap_kernel, real_total, order),
        grid_spec=spec,
        out_shape=jax.ShapeDtypeStruct((groups, rows, width), BF),
        compiler_params=pltpu.CompilerParams(vmem_limit_bytes=14 * 2**20),
        cost_estimate=pl.CostEstimate(
            flops=2 * groups * rows * classes * width, bytes_accessed=3 * 2**20, transcendentals=0
        ),
    )(me, keep, got, noise, labels, after)


NT = (((1,), (1,)), ((), ()))


def sent_kernel(me_ref, wave_ref, rows_ref, freq_ref, a, b, c, send_ref, pre_ref):
    tile = wave_ref.shape[3]
    part = tile // 2

    @pl.when(pl.program_id(0) == 0)
    def _():
        for place in range(4):
            for h in range(2):
                grad = rows_ref[4 * h + 2 * (place % 2) + place // 2].astype(F32)
                lanes = slice(h * part, (h + 1) * part)
                pre = wave_ref[place, 0, :, lanes] * grad[:, part:]
                pre = pre - wave_ref[place, 1, :, lanes] * grad[:, :part]
                at = place * tile + h * part
                pre_ref[:, at : at + part] = pre.astype(BF)

    out = lax.dot_general(freq_ref[...], pre_ref[...], NT, preferred_element_type=F32)
    send_ref[0] = out.astype(BF)


def kept_kernel(me_ref, pre_ref, freq_ref, keep_ref):
    keep_ref[0] = lax.dot_general(freq_ref[...], pre_ref[...], NT, preferred_element_type=F32)


def image_grads(me, freq, cols, arrays, after, kept=None):
    k, n = freq.shape
    sent = kept is None
    rows = arrays[1].shape[1] if sent else arrays[0].shape[0]
    count = 2 if sent else 1
    whole = lambda shape: block(shape, lambda s, me: (0,) * len(shape))

    def source(s, me):
        return (me[0] ^ (2 * (1 - s)) ^ 1, 0) if sent else (me[0] ^ (2 * (1 - kept)), 0)

    out = block((1, cols, rows), lambda s, me: (s, 0, 0))
    shape = jax.ShapeDtypeStruct((count, cols, rows), BF if sent else F32)
    pre = jax.ShapeDtypeStruct((rows, n), BF)
    spec = pltpu.PrefetchScalarGridSpec(
        num_scalar_prefetch=1,
        grid=(count,),
        in_specs=[whole(x.shape) for x in arrays]
        + [block((cols, n), source)]
        + [pl.BlockSpec(memory_space=pl.ANY)] * len(after),
        out_specs=[out, whole(pre.shape)] if sent else out,
    )
    return pl.pallas_call(
        sent_kernel if sent else kept_kernel,
        grid_spec=spec,
        out_shape=[shape, pre] if sent else shape,
        compiler_params=pltpu.CompilerParams(vmem_limit_bytes=52 * 2**20),
        cost_estimate=pl.CostEstimate(flops=k * n * rows, bytes_accessed=k * n, transcendentals=0),
    )(me, *arrays, freq, *after)


def first_add_kernel(a, b, out):
    out[...] = (a[0] + b[0].astype(F32)).astype(BF)


def first_add(keep, got):
    _, cols, rows = keep.shape
    one = block((1, cols, rows), lambda h: (0, 0, 0))
    return pl.pallas_call(
        first_add_kernel,
        grid=(1,),
        in_specs=[one, one],
        out_specs=block((cols, rows), lambda h: (0, 0)),
        out_shape=jax.ShapeDtypeStruct((cols, rows), BF),
        compiler_params=pltpu.CompilerParams(vmem_limit_bytes=8 * 2**20),
        cost_estimate=pl.CostEstimate(flops=0, bytes_accessed=2**20, transcendentals=0),
    )(keep, got)


def out_kernel(keep, near, far, image, out):
    grad = (keep[0] + near[0].astype(F32) + far[...].astype(F32)).T
    grad = grad * (1.0 - jnp.square(image[...].astype(F32)))
    out[...] = grad.astype(BF)


def out_grads(keep, near, far, image):
    _, cols, rows = keep.shape
    one = lambda i: block((1, cols, rows), lambda h: (i, 0, 0))
    return pl.pallas_call(
        out_kernel,
        grid=(1,),
        in_specs=[one(0), one(1), block((cols, rows), lambda h: (0, 0)), block((rows, cols), lambda h: (0, 0))],
        out_specs=block((rows, cols), lambda h: (0, 0)),
        out_shape=jax.ShapeDtypeStruct(image.shape, BF),
        compiler_params=pltpu.CompilerParams(vmem_limit_bytes=8 * 2**20),
        cost_estimate=pl.CostEstimate(flops=0, bytes_accessed=2**20, transcendentals=0),
    )(keep, near, far, image)


def hidden_kernel(me_ref, w_ref, *refs):
    grads = refs[:4]
    send, keep = refs[5:]
    core = me_ref[0] % 2
    out = [lax.dot_general(w_ref[...], g[...], NT, preferred_element_type=F32) for g in grads]
    for i in range(2):
        keep[i] = jnp.where(core == 0, out[2 * i], out[2 * i + 1])
        send[i] = jnp.where(core == 0, out[2 * i + 1], out[2 * i]).astype(BF)


def hidden_grads(me, w_out, grads, mine, after):
    rows, cols = grads[0].shape
    whole = lambda shape: block(shape, lambda r, me: (0,) * len(shape))
    spec = pltpu.PrefetchScalarGridSpec(
        num_scalar_prefetch=1,
        grid=(1,),
        in_specs=[block((mine, cols), lambda r, me: (me[4], 0))] + [whole((rows, cols))] * 4
        + [pl.BlockSpec(memory_space=pl.ANY)],
        out_specs=[whole((2, mine, rows))] * 2,
    )
    return pl.pallas_call(
        hidden_kernel,
        grid_spec=spec,
        out_shape=[jax.ShapeDtypeStruct((2, mine, rows), t) for t in (BF, F32)],
        compiler_params=pltpu.CompilerParams(vmem_limit_bytes=8 * 2**20),
        cost_estimate=pl.CostEstimate(
            flops=8 * mine * cols * rows, bytes_accessed=2 * 5 * mine * cols, transcendentals=0
        ),
    )(me, w_out, *grads, after)


def add_kernel(a, b, out):
    out[...] = (a[...].astype(F32) + b[...].astype(F32)).astype(out.dtype)


def add(a, b, kind):
    return pl.pallas_call(
        add_kernel,
        out_shape=jax.ShapeDtypeStruct(a.shape, kind),
        compiler_params=pltpu.CompilerParams(vmem_limit_bytes=8 * 2**20),
        cost_estimate=pl.CostEstimate(flops=0, bytes_accessed=2**20, transcendentals=0),
    )(a, b)


def weight_kernel(me_ref, hidden_ref, *refs):
    out_ref, token = refs[-2:]
    token[...] = jnp.zeros_like(token)
    acc = None
    for mask, grad in enumerate(refs[:-2]):
        rows = grad.shape[0]
        at = slice(mask * rows, (mask + 1) * rows)
        d = jnp.dot(hidden_ref[:, at], grad[...], preferred_element_type=F32)
        acc = d if acc is None else acc + d
    out_ref[...] = acc


def weight_grads(me, hidden, grads):
    rows, cols = grads[0].shape
    mine, total = hidden.shape
    spec = pltpu.PrefetchScalarGridSpec(
        num_scalar_prefetch=1,
        grid=(1,),
        in_specs=[block((mine, total), lambda h, me: (0, 0))]
        + [block((rows, cols), lambda h, me: (0, 0)) for _ in grads],
        out_specs=[block((mine, cols), lambda h, me: (0, 0)), block((8, 128), lambda h, me: (0, 0))],
    )
    return pl.pallas_call(
        weight_kernel,
        grid_spec=spec,
        out_shape=[pltpu.HBM((mine, cols), F32), jax.ShapeDtypeStruct((8, 128), F32)],
        compiler_params=pltpu.CompilerParams(vmem_limit_bytes=12 * 2**20),
        cost_estimate=pl.CostEstimate(
            flops=2 * mine * total * cols, bytes_accessed=4 * 2**20, transcendentals=0
        ),
    )(me, hidden, *grads)


def last_kernel(me_ref, gate_ref, lhs_ref, p0, q0, p1, q1, after, out_ref):
    rows = p0.shape[2]
    acc = None
    for h, (p, q) in enumerate(((p0, q0), (p1, q1))):
        for i in range(2):
            place = 4 * (me_ref[0] % 2) + 2 * i + h
            at = pl.ds(pl.multiple_of(place * rows, 128), rows)
            grad = p[i].astype(F32) + q[i].astype(F32)
            grad = jnp.where(gate_ref[:, at].astype(F32) > 0, grad, 0.0).astype(BF)
            d = lax.dot_general(lhs_ref[:, at], grad, NT, preferred_element_type=F32)
            acc = d if acc is None else acc + d
    out_ref[...] = acc


def last_grads(me, gate, lhs, parts, after):
    count, total = lhs.shape
    mine = gate.shape[0]
    args = (gate, lhs, *parts)
    whole = lambda shape: block(shape, lambda h, me: (0,) * len(shape))
    spec = pltpu.PrefetchScalarGridSpec(
        num_scalar_prefetch=1,
        grid=(1,),
        in_specs=[whole(x.shape) for x in args] + [pl.BlockSpec(memory_space=pl.ANY)],
        out_specs=whole((count, mine)),
    )
    return pl.pallas_call(
        last_kernel,
        grid_spec=spec,
        out_shape=jax.ShapeDtypeStruct((count, mine), F32),
        compiler_params=pltpu.CompilerParams(vmem_limit_bytes=12 * 2**20),
        cost_estimate=pl.CostEstimate(
            flops=total * count * mine, bytes_accessed=2 * 2**20, transcendentals=0
        ),
    )(me, *args, after)


def outputs_kernel(own, other, latent, embed):
    dz = latent.shape[0]
    latent[...] = own[:dz] + other[:dz]
    embed[...] = own[dz:] + other[dz:]


def outputs(own, other, dz):
    count, mine = own.shape
    return pl.pallas_call(
        outputs_kernel,
        out_shape=[jax.ShapeDtypeStruct((c, mine), F32) for c in (dz, count - dz)],
        compiler_params=pltpu.CompilerParams(vmem_limit_bytes=8 * 2**20),
        cost_estimate=pl.CostEstimate(flops=0, bytes_accessed=2**20, transcendentals=0),
    )(own, other)


def tie(first, later):
    return lax.optimization_barrier((first, later))


def eight_by_four(
    records, real_labels, frequencies, class_noise, latents, syn_labels, w_latent, class_embed, w_out
):
    classes, hid = class_embed.shape
    groups = lax.axis_size("rec")
    rec = lax.axis_index("rec")
    feat = lax.axis_index("feat")
    rows, dz = latents.shape
    cols = w_out.shape[1]
    real_total = records.shape[0] * groups
    syn_total = rows * groups
    x, z_low, z_high = rec % 2, (rec // 2) % 2, rec // 4
    place = 2 * x + z_low
    me = jnp.stack([feat, x, z_low, z_high, rec, place]).astype(jnp.int32)

    table = one_hot(syn_labels, classes, BF)
    preact = jnp.dot(latents, w_latent, preferred_element_type=F32) + jnp.dot(
        table, class_embed, preferred_element_type=F32
    )
    hidden = jnp.maximum(preact, 0.0).astype(BF)
    own = jnp.tanh(jnp.dot(hidden, w_out, preferred_element_type=F32)).astype(BF)
    far = swap(own, "feat", 2)

    order = (0, 4, 2, 6, 1, 5, 3, 7)
    label_row = jnp.zeros((16, dz), BF).at[0, :].set(syn_labels.astype(BF))
    packed = jnp.concatenate([latents, label_row], axis=0)[None]
    far, pair = tie(far, swap(packed, "rec", 4))
    images = [own, far, swap(own, "feat", 1), swap(far, "feat", 1)]
    packed, real_labels = tie(jnp.concatenate([packed, pair], axis=0), real_labels)
    pair = swap(packed, "rec", 2)

    masks = (0, 2, 1, 3)
    totals = (real_total, syn_total)
    send_a, keep_a, send_b, keep_b, both, waves, token = feature_sums(
        False, me, real_labels, syn_labels, masks, images, records, frequencies, classes, totals, me
    )
    first_a = swap(send_a, "rec", 1)
    first_b = swap(send_b, "rec", 2)
    pair, token = tie(pair, token)
    last_a, last_b, waves, token = feature_sums(
        True, me, real_labels, syn_labels, masks, both, records, frequencies, classes, totals, token, waves
    )

    send_a, send_b, token = stage_two_send(keep_a, first_a, keep_b, first_b, token)
    got_a = swap(send_a, "rec", 2)
    got_b = swap(send_b, "rec", 1)
    part = frequencies.shape[1] // groups
    noise = lax.dynamic_slice_in_dim(class_noise, (2 * place + z_high) * part, part, 2)
    noise = noise.reshape(classes, 2 * part)
    send, keep, token = stage_three(me, last_a, first_a, got_a, last_b, first_b, got_b, (noise, token, token))
    got = swap(send, "rec", 4)
    pair, token = tie(pair, token)
    quad = jnp.concatenate([packed, pair], axis=0)
    eight = jnp.concatenate([quad, swap(quad, "rec", 1)], axis=0)
    all_latents = eight[:, :rows].reshape(syn_total, dz)
    all_labels = eight[:, rows].reshape(syn_total).astype(jnp.int32)
    all_table = one_hot(all_labels, classes, BF)
    mine = hid // groups
    lhs = jnp.concatenate([all_latents, all_table], axis=1).T
    w = jnp.concatenate(
        [
            lax.dynamic_slice_in_dim(w_latent, rec * mine, mine, 1),
            lax.dynamic_slice_in_dim(class_embed, rec * mine, mine, 1),
        ],
        axis=0,
    )
    all_preact = lax.dot_general(w, lhs, (((0,), (0,)), ((), ())), preferred_element_type=F32)
    all_hidden = jnp.maximum(all_preact, 0.0).astype(BF)
    gate = (all_preact > 0).astype(BF)

    feat_grad = gap_rows(me, keep, got, noise, all_labels.reshape(groups, rows), real_total, order, token)
    feat_grad = lax.all_to_all(feat_grad, "rec", 0, 0, tiled=True)

    send, pre_grad = image_grads(
        me, frequencies, cols, (waves, feat_grad), (gate, all_hidden, lhs)
    )
    near = swap(send, "feat", 1)
    keep = image_grads(me, frequencies, cols, (pre_grad,), (), 0)
    far = swap(first_add(keep, near), "feat", 2)
    keep = image_grads(me, frequencies, cols, (pre_grad,), (), 1)
    out_grad = out_grads(keep, near, far, own)

    by = {0: out_grad}
    by[4] = swap(out_grad, "rec", 4)
    by[2] = swap(out_grad, "rec", 2)
    by[1] = swap(out_grad, "rec", 1)
    by[2], by[1] = tie(by[2], by[1])
    by[3] = swap(by[2], "rec", 1)
    by[6] = swap(by[4], "rec", 2)
    by[5] = swap(by[4], "rec", 1)

    def reduced(send, keep):
        part = add(keep, swap(send, "feat", 1), BF)
        return [part, swap(part, "feat", 2)]

    by[7] = swap(by[6], "rec", 1)
    send, keep = hidden_grads(me, w_out, [by[i] for i in range(4)], mine, by[5])
    parts = reduced(send, keep)
    parts += reduced(*hidden_grads(me, w_out, [by[4 + i] for i in range(4)], mine, parts[0]))
    grad_w_out, token = weight_grads(me, all_hidden, [by[mask] for mask in order])
    grads = last_grads(me, gate, lhs, parts, token)
    grad_w_latent, grad_embed = outputs(grads, swap(grads, "feat", 1), dz)
    return grad_w_out, grad_w_latent, grad_embed


def solution(mesh):
    shape = (mesh.shape["rec"], mesh.shape["feat"])
    in_specs = (
        P("rec", None),
        P("rec"),
        P(None, "feat"),
        P(None, None, "feat"),
        P("rec", None),
        P("rec"),
        P(),
        P(),
        P(None, "feat"),
    )
    out_specs = (P("rec", "feat"), P(None, "rec"), P(None, "rec"))
    return jax.shard_map(
        eight_by_four if shape == (8, 4) else general, mesh=mesh, in_specs=in_specs, out_specs=out_specs, check_vma=False
    )
```

```python
import functools

import jax
import jax.numpy as jnp
from jax import lax
from jax.experimental import pallas as pl
from jax.experimental.pallas import tpu as pltpu
from jax.sharding import PartitionSpec as P

BF = jnp.bfloat16
F32 = jnp.float32

TURN = 0.15915494309189535
SIN = (4.44286783702217, -7.307441307726672, 3.59477116396636, -0.7843353598850176)
COS = (1.4142134962552275, -6.978850948563815, 5.739460376907241, -1.883557905986894, 0.3106880275267554)


def cos_sin(x):
    turns = x * TURN
    u = turns - jnp.round(turns)
    sq = u * u
    p = SIN[-1]
    for c in SIN[-2::-1]:
        p = p * sq + c
    q = COS[-1]
    for c in COS[-2::-1]:
        q = q * sq + c
    s = u * p
    return 1.0 - s * s, s * q


def one_hot(labels, count, dtype):
    return (labels[:, None] == jnp.arange(count, dtype=jnp.int32)[None, :]).astype(dtype)


def real_kernel(rows, labels_ref, records_ref, freq_ref, out_ref, table_ref):
    total = records_ref.shape[0]
    classes = table_ref.shape[0]
    owners, _, width = out_ref.shape
    part = width // 2

    @pl.when(pl.program_id(0) == 0)
    def _():
        ids = lax.broadcasted_iota(jnp.int32, (classes, total), 0)
        table_ref[...] = jnp.where(ids == labels_ref[...], 1.0, 0.0).astype(BF)

    freq = freq_ref[...]
    block = freq.shape[1]

    def sums(i, pre):
        co, si = cos_sin(pre)
        phi = jnp.concatenate([co.astype(BF), si.astype(BF)], axis=1)
        return jnp.dot(table_ref[:, i * rows : (i + 1) * rows], phi, preferred_element_type=F32)

    acc = None
    before = None
    steps = total // rows
    for i in range(steps + 1):
        pre = None
        if i < steps:
            pre = jnp.dot(records_ref[i * rows : (i + 1) * rows, :], freq, preferred_element_type=F32)
        if i > 0:
            d = sums(i - 1, before)
            acc = d if acc is None else acc + d
        before = pre
    for o in range(owners):
        out_ref[o, :, :part] = acc[:, o * part : (o + 1) * part]
        out_ref[o, :, part:] = acc[:, block + o * part : block + (o + 1) * part]


def real_sums(labels, records, freq, classes, owners):
    m, k = records.shape
    n = freq.shape[1]
    block = min(512, n)
    rows = 512
    part = n // owners
    per = block // part
    return pl.pallas_call(
        functools.partial(real_kernel, rows),
        grid=(n // block,),
        in_specs=[
            pl.BlockSpec((1, m), lambda j: (0, 0)),
            pl.BlockSpec((m, k), lambda j: (0, 0)),
            pl.BlockSpec((k, block), lambda j: (0, j)),
        ],
        out_specs=pl.BlockSpec((per, classes, 2 * part), lambda j: (j, 0, 0)),
        out_shape=jax.ShapeDtypeStruct((owners, classes, 2 * part), F32),
        scratch_shapes=[pltpu.VMEM((classes, m), BF)],
        compiler_params=pltpu.CompilerParams(vmem_limit_bytes=56 * 2**20),
        cost_estimate=pl.CostEstimate(
            flops=2 * m * n * (k + 2 * classes), bytes_accessed=2 * (m * k + k * n), transcendentals=0
        ),
    )(labels.reshape(1, m), records, freq)


def bits_of(n):
    return [1 << b for b in range(n.bit_length() - 1)]


def swap(x, axis, bit):
    n = lax.axis_size(axis)
    return lax.ppermute(x, axis, [(i, i ^ bit) for i in range(n)])


def pick(x, index, dim):
    return lax.dynamic_index_in_dim(x, index, dim, keepdims=False)


def halving(x, axis, order, count):
    me = lax.axis_index(axis)
    nbits = len(order)
    x = x.reshape((2,) * nbits + x.shape[1:])
    left = sorted(order, reverse=True)
    for bit in order:
        dim = left.index(bit)
        left.remove(bit)
        mine = (me // bit) % 2
        got = swap(pick(x, 1 - mine, dim).astype(BF), axis, bit)
        x = pick(x, mine, dim).astype(F32) + got.astype(F32)
    return x


def general(
    records, real_labels, frequencies, class_noise, latents, syn_labels, w_latent, class_embed, w_out
):
    classes = class_embed.shape[0]
    hid = class_embed.shape[1]
    groups = lax.axis_size("rec")
    feats = lax.axis_size("feat")
    rec = lax.axis_index("rec")
    nf = frequencies.shape[1]
    part = nf // groups
    rows, dz = latents.shape
    cols = w_out.shape[1]
    real_total = records.shape[0] * groups
    syn_total = rows * groups

    label_row = jnp.zeros((16, dz), BF).at[0, :].set(syn_labels.astype(BF))
    packed = jnp.concatenate([latents, label_row], axis=0)
    packed = lax.all_to_all(
        jnp.broadcast_to(packed[None], (groups,) + packed.shape), "rec", 0, 0, tiled=True
    )
    all_latents = packed[:, :rows].reshape(syn_total, dz)
    all_labels = packed[:, rows].reshape(syn_total).astype(jnp.int32)
    all_table = one_hot(all_labels, classes, BF)

    table = one_hot(syn_labels, classes, BF)
    preact = jnp.dot(latents, w_latent, preferred_element_type=F32) + jnp.dot(
        table, class_embed, preferred_element_type=F32
    )
    hidden = jnp.maximum(preact, 0.0).astype(BF)
    own_images = jnp.tanh(jnp.dot(hidden, w_out, preferred_element_type=F32)).astype(BF)
    images = lax.all_gather(own_images, "feat", axis=0)
    images = images.transpose(1, 0, 2).reshape(rows, feats * cols)
    syn_pre = jnp.dot(images, frequencies, preferred_element_type=F32)
    syn_cos, syn_sin = cos_sin(syn_pre)
    syn_phi = jnp.concatenate(
        [syn_cos.reshape(rows, groups, part), syn_sin.reshape(rows, groups, part)], axis=2
    ).astype(BF)
    syn_sum = lax.dot_general(
        table, syn_phi.reshape(rows, 2 * nf), (((0,), (0,)), ((), ())), preferred_element_type=F32
    )
    syn_sum = syn_sum.reshape(classes, groups, 2 * part).transpose(1, 0, 2)

    real_sum = real_sums(real_labels, records, frequencies, classes, groups)
    gap = syn_sum * (1.0 / syn_total) - real_sum * (1.0 / real_total)
    half = classes // 2
    order = bits_of(groups)
    other = [order[1], order[0]] + order[2:]
    gap = jnp.concatenate(
        [halving(gap[:, :half], "rec", order, groups), halving(gap[:, half:], "rec", other, groups)], axis=0
    )
    noise = lax.dynamic_slice_in_dim(class_noise, rec * part, part, 2).reshape(classes, 2 * part)
    gap = (16.0 * (gap - noise * (1.0 / real_total))).astype(BF)

    feat_grad = jnp.dot(all_table, gap, preferred_element_type=F32).astype(BF)
    feat_grad = lax.all_to_all(feat_grad.reshape(groups, rows, 2 * part), "rec", 0, 0, tiled=True)
    feat_grad = feat_grad.transpose(1, 0, 2).astype(F32)
    pre_grad = (
        -syn_sin.reshape(rows, groups, part) * feat_grad[:, :, :part]
        + syn_cos.reshape(rows, groups, part) * feat_grad[:, :, part:]
    )
    pre_grad = pre_grad.astype(BF).reshape(rows, nf)
    image_grad = lax.dot_general(
        frequencies, pre_grad, (((1,), (1,)), ((), ())), preferred_element_type=F32
    )
    image_grad = halving(image_grad.reshape(feats, cols, rows), "feat", bits_of(feats), feats)
    image_grad = image_grad.T
    out_grad = (image_grad * (1.0 - jnp.square(own_images.astype(F32)))).astype(BF)

    out_grad = lax.all_to_all(
        jnp.broadcast_to(out_grad[None], (groups, rows, cols)), "rec", 0, 0, tiled=True
    ).reshape(syn_total, cols)

    mine = hid // groups
    start = rec * mine
    all_preact = jnp.dot(
        all_latents, lax.dynamic_slice_in_dim(w_latent, start, mine, 1), preferred_element_type=F32
    ) + jnp.dot(
        all_table, lax.dynamic_slice_in_dim(class_embed, start, mine, 1), preferred_element_type=F32
    )
    all_hidden = jnp.maximum(all_preact, 0.0).astype(BF)
    grad_w_out = lax.dot_general(
        all_hidden, out_grad, (((0,), (0,)), ((), ())), preferred_element_type=F32
    )
    hidden_grad = lax.dot_general(
        out_grad,
        lax.dynamic_slice_in_dim(w_out, start, mine, 0),
        (((1,), (1,)), ((), ())),
        preferred_element_type=F32,
    )
    core = lax.axis_index("feat") % 2
    half = syn_total // 2
    hidden_grad = hidden_grad.reshape(2, half, mine)
    got = swap(pick(hidden_grad, 1 - core, 0).astype(BF), "feat", 1)
    hidden_grad = pick(hidden_grad, core, 0) + got.astype(F32)
    for bit in bits_of(feats)[1:]:
        send = hidden_grad.astype(BF)
        hidden_grad = send.astype(F32) + swap(send, "feat", bit).astype(F32)
    my_preact = lax.dynamic_slice_in_dim(all_preact, core * half, half, 0)
    pre_hidden = jnp.where(my_preact > 0, hidden_grad, 0.0).astype(BF)
    lhs = jnp.concatenate([all_latents, all_table], axis=1)
    lhs = lax.dynamic_slice_in_dim(lhs, core * half, half, 0)
    grads = lax.dot_general(lhs, pre_hidden, (((0,), (0,)), ((), ())), preferred_element_type=F32)
    grads = grads + swap(grads, "feat", 1)
    return grad_w_out, grads[:dz], grads[dz:]


def block(shape, index):
    return pl.BlockSpec(shape, index)


def sums(table, pre):
    co, si = cos_sin(pre)
    phi = jnp.concatenate([co.astype(BF), si.astype(BF)], axis=1)
    return jnp.dot(table, phi, preferred_element_type=F32)


def features_kernel(
    masks, last, real_total, syn_total, me_ref, real_labels_ref, syn_labels_ref, *refs
):
    count = 1 if last else len(masks)
    images = [refs[0].at[i] for i in range(len(masks))] if last else refs[:count]
    records_hbm, freq_ref = refs[count : count + 2]
    outs = refs[count + (4 if last else 3) : -4]
    wave, token = outs[-2:]
    records, real_table, syn_table, sem = refs[-4:]
    classes, total = real_table.shape
    size = 512
    steps = total // size
    step = pl.program_id(0)
    cols = images[0].shape[1]
    half = classes // 2
    token[...] = jnp.zeros_like(token)

    def copy(i):
        at = pl.ds(i * size, size)
        return pltpu.make_async_copy(records_hbm.at[at, :], records.at[at, :], sem.at[i])

    def work(wait):
        if wait:
            for i in range(steps):
                copy(i).start()
            ids = lax.broadcasted_iota(jnp.int32, (classes, total), 0)
            real_table[...] = jnp.where(ids == real_labels_ref[...], 1.0, 0.0).astype(BF)
            ids = lax.broadcasted_iota(jnp.int32, syn_table.shape, 0)
            syn_table[...] = jnp.where(ids == syn_labels_ref[...], 1.0, 0.0).astype(BF)
        syn_pre = None
        for mask, image in zip(masks, images):
            at = pl.multiple_of((me_ref[0] ^ mask) * cols, 128)
            d = jnp.dot(image[...], freq_ref[pl.ds(at, cols), :], preferred_element_type=F32)
            syn_pre = d if syn_pre is None else syn_pre + d
        freq = freq_ref[...]
        acc = None
        before = None
        for i in range(steps + 1):
            if i < steps:
                if wait:
                    copy(i).wait()
                pre = jnp.dot(records[i * size : (i + 1) * size, :], freq, preferred_element_type=F32)
            if i == 0:
                co, si = cos_sin(syn_pre)
                wave[0, 0] = co
                wave[0, 1] = si
                phi = jnp.concatenate([co.astype(BF), si.astype(BF)], axis=1)
                syn = jnp.dot(syn_table[...], phi, preferred_element_type=F32)
            else:
                d = sums(real_table[:, (i - 1) * size : i * size], before)
                acc = d if acc is None else acc + d
            before = pre
        gap = syn * (1.0 / syn_total) - acc * (1.0 / real_total)
        width = gap.shape[1] // 4
        return [
            jnp.concatenate(
                [gap[:, h * width : (h + 1) * width], gap[:, (h + 2) * width : (h + 3) * width]], axis=1
            )
            for h in range(2)
        ]

    if last:
        parts = work(True)
        for h in range(2):
            outs[0][h] = parts[h][:half]
            outs[1][h] = parts[h][half:]
        return
    send_a, keep_a, send_b, keep_b, both = outs[:5]

    @pl.when(step == 0)
    def _():
        for i in range(count):
            both[i] = images[i][...]
        parts = work(True)
        for h in range(2):
            send_a[0, h] = parts[h][:half].astype(BF)
            send_b[0, h] = parts[h][half:].astype(BF)

    @pl.when(step > 0)
    def _():
        parts = work(False)

        @pl.when(step == 1)
        def _():
            for h in range(2):
                send_a[0, h] = parts[h][:half].astype(BF)
                keep_b[h] = parts[h][half:]

        @pl.when(step == 2)
        def _():
            for h in range(2):
                keep_a[h] = parts[h][:half]
                send_b[0, h] = parts[h][half:].astype(BF)


def feature_sums(
    last, me, real_labels, syn_labels, masks, images, records, freq, classes, totals, after, waves=None
):
    total, k = records.shape
    n = freq.shape[1]
    rows, cols = images.shape[1:] if last else images[0].shape
    half = classes // 2
    tile = n // 4
    tiles = 1 if last else 3
    whole = lambda shape: block(shape, lambda j, me: (0,) * len(shape))
    kept = jax.ShapeDtypeStruct((2, half, tile), F32)
    sent = jax.ShapeDtypeStruct((2, 2, half, tile), BF)
    both = (len(masks), rows, cols)
    place = lambda j, me: me[5] ^ (0 if last else 3 - j)
    anywhere = pl.BlockSpec(memory_space=pl.ANY)
    shapes = [pltpu.HBM((4, 2, rows, tile), F32), jax.ShapeDtypeStruct((8, 128), F32)]
    specs = [block((1, 2, rows, tile), lambda j, me: (place(j, me), 0, 0, 0)), whole((8, 128))]
    if last:
        shapes = [kept, kept] + shapes
        specs = [whole(kept.shape), whole(kept.shape)] + specs
        images = (images,)
        extra = (after, waves)
    else:
        shapes = [sent, kept, sent, kept, jax.ShapeDtypeStruct(both, BF)] + shapes
        specs = [
            block((1, 2, half, tile), lambda j, me: (jnp.minimum(j, 1), 0, 0, 0)),
            whole(kept.shape),
            block((1, 2, half, tile), lambda j, me: (j // 2, 0, 0, 0)),
            whole(kept.shape),
            whole(both),
        ] + specs
        extra = (after,)
    grid_spec = pltpu.PrefetchScalarGridSpec(
        num_scalar_prefetch=1,
        grid=(tiles,),
        in_specs=[whole((1, total)), whole((1, rows))]
        + [whole(image.shape) for image in images]
        + [anywhere, block((k, tile), lambda j, me: (0, place(j, me)))]
        + [anywhere] * len(extra),
        out_specs=specs,
        scratch_shapes=[
            pltpu.VMEM((total, k), BF),
            pltpu.VMEM((classes, total), BF),
            pltpu.VMEM((classes, rows), BF),
            pltpu.SemaphoreType.DMA((total // 512,)),
        ],
    )
    return pl.pallas_call(
        functools.partial(features_kernel, masks, last, *totals),
        grid_spec=grid_spec,
        out_shape=shapes,
        input_output_aliases={7: 2} if last else {},
        compiler_params=pltpu.CompilerParams(vmem_limit_bytes=44 * 2**20),
        cost_estimate=pl.CostEstimate(
            flops=2 * (total + rows) * tiles * tile * (k + 2 * classes),
            bytes_accessed=2 * (total * k + k * tiles * tile),
            transcendentals=0,
        ),
    )(me, real_labels.reshape(1, -1), syn_labels.reshape(1, -1), *images, records, freq, *extra)


def stage_two_send_kernel(ka, ga, kb, gb, after, sa, sb, token):
    token[...] = jnp.zeros_like(token)
    sa[...] = (ka[...] + ga[0].astype(F32)).astype(BF)
    sb[...] = (kb[...] + gb[0].astype(F32)).astype(BF)


def stage_two_send(keep_a, got_a, keep_b, got_b, after):
    return pl.pallas_call(
        stage_two_send_kernel,
        in_specs=[pl.BlockSpec()] * 4 + [pl.BlockSpec(memory_space=pl.ANY)],
        out_shape=[jax.ShapeDtypeStruct(keep_a.shape, BF)] * 2 + [jax.ShapeDtypeStruct((8, 128), F32)],
        compiler_params=pltpu.CompilerParams(vmem_limit_bytes=10 * 2**20),
        cost_estimate=pl.CostEstimate(flops=0, bytes_accessed=3 * 2**20, transcendentals=0),
    )(keep_a, got_a, keep_b, got_b, after)


def stage_three_kernel(me_ref, na, fa, ga, nb, fb, gb, a, b, c, send, keep, token):
    token[...] = jnp.zeros_like(token)
    high = me_ref[3]
    half = na.shape[1]
    for flip, out in ((1, send), (0, keep)):
        at = high ^ flip
        out[:half] = (na[at] + fa[1, at].astype(F32) + ga[at].astype(F32)).astype(out.dtype)
        out[half:] = (nb[at] + fb[1, at].astype(F32) + gb[at].astype(F32)).astype(out.dtype)


def stage_three(me, keep_a, first_a, got_a, keep_b, first_b, got_b, after):
    _, half, width = keep_a.shape
    args = (keep_a, first_a, got_a, keep_b, first_b, got_b)
    whole = lambda shape: block(shape, lambda h, me: (0,) * len(shape))
    spec = pltpu.PrefetchScalarGridSpec(
        num_scalar_prefetch=1,
        grid=(1,),
        in_specs=[whole(x.shape) for x in args] + [pl.BlockSpec(memory_space=pl.ANY)] * 3,
        out_specs=[whole((2 * half, width))] * 2 + [whole((8, 128))],
    )
    return pl.pallas_call(
        stage_three_kernel,
        grid_spec=spec,
        out_shape=[jax.ShapeDtypeStruct((2 * half, width), t) for t in (BF, F32)]
        + [jax.ShapeDtypeStruct((8, 128), F32)],
        compiler_params=pltpu.CompilerParams(vmem_limit_bytes=12 * 2**20),
        cost_estimate=pl.CostEstimate(flops=0, bytes_accessed=3 * 2**20, transcendentals=0),
    )(me, *args, *after)


def gap_kernel(real_total, order, me_ref, keep_ref, got_ref, noise_ref, labels_ref, after, out_ref):
    classes = keep_ref.shape[0]
    rows = labels_ref.shape[1]
    gap = keep_ref[...] + got_ref[...].astype(F32) - noise_ref[...] * (1.0 / real_total)
    gap = (16.0 * gap).astype(BF)
    ids = lax.broadcasted_iota(jnp.int32, (classes, rows), 0)
    for i, mask in enumerate(order):
        table = jnp.where(ids == labels_ref[i : i + 1, :], 1.0, 0.0).astype(BF)
        out = lax.dot_general(table, gap, (((0,), (0,)), ((), ())), preferred_element_type=F32)
        out_ref[me_ref[4] ^ mask] = out.astype(BF)


def gap_rows(me, keep, got, noise, labels, real_total, order, after):
    classes, width = keep.shape
    groups, rows = labels.shape
    whole = lambda shape: block(shape, lambda h, me: (0,) * len(shape))
    spec = pltpu.PrefetchScalarGridSpec(
        num_scalar_prefetch=1,
        grid=(1,),
        in_specs=[whole(x.shape) for x in (keep, got, noise, labels)]
        + [pl.BlockSpec(memory_space=pl.ANY)],
        out_specs=whole((groups, rows, width)),
    )
    return pl.pallas_call(
        functools.partial(gap_kernel, real_total, order),
        grid_spec=spec,
        out_shape=jax.ShapeDtypeStruct((groups, rows, width), BF),
        compiler_params=pltpu.CompilerParams(vmem_limit_bytes=14 * 2**20),
        cost_estimate=pl.CostEstimate(
            flops=2 * groups * rows * classes * width, bytes_accessed=3 * 2**20, transcendentals=0
        ),
    )(me, keep, got, noise, labels, after)


NT = (((1,), (1,)), ((), ()))


def sent_kernel(me_ref, wave_ref, rows_ref, freq_ref, a, b, c, send_ref, pre_ref):
    tile = wave_ref.shape[3]
    part = tile // 2

    @pl.when(pl.program_id(0) == 0)
    def _():
        for place in range(4):
            for h in range(2):
                grad = rows_ref[4 * h + 2 * (place % 2) + place // 2].astype(F32)
                lanes = slice(h * part, (h + 1) * part)
                pre = wave_ref[place, 0, :, lanes] * grad[:, part:]
                pre = pre - wave_ref[place, 1, :, lanes] * grad[:, :part]
                at = place * tile + h * part
                pre_ref[:, at : at + part] = pre.astype(BF)

    out = lax.dot_general(freq_ref[...], pre_ref[...], NT, preferred_element_type=F32)
    send_ref[0] = out.astype(BF)


def kept_kernel(me_ref, pre_ref, freq_ref, keep_ref):
    keep_ref[0] = lax.dot_general(freq_ref[...], pre_ref[...], NT, preferred_element_type=F32)


def image_grads(me, freq, cols, arrays, after, kept=None):
    k, n = freq.shape
    sent = kept is None
    rows = arrays[1].shape[1] if sent else arrays[0].shape[0]
    count = 2
    whole = lambda shape: block(shape, lambda s, me: (0,) * len(shape))

    def source(s, me):
        return (me[0] ^ (2 * (1 - s)) ^ 1, 0) if sent else (2 * (me[0] ^ (2 * (1 - kept))) + s, 0)

    size = cols if sent else cols // 2
    out = block((1, size, rows), (lambda s, me: (s, 0, 0)) if sent else (lambda s, me: (0, s, 0)))
    shape = jax.ShapeDtypeStruct((2 if sent else 1, cols, rows), BF if sent else F32)
    pre = jax.ShapeDtypeStruct((rows, n), BF)
    spec = pltpu.PrefetchScalarGridSpec(
        num_scalar_prefetch=1,
        grid=(count,),
        in_specs=[whole(x.shape) for x in arrays]
        + [block((size, n), source)]
        + [pl.BlockSpec(memory_space=pl.ANY)] * len(after),
        out_specs=[out, whole(pre.shape)] if sent else out,
    )
    return pl.pallas_call(
        sent_kernel if sent else kept_kernel,
        grid_spec=spec,
        out_shape=[shape, pre] if sent else shape,
        compiler_params=pltpu.CompilerParams(vmem_limit_bytes=52 * 2**20),
        cost_estimate=pl.CostEstimate(flops=k * n * rows, bytes_accessed=k * n, transcendentals=0),
    )(me, *arrays, freq, *after)


def first_add_kernel(a, b, out):
    out[...] = (a[0] + b[0].astype(F32)).astype(BF)


def first_add(keep, got):
    _, cols, rows = keep.shape
    one = block((1, cols, rows), lambda h: (0, 0, 0))
    return pl.pallas_call(
        first_add_kernel,
        grid=(1,),
        in_specs=[one, one],
        out_specs=block((cols, rows), lambda h: (0, 0)),
        out_shape=jax.ShapeDtypeStruct((cols, rows), BF),
        compiler_params=pltpu.CompilerParams(vmem_limit_bytes=8 * 2**20),
        cost_estimate=pl.CostEstimate(flops=0, bytes_accessed=2**20, transcendentals=0),
    )(keep, got)


def out_kernel(keep, near, far, image, out):
    grad = (keep[0] + near[0].astype(F32) + far[...].astype(F32)).T
    grad = grad * (1.0 - jnp.square(image[...].astype(F32)))
    out[...] = grad.astype(BF)


def out_grads(keep, near, far, image):
    _, cols, rows = keep.shape
    one = lambda i: block((1, cols, rows), lambda h: (i, 0, 0))
    return pl.pallas_call(
        out_kernel,
        grid=(1,),
        in_specs=[one(0), one(1), block((cols, rows), lambda h: (0, 0)), block((rows, cols), lambda h: (0, 0))],
        out_specs=block((rows, cols), lambda h: (0, 0)),
        out_shape=jax.ShapeDtypeStruct(image.shape, BF),
        compiler_params=pltpu.CompilerParams(vmem_limit_bytes=8 * 2**20),
        cost_estimate=pl.CostEstimate(flops=0, bytes_accessed=2**20, transcendentals=0),
    )(keep, near, far, image)


def hidden_kernel(me_ref, w_ref, *refs):
    grads = refs[:4]
    send, keep = refs[5:]
    core = me_ref[0] % 2
    out = [lax.dot_general(w_ref[...], g[...], NT, preferred_element_type=F32) for g in grads]
    for i in range(2):
        keep[i] = jnp.where(core == 0, out[2 * i], out[2 * i + 1])
        send[i] = jnp.where(core == 0, out[2 * i + 1], out[2 * i]).astype(BF)


def hidden_grads(me, w_out, grads, mine, after):
    rows, cols = grads[0].shape
    whole = lambda shape: block(shape, lambda r, me: (0,) * len(shape))
    spec = pltpu.PrefetchScalarGridSpec(
        num_scalar_prefetch=1,
        grid=(1,),
        in_specs=[block((mine, cols), lambda r, me: (me[4], 0))] + [whole((rows, cols))] * 4
        + [pl.BlockSpec(memory_space=pl.ANY)],
        out_specs=[whole((2, mine, rows))] * 2,
    )
    return pl.pallas_call(
        hidden_kernel,
        grid_spec=spec,
        out_shape=[jax.ShapeDtypeStruct((2, mine, rows), t) for t in (BF, F32)],
        compiler_params=pltpu.CompilerParams(vmem_limit_bytes=8 * 2**20),
        cost_estimate=pl.CostEstimate(
            flops=8 * mine * cols * rows, bytes_accessed=2 * 5 * mine * cols, transcendentals=0
        ),
    )(me, w_out, *grads, after)


def add_kernel(a, b, out):
    out[...] = (a[...].astype(F32) + b[...].astype(F32)).astype(out.dtype)


def add(a, b, kind):
    return pl.pallas_call(
        add_kernel,
        out_shape=jax.ShapeDtypeStruct(a.shape, kind),
        compiler_params=pltpu.CompilerParams(vmem_limit_bytes=8 * 2**20),
        cost_estimate=pl.CostEstimate(flops=0, bytes_accessed=2**20, transcendentals=0),
    )(a, b)


def weight_kernel(me_ref, hidden_ref, *refs):
    out_ref, token = refs[-2:]
    token[...] = jnp.zeros_like(token)
    acc = None
    for mask, grad in enumerate(refs[:-2]):
        rows = grad.shape[0]
        at = slice(mask * rows, (mask + 1) * rows)
        d = jnp.dot(hidden_ref[:, at], grad[...], preferred_element_type=F32)
        acc = d if acc is None else acc + d
    out_ref[...] = acc


def weight_grads(me, hidden, grads):
    rows, cols = grads[0].shape
    mine, total = hidden.shape
    spec = pltpu.PrefetchScalarGridSpec(
        num_scalar_prefetch=1,
        grid=(1,),
        in_specs=[block((mine, total), lambda h, me: (0, 0))]
        + [block((rows, cols), lambda h, me: (0, 0)) for _ in grads],
        out_specs=[block((mine, cols), lambda h, me: (0, 0)), block((8, 128), lambda h, me: (0, 0))],
    )
    return pl.pallas_call(
        weight_kernel,
        grid_spec=spec,
        out_shape=[pltpu.HBM((mine, cols), F32), jax.ShapeDtypeStruct((8, 128), F32)],
        compiler_params=pltpu.CompilerParams(vmem_limit_bytes=12 * 2**20),
        cost_estimate=pl.CostEstimate(
            flops=2 * mine * total * cols, bytes_accessed=4 * 2**20, transcendentals=0
        ),
    )(me, hidden, *grads)


def last_kernel(me_ref, gate_ref, lhs_ref, p0, q0, p1, q1, after, out_ref):
    rows = p0.shape[2]
    acc = None
    for h, (p, q) in enumerate(((p0, q0), (p1, q1))):
        for i in range(2):
            place = 4 * (me_ref[0] % 2) + 2 * i + h
            at = pl.ds(pl.multiple_of(place * rows, 128), rows)
            grad = p[i].astype(F32) + q[i].astype(F32)
            grad = jnp.where(gate_ref[:, at].astype(F32) > 0, grad, 0.0).astype(BF)
            d = lax.dot_general(lhs_ref[:, at], grad, NT, preferred_element_type=F32)
            acc = d if acc is None else acc + d
    out_ref[...] = acc


def last_grads(me, gate, lhs, parts, after):
    count, total = lhs.shape
    mine = gate.shape[0]
    args = (gate, lhs, *parts)
    whole = lambda shape: block(shape, lambda h, me: (0,) * len(shape))
    spec = pltpu.PrefetchScalarGridSpec(
        num_scalar_prefetch=1,
        grid=(1,),
        in_specs=[whole(x.shape) for x in args] + [pl.BlockSpec(memory_space=pl.ANY)],
        out_specs=whole((count, mine)),
    )
    return pl.pallas_call(
        last_kernel,
        grid_spec=spec,
        out_shape=jax.ShapeDtypeStruct((count, mine), F32),
        compiler_params=pltpu.CompilerParams(vmem_limit_bytes=12 * 2**20),
        cost_estimate=pl.CostEstimate(
            flops=total * count * mine, bytes_accessed=2 * 2**20, transcendentals=0
        ),
    )(me, *args, after)


def outputs_kernel(own, other, latent, embed):
    dz = latent.shape[0]
    latent[...] = own[:dz] + other[:dz]
    embed[...] = own[dz:] + other[dz:]


def outputs(own, other, dz):
    count, mine = own.shape
    return pl.pallas_call(
        outputs_kernel,
        out_shape=[jax.ShapeDtypeStruct((c, mine), F32) for c in (dz, count - dz)],
        compiler_params=pltpu.CompilerParams(vmem_limit_bytes=8 * 2**20),
        cost_estimate=pl.CostEstimate(flops=0, bytes_accessed=2**20, transcendentals=0),
    )(own, other)


def tie(first, later):
    return lax.optimization_barrier((first, later))


def eight_by_four(
    records, real_labels, frequencies, class_noise, latents, syn_labels, w_latent, class_embed, w_out
):
    classes, hid = class_embed.shape
    groups = lax.axis_size("rec")
    rec = lax.axis_index("rec")
    feat = lax.axis_index("feat")
    rows, dz = latents.shape
    cols = w_out.shape[1]
    real_total = records.shape[0] * groups
    syn_total = rows * groups
    x, z_low, z_high = rec % 2, (rec // 2) % 2, rec // 4
    place = 2 * x + z_low
    me = jnp.stack([feat, x, z_low, z_high, rec, place]).astype(jnp.int32)

    table = one_hot(syn_labels, classes, BF)
    preact = jnp.dot(latents, w_latent, preferred_element_type=F32) + jnp.dot(
        table, class_embed, preferred_element_type=F32
    )
    hidden = jnp.maximum(preact, 0.0).astype(BF)
    own = jnp.tanh(jnp.dot(hidden, w_out, preferred_element_type=F32)).astype(BF)
    far = swap(own, "feat", 2)

    order = (0, 4, 2, 6, 1, 5, 3, 7)
    label_row = jnp.zeros((16, dz), BF).at[0, :].set(syn_labels.astype(BF))
    packed = jnp.concatenate([latents, label_row], axis=0)[None]
    far, pair = tie(far, swap(packed, "rec", 4))
    images = [own, far, swap(own, "feat", 1), swap(far, "feat", 1)]
    packed, real_labels = tie(jnp.concatenate([packed, pair], axis=0), real_labels)
    pair = swap(packed, "rec", 2)

    masks = (0, 2, 1, 3)
    totals = (real_total, syn_total)
    send_a, keep_a, send_b, keep_b, both, waves, token = feature_sums(
        False, me, real_labels, syn_labels, masks, images, records, frequencies, classes, totals, me
    )
    first_a = swap(send_a, "rec", 1)
    first_b = swap(send_b, "rec", 2)
    pair, token = tie(pair, token)
    last_a, last_b, waves, token = feature_sums(
        True, me, real_labels, syn_labels, masks, both, records, frequencies, classes, totals, token, waves
    )

    send_a, send_b, token = stage_two_send(keep_a, first_a, keep_b, first_b, token)
    got_a = swap(send_a, "rec", 2)
    got_b = swap(send_b, "rec", 1)
    part = frequencies.shape[1] // groups
    noise = lax.dynamic_slice_in_dim(class_noise, (2 * place + z_high) * part, part, 2)
    noise = noise.reshape(classes, 2 * part)
    send, keep, token = stage_three(me, last_a, first_a, got_a, last_b, first_b, got_b, (noise, token, token))
    got = swap(send, "rec", 4)
    pair, token = tie(pair, token)
    quad = jnp.concatenate([packed, pair], axis=0)
    eight = jnp.concatenate([quad, swap(quad, "rec", 1)], axis=0)
    all_latents = eight[:, :rows].reshape(syn_total, dz)
    all_labels = eight[:, rows].reshape(syn_total).astype(jnp.int32)
    all_table = one_hot(all_labels, classes, BF)
    mine = hid // groups
    lhs = jnp.concatenate([all_latents, all_table], axis=1).T
    w = jnp.concatenate(
        [
            lax.dynamic_slice_in_dim(w_latent, rec * mine, mine, 1),
            lax.dynamic_slice_in_dim(class_embed, rec * mine, mine, 1),
        ],
        axis=0,
    )
    all_preact = lax.dot_general(w, lhs, (((0,), (0,)), ((), ())), preferred_element_type=F32)
    all_hidden = jnp.maximum(all_preact, 0.0).astype(BF)
    gate = (all_preact > 0).astype(BF)

    feat_grad = gap_rows(me, keep, got, noise, all_labels.reshape(groups, rows), real_total, order, token)
    feat_grad = lax.all_to_all(feat_grad, "rec", 0, 0, tiled=True)

    send, pre_grad = image_grads(
        me, frequencies, cols, (waves, feat_grad), (gate, all_hidden, lhs)
    )
    near = swap(send, "feat", 1)
    keep = image_grads(me, frequencies, cols, (pre_grad,), (), 0)
    far = swap(first_add(keep, near), "feat", 2)
    keep = image_grads(me, frequencies, cols, (pre_grad,), (), 1)
    out_grad = out_grads(keep, near, far, own)

    by = {0: out_grad}
    by[4] = swap(out_grad, "rec", 4)
    by[2] = swap(out_grad, "rec", 2)
    by[1] = swap(out_grad, "rec", 1)
    by[2], by[1] = tie(by[2], by[1])
    by[3] = swap(by[2], "rec", 1)
    by[6] = swap(by[4], "rec", 2)
    by[5] = swap(by[4], "rec", 1)

    def reduced(send, keep):
        part = add(keep, swap(send, "feat", 1), BF)
        return [part, swap(part, "feat", 2)]

    by[7] = swap(by[6], "rec", 1)
    send, keep = hidden_grads(me, w_out, [by[i] for i in range(4)], mine, by[5])
    parts = reduced(send, keep)
    parts += reduced(*hidden_grads(me, w_out, [by[4 + i] for i in range(4)], mine, parts[0]))
    grad_w_out, token = weight_grads(me, all_hidden, [by[mask] for mask in order])
    grads = last_grads(me, gate, lhs, parts, token)
    grad_w_latent, grad_embed = outputs(grads, swap(grads, "feat", 1), dz)
    return grad_w_out, grad_w_latent, grad_embed


def solution(mesh):
    shape = (mesh.shape["rec"], mesh.shape["feat"])
    in_specs = (
        P("rec", None),
        P("rec"),
        P(None, "feat"),
        P(None, None, "feat"),
        P("rec", None),
        P("rec"),
        P(),
        P(),
        P(None, "feat"),
    )
    out_specs = (P("rec", "feat"), P(None, "rec"), P(None, "rec"))
    return jax.shard_map(
        eight_by_four if shape == (8, 4) else general, mesh=mesh, in_specs=in_specs, out_specs=out_specs, check_vma=False
    )
```

```python
import functools

import jax
import jax.numpy as jnp
from jax import lax
from jax.experimental import pallas as pl
from jax.experimental.pallas import tpu as pltpu
from jax.sharding import PartitionSpec as P

BF = jnp.bfloat16
F32 = jnp.float32

TURN = 0.15915494309189535
SIN = (4.44286783702217, -7.307441307726672, 3.59477116396636, -0.7843353598850176)
COS = (1.4142134962552275, -6.978850948563815, 5.739460376907241, -1.883557905986894, 0.3106880275267554)


def cos_sin(x):
    turns = x * TURN
    u = turns - jnp.round(turns)
    sq = u * u
    p = SIN[-1]
    for c in SIN[-2::-1]:
        p = p * sq + c
    q = COS[-1]
    for c in COS[-2::-1]:
        q = q * sq + c
    s = u * p
    return 1.0 - s * s, s * q


def one_hot(labels, count, dtype):
    return (labels[:, None] == jnp.arange(count, dtype=jnp.int32)[None, :]).astype(dtype)


def real_kernel(rows, labels_ref, records_ref, freq_ref, out_ref, table_ref):
    total = records_ref.shape[0]
    classes = table_ref.shape[0]
    owners, _, width = out_ref.shape
    part = width // 2

    @pl.when(pl.program_id(0) == 0)
    def _():
        ids = lax.broadcasted_iota(jnp.int32, (classes, total), 0)
        table_ref[...] = jnp.where(ids == labels_ref[...], 1.0, 0.0).astype(BF)

    freq = freq_ref[...]
    block = freq.shape[1]

    def sums(i, pre):
        co, si = cos_sin(pre)
        phi = jnp.concatenate([co.astype(BF), si.astype(BF)], axis=1)
        return jnp.dot(table_ref[:, i * rows : (i + 1) * rows], phi, preferred_element_type=F32)

    acc = None
    before = None
    steps = total // rows
    for i in range(steps + 1):
        pre = None
        if i < steps:
            pre = jnp.dot(records_ref[i * rows : (i + 1) * rows, :], freq, preferred_element_type=F32)
        if i > 0:
            d = sums(i - 1, before)
            acc = d if acc is None else acc + d
        before = pre
    for o in range(owners):
        out_ref[o, :, :part] = acc[:, o * part : (o + 1) * part]
        out_ref[o, :, part:] = acc[:, block + o * part : block + (o + 1) * part]


def real_sums(labels, records, freq, classes, owners):
    m, k = records.shape
    n = freq.shape[1]
    block = min(512, n)
    rows = 512
    part = n // owners
    per = block // part
    return pl.pallas_call(
        functools.partial(real_kernel, rows),
        grid=(n // block,),
        in_specs=[
            pl.BlockSpec((1, m), lambda j: (0, 0)),
            pl.BlockSpec((m, k), lambda j: (0, 0)),
            pl.BlockSpec((k, block), lambda j: (0, j)),
        ],
        out_specs=pl.BlockSpec((per, classes, 2 * part), lambda j: (j, 0, 0)),
        out_shape=jax.ShapeDtypeStruct((owners, classes, 2 * part), F32),
        scratch_shapes=[pltpu.VMEM((classes, m), BF)],
        compiler_params=pltpu.CompilerParams(vmem_limit_bytes=56 * 2**20),
        cost_estimate=pl.CostEstimate(
            flops=2 * m * n * (k + 2 * classes), bytes_accessed=2 * (m * k + k * n), transcendentals=0
        ),
    )(labels.reshape(1, m), records, freq)


def bits_of(n):
    return [1 << b for b in range(n.bit_length() - 1)]


def swap(x, axis, bit):
    n = lax.axis_size(axis)
    return lax.ppermute(x, axis, [(i, i ^ bit) for i in range(n)])


def pick(x, index, dim):
    return lax.dynamic_index_in_dim(x, index, dim, keepdims=False)


def halving(x, axis, order, count):
    me = lax.axis_index(axis)
    nbits = len(order)
    x = x.reshape((2,) * nbits + x.shape[1:])
    left = sorted(order, reverse=True)
    for bit in order:
        dim = left.index(bit)
        left.remove(bit)
        mine = (me // bit) % 2
        got = swap(pick(x, 1 - mine, dim).astype(BF), axis, bit)
        x = pick(x, mine, dim).astype(F32) + got.astype(F32)
    return x


def general(
    records, real_labels, frequencies, class_noise, latents, syn_labels, w_latent, class_embed, w_out
):
    classes = class_embed.shape[0]
    hid = class_embed.shape[1]
    groups = lax.axis_size("rec")
    feats = lax.axis_size("feat")
    rec = lax.axis_index("rec")
    nf = frequencies.shape[1]
    part = nf // groups
    rows, dz = latents.shape
    cols = w_out.shape[1]
    real_total = records.shape[0] * groups
    syn_total = rows * groups

    label_row = jnp.zeros((16, dz), BF).at[0, :].set(syn_labels.astype(BF))
    packed = jnp.concatenate([latents, label_row], axis=0)
    packed = lax.all_to_all(
        jnp.broadcast_to(packed[None], (groups,) + packed.shape), "rec", 0, 0, tiled=True
    )
    all_latents = packed[:, :rows].reshape(syn_total, dz)
    all_labels = packed[:, rows].reshape(syn_total).astype(jnp.int32)
    all_table = one_hot(all_labels, classes, BF)

    table = one_hot(syn_labels, classes, BF)
    preact = jnp.dot(latents, w_latent, preferred_element_type=F32) + jnp.dot(
        table, class_embed, preferred_element_type=F32
    )
    hidden = jnp.maximum(preact, 0.0).astype(BF)
    own_images = jnp.tanh(jnp.dot(hidden, w_out, preferred_element_type=F32)).astype(BF)
    images = lax.all_gather(own_images, "feat", axis=0)
    images = images.transpose(1, 0, 2).reshape(rows, feats * cols)
    syn_pre = jnp.dot(images, frequencies, preferred_element_type=F32)
    syn_cos, syn_sin = cos_sin(syn_pre)
    syn_phi = jnp.concatenate(
        [syn_cos.reshape(rows, groups, part), syn_sin.reshape(rows, groups, part)], axis=2
    ).astype(BF)
    syn_sum = lax.dot_general(
        table, syn_phi.reshape(rows, 2 * nf), (((0,), (0,)), ((), ())), preferred_element_type=F32
    )
    syn_sum = syn_sum.reshape(classes, groups, 2 * part).transpose(1, 0, 2)

    real_sum = real_sums(real_labels, records, frequencies, classes, groups)
    gap = syn_sum * (1.0 / syn_total) - real_sum * (1.0 / real_total)
    half = classes // 2
    order = bits_of(groups)
    other = [order[1], order[0]] + order[2:]
    gap = jnp.concatenate(
        [halving(gap[:, :half], "rec", order, groups), halving(gap[:, half:], "rec", other, groups)], axis=0
    )
    noise = lax.dynamic_slice_in_dim(class_noise, rec * part, part, 2).reshape(classes, 2 * part)
    gap = (16.0 * (gap - noise * (1.0 / real_total))).astype(BF)

    feat_grad = jnp.dot(all_table, gap, preferred_element_type=F32).astype(BF)
    feat_grad = lax.all_to_all(feat_grad.reshape(groups, rows, 2 * part), "rec", 0, 0, tiled=True)
    feat_grad = feat_grad.transpose(1, 0, 2).astype(F32)
    pre_grad = (
        -syn_sin.reshape(rows, groups, part) * feat_grad[:, :, :part]
        + syn_cos.reshape(rows, groups, part) * feat_grad[:, :, part:]
    )
    pre_grad = pre_grad.astype(BF).reshape(rows, nf)
    image_grad = lax.dot_general(
        frequencies, pre_grad, (((1,), (1,)), ((), ())), preferred_element_type=F32
    )
    image_grad = halving(image_grad.reshape(feats, cols, rows), "feat", bits_of(feats), feats)
    image_grad = image_grad.T
    out_grad = (image_grad * (1.0 - jnp.square(own_images.astype(F32)))).astype(BF)

    out_grad = lax.all_to_all(
        jnp.broadcast_to(out_grad[None], (groups, rows, cols)), "rec", 0, 0, tiled=True
    ).reshape(syn_total, cols)

    mine = hid // groups
    start = rec * mine
    all_preact = jnp.dot(
        all_latents, lax.dynamic_slice_in_dim(w_latent, start, mine, 1), preferred_element_type=F32
    ) + jnp.dot(
        all_table, lax.dynamic_slice_in_dim(class_embed, start, mine, 1), preferred_element_type=F32
    )
    all_hidden = jnp.maximum(all_preact, 0.0).astype(BF)
    grad_w_out = lax.dot_general(
        all_hidden, out_grad, (((0,), (0,)), ((), ())), preferred_element_type=F32
    )
    hidden_grad = lax.dot_general(
        out_grad,
        lax.dynamic_slice_in_dim(w_out, start, mine, 0),
        (((1,), (1,)), ((), ())),
        preferred_element_type=F32,
    )
    core = lax.axis_index("feat") % 2
    half = syn_total // 2
    hidden_grad = hidden_grad.reshape(2, half, mine)
    got = swap(pick(hidden_grad, 1 - core, 0).astype(BF), "feat", 1)
    hidden_grad = pick(hidden_grad, core, 0) + got.astype(F32)
    for bit in bits_of(feats)[1:]:
        send = hidden_grad.astype(BF)
        hidden_grad = send.astype(F32) + swap(send, "feat", bit).astype(F32)
    my_preact = lax.dynamic_slice_in_dim(all_preact, core * half, half, 0)
    pre_hidden = jnp.where(my_preact > 0, hidden_grad, 0.0).astype(BF)
    lhs = jnp.concatenate([all_latents, all_table], axis=1)
    lhs = lax.dynamic_slice_in_dim(lhs, core * half, half, 0)
    grads = lax.dot_general(lhs, pre_hidden, (((0,), (0,)), ((), ())), preferred_element_type=F32)
    grads = grads + swap(grads, "feat", 1)
    return grad_w_out, grads[:dz], grads[dz:]


def block(shape, index):
    return pl.BlockSpec(shape, index)


def sums(table, pre):
    co, si = cos_sin(pre)
    phi = jnp.concatenate([co.astype(BF), si.astype(BF)], axis=1)
    return jnp.dot(table, phi, preferred_element_type=F32)


def features_kernel(
    masks, last, real_total, syn_total, me_ref, real_labels_ref, syn_labels_ref, *refs
):
    count = 1 if last else len(masks)
    images = [refs[0].at[i] for i in range(len(masks))] if last else refs[:count]
    records_hbm, freq_ref = refs[count : count + 2]
    outs = refs[count + (4 if last else 3) : -4]
    wave, token = outs[-2:]
    records, real_table, syn_table, sem = refs[-4:]
    classes, total = real_table.shape
    size = 512
    steps = total // size
    step = pl.program_id(0)
    cols = images[0].shape[1]
    half = classes // 2
    token[...] = jnp.zeros_like(token)

    def copy(i):
        at = pl.ds(i * size, size)
        return pltpu.make_async_copy(records_hbm.at[at, :], records.at[at, :], sem.at[i])

    def work(wait):
        if wait:
            for i in range(steps):
                copy(i).start()
            ids = lax.broadcasted_iota(jnp.int32, (classes, total), 0)
            real_table[...] = jnp.where(ids == real_labels_ref[...], 1.0, 0.0).astype(BF)
            ids = lax.broadcasted_iota(jnp.int32, syn_table.shape, 0)
            syn_table[...] = jnp.where(ids == syn_labels_ref[...], 1.0, 0.0).astype(BF)
        syn_pre = None
        for mask, image in zip(masks, images):
            at = pl.multiple_of((me_ref[0] ^ mask) * cols, 128)
            d = jnp.dot(image[...], freq_ref[pl.ds(at, cols), :], preferred_element_type=F32)
            syn_pre = d if syn_pre is None else syn_pre + d
        freq = freq_ref[...]
        acc = None
        before = None
        for i in range(steps + 1):
            if i < steps:
                if wait:
                    copy(i).wait()
                pre = jnp.dot(records[i * size : (i + 1) * size, :], freq, preferred_element_type=F32)
            if i == 0:
                co, si = cos_sin(syn_pre)
                wave[0, 0] = co
                wave[0, 1] = si
                phi = jnp.concatenate([co.astype(BF), si.astype(BF)], axis=1)
                syn = jnp.dot(syn_table[...], phi, preferred_element_type=F32)
            else:
                d = sums(real_table[:, (i - 1) * size : i * size], before)
                acc = d if acc is None else acc + d
            before = pre
        gap = syn * (1.0 / syn_total) - acc * (1.0 / real_total)
        width = gap.shape[1] // 4
        return [
            jnp.concatenate(
                [gap[:, h * width : (h + 1) * width], gap[:, (h + 2) * width : (h + 3) * width]], axis=1
            )
            for h in range(2)
        ]

    if last:
        parts = work(True)
        for h in range(2):
            outs[0][h] = parts[h][:half]
            outs[1][h] = parts[h][half:]
        return
    send_a, keep_a, send_b, keep_b, both = outs[:5]

    @pl.when(step == 0)
    def _():
        for i in range(count):
            both[i] = images[i][...]
        parts = work(True)
        for h in range(2):
            send_a[0, h] = parts[h][:half].astype(BF)
            send_b[0, h] = parts[h][half:].astype(BF)

    @pl.when(step > 0)
    def _():
        parts = work(False)

        @pl.when(step == 1)
        def _():
            for h in range(2):
                send_a[0, h] = parts[h][:half].astype(BF)
                keep_b[h] = parts[h][half:]

        @pl.when(step == 2)
        def _():
            for h in range(2):
                keep_a[h] = parts[h][:half]
                send_b[0, h] = parts[h][half:].astype(BF)


def feature_sums(
    last, me, real_labels, syn_labels, masks, images, records, freq, classes, totals, after, waves=None
):
    total, k = records.shape
    n = freq.shape[1]
    rows, cols = images.shape[1:] if last else images[0].shape
    half = classes // 2
    tile = n // 4
    tiles = 1 if last else 3
    whole = lambda shape: block(shape, lambda j, me: (0,) * len(shape))
    kept = jax.ShapeDtypeStruct((2, half, tile), F32)
    sent = jax.ShapeDtypeStruct((2, 2, half, tile), BF)
    both = (len(masks), rows, cols)
    place = lambda j, me: me[5] ^ (0 if last else 3 - j)
    anywhere = pl.BlockSpec(memory_space=pl.ANY)
    shapes = [pltpu.HBM((4, 2, rows, tile), F32), jax.ShapeDtypeStruct((8, 128), F32)]
    specs = [block((1, 2, rows, tile), lambda j, me: (place(j, me), 0, 0, 0)), whole((8, 128))]
    if last:
        shapes = [kept, kept] + shapes
        specs = [whole(kept.shape), whole(kept.shape)] + specs
        images = (images,)
        extra = (after, waves)
    else:
        shapes = [sent, kept, sent, kept, jax.ShapeDtypeStruct(both, BF)] + shapes
        specs = [
            block((1, 2, half, tile), lambda j, me: (jnp.minimum(j, 1), 0, 0, 0)),
            whole(kept.shape),
            block((1, 2, half, tile), lambda j, me: (j // 2, 0, 0, 0)),
            whole(kept.shape),
            whole(both),
        ] + specs
        extra = (after,)
    grid_spec = pltpu.PrefetchScalarGridSpec(
        num_scalar_prefetch=1,
        grid=(tiles,),
        in_specs=[whole((1, total)), whole((1, rows))]
        + [whole(image.shape) for image in images]
        + [anywhere, block((k, tile), lambda j, me: (0, place(j, me)))]
        + [anywhere] * len(extra),
        out_specs=specs,
        scratch_shapes=[
            pltpu.VMEM((total, k), BF),
            pltpu.VMEM((classes, total), BF),
            pltpu.VMEM((classes, rows), BF),
            pltpu.SemaphoreType.DMA((total // 512,)),
        ],
    )
    return pl.pallas_call(
        functools.partial(features_kernel, masks, last, *totals),
        grid_spec=grid_spec,
        out_shape=shapes,
        input_output_aliases={7: 2} if last else {},
        compiler_params=pltpu.CompilerParams(vmem_limit_bytes=44 * 2**20),
        cost_estimate=pl.CostEstimate(
            flops=2 * (total + rows) * tiles * tile * (k + 2 * classes),
            bytes_accessed=2 * (total * k + k * tiles * tile),
            transcendentals=0,
        ),
    )(me, real_labels.reshape(1, -1), syn_labels.reshape(1, -1), *images, records, freq, *extra)


def stage_two_send_kernel(ka, ga, kb, gb, after, sa, sb, token):
    token[...] = jnp.zeros_like(token)
    sa[...] = (ka[...] + ga[0].astype(F32)).astype(BF)
    sb[...] = (kb[...] + gb[0].astype(F32)).astype(BF)


def stage_two_send(keep_a, got_a, keep_b, got_b, after):
    return pl.pallas_call(
        stage_two_send_kernel,
        in_specs=[pl.BlockSpec()] * 4 + [pl.BlockSpec(memory_space=pl.ANY)],
        out_shape=[jax.ShapeDtypeStruct(keep_a.shape, BF)] * 2 + [jax.ShapeDtypeStruct((8, 128), F32)],
        compiler_params=pltpu.CompilerParams(vmem_limit_bytes=10 * 2**20),
        cost_estimate=pl.CostEstimate(flops=0, bytes_accessed=3 * 2**20, transcendentals=0),
    )(keep_a, got_a, keep_b, got_b, after)


def stage_three_kernel(me_ref, na, fa, ga, nb, fb, gb, a, b, c, send, keep, token):
    token[...] = jnp.zeros_like(token)
    high = me_ref[3]
    half = na.shape[1]
    for flip, out in ((1, send), (0, keep)):
        at = high ^ flip
        out[:half] = (na[at] + fa[1, at].astype(F32) + ga[at].astype(F32)).astype(out.dtype)
        out[half:] = (nb[at] + fb[1, at].astype(F32) + gb[at].astype(F32)).astype(out.dtype)


def stage_three(me, keep_a, first_a, got_a, keep_b, first_b, got_b, after):
    _, half, width = keep_a.shape
    args = (keep_a, first_a, got_a, keep_b, first_b, got_b)
    whole = lambda shape: block(shape, lambda h, me: (0,) * len(shape))
    spec = pltpu.PrefetchScalarGridSpec(
        num_scalar_prefetch=1,
        grid=(1,),
        in_specs=[whole(x.shape) for x in args] + [pl.BlockSpec(memory_space=pl.ANY)] * 3,
        out_specs=[whole((2 * half, width))] * 2 + [whole((8, 128))],
    )
    return pl.pallas_call(
        stage_three_kernel,
        grid_spec=spec,
        out_shape=[jax.ShapeDtypeStruct((2 * half, width), t) for t in (BF, F32)]
        + [jax.ShapeDtypeStruct((8, 128), F32)],
        compiler_params=pltpu.CompilerParams(vmem_limit_bytes=12 * 2**20),
        cost_estimate=pl.CostEstimate(flops=0, bytes_accessed=3 * 2**20, transcendentals=0),
    )(me, *args, *after)


def gap_kernel(real_total, order, me_ref, keep_ref, got_ref, noise_ref, labels_ref, after, out_ref):
    classes = keep_ref.shape[0]
    rows = labels_ref.shape[1]
    gap = keep_ref[...] + got_ref[...].astype(F32) - noise_ref[...] * (1.0 / real_total)
    gap = (16.0 * gap).astype(BF)
    ids = lax.broadcasted_iota(jnp.int32, (classes, rows), 0)
    for i, mask in enumerate(order):
        table = jnp.where(ids == labels_ref[i : i + 1, :], 1.0, 0.0).astype(BF)
        out = lax.dot_general(table, gap, (((0,), (0,)), ((), ())), preferred_element_type=F32)
        out_ref[me_ref[4] ^ mask] = out.astype(BF)


def gap_rows(me, keep, got, noise, labels, real_total, order, after):
    classes, width = keep.shape
    groups, rows = labels.shape
    whole = lambda shape: block(shape, lambda h, me: (0,) * len(shape))
    spec = pltpu.PrefetchScalarGridSpec(
        num_scalar_prefetch=1,
        grid=(1,),
        in_specs=[whole(x.shape) for x in (keep, got, noise, labels)]
        + [pl.BlockSpec(memory_space=pl.ANY)],
        out_specs=whole((groups, rows, width)),
    )
    return pl.pallas_call(
        functools.partial(gap_kernel, real_total, order),
        grid_spec=spec,
        out_shape=jax.ShapeDtypeStruct((groups, rows, width), BF),
        compiler_params=pltpu.CompilerParams(vmem_limit_bytes=14 * 2**20),
        cost_estimate=pl.CostEstimate(
            flops=2 * groups * rows * classes * width, bytes_accessed=3 * 2**20, transcendentals=0
        ),
    )(me, keep, got, noise, labels, after)


NT = (((1,), (1,)), ((), ()))


def sent_kernel(me_ref, wave_ref, rows_ref, freq_ref, a, b, c, send_ref, pre_ref):
    tile = wave_ref.shape[3]
    part = tile // 2

    @pl.when(pl.program_id(0) == 0)
    def _():
        for place in range(4):
            for h in range(2):
                grad = rows_ref[4 * h + 2 * (place % 2) + place // 2].astype(F32)
                lanes = slice(h * part, (h + 1) * part)
                pre = wave_ref[place, 0, :, lanes] * grad[:, part:]
                pre = pre - wave_ref[place, 1, :, lanes] * grad[:, :part]
                at = place * tile + h * part
                pre_ref[:, at : at + part] = pre.astype(BF)

    out = lax.dot_general(freq_ref[...], pre_ref[...], NT, preferred_element_type=F32)
    send_ref[0] = out.astype(BF)


def kept_kernel(me_ref, pre_ref, freq_ref, keep_ref):
    keep_ref[0] = lax.dot_general(freq_ref[...], pre_ref[...], NT, preferred_element_type=F32)


def image_grads(me, freq, cols, arrays, after, kept=None):
    k, n = freq.shape
    sent = kept is None
    rows = arrays[1].shape[1] if sent else arrays[0].shape[0]
    count = 4 if sent else 2
    whole = lambda shape: block(shape, lambda s, me: (0,) * len(shape))

    def source(s, me):
        return (2 * (me[0] ^ (2 * (1 - s // 2)) ^ 1) + s % 2, 0) if sent else (2 * (me[0] ^ (2 * (1 - kept))) + s, 0)

    size = cols // 2
    out = block((1, size, rows), lambda s, me: (s // 2, s % 2, 0))
    shape = jax.ShapeDtypeStruct((2 if sent else 1, cols, rows), BF if sent else F32)
    pre = jax.ShapeDtypeStruct((rows, n), BF)
    spec = pltpu.PrefetchScalarGridSpec(
        num_scalar_prefetch=1,
        grid=(count,),
        in_specs=[whole(x.shape) for x in arrays]
        + [block((size, n), source)]
        + [pl.BlockSpec(memory_space=pl.ANY)] * len(after),
        out_specs=[out, whole(pre.shape)] if sent else out,
    )
    return pl.pallas_call(
        sent_kernel if sent else kept_kernel,
        grid_spec=spec,
        out_shape=[shape, pre] if sent else shape,
        compiler_params=pltpu.CompilerParams(vmem_limit_bytes=52 * 2**20),
        cost_estimate=pl.CostEstimate(flops=k * n * rows, bytes_accessed=k * n, transcendentals=0),
    )(me, *arrays, freq, *after)


def first_add_kernel(a, b, out):
    out[...] = (a[0] + b[0].astype(F32)).astype(BF)


def first_add(keep, got):
    _, cols, rows = keep.shape
    one = block((1, cols, rows), lambda h: (0, 0, 0))
    return pl.pallas_call(
        first_add_kernel,
        grid=(1,),
        in_specs=[one, one],
        out_specs=block((cols, rows), lambda h: (0, 0)),
        out_shape=jax.ShapeDtypeStruct((cols, rows), BF),
        compiler_params=pltpu.CompilerParams(vmem_limit_bytes=8 * 2**20),
        cost_estimate=pl.CostEstimate(flops=0, bytes_accessed=2**20, transcendentals=0),
    )(keep, got)


def out_kernel(keep, near, far, image, out):
    grad = (keep[0] + near[0].astype(F32) + far[...].astype(F32)).T
    grad = grad * (1.0 - jnp.square(image[...].astype(F32)))
    out[...] = grad.astype(BF)


def out_grads(keep, near, far, image):
    _, cols, rows = keep.shape
    one = lambda i: block((1, cols, rows), lambda h: (i, 0, 0))
    return pl.pallas_call(
        out_kernel,
        grid=(1,),
        in_specs=[one(0), one(1), block((cols, rows), lambda h: (0, 0)), block((rows, cols), lambda h: (0, 0))],
        out_specs=block((rows, cols), lambda h: (0, 0)),
        out_shape=jax.ShapeDtypeStruct(image.shape, BF),
        compiler_params=pltpu.CompilerParams(vmem_limit_bytes=8 * 2**20),
        cost_estimate=pl.CostEstimate(flops=0, bytes_accessed=2**20, transcendentals=0),
    )(keep, near, far, image)


def hidden_kernel(me_ref, w_ref, *refs):
    grads = refs[:4]
    send, keep = refs[5:]
    core = me_ref[0] % 2
    out = [lax.dot_general(w_ref[...], g[...], NT, preferred_element_type=F32) for g in grads]
    for i in range(2):
        keep[i] = jnp.where(core == 0, out[2 * i], out[2 * i + 1])
        send[i] = jnp.where(core == 0, out[2 * i + 1], out[2 * i]).astype(BF)


def hidden_grads(me, w_out, grads, mine, after):
    rows, cols = grads[0].shape
    whole = lambda shape: block(shape, lambda r, me: (0,) * len(shape))
    spec = pltpu.PrefetchScalarGridSpec(
        num_scalar_prefetch=1,
        grid=(1,),
        in_specs=[block((mine, cols), lambda r, me: (me[4], 0))] + [whole((rows, cols))] * 4
        + [pl.BlockSpec(memory_space=pl.ANY)],
        out_specs=[whole((2, mine, rows))] * 2,
    )
    return pl.pallas_call(
        hidden_kernel,
        grid_spec=spec,
        out_shape=[jax.ShapeDtypeStruct((2, mine, rows), t) for t in (BF, F32)],
        compiler_params=pltpu.CompilerParams(vmem_limit_bytes=8 * 2**20),
        cost_estimate=pl.CostEstimate(
            flops=8 * mine * cols * rows, bytes_accessed=2 * 5 * mine * cols, transcendentals=0
        ),
    )(me, w_out, *grads, after)


def add_kernel(a, b, out):
    out[...] = (a[...].astype(F32) + b[...].astype(F32)).astype(out.dtype)


def add(a, b, kind):
    return pl.pallas_call(
        add_kernel,
        out_shape=jax.ShapeDtypeStruct(a.shape, kind),
        compiler_params=pltpu.CompilerParams(vmem_limit_bytes=8 * 2**20),
        cost_estimate=pl.CostEstimate(flops=0, bytes_accessed=2**20, transcendentals=0),
    )(a, b)


def weight_kernel(me_ref, hidden_ref, *refs):
    out_ref, token = refs[-2:]
    token[...] = jnp.zeros_like(token)
    acc = None
    for mask, grad in enumerate(refs[:-2]):
        rows = grad.shape[0]
        at = slice(mask * rows, (mask + 1) * rows)
        d = jnp.dot(hidden_ref[:, at], grad[...], preferred_element_type=F32)
        acc = d if acc is None else acc + d
    out_ref[...] = acc


def weight_grads(me, hidden, grads):
    rows, cols = grads[0].shape
    mine, total = hidden.shape
    spec = pltpu.PrefetchScalarGridSpec(
        num_scalar_prefetch=1,
        grid=(1,),
        in_specs=[block((mine, total), lambda h, me: (0, 0))]
        + [block((rows, cols), lambda h, me: (0, 0)) for _ in grads],
        out_specs=[block((mine, cols), lambda h, me: (0, 0)), block((8, 128), lambda h, me: (0, 0))],
    )
    return pl.pallas_call(
        weight_kernel,
        grid_spec=spec,
        out_shape=[pltpu.HBM((mine, cols), F32), jax.ShapeDtypeStruct((8, 128), F32)],
        compiler_params=pltpu.CompilerParams(vmem_limit_bytes=12 * 2**20),
        cost_estimate=pl.CostEstimate(
            flops=2 * mine * total * cols, bytes_accessed=4 * 2**20, transcendentals=0
        ),
    )(me, hidden, *grads)


def last_kernel(me_ref, gate_ref, lhs_ref, p0, q0, p1, q1, after, out_ref):
    rows = p0.shape[2]
    acc = None
    for h, (p, q) in enumerate(((p0, q0), (p1, q1))):
        for i in range(2):
            place = 4 * (me_ref[0] % 2) + 2 * i + h
            at = pl.ds(pl.multiple_of(place * rows, 128), rows)
            grad = p[i].astype(F32) + q[i].astype(F32)
            grad = jnp.where(gate_ref[:, at].astype(F32) > 0, grad, 0.0).astype(BF)
            d = lax.dot_general(lhs_ref[:, at], grad, NT, preferred_element_type=F32)
            acc = d if acc is None else acc + d
    out_ref[...] = acc


def last_grads(me, gate, lhs, parts, after):
    count, total = lhs.shape
    mine = gate.shape[0]
    args = (gate, lhs, *parts)
    whole = lambda shape: block(shape, lambda h, me: (0,) * len(shape))
    spec = pltpu.PrefetchScalarGridSpec(
        num_scalar_prefetch=1,
        grid=(1,),
        in_specs=[whole(x.shape) for x in args] + [pl.BlockSpec(memory_space=pl.ANY)],
        out_specs=whole((count, mine)),
    )
    return pl.pallas_call(
        last_kernel,
        grid_spec=spec,
        out_shape=jax.ShapeDtypeStruct((count, mine), F32),
        compiler_params=pltpu.CompilerParams(vmem_limit_bytes=12 * 2**20),
        cost_estimate=pl.CostEstimate(
            flops=total * count * mine, bytes_accessed=2 * 2**20, transcendentals=0
        ),
    )(me, *args, after)


def outputs_kernel(own, other, latent, embed):
    dz = latent.shape[0]
    latent[...] = own[:dz] + other[:dz]
    embed[...] = own[dz:] + other[dz:]


def outputs(own, other, dz):
    count, mine = own.shape
    return pl.pallas_call(
        outputs_kernel,
        out_shape=[jax.ShapeDtypeStruct((c, mine), F32) for c in (dz, count - dz)],
        compiler_params=pltpu.CompilerParams(vmem_limit_bytes=8 * 2**20),
        cost_estimate=pl.CostEstimate(flops=0, bytes_accessed=2**20, transcendentals=0),
    )(own, other)


def tie(first, later):
    return lax.optimization_barrier((first, later))


def eight_by_four(
    records, real_labels, frequencies, class_noise, latents, syn_labels, w_latent, class_embed, w_out
):
    classes, hid = class_embed.shape
    groups = lax.axis_size("rec")
    rec = lax.axis_index("rec")
    feat = lax.axis_index("feat")
    rows, dz = latents.shape
    cols = w_out.shape[1]
    real_total = records.shape[0] * groups
    syn_total = rows * groups
    x, z_low, z_high = rec % 2, (rec // 2) % 2, rec // 4
    place = 2 * x + z_low
    me = jnp.stack([feat, x, z_low, z_high, rec, place]).astype(jnp.int32)

    table = one_hot(syn_labels, classes, BF)
    preact = jnp.dot(latents, w_latent, preferred_element_type=F32) + jnp.dot(
        table, class_embed, preferred_element_type=F32
    )
    hidden = jnp.maximum(preact, 0.0).astype(BF)
    own = jnp.tanh(jnp.dot(hidden, w_out, preferred_element_type=F32)).astype(BF)
    far = swap(own, "feat", 2)

    order = (0, 4, 2, 6, 1, 5, 3, 7)
    label_row = jnp.zeros((16, dz), BF).at[0, :].set(syn_labels.astype(BF))
    packed = jnp.concatenate([latents, label_row], axis=0)[None]
    far, pair = tie(far, swap(packed, "rec", 4))
    images = [own, far, swap(own, "feat", 1), swap(far, "feat", 1)]
    packed, real_labels = tie(jnp.concatenate([packed, pair], axis=0), real_labels)
    pair = swap(packed, "rec", 2)

    masks = (0, 2, 1, 3)
    totals = (real_total, syn_total)
    send_a, keep_a, send_b, keep_b, both, waves, token = feature_sums(
        False, me, real_labels, syn_labels, masks, images, records, frequencies, classes, totals, me
    )
    first_a = swap(send_a, "rec", 1)
    first_b = swap(send_b, "rec", 2)
    pair, token = tie(pair, token)
    last_a, last_b, waves, token = feature_sums(
        True, me, real_labels, syn_labels, masks, both, records, frequencies, classes, totals, token, waves
    )

    send_a, send_b, token = stage_two_send(keep_a, first_a, keep_b, first_b, token)
    got_a = swap(send_a, "rec", 2)
    got_b = swap(send_b, "rec", 1)
    part = frequencies.shape[1] // groups
    noise = lax.dynamic_slice_in_dim(class_noise, (2 * place + z_high) * part, part, 2)
    noise = noise.reshape(classes, 2 * part)
    send, keep, token = stage_three(me, last_a, first_a, got_a, last_b, first_b, got_b, (noise, token, token))
    got = swap(send, "rec", 4)
    pair, token = tie(pair, token)
    quad = jnp.concatenate([packed, pair], axis=0)
    eight = jnp.concatenate([quad, swap(quad, "rec", 1)], axis=0)
    all_latents = eight[:, :rows].reshape(syn_total, dz)
    all_labels = eight[:, rows].reshape(syn_total).astype(jnp.int32)
    all_table = one_hot(all_labels, classes, BF)
    mine = hid // groups
    lhs = jnp.concatenate([all_latents, all_table], axis=1).T
    w = jnp.concatenate(
        [
            lax.dynamic_slice_in_dim(w_latent, rec * mine, mine, 1),
            lax.dynamic_slice_in_dim(class_embed, rec * mine, mine, 1),
        ],
        axis=0,
    )
    all_preact = lax.dot_general(w, lhs, (((0,), (0,)), ((), ())), preferred_element_type=F32)
    all_hidden = jnp.maximum(all_preact, 0.0).astype(BF)
    gate = (all_preact > 0).astype(BF)

    feat_grad = gap_rows(me, keep, got, noise, all_labels.reshape(groups, rows), real_total, order, token)
    feat_grad = lax.all_to_all(feat_grad, "rec", 0, 0, tiled=True)

    send, pre_grad = image_grads(
        me, frequencies, cols, (waves, feat_grad), (gate, all_hidden, lhs)
    )
    near = swap(send, "feat", 1)
    keep = image_grads(me, frequencies, cols, (pre_grad,), (), 0)
    far = swap(first_add(keep, near), "feat", 2)
    keep = image_grads(me, frequencies, cols, (pre_grad,), (), 1)
    out_grad = out_grads(keep, near, far, own)

    by = {0: out_grad}
    by[4] = swap(out_grad, "rec", 4)
    by[2] = swap(out_grad, "rec", 2)
    by[1] = swap(out_grad, "rec", 1)
    by[2], by[1] = tie(by[2], by[1])
    by[3] = swap(by[2], "rec", 1)
    by[6] = swap(by[4], "rec", 2)
    by[5] = swap(by[4], "rec", 1)

    def reduced(send, keep):
        part = add(keep, swap(send, "feat", 1), BF)
        return [part, swap(part, "feat", 2)]

    by[7] = swap(by[6], "rec", 1)
    send, keep = hidden_grads(me, w_out, [by[i] for i in range(4)], mine, by[5])
    parts = reduced(send, keep)
    parts += reduced(*hidden_grads(me, w_out, [by[4 + i] for i in range(4)], mine, parts[0]))
    grad_w_out, token = weight_grads(me, all_hidden, [by[mask] for mask in order])
    grads = last_grads(me, gate, lhs, parts, token)
    grad_w_latent, grad_embed = outputs(grads, swap(grads, "feat", 1), dz)
    return grad_w_out, grad_w_latent, grad_embed


def solution(mesh):
    shape = (mesh.shape["rec"], mesh.shape["feat"])
    in_specs = (
        P("rec", None),
        P("rec"),
        P(None, "feat"),
        P(None, None, "feat"),
        P("rec", None),
        P("rec"),
        P(),
        P(),
        P(None, "feat"),
    )
    out_specs = (P("rec", "feat"), P(None, "rec"), P(None, "rec"))
    return jax.shard_map(
        eight_by_four if shape == (8, 4) else general, mesh=mesh, in_specs=in_specs, out_specs=out_specs, check_vma=False
    )
```
